32 devices in a mesh: dp: 4 (over y, x), ctx: 8 (over z, core).
Axes of the slice: x: 2, y: 2, z: 4, core: 2. Of those that a mesh axis runs over, the one named last changes fastest.
Arguments:
- tokens: bfloat16 [1024, 8, 1024], P('ctx', 'dp'), may hold values from -6 to 6
- cotangent: bfloat16 [1024, 8, 1024], P('ctx', 'dp'), may hold values from -6 to 6
- segments: int32 [8, 1024], P('dp'), may hold values from 0 to 8, as said below
- w_qkv: bfloat16 [1024, 3072], P(('dp', 'ctx')), may hold values from -0.1875 to 0.1875
- b_qkv: bfloat16 [3072], P(('dp', 'ctx')), may hold values from -2 to 2
- w_out: bfloat16 [1024, 1024], P(('dp', 'ctx')), may hold values from -0.75 to 0.75
- b_out: bfloat16 [1024], P(('dp', 'ctx')), may hold values from -2 to 2
- w_up: bfloat16 [1024, 4096], P(('dp', 'ctx')), may hold values from -0.1875 to 0.1875
- b_up: bfloat16 [4096], P(('dp', 'ctx')), may hold values from -2 to 2
- w_down: bfloat16 [4096, 1024], P(('dp', 'ctx')), may hold values from -0.09375 to 0.09375
- b_down: bfloat16 [1024], P(('dp', 'ctx')), may hold values from -2 to 2
- norm1_gain: bfloat16 [1024], P(('dp', 'ctx')), may hold values from 0.099609375 to 1.8984375
- norm1_bias: bfloat16 [1024], P(('dp', 'ctx')), may hold values from -2 to 2
- norm2_gain: bfloat16 [1024], P(('dp', 'ctx')), may hold values from 0.099609375 to 1.8984375
- norm2_bias: bfloat16 [1024], P(('dp', 'ctx')), may hold values from -2 to 2
Outputs:
- mixed: bfloat16 [1024, 8, 1024], P('ctx', 'dp')
- tokens_grad: bfloat16 [1024, 8, 1024], P('ctx', 'dp')
- w_qkv_grad: float32 [1024, 3072], P(('dp', 'ctx'))
- b_qkv_grad: float32 [3072], P(('dp', 'ctx'))
- w_out_grad: float32 [1024, 1024], P(('dp', 'ctx'))
- b_out_grad: float32 [1024], P(('dp', 'ctx'))
- w_up_grad: float32 [1024, 4096], P(('dp', 'ctx'))
- b_up_grad: float32 [4096], P(('dp', 'ctx'))
- w_down_grad: float32 [4096, 1024], P(('dp', 'ctx'))
- b_down_grad: float32 [1024], P(('dp', 'ctx'))
- norm1_gain_grad: float32 [1024], P(('dp', 'ctx'))
- norm1_bias_grad: float32 [1024], P(('dp', 'ctx'))
- norm2_gain_grad: float32 [1024], P(('dp', 'ctx'))
- norm2_bias_grad: float32 [1024], P(('dp', 'ctx'))
The draws below stay inside these ranges and needn't reach their ends.
Inputs may be any that keep to these rules, and one draw needn't show every extreme that they name: `segments`: in each sequence the ids never fall before a tail of one or more padding zeros; id 0 appears only there. Of the 2 sequences of each index of dp, one holds a document that starts within its first 128 tokens and ends within its last 128.
All inputs are finite; a program needn't handle non-finite values.
Results may differ from the reference program's by a relative error of at most 0.011.
Values may be sent and summed in bfloat16 or wider, within the bound.
A program may use at most 256 MiB of HBM per device.

```python
from functools import partial
import jax
import jax.numpy as jnp
from jax import lax

D = 1024
HEADS = 16
HEAD = 64
ROT = 16
FF = 4096
SEQ = 1024
MICRO = 2
DOCS = 8
TOK_DEV = 128
SEQS = 8


def draw_segments(key, part):
    key = jax.random.fold_in(key, 11)
    key_list = jax.random.split(key, 4)
    head_reach = max(TOK_DEV // 2, 2)
    positions = jnp.arange(SEQ, dtype=jnp.int32)
    wide_cuts = jax.random.randint(key_list[0], (SEQS, DOCS - 1), 1, SEQ)
    head_cuts = jax.random.randint(key_list[1], (SEQS, DOCS - 1), 1, head_reach)
    chosen = jax.random.randint(key_list[2], (SEQS // MICRO,), 0, MICRO)
    spanning = jnp.arange(SEQS, dtype=jnp.int32) % MICRO == jnp.repeat(chosen, MICRO)
    doc_cuts = jnp.where(spanning[:, None], head_cuts, wide_cuts)
    padding = jax.random.randint(key_list[3], (SEQS,), 1, head_reach + 1)
    doc_ids = 1 + jnp.sum((doc_cuts[:, :, None] <= positions[None, None, :]).astype(jnp.int32), axis=1)
    return jnp.where(positions[None, :] >= SEQ - padding[:, None], 0, doc_ids).astype(jnp.int32)


def steps_of(rng, extent, shards, least, top_value):
    level, own = 1.0, jax.random.fold_in(rng, 6)
    for position, parts in shards:
        steps = jnp.exp(jax.random.uniform(jax.random.fold_in(own, position), (parts,), jnp.float32, least / len(shards), top_value / len(shards)))
        level = level * jnp.repeat(steps, extent[position] // parts).reshape([-1 if axis == position else 1 for axis in range(len(extent))])
    return level


def scatter_about(key, dims, scale, bound, cuts=(), kind=jnp.bfloat16):
    array = scale * jax.random.normal(key, dims, jnp.float32)
    if cuts:
        array = array * steps_of(key, dims, cuts, -0.22, 0.18)
    return jnp.clip(array, -bound, bound).astype(kind)


def setup_inputs(seed: int = 0) -> dict:
    streams_of = jax.random.split(jax.random.key(seed), 16)
    tokens = scatter_about(streams_of[0], (SEQ, SEQS, D), 1.0, 6.0, ((0, 8), (1, 4)))
    cotangent = scatter_about(streams_of[1], (SEQ, SEQS, D), 1.0, 6.0, ((0, 8), (1, 4)))
    segments = draw_segments(jax.random.fold_in(streams_of[15], 71), 0)
    w_qkv = scatter_about(streams_of[3], (D, 3 * D), D ** -0.5, 0.1875, ((0, 32),))
    b_qkv = scatter_about(streams_of[4], (3 * D,), 0.3, 2.0, ((0, 32),))
    w_out = scatter_about(streams_of[5], (D, D), (D // 16) ** -0.5, 0.75, ((0, 32),))
    b_out = scatter_about(streams_of[6], (D,), 0.3, 2.0, ((0, 32),))
    w_up = scatter_about(streams_of[7], (D, FF), D ** -0.5, 0.1875, ((0, 32),))
    b_up = scatter_about(streams_of[8], (FF,), 0.3, 2.0, ((0, 32),))
    w_down = scatter_about(streams_of[9], (FF, D), FF ** -0.5, 0.09375, ((0, 32),))
    b_down = scatter_about(streams_of[10], (D,), 0.3, 2.0, ((0, 32),))
    norm1_gain = jnp.clip(1.0 + 0.18 * jax.random.normal(streams_of[11], (D,), jnp.float32), 0.099609375, 1.8984375).astype(jnp.bfloat16)
    norm1_bias = scatter_about(streams_of[12], (D,), 0.3, 2.0, ((0, 32),))
    norm2_gain = jnp.clip(1.0 + 0.18 * jax.random.normal(streams_of[13], (D,), jnp.float32), 0.099609375, 1.8984375).astype(jnp.bfloat16)
    norm2_bias = scatter_about(streams_of[14], (D,), 0.3, 2.0, ((0, 32),))
    return {"tokens": tokens, "cotangent": cotangent, "segments": segments, "w_qkv": w_qkv, "b_qkv": b_qkv, "w_out": w_out, "b_out": b_out, "w_up": w_up, "b_up": b_up, "w_down": w_down, "b_down": b_down, "norm1_gain": norm1_gain, "norm1_bias": norm1_bias, "norm2_gain": norm2_gain, "norm2_bias": norm2_bias}


@jax.custom_vjp
def low(v):
    return lax.optimization_barrier(v.astype(jnp.bfloat16)).astype(jnp.float32)

@jax.custom_vjp
def low_back(v):
    return v

def low_keep(v):
    return (low(v), None)

def low_pass(kept, grad):
    return (grad,)

def back_keep(v):
    return (v, None)

def back_low(kept, grad):
    return (low(grad),)
low.defvjp(low_keep, low_pass)
low_back.defvjp(back_keep, back_low)

def layer_norm(values, gain, shift):
    center = lax.optimization_barrier(jnp.mean(values, axis=-1, keepdims=True))
    centered = values - center
    spread = lax.optimization_barrier(jnp.mean(centered * centered, axis=-1, keepdims=True))
    return centered * lax.rsqrt(spread + 1e-05) * gain + shift

def rotary_tables(positions):
    half_rot = ROT // 2
    inverse = 10000.0 ** (-(2.0 * jnp.arange(half_rot, dtype=jnp.float32)) / ROT)
    angles = positions[:, None] * inverse[None, :]
    angles = jnp.concatenate([angles, angles], axis=-1)
    return (jnp.cos(angles)[:, None, :], jnp.sin(angles)[:, None, :])

def rotate(values, cosine, sine):
    half_rot = ROT // 2
    leading = values[..., :ROT]
    turned = jnp.concatenate([-leading[..., half_rot:], leading[..., :half_rot]], axis=-1)
    return jnp.concatenate([leading * cosine + turned * sine, values[..., ROT:]], axis=-1)

def allowed(query_pos, key_pos, query_docs, key_docs):
    same_doc = (key_docs[None, :] == query_docs[:, None]) & (query_docs[:, None] > 0)
    causal = key_pos[None, :] <= query_pos[:, None]
    return same_doc & causal | (key_pos[None, :] == query_pos[:, None])

def sequence_forward(params, pair):
    inputs_f, doc_ids = pair
    w_qkv, b_qkv, w_out, b_out, w_up, b_up, w_down, b_down, gain_one, shift_one, gain_two, shift_two = params
    highest = lax.Precision.HIGHEST
    normed_one = low(layer_norm(inputs_f, gain_one, shift_one))
    normed_two = low(layer_norm(inputs_f, gain_two, shift_two))
    joined = low_back(jnp.dot(normed_one, w_qkv, precision=highest) + b_qkv)
    joined = joined.reshape(SEQ, 3, HEADS, HEAD)
    key_pos = jnp.arange(SEQ, dtype=jnp.int32)
    cosine, sine = rotary_tables(key_pos.astype(jnp.float32))
    queries = low(rotate(joined[:, 0], cosine, sine))
    keys_rot = low(rotate(joined[:, 1], cosine, sine))
    values_low = low(joined[:, 2])
    row_block = min(512, SEQ)
    score_scale = HEAD ** (-0.5)

    def attend(index):
        row_start = index * row_block
        query_part = lax.dynamic_slice_in_dim(queries, row_start, row_block, 0)
        query_pos = row_start + jnp.arange(row_block, dtype=jnp.int32)
        query_docs = lax.dynamic_slice_in_dim(doc_ids, row_start, row_block, 0)
        raw = jnp.einsum('qhd,khd->hqk', query_part, keys_rot, precision=highest) * score_scale
        raw = low_back(raw)
        permitted = allowed(query_pos, key_pos, query_docs, doc_ids)
        masked = jnp.where(permitted[None], raw, -1e+30)
        row_max = lax.optimization_barrier(jnp.max(masked, axis=-1, keepdims=True))
        weights = jnp.exp(masked - row_max)
        probs = low(weights / lax.optimization_barrier(jnp.sum(weights, axis=-1, keepdims=True)))
        return jnp.einsum('hqk,khd->qhd', probs, values_low, precision=highest)
    pieces = lax.map(jax.checkpoint(attend), jnp.arange(SEQ // row_block, dtype=jnp.int32))
    context = pieces.reshape(SEQ, HEADS * HEAD)
    context = low(low_back(context))
    attention = jnp.dot(context, w_out, precision=highest) + b_out
    act = low_back(jnp.dot(normed_two, w_up, precision=highest) + b_up)
    hidden = low(jax.nn.gelu(act, approximate=False))
    feed = jnp.dot(hidden, w_down, precision=highest) + b_down
    return inputs_f + attention + feed

def reference(tokens, cotangent, segments, w_qkv, b_qkv, w_out, b_out, w_up, b_up, w_down, b_down, norm1_gain, norm1_bias, norm2_gain, norm2_bias):
    params = tuple((p.astype(jnp.float32) for p in (w_qkv, b_qkv, w_out, b_out, w_up, b_up, w_down, b_down, norm1_gain, norm1_bias, norm2_gain, norm2_bias)))
    inputs_f = jnp.transpose(tokens.astype(jnp.float32), (1, 0, 2))

    def forward(inputs_all, weights_all):
        return lax.map(jax.checkpoint(partial(sequence_forward, weights_all)), (inputs_all, segments))
    result, pullback = jax.vjp(forward, inputs_f, params)
    back = jnp.transpose(cotangent.astype(jnp.float32), (1, 0, 2))
    grad_in, grads = pullback(back)
    mixed = jnp.transpose(result, (1, 0, 2)).astype(jnp.bfloat16)
    tokens_grad = jnp.transpose(grad_in, (1, 0, 2)).astype(jnp.bfloat16)
    return (mixed, tokens_grad, grads[0], grads[1], grads[2], grads[3], grads[4], grads[5], grads[6], grads[7], grads[8], grads[9], grads[10], grads[11])
```

```python
from functools import partial

import jax
import jax.numpy as jnp
from jax import lax
from jax.experimental import pallas as pl
from jax.experimental.pallas import tpu as pltpu
from jax.sharding import PartitionSpec as P

HEAD = 64
ROT = 16
MIB = 1 << 20
MESH = pl.DeviceIdType.MESH
ANY = pl.BlockSpec(memory_space=pl.ANY)
F32 = jnp.float32
BF16 = jnp.bfloat16


class Place:
    def __init__(self, ndp, n):
        self.ndp, self.n, self.nz = ndp, n, n // 2
        self.dp = lax.axis_index("dp")
        self.c = lax.axis_index("ctx")
        self.z = self.c // 2
        self.core = lax.rem(self.c, 2)
        self.sib = self.c + 1 - 2 * self.core
        self.has_up = self.z + 1 < self.nz
        self.has_down = self.z > 0

    def barrier(self, ctx_all, dp_all):
        bar = pltpu.get_barrier_semaphore()
        count = 0
        if ctx_all:
            for j in range(1, self.n):
                peer = lax.rem(self.c + j, self.n)
                pl.semaphore_signal(bar, inc=1, device_id=(self.dp, peer), device_id_type=MESH)
                count += 1
        else:
            pl.semaphore_signal(bar, inc=1, device_id=(self.dp, self.sib), device_id_type=MESH)
            count += 1
            for ok, peer in ((self.has_up, self.c + 2), (self.has_down, self.c - 2)):

                @pl.when(ok)
                def _():
                    pl.semaphore_signal(bar, inc=1, device_id=(self.dp, peer), device_id_type=MESH)

        if dp_all:
            for j in range(1, self.ndp):
                peer = lax.rem(self.dp + j, self.ndp)
                pl.semaphore_signal(bar, inc=1, device_id=(peer, self.c), device_id_type=MESH)
                count += 1
        if not ctx_all:
            count = count + self.has_up.astype(jnp.int32) + self.has_down.astype(jnp.int32)
        pl.semaphore_wait(bar, count)


def remote(src, dst, send, recv, dp, c):
    return pltpu.make_async_remote_copy(
        src_ref=src,
        dst_ref=dst,
        send_sem=send,
        recv_sem=recv,
        device_id=(dp, c),
        device_id_type=MESH,
    )


class Gather:
    def __init__(self, at, src, dst, tok, sends, recvs):
        self.at, self.src, self.dst, self.tok, self.sends, self.recvs = at, src, dst, tok, sends, recvs

    def rows(self, c):
        return self.dst.at[:, pl.ds(pl.multiple_of(c * self.tok, self.tok), self.tok)]

    def copy(self, block, slot, c, src=None):
        at = self.at
        src = self.rows(block) if src is None else src
        return remote(src, self.rows(block), self.sends.at[slot], self.recvs.at[block], at.dp, c)

    def start(self):
        at = self.at

        @pl.when(at.has_up)
        def _():
            self.copy(at.c, 0, at.c + 2, self.src).start()

        @pl.when(at.has_down)
        def _():
            self.copy(at.c, 1, at.c - 2, self.src).start()

        self.copy(at.c, 2, at.sib, self.src).start()

    def step(self, k):
        at = self.at
        low, high = at.c - 2 * k, at.c + 2 * k

        @pl.when(at.z >= k)
        def _():
            self.copy(low, 0, at.c).wait_recv()

            @pl.when(at.has_up)
            def _():
                self.copy(low, 3 * k, at.c + 2).start()

            self.copy(low, 3 * k + 2, at.sib).start()

        @pl.when(at.z + k < at.nz)
        def _():
            self.copy(high, 0, at.c).wait_recv()

            @pl.when(at.has_down)
            def _():
                self.copy(high, 3 * k + 1, at.c - 2).start()

            self.copy(high, 3 * at.nz + k, at.sib).start()

    def finish(self):
        at = self.at
        for z in range(at.nz):
            self.copy(2 * z + 1 - at.core, 0, at.c).wait_recv()
        self.copy(at.c, 2, at.sib, self.src).wait_send()
        for k in range(at.nz):

            @pl.when((at.z >= k) & at.has_up)
            def _():
                self.copy(at.c, 3 * k, at.c).wait_send()

            @pl.when((at.z + k < at.nz) & at.has_down)
            def _():
                self.copy(at.c, 3 * k + 1, at.c).wait_send()

            if k:

                @pl.when(at.z >= k)
                def _():
                    self.copy(at.c, 3 * k + 2, at.c).wait_send()

                @pl.when(at.z + k < at.nz)
                def _():
                    self.copy(at.c, 3 * at.nz + k, at.c).wait_send()


def gather_slots(nz):
    return 4 * nz


class Exchange:
    def __init__(self, at, axis, src, dst, sends, recvs):
        self.at, self.axis, self.src, self.dst, self.sends, self.recvs = at, axis, src, dst, sends, recvs
        self.me, self.count = (at.c, at.n) if axis == "ctx" else (at.dp, at.ndp)

    def copy(self, peer, sender):
        at = self.at
        to = (at.dp, peer) if self.axis == "ctx" else (peer, at.c)
        return remote(self.src(peer), self.dst(sender), self.sends.at[peer], self.recvs.at[sender], *to)

    def start(self):
        for j in range(1, self.count):
            self.copy(lax.rem(self.me + j, self.count), self.me).start()

    def wait_recv(self):
        for j in range(1, self.count):
            peer = lax.rem(self.me + j, self.count)
            self.copy(peer, peer).wait_recv()

    def wait_send(self):
        for j in range(1, self.count):
            peer = lax.rem(self.me + j, self.count)
            self.copy(peer, self.me).wait_send()


def gather_kernel(ndp, n, tok_ref, cot_ref, wp_ref, wd_ref, wo_ref, vec_ref, x_out, g_out, w_out, wd_out, wo_out, vec_out, *sems):
    at = Place(ndp, n)
    tok = tok_ref.shape[1]
    (x_send, x_recv, g_send, g_recv, w1s, w1r, w2s, w2r, v1s, v1r, v2s, v2r, ds, dr, o1s, o1r, o2s, o2r, local) = sems
    at.barrier(True, True)
    own = (
        pltpu.make_async_copy(wp_ref.at[at.c], w_out.at[at.dp, at.c], local.at[0]),
        pltpu.make_async_copy(vec_ref, vec_out.at[at.dp, at.c], local.at[1]),
        pltpu.make_async_copy(wd_ref, wd_out.at[at.dp], local.at[2]),
        pltpu.make_async_copy(tok_ref, x_out.at[:, pl.ds(pl.multiple_of(at.c * tok, tok), tok)], local.at[3]),
        pltpu.make_async_copy(cot_ref, g_out.at[:, pl.ds(pl.multiple_of(at.c * tok, tok), tok)], local.at[4]),
    )
    for copy in own:
        copy.start()
    down_w = Exchange(at, "dp", lambda p: wd_ref, lambda s: wd_out.at[s], ds, dr)
    cols = Exchange(at, "ctx", lambda p: wp_ref.at[p], lambda s: w_out.at[at.dp, s], w1s, w1r)
    vecs = Exchange(at, "ctx", lambda p: vec_ref, lambda s: vec_out.at[at.dp, s], v1s, v1r)
    plane_w = Exchange(at, "dp", lambda p: w_out.at[at.dp], lambda s: w_out.at[s], w2s, w2r)
    plane_v = Exchange(at, "dp", lambda p: vec_out.at[at.dp], lambda s: vec_out.at[s], v2s, v2r)
    plane_o = Exchange(at, "dp", lambda p: wo_out, lambda s: wo_out, o2s, o2r)
    cols.start()
    vecs.start()
    index = at.dp * n + at.c
    heads_of, slot = index // ndp, lax.rem(index, ndp)

    def out_rows(b, c):
        return remote(wo_ref, wo_out.at[b], o1s, o1r.at[b], at.dp, c)

    @pl.when(heads_of != at.c)
    def _():
        out_rows(slot, heads_of).start()

    own_rows = pltpu.make_async_copy(wo_ref, wo_out.at[slot], local.at[5])

    @pl.when(heads_of == at.c)
    def _():
        own_rows.start()

    down_w.start()
    x_ag = Gather(at, tok_ref, x_out, tok, x_send, x_recv)
    g_ag = Gather(at, cot_ref, g_out, tok, g_send, g_recv)
    x_ag.start()
    own[0].wait()
    cols.wait_recv()
    plane_w.start()
    own[1].wait()
    vecs.wait_recv()
    plane_v.start()
    first = at.c * ndp // n

    @pl.when(at.dp == first)
    def _():
        for b in range(ndp):
            src = lax.rem(at.c * ndp + b, n)

            @pl.when(src != at.c)
            def _():
                out_rows(b, at.c).wait_recv()

            @pl.when(src == at.c)
            def _():
                own_rows.wait()

        plane_o.start()

    for k in range(1, at.nz):
        x_ag.step(k)
        if k == 1:
            g_ag.start()
    for k in range(1, at.nz):
        g_ag.step(k)
    x_ag.finish()
    g_ag.finish()

    @pl.when(heads_of != at.c)
    def _():
        out_rows(slot, heads_of).wait_send()

    @pl.when((heads_of == at.c) & (at.dp != first))
    def _():
        own_rows.wait()

    @pl.when(at.dp == first)
    def _():
        plane_o.wait_send()

    @pl.when(at.dp != first)
    def _():
        plane_o.copy(first, first).wait_recv()

    for copy in own[2:]:
        copy.wait()
    for part in (down_w, plane_w, plane_v):
        part.wait_recv()
    for part in (down_w, cols, vecs, plane_w, plane_v):
        part.wait_send()


def gather_all(ndp, n, tok, cot, wp, wd, wo, vec):
    mb, rows, width = tok.shape
    dma = pltpu.SemaphoreType.DMA
    slots = gather_slots(n // 2)
    return pl.pallas_call(
        partial(gather_kernel, ndp, n),
        out_shape=(
            jax.ShapeDtypeStruct((mb, rows * n, width), BF16),
            jax.ShapeDtypeStruct((mb, rows * n, width), BF16),
            jax.ShapeDtypeStruct((ndp,) + wp.shape, BF16),
            jax.ShapeDtypeStruct((ndp,) + wd.shape, BF16),
            jax.ShapeDtypeStruct((ndp,) + wo.shape, BF16),
            jax.ShapeDtypeStruct((ndp, n) + vec.shape, vec.dtype),
        ),
        in_specs=[ANY] * 6,
        out_specs=[ANY] * 6,
        scratch_shapes=[
            dma((slots,)), dma((n,)), dma((slots,)), dma((n,)),
            dma((n,)), dma((n,)), dma((ndp,)), dma((ndp,)),
            dma((n,)), dma((n,)), dma((ndp,)), dma((ndp,)),
            dma((ndp,)), dma((ndp,)),
            dma, dma((ndp,)), dma((ndp,)), dma((ndp,)),
            dma((6,)),
        ],
        compiler_params=pltpu.CompilerParams(collective_id=0, has_side_effects=True),
    )(tok, cot, wp, wd, wo, vec)


class Scatter:
    def __init__(self, at, part, out, sib_buf, low_buf, high_buf, stage, tok, sems):
        self.at, self.part, self.out, self.tok = at, part, out, tok
        self.sib_buf, self.low_buf, self.high_buf, self.stage = sib_buf, low_buf, high_buf, stage
        self.s_send, self.s_recv, self.up_send, self.up_recv, self.dn_send, self.dn_recv = sems

    def rows(self, c):
        return pl.ds(pl.multiple_of(c * self.tok, self.tok), self.tok)

    def cross(self, z):
        at = self.at
        src = self.part.at[:, self.rows(2 * z + 1 - at.core)]
        return remote(src, self.sib_buf.at[z], self.s_send.at[z], self.s_recv.at[z], at.dp, at.sib)

    def up(self, z):
        at = self.at
        return remote(self.stage.at[z], self.low_buf.at[z], self.up_send.at[z], self.up_recv.at[z], at.dp, at.c + 2)

    def down(self, z):
        at = self.at
        return remote(self.stage.at[z], self.high_buf.at[z], self.dn_send.at[z], self.dn_recv.at[z], at.dp, at.c - 2)

    def order(self):
        nz = self.at.nz
        for i in range(nz):
            yield nz - 1 - i
            if i != nz - 1 - i:
                pass

    def start(self):
        for i in range(self.at.nz):
            self.cross(i).start()

    def chip_sum(self, z):
        at = self.at
        mine = self.part[:, self.rows(2 * z + at.core)].astype(F32)
        return mine + self.sib_buf[z].astype(F32)

    def step(self, i):
        at = self.at
        up_z, dn_z = at.nz - 1 - i, i

        @pl.when(up_z > at.z)
        def _():
            self.cross(up_z).wait_recv()
            self.stage[up_z] = self.chip_sum(up_z).astype(BF16)

            @pl.when(at.has_down)
            def _():
                self.up(up_z).wait_recv()
                self.stage[up_z] = (self.stage[up_z].astype(F32) + self.low_buf[up_z].astype(F32)).astype(BF16)

            self.up(up_z).start()

        @pl.when(dn_z < at.z)
        def _():
            self.cross(dn_z).wait_recv()
            self.stage[dn_z] = self.chip_sum(dn_z).astype(BF16)

            @pl.when(at.has_up)
            def _():
                self.down(dn_z).wait_recv()
                self.stage[dn_z] = (self.stage[dn_z].astype(F32) + self.high_buf[dn_z].astype(F32)).astype(BF16)

            self.down(dn_z).start()

    def finish(self):
        at = self.at
        self.cross(at.z).wait_recv()
        self.out[...] = self.chip_sum(at.z)

        @pl.when(at.has_down)
        def _():
            self.up(at.z).wait_recv()
            self.out[...] += self.low_buf[at.z].astype(F32)

        @pl.when(at.has_up)
        def _():
            self.down(at.z).wait_recv()
            self.out[...] += self.high_buf[at.z].astype(F32)

        for z in range(at.nz):
            self.cross(z).wait_send()

            @pl.when(z > at.z)
            def _():
                self.up(z).wait_send()

            @pl.when(z < at.z)
            def _():
                self.down(z).wait_send()


def scatter_kernel(ndp, n, part_ref, out_ref, sib_buf, low_buf, high_buf, stage, *sems):
    at = Place(ndp, n)
    at.barrier(False, False)
    work = Scatter(at, part_ref, out_ref, sib_buf, low_buf, high_buf, stage, out_ref.shape[1], sems)
    work.start()
    for i in range(at.nz - 1):
        work.step(i)
    work.finish()


def scatter_ctx(ndp, n, part, collective):
    mb, seq, width = part.shape
    nz, tok = n // 2, seq // n
    dma = pltpu.SemaphoreType.DMA
    buf = pltpu.VMEM((nz, mb, tok, width), BF16)
    vmem = pl.BlockSpec(memory_space=pltpu.VMEM)
    return pl.pallas_call(
        partial(scatter_kernel, ndp, n),
        out_shape=jax.ShapeDtypeStruct((mb, tok, width), F32),
        in_specs=[vmem],
        out_specs=vmem,
        scratch_shapes=[buf, buf, buf, buf] + [dma((nz,))] * 6,
        compiler_params=pltpu.CompilerParams(collective_id=collective, has_side_effects=True, vmem_limit_bytes=48 * MIB),
    )(part)


def grads_kernel(ndp, n, wp_ref, wd_ref, wo_ref, v_ref, w_out, wd_out, wo_out, v_out, wbuf, wsum, dbuf, obuf, osum, vbuf, vsum, *sems):
    at = Place(ndp, n)
    (w1s, w1r, ds, dr, o1s, o1r, v1s, v1r, w2s, w2r, v2s, v2r, o2s, o2r, local) = sems
    at.barrier(True, True)
    first = at.c * ndp // n
    w1 = Exchange(at, "dp", lambda p: wp_ref.at[p], lambda s: wbuf.at[s], w1s, w1r)
    d1 = Exchange(at, "dp", lambda p: wd_ref.at[p], lambda s: dbuf.at[s], ds, dr)
    v1 = Exchange(at, "dp", lambda p: v_ref, lambda s: vbuf.at[s], v1s, v1r)
    o1 = Exchange(at, "dp", lambda p: wo_ref, lambda s: obuf.at[s], o1s, o1r)
    w1.start()
    v1.start()

    @pl.when(at.dp != first)
    def _():
        o1.copy(first, at.dp).start()

    d1.start()

    def total(ref, mine, get):
        ref[...] = mine
        for j in range(1, ndp):
            ref[...] += get(lax.rem(at.dp + j, ndp)).astype(F32)

    w1.wait_recv()
    total(wsum, wp_ref[at.dp].astype(F32), lambda s: wbuf[s])
    wbuf[at.dp] = wsum[...].astype(BF16)
    w2 = Exchange(at, "ctx", lambda p: wbuf.at[at.dp, p], lambda s: w_out.at[s], w2s, w2r)
    w2.start()
    w_out[at.c] = wbuf[at.dp, at.c]
    v1.wait_recv()
    total(vsum, v_ref[...], lambda s: vbuf[s])
    v2 = Exchange(at, "ctx", lambda p: vsum, lambda s: v_out.at[s], v2s, v2r)
    v2.start()
    v_out[at.c] = vsum[...]

    index = at.dp * n + at.c
    heads_of, slot = index // ndp, lax.rem(index, ndp)

    def out_rows(b, c):
        return remote(osum.at[b], wo_out, o2s.at[b], o2r, at.dp, c)

    @pl.when(at.dp == first)
    def _():
        o1.wait_recv()
        rows = wo_ref[...].astype(F32)
        for j in range(1, ndp):
            rows += obuf[lax.rem(at.dp + j, ndp)].astype(F32)
        osum[...] = rows.astype(BF16)
        for b in range(ndp):
            owner = lax.rem(at.c * ndp + b, n)

            @pl.when(owner != at.c)
            def _():
                out_rows(b, owner).start()

            @pl.when(owner == at.c)
            def _():
                wo_out[...] = osum[b]

    d1.wait_recv()
    total(wd_out, wd_ref[at.dp].astype(F32), lambda s: dbuf[s])

    @pl.when(heads_of != at.c)
    def _():
        out_rows(slot, at.c).wait_recv()

    w2.wait_recv()
    v2.wait_recv()
    for part in (w1, v1, d1, w2, v2):
        part.wait_send()

    @pl.when(at.dp != first)
    def _():
        o1.copy(first, at.dp).wait_send()

    @pl.when(at.dp == first)
    def _():
        for b in range(ndp):
            owner = lax.rem(at.c * ndp + b, n)

            @pl.when(owner != at.c)
            def _():
                out_rows(b, owner).wait_send()


def grads_all(ndp, n, wp, wd, wo, v):
    dma = pltpu.SemaphoreType.DMA
    vmem = pl.BlockSpec(memory_space=pltpu.VMEM)
    return pl.pallas_call(
        partial(grads_kernel, ndp, n),
        out_shape=(
            jax.ShapeDtypeStruct(wp.shape[1:], BF16),
            jax.ShapeDtypeStruct(wd.shape[1:], F32),
            jax.ShapeDtypeStruct(wo.shape[1:], BF16),
            jax.ShapeDtypeStruct((n,) + v.shape, F32),
        ),
        in_specs=[vmem] * 4,
        out_specs=[vmem] * 4,
        scratch_shapes=[
            pltpu.VMEM(wp.shape, BF16),
            pltpu.VMEM(wp.shape[1:], F32),
            pltpu.VMEM(wd.shape, BF16),
            pltpu.VMEM((ndp,) + wo.shape, BF16),
            pltpu.VMEM(wo.shape, BF16),
            pltpu.VMEM((ndp,) + v.shape, F32),
            pltpu.VMEM(v.shape, F32),
            dma((ndp,)), dma((ndp,)), dma((ndp,)), dma((ndp,)), dma((ndp,)), dma((ndp,)), dma((ndp,)), dma((ndp,)),
            dma((n,)), dma((n,)), dma((n,)), dma((n,)), dma((ndp,)), dma,
            dma((1,)),
        ],
        compiler_params=pltpu.CompilerParams(collective_id=3, has_side_effects=True, vmem_limit_bytes=48 * MIB),
    )(wp, wd, wo, v)


def rotary_tables(seq):
    half_rot = ROT // 2
    inverse = 10000.0 ** (-(2.0 * jnp.arange(half_rot, dtype=F32)) / ROT)
    angles = jnp.arange(seq, dtype=jnp.int32).astype(F32)[:, None] * inverse[None, :]
    angles = jnp.concatenate([angles, angles], axis=-1)
    return (jnp.cos(angles)[None, :, None, :], jnp.sin(angles)[None, :, None, :])


def rotate(values, cosine, sine, back=False):
    half_rot = ROT // 2
    lead = values[..., :ROT]
    if back:
        u = lead * sine
        turned = jnp.concatenate([u[..., half_rot:], -u[..., :half_rot]], axis=-1)
        return jnp.concatenate([lead * cosine + turned, values[..., ROT:]], axis=-1)
    turned = jnp.concatenate([-lead[..., half_rot:], lead[..., :half_rot]], axis=-1)
    return jnp.concatenate([lead * cosine + turned * sine, values[..., ROT:]], axis=-1)


def dot(a, b, dims=((1,), (0,))):
    return lax.dot_general(a, b, (dims, ((), ())), preferred_element_type=F32)


def per_device(ndp, n, tokens, cotangent, segments, w_qkv, b_qkv, w_out, b_out, w_up, b_up, w_down, b_down, g1, s1, g2, s2):
    tok, mb, width = tokens.shape
    seq = segments.shape[1]
    heads_all = width // HEAD
    hc = width // n
    heads = hc // HEAD
    rows_w = w_qkv.shape[0]
    rows_d = w_down.shape[0]
    fu = ndp * rows_d
    c = lax.axis_index("ctx")
    dp = lax.axis_index("dp")
    scale = HEAD ** (-0.5)

    cot = jnp.transpose(cotangent, (1, 0, 2))
    toks = jnp.transpose(tokens, (1, 0, 2))
    qkv_cols = w_qkv.reshape(rows_w, 3, n, hc).transpose(2, 0, 1, 3).reshape(n, rows_w, 3 * hc)
    up_cols = w_up.reshape(rows_w, ndp, n, rows_d).transpose(2, 0, 1, 3).reshape(n, rows_w, fu)
    wp = jnp.concatenate([qkv_cols, up_cols], axis=2)
    shard_vecs = (b_qkv, b_out, b_up, b_down, g1, s1, g2, s2)
    sizes = [v.shape[0] for v in shard_vecs]
    vec = jnp.concatenate(shard_vecs)
    lanes = 128
    per_vec = 16 * lanes
    vec = jnp.pad(vec, (0, per_vec - vec.shape[0])).reshape(16, lanes)
    x, g, w, wd, wo, vecs = gather_all(ndp, n, toks, cot, wp, w_down, w_out, vec)
    w = w.reshape(width, 3 * hc + fu)
    wq, wu = w[:, : 3 * hc], w[:, 3 * hc :]
    wd = wd.reshape(fu, width)
    wo = wo.reshape(hc, width)
    flat = vecs.reshape(ndp * n, per_vec).astype(F32)
    starts = [sum(sizes[:i]) for i in range(len(sizes))]
    full = [flat[:, s : s + z].reshape(-1) for s, z in zip(starts, sizes)]
    bq_all, bo, bu_all, bd, gain1, shift1, gain2, shift2 = full
    bq = lax.dynamic_index_in_dim(bq_all.reshape(3, n, hc), c, 1, keepdims=False).reshape(3 * hc)
    bu = lax.dynamic_index_in_dim(bu_all.reshape(ndp, n, rows_d), c, 1, keepdims=False).reshape(fu)

    xf = x.reshape(mb * seq, width).astype(F32)
    gl = g.reshape(mb * seq, width)
    mean = jnp.mean(xf, axis=-1, keepdims=True)
    cen = xf - mean
    rstd = lax.rsqrt(jnp.mean(cen * cen, axis=-1, keepdims=True) + 1e-05)
    normed = cen * rstd
    h1 = (normed * gain1 + shift1).astype(BF16)
    h2 = (normed * gain2 + shift2).astype(BF16)
    joined = (dot(h1, wq) + bq).reshape(mb, seq, 3, heads, HEAD)
    cosine, sine = rotary_tables(seq)
    q = rotate(joined[:, :, 0], cosine, sine).astype(BF16)
    k = rotate(joined[:, :, 1], cosine, sine).astype(BF16)
    v = joined[:, :, 2].astype(BF16)
    pos = jnp.arange(seq, dtype=jnp.int32)
    same = (segments[:, None, :] == segments[:, :, None]) & (segments[:, :, None] > 0)
    allow = (same & (pos[None, None, :] <= pos[None, :, None])) | (pos[None, None, :] == pos[None, :, None])
    scores = jnp.einsum("sqhd,skhd->shqk", q, k, preferred_element_type=F32) * scale
    scores = jnp.where(allow[:, None], scores, -1e30)
    top = jnp.max(scores, axis=-1, keepdims=True)
    e = jnp.exp(scores - top)
    probs = e / jnp.sum(e, axis=-1, keepdims=True)
    pl_low = probs.astype(BF16)
    ctx_f = jnp.einsum("shqk,skhd->sqhd", pl_low, v, preferred_element_type=F32)
    ctx = ctx_f.astype(BF16).reshape(mb * seq, hc)
    act = dot(h2, wu) + bu
    hidden = jax.nn.gelu(act, approximate=False).astype(BF16)
    part = (dot(ctx, wo) + dot(hidden, wd)).astype(BF16).reshape(mb, seq, width)
    mixed_sum = scatter_ctx(ndp, n, part, 1)
    mixed = (toks.astype(F32) + mixed_sum + bo + bd).astype(BF16)

    gf = gl.astype(F32)
    d_wd = dot(hidden, gl, ((0,), (0,)))
    d_wo = dot(ctx, gl, ((0,), (0,)))
    d_hidden = dot(gl, wd, ((1,), (1,)))
    _, pull = jax.vjp(partial(jax.nn.gelu, approximate=False), act)
    d_act = pull(d_hidden)[0].astype(BF16)
    d_wu = dot(h2, d_act, ((0,), (0,)))
    d_bu = jnp.sum(d_act.astype(F32), axis=0)
    d_h2 = dot(d_act, wu, ((1,), (1,)))
    d_ctx = dot(gl, wo, ((1,), (1,))).astype(BF16).reshape(mb, seq, heads, HEAD)
    d_probs = jnp.einsum("sqhd,skhd->shqk", d_ctx, v, preferred_element_type=F32)
    delta = jnp.sum(probs * d_probs, axis=-1, keepdims=True)
    d_scores = jnp.where(allow[:, None], probs * (d_probs - delta), 0.0).astype(BF16)
    d_q = jnp.einsum("shqk,skhd->sqhd", d_scores, k, preferred_element_type=F32) * scale
    d_k = jnp.einsum("shqk,sqhd->skhd", d_scores, q, preferred_element_type=F32) * scale
    d_v = jnp.einsum("shqk,sqhd->skhd", pl_low, d_ctx, preferred_element_type=F32)
    d_q = rotate(d_q, cosine, sine, True)
    d_k = rotate(d_k, cosine, sine, True)
    d_qkv = jnp.stack([d_q, d_k, d_v], axis=2).astype(BF16).reshape(mb * seq, 3 * hc)
    d_wq = dot(h1, d_qkv, ((0,), (0,)))
    d_bq = jnp.sum(d_qkv.astype(F32), axis=0)
    d_h1 = dot(d_qkv, wq, ((1,), (1,)))
    e_sum = (d_h1 * gain1 + d_h2 * gain2).astype(BF16).reshape(mb, seq, width)
    e_own = scatter_ctx(ndp, n, e_sum, 2)
    own_x = toks.astype(F32)
    o_mean = jnp.mean(own_x, axis=-1, keepdims=True)
    o_cen = own_x - o_mean
    o_rstd = lax.rsqrt(jnp.mean(o_cen * o_cen, axis=-1, keepdims=True) + 1e-05)
    o_n = o_cen * o_rstd
    t_grad = o_rstd * (e_own - jnp.mean(e_own, axis=-1, keepdims=True) - o_n * jnp.mean(e_own * o_n, axis=-1, keepdims=True))
    tokens_grad = (cot.astype(F32) + t_grad).astype(BF16)

    rows = [
        jnp.pad(d_bq, (0, width - 3 * hc)),
        jnp.pad(d_bu, (0, width - fu)),
        jnp.sum(d_h1 * normed, axis=0),
        jnp.sum(d_h1, axis=0),
        jnp.sum(d_h2 * normed, axis=0),
        jnp.sum(d_h2, axis=0),
        jnp.sum(gf, axis=0),
        jnp.zeros((width,), F32),
    ]
    dwp = jnp.concatenate([d_wq, d_wu], axis=1).astype(BF16).reshape(ndp, n, rows_w, 3 * hc + fu)
    dw, dwd, dwo, dv = grads_all(
        ndp, n, dwp, d_wd.astype(BF16).reshape(ndp, rows_d, width), d_wo.astype(BF16).reshape(ndp, rows_w, width), jnp.stack(rows)
    )
    index = dp * n + c
    g_qkv = dw[:, :, : 3 * hc].reshape(n, rows_w, 3, hc).transpose(1, 2, 0, 3).reshape(rows_w, 3 * width).astype(F32)
    g_up = dw[:, :, 3 * hc :].reshape(n, rows_w, ndp, rows_d).transpose(1, 2, 0, 3).reshape(rows_w, -1).astype(F32)
    g_bq = lax.dynamic_slice_in_dim(dv[:, 0, : 3 * hc].reshape(n, 3, hc).transpose(1, 0, 2).reshape(-1), index * sizes[0], sizes[0])
    own = lax.dynamic_index_in_dim(dv, c, 0, keepdims=False)
    g_bu = lax.dynamic_slice_in_dim(own[1], dp * rows_d, rows_d)
    four = lax.dynamic_slice_in_dim(jnp.sum(dv[:, 2:6], axis=0), index * rows_w, rows_w, axis=1)
    g_b = lax.dynamic_slice_in_dim(own[6], index * rows_w, rows_w)
    return (
        jnp.transpose(mixed, (1, 0, 2)),
        jnp.transpose(tokens_grad, (1, 0, 2)),
        g_qkv,
        g_bq,
        dwo.astype(F32),
        g_b,
        g_up,
        g_bu,
        dwd,
        g_b,
        four[0],
        four[1],
        four[2],
        four[3],
    )


def solution(mesh):
    every = ("dp", "ctx")
    mat, vec, act = P(every, None), P(every), P("ctx", "dp", None)
    placed = (act, act, P("dp", None), mat, vec, mat, vec, mat, vec, mat, vec, vec, vec, vec, vec)
    return jax.shard_map(
        partial(per_device, mesh.shape["dp"], mesh.shape["ctx"]),
        mesh=mesh,
        in_specs=placed,
        out_specs=(act, act, mat, vec, mat, vec, mat, vec, mat, vec, vec, vec, vec, vec),
        check_vma=False,
    )
```

```python
from functools import partial

import jax
import jax.numpy as jnp
import numpy as np
from jax import lax
from jax.experimental import pallas as pl
from jax.experimental.pallas import tpu as pltpu
from jax.sharding import PartitionSpec as P

HEAD = 64
ROT = 16
MIB = 1 << 20
MESH = pl.DeviceIdType.MESH
ANY = pl.BlockSpec(memory_space=pl.ANY)
F32 = jnp.float32
BF16 = jnp.bfloat16


class Place:
    def __init__(self, ndp, n):
        self.ndp, self.n, self.nz = ndp, n, n // 2
        self.dp = lax.axis_index("dp")
        self.c = lax.axis_index("ctx")
        self.z = self.c // 2
        self.core = lax.rem(self.c, 2)
        self.sib = self.c + 1 - 2 * self.core
        self.has_up = self.z + 1 < self.nz
        self.has_down = self.z > 0

    def barrier(self, ctx_all, dp_all):
        bar = pltpu.get_barrier_semaphore()
        count = 0
        if ctx_all:
            for j in range(1, self.n):
                peer = lax.rem(self.c + j, self.n)
                pl.semaphore_signal(bar, inc=1, device_id=(self.dp, peer), device_id_type=MESH)
                count += 1
        else:
            pl.semaphore_signal(bar, inc=1, device_id=(self.dp, self.sib), device_id_type=MESH)
            count += 1
            for ok, peer in ((self.has_up, self.c + 2), (self.has_down, self.c - 2)):

                @pl.when(ok)
                def _():
                    pl.semaphore_signal(bar, inc=1, device_id=(self.dp, peer), device_id_type=MESH)

        if dp_all:
            for j in range(1, self.ndp):
                peer = lax.rem(self.dp + j, self.ndp)
                pl.semaphore_signal(bar, inc=1, device_id=(peer, self.c), device_id_type=MESH)
                count += 1
        if not ctx_all:
            count = count + self.has_up.astype(jnp.int32) + self.has_down.astype(jnp.int32)
        pl.semaphore_wait(bar, count)


def remote(src, dst, send, recv, dp, c):
    return pltpu.make_async_remote_copy(
        src_ref=src,
        dst_ref=dst,
        send_sem=send,
        recv_sem=recv,
        device_id=(dp, c),
        device_id_type=MESH,
    )


class Gather:
    def __init__(self, at, src, dst, tok, sends, recvs):
        self.at, self.src, self.dst, self.tok, self.sends, self.recvs = at, src, dst, tok, sends, recvs

    def rows(self, c):
        return self.dst.at[:, pl.ds(pl.multiple_of(c * self.tok, self.tok), self.tok)]

    def copy(self, block, slot, c, src=None):
        at = self.at
        src = self.rows(block) if src is None else src
        return remote(src, self.rows(block), self.sends.at[slot], self.recvs.at[block], at.dp, c)

    def start(self):
        at = self.at

        @pl.when(at.has_up)
        def _():
            self.copy(at.c, 0, at.c + 2, self.src).start()

        @pl.when(at.has_down)
        def _():
            self.copy(at.c, 1, at.c - 2, self.src).start()

        self.copy(at.c, 2, at.sib, self.src).start()

    def step(self, k):
        at = self.at
        low, high = at.c - 2 * k, at.c + 2 * k

        @pl.when(at.z >= k)
        def _():
            self.copy(low, 0, at.c).wait_recv()

            @pl.when(at.has_up)
            def _():
                self.copy(low, 3 * k, at.c + 2).start()

            self.copy(low, 3 * k + 2, at.sib).start()

        @pl.when(at.z + k < at.nz)
        def _():
            self.copy(high, 0, at.c).wait_recv()

            @pl.when(at.has_down)
            def _():
                self.copy(high, 3 * k + 1, at.c - 2).start()

            self.copy(high, 3 * at.nz + k, at.sib).start()

    def finish(self):
        at = self.at
        for z in range(at.nz):
            self.copy(2 * z + 1 - at.core, 0, at.c).wait_recv()
        self.copy(at.c, 2, at.sib, self.src).wait_send()
        for k in range(at.nz):

            @pl.when((at.z >= k) & at.has_up)
            def _():
                self.copy(at.c, 3 * k, at.c).wait_send()

            @pl.when((at.z + k < at.nz) & at.has_down)
            def _():
                self.copy(at.c, 3 * k + 1, at.c).wait_send()

            if k:

                @pl.when(at.z >= k)
                def _():
                    self.copy(at.c, 3 * k + 2, at.c).wait_send()

                @pl.when(at.z + k < at.nz)
                def _():
                    self.copy(at.c, 3 * at.nz + k, at.c).wait_send()


def gather_slots(nz):
    return 4 * nz


class Exchange:
    def __init__(self, at, axis, src, dst, sends, recvs):
        self.at, self.axis, self.src, self.dst, self.sends, self.recvs = at, axis, src, dst, sends, recvs
        self.me, self.count = (at.c, at.n) if axis == "ctx" else (at.dp, at.ndp)

    def copy(self, peer, sender):
        at = self.at
        to = (at.dp, peer) if self.axis == "ctx" else (peer, at.c)
        return remote(self.src(peer), self.dst(sender), self.sends.at[peer], self.recvs.at[sender], *to)

    def start(self):
        for j in range(1, self.count):
            self.copy(lax.rem(self.me + j, self.count), self.me).start()

    def wait_recv(self):
        for j in range(1, self.count):
            peer = lax.rem(self.me + j, self.count)
            self.copy(peer, peer).wait_recv()

    def wait_send(self):
        for j in range(1, self.count):
            peer = lax.rem(self.me + j, self.count)
            self.copy(peer, self.me).wait_send()


def gather_kernel(ndp, n, tok_ref, cot_ref, wp_ref, wd_ref, wo_ref, vec_ref, x_out, g_out, w_out, wd_out, wo_out, vec_out, *sems):
    at = Place(ndp, n)
    tok = tok_ref.shape[1]
    (x_send, x_recv, g_send, g_recv, w1s, w1r, w2s, w2r, v1s, v1r, v2s, v2r, ds, dr, o1s, o1r, o2s, o2r, local) = sems
    at.barrier(True, True)
    own = (
        pltpu.make_async_copy(wp_ref.at[at.c], w_out.at[at.dp, at.c], local.at[0]),
        pltpu.make_async_copy(vec_ref, vec_out.at[at.dp, at.c], local.at[1]),
        pltpu.make_async_copy(wd_ref, wd_out.at[at.dp], local.at[2]),
        pltpu.make_async_copy(tok_ref, x_out.at[:, pl.ds(pl.multiple_of(at.c * tok, tok), tok)], local.at[3]),
        pltpu.make_async_copy(cot_ref, g_out.at[:, pl.ds(pl.multiple_of(at.c * tok, tok), tok)], local.at[4]),
    )
    for copy in own:
        copy.start()
    down_w = Exchange(at, "dp", lambda p: wd_ref, lambda s: wd_out.at[s], ds, dr)
    cols = Exchange(at, "ctx", lambda p: wp_ref.at[p], lambda s: w_out.at[at.dp, s], w1s, w1r)
    vecs = Exchange(at, "ctx", lambda p: vec_ref, lambda s: vec_out.at[at.dp, s], v1s, v1r)
    plane_w = Exchange(at, "dp", lambda p: w_out.at[at.dp], lambda s: w_out.at[s], w2s, w2r)
    plane_v = Exchange(at, "dp", lambda p: vec_out.at[at.dp], lambda s: vec_out.at[s], v2s, v2r)
    plane_o = Exchange(at, "dp", lambda p: wo_out, lambda s: wo_out, o2s, o2r)
    cols.start()
    vecs.start()
    index = at.dp * n + at.c
    heads_of, slot = index // ndp, lax.rem(index, ndp)

    def out_rows(b, c):
        return remote(wo_ref, wo_out.at[b], o1s, o1r.at[b], at.dp, c)

    @pl.when(heads_of != at.c)
    def _():
        out_rows(slot, heads_of).start()

    own_rows = pltpu.make_async_copy(wo_ref, wo_out.at[slot], local.at[5])

    @pl.when(heads_of == at.c)
    def _():
        own_rows.start()

    down_w.start()
    x_ag = Gather(at, tok_ref, x_out, tok, x_send, x_recv)
    g_ag = Gather(at, cot_ref, g_out, tok, g_send, g_recv)
    x_ag.start()
    own[0].wait()
    cols.wait_recv()
    plane_w.start()
    own[1].wait()
    vecs.wait_recv()
    plane_v.start()
    first = at.c * ndp // n

    @pl.when(at.dp == first)
    def _():
        for b in range(ndp):
            src = lax.rem(at.c * ndp + b, n)

            @pl.when(src != at.c)
            def _():
                out_rows(b, at.c).wait_recv()

            @pl.when(src == at.c)
            def _():
                own_rows.wait()

        plane_o.start()

    for k in range(1, at.nz):
        x_ag.step(k)
        if k == 1:
            g_ag.start()
    for k in range(1, at.nz):
        g_ag.step(k)
    x_ag.finish()
    g_ag.finish()

    @pl.when(heads_of != at.c)
    def _():
        out_rows(slot, heads_of).wait_send()

    @pl.when((heads_of == at.c) & (at.dp != first))
    def _():
        own_rows.wait()

    @pl.when(at.dp == first)
    def _():
        plane_o.wait_send()

    @pl.when(at.dp != first)
    def _():
        plane_o.copy(first, first).wait_recv()

    for copy in own[2:]:
        copy.wait()
    for part in (down_w, plane_w, plane_v):
        part.wait_recv()
    for part in (down_w, cols, vecs, plane_w, plane_v):
        part.wait_send()


def gather_all(ndp, n, tok, cot, wp, wd, wo, vec):
    mb, rows, width = tok.shape
    dma = pltpu.SemaphoreType.DMA
    slots = gather_slots(n // 2)
    return pl.pallas_call(
        partial(gather_kernel, ndp, n),
        out_shape=(
            jax.ShapeDtypeStruct((mb, rows * n, width), BF16),
            jax.ShapeDtypeStruct((mb, rows * n, width), BF16),
            jax.ShapeDtypeStruct((ndp,) + wp.shape, BF16),
            jax.ShapeDtypeStruct((ndp,) + wd.shape, BF16),
            jax.ShapeDtypeStruct((ndp,) + wo.shape, BF16),
            jax.ShapeDtypeStruct((ndp, n) + vec.shape, vec.dtype),
        ),
        in_specs=[ANY] * 6,
        out_specs=[ANY] * 6,
        scratch_shapes=[
            dma((slots,)), dma((n,)), dma((slots,)), dma((n,)),
            dma((n,)), dma((n,)), dma((ndp,)), dma((ndp,)),
            dma((n,)), dma((n,)), dma((ndp,)), dma((ndp,)),
            dma((ndp,)), dma((ndp,)),
            dma, dma((ndp,)), dma((ndp,)), dma((ndp,)),
            dma((6,)),
        ],
        compiler_params=pltpu.CompilerParams(collective_id=0, has_side_effects=True),
    )(tok, cot, wp, wd, wo, vec)


class Scatter:
    def __init__(self, at, part, out, sib_buf, low_buf, high_buf, stage, tok, sems):
        self.at, self.part, self.out, self.tok = at, part, out, tok
        self.sib_buf, self.low_buf, self.high_buf, self.stage = sib_buf, low_buf, high_buf, stage
        self.s_send, self.s_recv, self.up_send, self.up_recv, self.dn_send, self.dn_recv = sems

    def rows(self, c):
        return pl.ds(pl.multiple_of(c * self.tok, self.tok), self.tok)

    def cross(self, z):
        at = self.at
        src = self.part.at[:, self.rows(2 * z + 1 - at.core)]
        return remote(src, self.sib_buf.at[z], self.s_send.at[z], self.s_recv.at[z], at.dp, at.sib)

    def up(self, z):
        at = self.at
        return remote(self.stage.at[z], self.low_buf.at[z], self.up_send.at[z], self.up_recv.at[z], at.dp, at.c + 2)

    def down(self, z):
        at = self.at
        return remote(self.stage.at[z], self.high_buf.at[z], self.dn_send.at[z], self.dn_recv.at[z], at.dp, at.c - 2)

    def order(self):
        nz = self.at.nz
        for i in range(nz):
            yield nz - 1 - i
            if i != nz - 1 - i:
                pass

    def start(self):
        for i in range(self.at.nz):
            self.cross(i).start()

    def chip_sum(self, z):
        at = self.at
        mine = self.part[:, self.rows(2 * z + at.core)].astype(F32)
        return mine + self.sib_buf[z].astype(F32)

    def step(self, i):
        at = self.at
        up_z, dn_z = at.nz - 1 - i, i

        @pl.when(up_z > at.z)
        def _():
            self.cross(up_z).wait_recv()
            self.stage[up_z] = self.chip_sum(up_z).astype(BF16)

            @pl.when(at.has_down)
            def _():
                self.up(up_z).wait_recv()
                self.stage[up_z] = (self.stage[up_z].astype(F32) + self.low_buf[up_z].astype(F32)).astype(BF16)

            self.up(up_z).start()

        @pl.when(dn_z < at.z)
        def _():
            self.cross(dn_z).wait_recv()
            self.stage[dn_z] = self.chip_sum(dn_z).astype(BF16)

            @pl.when(at.has_up)
            def _():
                self.down(dn_z).wait_recv()
                self.stage[dn_z] = (self.stage[dn_z].astype(F32) + self.high_buf[dn_z].astype(F32)).astype(BF16)

            self.down(dn_z).start()

    def finish(self):
        at = self.at
        self.cross(at.z).wait_recv()
        self.out[...] = self.chip_sum(at.z)

        @pl.when(at.has_down)
        def _():
            self.up(at.z).wait_recv()
            self.out[...] += self.low_buf[at.z].astype(F32)

        @pl.when(at.has_up)
        def _():
            self.down(at.z).wait_recv()
            self.out[...] += self.high_buf[at.z].astype(F32)

        for z in range(at.nz):
            self.cross(z).wait_send()

            @pl.when(z > at.z)
            def _():
                self.up(z).wait_send()

            @pl.when(z < at.z)
            def _():
                self.down(z).wait_send()


def scatter_kernel(ndp, n, part_ref, out_ref, sib_buf, low_buf, high_buf, stage, *sems):
    at = Place(ndp, n)
    at.barrier(False, False)
    work = Scatter(at, part_ref, out_ref, sib_buf, low_buf, high_buf, stage, out_ref.shape[1], sems)
    work.start()
    for i in range(at.nz - 1):
        work.step(i)
    work.finish()


def scatter_ctx(ndp, n, part, collective):
    mb, seq, width = part.shape
    nz, tok = n // 2, seq // n
    dma = pltpu.SemaphoreType.DMA
    buf = pltpu.VMEM((nz, mb, tok, width), BF16)
    vmem = pl.BlockSpec(memory_space=pltpu.VMEM)
    return pl.pallas_call(
        partial(scatter_kernel, ndp, n),
        out_shape=jax.ShapeDtypeStruct((mb, tok, width), F32),
        in_specs=[vmem],
        out_specs=vmem,
        scratch_shapes=[buf, buf, buf, buf] + [dma((nz,))] * 6,
        compiler_params=pltpu.CompilerParams(collective_id=collective, has_side_effects=True, vmem_limit_bytes=48 * MIB),
    )(part)


def grads_kernel(ndp, n, wp_ref, wd_ref, wo_ref, v_ref, w_out, wd_out, wo_out, v_out, wbuf, wsum, dbuf, obuf, osum, vbuf, vsum, *sems):
    at = Place(ndp, n)
    (w1s, w1r, ds, dr, o1s, o1r, v1s, v1r, w2s, w2r, v2s, v2r, o2s, o2r, local) = sems
    at.barrier(True, True)
    first = at.c * ndp // n
    w1 = Exchange(at, "dp", lambda p: wp_ref.at[p], lambda s: wbuf.at[s], w1s, w1r)
    d1 = Exchange(at, "dp", lambda p: wd_ref.at[p], lambda s: dbuf.at[s], ds, dr)
    v1 = Exchange(at, "dp", lambda p: v_ref, lambda s: vbuf.at[s], v1s, v1r)
    o1 = Exchange(at, "dp", lambda p: wo_ref, lambda s: obuf.at[s], o1s, o1r)
    w1.start()
    v1.start()

    @pl.when(at.dp != first)
    def _():
        o1.copy(first, at.dp).start()

    d1.start()

    def total(ref, mine, get):
        ref[...] = mine
        for j in range(1, ndp):
            ref[...] += get(lax.rem(at.dp + j, ndp)).astype(F32)

    w1.wait_recv()
    total(wsum, wp_ref[at.dp].astype(F32), lambda s: wbuf[s])
    wbuf[at.dp] = wsum[...].astype(BF16)
    w2 = Exchange(at, "ctx", lambda p: wbuf.at[at.dp, p], lambda s: w_out.at[s], w2s, w2r)
    w2.start()
    w_out[at.c] = wbuf[at.dp, at.c]
    v1.wait_recv()
    total(vsum, v_ref[...], lambda s: vbuf[s])
    v2 = Exchange(at, "ctx", lambda p: vsum, lambda s: v_out.at[s], v2s, v2r)
    v2.start()
    v_out[at.c] = vsum[...]

    index = at.dp * n + at.c
    heads_of, slot = index // ndp, lax.rem(index, ndp)

    def out_rows(b, c):
        return remote(osum.at[b], wo_out, o2s.at[b], o2r, at.dp, c)

    @pl.when(at.dp == first)
    def _():
        o1.wait_recv()
        rows = wo_ref[...].astype(F32)
        for j in range(1, ndp):
            rows += obuf[lax.rem(at.dp + j, ndp)].astype(F32)
        osum[...] = rows.astype(BF16)
        for b in range(ndp):
            owner = lax.rem(at.c * ndp + b, n)

            @pl.when(owner != at.c)
            def _():
                out_rows(b, owner).start()

            @pl.when(owner == at.c)
            def _():
                wo_out[...] = osum[b]

    d1.wait_recv()
    total(wd_out, wd_ref[at.dp].astype(F32), lambda s: dbuf[s])

    @pl.when(heads_of != at.c)
    def _():
        out_rows(slot, at.c).wait_recv()

    w2.wait_recv()
    v2.wait_recv()
    for part in (w1, v1, d1, w2, v2):
        part.wait_send()

    @pl.when(at.dp != first)
    def _():
        o1.copy(first, at.dp).wait_send()

    @pl.when(at.dp == first)
    def _():
        for b in range(ndp):
            owner = lax.rem(at.c * ndp + b, n)

            @pl.when(owner != at.c)
            def _():
                out_rows(b, owner).wait_send()


def grads_all(ndp, n, wp, wd, wo, v):
    dma = pltpu.SemaphoreType.DMA
    vmem = pl.BlockSpec(memory_space=pltpu.VMEM)
    return pl.pallas_call(
        partial(grads_kernel, ndp, n),
        out_shape=(
            jax.ShapeDtypeStruct(wp.shape[1:], BF16),
            jax.ShapeDtypeStruct(wd.shape[1:], F32),
            jax.ShapeDtypeStruct(wo.shape[1:], BF16),
            jax.ShapeDtypeStruct((n,) + v.shape, F32),
        ),
        in_specs=[vmem] * 4,
        out_specs=[vmem] * 4,
        scratch_shapes=[
            pltpu.VMEM(wp.shape, BF16),
            pltpu.VMEM(wp.shape[1:], F32),
            pltpu.VMEM(wd.shape, BF16),
            pltpu.VMEM((ndp,) + wo.shape, BF16),
            pltpu.VMEM(wo.shape, BF16),
            pltpu.VMEM((ndp,) + v.shape, F32),
            pltpu.VMEM(v.shape, F32),
            dma((ndp,)), dma((ndp,)), dma((ndp,)), dma((ndp,)), dma((ndp,)), dma((ndp,)), dma((ndp,)), dma((ndp,)),
            dma((n,)), dma((n,)), dma((n,)), dma((n,)), dma((ndp,)), dma,
            dma((1,)),
        ],
        compiler_params=pltpu.CompilerParams(collective_id=3, has_side_effects=True, vmem_limit_bytes=48 * MIB),
    )(wp, wd, wo, v)


def dot(a, b, dims=((1,), (0,))):
    return lax.dot_general(a, b, (dims, ((), ())), preferred_element_type=F32)


NT = ((1,), (1,))
TN = ((0,), (0,))


class SeqGather:
    def __init__(self, at, src, dst, tok, sends, recvs):
        self.at, self.src, self.dst, self.tok, self.sends, self.recvs = at, src, dst, tok, sends, recvs

    def rows(self, c):
        return self.dst.at[pl.ds(pl.multiple_of(c * self.tok, self.tok), self.tok)]

    def copy(self, block, slot, c, src=None):
        src = self.rows(block) if src is None else src
        return remote(src, self.rows(block), self.sends.at[slot], self.recvs.at[block], self.at.dp, c)

    def start(self):
        at = self.at

        @pl.when(at.has_up)
        def _():
            self.copy(at.c, 0, at.c + 2, self.src).start()

        @pl.when(at.has_down)
        def _():
            self.copy(at.c, 1, at.c - 2, self.src).start()

        self.copy(at.c, 2, at.sib, self.src).start()

    def step(self, k):
        at = self.at
        low, high = at.c - 2 * k, at.c + 2 * k

        @pl.when(at.z >= k)
        def _():
            self.copy(low, 0, at.c).wait_recv()

            @pl.when(at.has_up)
            def _():
                self.copy(low, 3 * k, at.c + 2).start()

            self.copy(low, 3 * k + 2, at.sib).start()

        @pl.when(at.z + k < at.nz)
        def _():
            self.copy(high, 0, at.c).wait_recv()

            @pl.when(at.has_down)
            def _():
                self.copy(high, 3 * k + 1, at.c - 2).start()

            self.copy(high, 3 * at.nz + k, at.sib).start()

    def land(self):
        at = self.at
        for z in range(at.nz):
            self.copy(2 * z + 1 - at.core, 0, at.c).wait_recv()

    def drain(self):
        at = self.at
        self.copy(at.c, 2, at.sib, self.src).wait_send()
        for k in range(at.nz):

            @pl.when((at.z >= k) & at.has_up)
            def _():
                self.copy(at.c, 3 * k, at.c).wait_send()

            @pl.when((at.z + k < at.nz) & at.has_down)
            def _():
                self.copy(at.c, 3 * k + 1, at.c).wait_send()

            if k:

                @pl.when(at.z >= k)
                def _():
                    self.copy(at.c, 3 * k + 2, at.c).wait_send()

                @pl.when(at.z + k < at.nz)
                def _():
                    self.copy(at.c, 3 * at.nz + k, at.c).wait_send()


class SeqScatter:
    def __init__(self, at, part, sib_buf, in_buf, tok, sems):
        self.at, self.part, self.sib_buf, self.in_buf, self.tok = at, part, sib_buf, in_buf, tok
        self.s_send, self.s_recv, self.up_send, self.up_recv, self.dn_send, self.dn_recv = sems

    def rows(self, c):
        return pl.ds(pl.multiple_of(c * self.tok, self.tok), self.tok)

    def cross(self, z):
        at = self.at
        src = self.part.at[self.rows(2 * z + 1 - at.core)]
        return remote(src, self.sib_buf.at[z], self.s_send.at[z], self.s_recv.at[z], at.dp, at.sib)

    def up(self, z):
        at = self.at
        return remote(self.sib_buf.at[z], self.in_buf.at[z], self.up_send.at[z], self.up_recv.at[z], at.dp, at.c + 2)

    def down(self, z, sender=None):
        at = self.at
        slot = jnp.where(z == (at.z - 1 if sender is None else sender - 1), at.nz, z)
        return remote(self.sib_buf.at[z], self.in_buf.at[slot], self.dn_send.at[z], self.dn_recv.at[z], at.dp, at.c - 2)

    def chip_sum(self, z):
        mine = self.part[self.rows(2 * z + self.at.core)].astype(F32)
        return mine + self.sib_buf[z].astype(F32)

    def step(self, i):
        self.step_up(self.at.nz - 1 - i)
        self.step_down(i)

    def step_up(self, z):
        at = self.at

        @pl.when(z > at.z)
        def _():
            self.cross(z).wait_recv()

            @pl.when(at.has_down)
            def _():
                self.up(z).wait_recv()
                self.sib_buf[z] = (self.chip_sum(z) + self.in_buf[z].astype(F32)).astype(BF16)

            @pl.when(jnp.logical_not(at.has_down))
            def _():
                self.sib_buf[z] = self.chip_sum(z).astype(BF16)

            self.up(z).start()

    def step_down(self, z):
        at = self.at

        @pl.when(z < at.z)
        def _():
            self.cross(z).wait_recv()

            @pl.when(at.has_up)
            def _():
                self.down(z, at.z + 1).wait_recv()
                self.sib_buf[z] = (self.chip_sum(z) + self.in_buf[z].astype(F32)).astype(BF16)

            @pl.when(jnp.logical_not(at.has_up))
            def _():
                self.sib_buf[z] = self.chip_sum(z).astype(BF16)

            self.down(z).start()

    def total(self, acc):
        at = self.at
        self.cross(at.z).wait_recv()
        acc[...] = self.chip_sum(at.z)

        @pl.when(at.has_down)
        def _():
            self.up(at.z).wait_recv()
            acc[...] += self.in_buf[at.z].astype(F32)

        @pl.when(at.has_up)
        def _():
            self.down(at.z, at.z + 1).wait_recv()
            acc[...] += self.in_buf[at.nz].astype(F32)

    def drain(self):
        at = self.at
        for z in range(at.nz):
            self.cross(z).wait_send()

            @pl.when(z > at.z)
            def _():
                self.up(z).wait_send()

            @pl.when(z < at.z)
            def _():
                self.down(z).wait_send()


def blocks(count, body, hooks=None):
    hooks = hooks or {}

    def one(i, carry):
        body(i)
        for index, events in hooks.items():

            @pl.when(i == index)
            def _():
                for event in events:
                    event()

        return carry

    lax.fori_loop(0, count, one, 0)


def fused_kernel(ndp, n, dims, *refs):
    mb, tok, width, seq, heads, rows_w, rows_d = dims
    nz, block, every = n // 2, 2 * tok, ndp * n
    fu = ndp * rows_d
    (tok_ref, cot_ref, wp_ref, wd_ref, wo_ref, vec_ref, seg_ref, cos_ref, sin_ref) = refs[:9]
    (mixed_out, grad_out, dwq_out, dwu_out, dwd_out, dwo_out, dv_out) = refs[9:16]
    (xs, gs, ws, wds, wos, vecs, segs, seg_col, cos_t, sin_t, g1, s1, g2, s2, bo, bq, bu, qkv, hid, gp, stat, ctx, part, ep, dctx, dqkv,
     dk, dv, acc_gain, acc_bu, acc_bq, m_sib, m_in, t_sib, t_in, dwq, dwu, dwd, dwo, wq_in, wu_in, wd_in, wo_in, vsum, vin, wq_st, wu_st,
     own) = refs[16:64]
    probs = refs[64 : 64 + nz]
    (x_s, x_r, c_s, c_r, w1s, w1r, w2s, w2r, v1s, v1r, v2s, v2r, d_s, d_r, o1s, o1r, o2s, o2r,
     ms_s, ms_r, mu_s, mu_r, md_s, md_r, ts_s, ts_r, tu_s, tu_r, td_s, td_r,
     gq1s, gq1r, gq2s, gq2r, gu1s, gu1r, gu2s, gu2r, gd_s, gd_r, go1s, go1r, go2s, go2r, gv1s, gv1r, gv2s, gv2r, local) = refs[64 + nz :]
    at = Place(ndp, n)
    at.barrier(True, True)
    index = at.dp * n + at.c
    first = at.c * ndp // n
    heads_of, slot = index // ndp, lax.rem(index, ndp)
    own_rows = pl.ds(pl.multiple_of(at.c * tok, tok), tok)

    cols = Exchange(at, "ctx", lambda p: wp_ref.at[p], lambda s: ws.at[at.dp, s], w1s, w1r)
    vec1 = Exchange(at, "ctx", lambda p: vec_ref, lambda s: vecs.at[at.dp, s], v1s, v1r)
    plane_w = Exchange(at, "dp", lambda p: ws.at[at.dp], lambda s: ws.at[s], w2s, w2r)
    plane_v = Exchange(at, "dp", lambda p: vecs.at[at.dp], lambda s: vecs.at[s], v2s, v2r)
    plane_d = Exchange(at, "dp", lambda p: wd_ref, lambda s: wds.at[s], d_s, d_r)
    plane_o = Exchange(at, "dp", lambda p: wos, lambda s: wos, o2s, o2r)
    x_ag = [SeqGather(at, tok_ref.at[s], xs.at[s], tok, x_s.at[s], x_r.at[s]) for s in range(mb)]
    c_ag = [SeqGather(at, cot_ref.at[s], gs.at[s], tok, c_s.at[s], c_r.at[s]) for s in range(mb)]
    copies = [
        pltpu.make_async_copy(wp_ref.at[at.c], ws.at[at.dp, at.c], local.at[0]),
        pltpu.make_async_copy(vec_ref, vecs.at[at.dp, at.c], local.at[1]),
        pltpu.make_async_copy(wd_ref, wds.at[at.dp], local.at[2]),
        pltpu.make_async_copy(seg_ref, segs, local.at[3]),
        pltpu.make_async_copy(cos_ref, cos_t, local.at[4]),
        pltpu.make_async_copy(sin_ref, sin_t, local.at[5]),
        pltpu.make_async_copy(tok_ref, xs.at[:, own_rows], local.at[6]),
        pltpu.make_async_copy(cot_ref, gs.at[:, own_rows], local.at[7]),
    ]

    def out_rows(b, c):
        return remote(wo_ref, wos.at[b], o1s, o1r.at[b], at.dp, c)

    own_out = pltpu.make_async_copy(wo_ref, wos.at[slot], local.at[8])
    cols.start()
    vec1.start()
    for copy in copies:
        copy.start()
    x_ag[0].start()
    copies[0].wait()
    copies[1].wait()
    vec1.wait_recv()
    plane_v.start()
    cols.wait_recv()
    plane_w.start()
    plane_d.start()

    @pl.when(heads_of != at.c)
    def _():
        out_rows(slot, heads_of).start()

    @pl.when(heads_of == at.c)
    def _():
        own_out.start()

    x_ag[0].step(1)
    x_ag[1].start()
    x_ag[0].step(2)
    x_ag[0].step(3)
    for copy in copies[2:]:
        copy.wait()

    plane_v.wait_recv()
    lane = lax.broadcasted_iota(jnp.int32, (16, 128), 1)
    per = 128 // rows_w
    for q in range(width // 128):
        piece = vecs[(per * q) // n, (per * q) % n]
        for u in range(1, per):
            d = per * q + u
            piece = jnp.where(lane >= u * rows_w, vecs[d // n, d % n], piece)
        span = pl.ds(q * 128, 128)
        bo[:, span] = piece[3:4] + piece[8:9]
        for ref, r in ((g1, 9), (s1, 10), (g2, 11), (s2, 12)):
            ref[:, span] = piece[r : r + 1]
    lane1 = lax.broadcasted_iota(jnp.int32, (1, 128), 1)
    for d in range(ndp):
        rows = vecs[d, at.c]
        piece = rows[4:5]
        for u in range(1, per):
            piece = jnp.where(lane1 >= u * rows_w, rows[4 + u : 5 + u], piece)
        bu[:, pl.ds(d * 128, 128)] = piece
    for p in range(3):
        piece = None
        for u in range(per):
            t = (p * width + at.c * 128) // rows_w + u
            d, r = t // 3, lax.rem(t, 3)
            rows = vecs[d // n, lax.rem(d, n)]
            row = jnp.where(r == 0, rows[0:1], jnp.where(r == 1, rows[1:2], rows[2:3]))
            piece = row if piece is None else jnp.where(lane1 >= u * rows_w, row, piece)
        bq[:, pl.ds(p * 128, 128)] = piece
    seg_t = jnp.transpose(segs[...])
    seg_col[...] = jnp.where(seg_t == 0.0, -1.0, seg_t)

    lanes = lax.broadcasted_iota(jnp.int32, (1, 128), 1)
    in_head = [(lanes >= h * HEAD) & (lanes < (h + 1) * HEAD) for h in range(heads)]
    low_half = (lanes & (HEAD - 1)) < ROT // 2
    w_q = lambda: ws[:, :, :, :384].reshape(width, 384)
    w_u = lambda: ws[:, :, :, 384:].reshape(width, fu)

    def rows_of(i):
        return pl.ds(pl.multiple_of(i * block, block), block)

    def turn(u, rows, sign):
        turned = jnp.where(low_half, pltpu.roll(u, 128 - ROT // 2, 1), pltpu.roll(u, ROT // 2, 1))
        if sign > 0:
            return u * cos_t[rows] + turned * sin_t[rows]
        return u * cos_t[rows] - turned * sin_t[rows]

    def normed_of(s, rows):
        return (xs[s, rows].astype(F32) - stat[s, rows, 0:1]) * stat[s, rows, 1:2]

    def forward_one(s):
        def body(i):
            rows = rows_of(i)
            x = xs[s, rows].astype(F32)
            mean = jnp.mean(x, axis=-1, keepdims=True)
            cen = x - mean
            rstd = lax.rsqrt(jnp.mean(cen * cen, axis=-1, keepdims=True) + 1e-05)
            stat[s, rows, 0:1] = mean
            stat[s, rows, 1:2] = rstd
            nrm = cen * rstd
            h1 = (nrm * g1[...] + s1[...]).astype(BF16)
            joined = dot(h1, w_q()) + bq[...]
            qkv[s, rows, 0:128] = (turn(joined[:, 0:128], rows, 1).astype(BF16).astype(F32) * (HEAD ** (-0.5))).astype(BF16)
            qkv[s, rows, 128:256] = turn(joined[:, 128:256], rows, 1).astype(BF16)
            qkv[s, rows, 256:384] = joined[:, 256:384].astype(BF16)
            h2 = (nrm * g2[...] + s2[...]).astype(BF16)
            act = dot(h2, w_u()) + bu[...]
            cdf = 0.5 + 0.5 * lax.erf(act * (0.5 ** 0.5))
            hid[s, rows] = (act * cdf).astype(BF16)
            gp[s, rows] = (cdf + act * (jnp.exp(-0.5 * act * act) * 0.3989422804014327)).astype(BF16)

        return body

    def attend(s, i):
        rows = pl.ds(i * block, block)
        keys = (i + 1) * block
        q_pos = lax.broadcasted_iota(jnp.int32, (block, keys), 0) + i * block
        k_pos = lax.broadcasted_iota(jnp.int32, (block, keys), 1)
        same = segs[s : s + 1, 0:keys] == seg_col[rows, s : s + 1]
        allow = (same & (k_pos <= q_pos)) | (k_pos == q_pos)
        q, k, v = qkv[s, rows, 0:128], qkv[s, 0:keys, 128:256], qkv[s, 0:keys, 256:384]
        out = None
        for h in range(heads):
            scores = dot(jnp.where(in_head[h], q, jnp.zeros_like(q)), k, NT)
            scores = jnp.where(allow, scores, -1e30)
            e = jnp.exp(scores - jnp.max(scores, axis=-1, keepdims=True))
            p = (e * (1.0 / jnp.sum(e, axis=-1, keepdims=True))).astype(BF16)
            probs[i][s, h] = p
            o = dot(p, v)
            out = o if out is None else jnp.where(in_head[h], o, out)
        ctx[s, rows] = out.astype(BF16)

    def project(s):
        def body(i):
            rows = rows_of(i)
            both = dot(ctx[s, rows], wos[...].reshape(128, width)) + dot(hid[s, rows], wds[...].reshape(fu, width))
            part[s, rows] = both.astype(BF16)

        return body

    def fold(ref, row, value):
        count, cols_ = value.shape
        ref[row, :, 0:cols_] += jnp.sum(value.reshape(count // 8, 8, cols_), axis=0)

    def backward_ffn(s):
        def body(i):
            rows = rows_of(i)
            g = gs[s, rows]
            dctx[s, rows] = dot(g, wos[...].reshape(128, width), NT).astype(BF16)
            d_act = (dot(g, wds[...].reshape(fu, width), NT) * gp[s, rows].astype(F32)).astype(BF16)
            gp[s, rows] = d_act
            fold(acc_gain, 4, g.astype(F32))
            fold(acc_bu, 0, d_act.astype(F32))
            d_h = dot(d_act, w_u(), NT)
            fold(acc_gain, 2, d_h * normed_of(s, rows))
            fold(acc_gain, 3, d_h)
            ep[s, rows] = (d_h * g2[...]).astype(BF16)

        return body

    def attend_back(s, i):
        rows = pl.ds(i * block, block)
        keys = (i + 1) * block
        span = pl.ds(0, keys)
        q, k, v = qkv[s, rows, 0:128], qkv[s, span, 128:256], qkv[s, span, 256:384]
        d_c = dctx[s, rows]
        zero = jnp.zeros_like(q)
        d_q = None
        for h in range(heads):
            p = probs[i][s, h]
            d_h = jnp.where(in_head[h], d_c, zero)
            d_p = dot(d_h, v, NT)
            p_f = p.astype(F32)
            delta = jnp.sum(p_f * d_p, axis=-1, keepdims=True)
            d_s = (p_f * (d_p - delta)).astype(BF16)
            o = dot(d_s, k)
            d_q = o if d_q is None else jnp.where(in_head[h], o, d_q)
            d_k = dot(d_s, jnp.where(in_head[h], q, zero), TN)
            d_v = dot(p, d_h, TN)
            if i == nz - 1 and h == 0:
                dk[...] = d_k
                dv[...] = d_v
            else:
                dk[span] += d_k
                dv[span] += d_v
        d_q = turn(d_q, rows, -1) * (HEAD ** (-0.5))
        d_all = jnp.concatenate([d_q, turn(dk[rows], rows, -1), dv[rows]], axis=1).astype(BF16)
        dqkv[s, rows] = d_all
        fold(acc_bq, 0, d_all.astype(F32))
        d_n = dot(d_all, w_q(), NT)
        fold(acc_gain, 0, d_n * normed_of(s, rows))
        fold(acc_gain, 1, d_n)
        ep[s, rows] = (d_n * g1[...] + ep[s, rows].astype(F32)).astype(BF16)

    def weight_cols(out, gain, shift, right):
        def body(kt):
            feat = pl.ds(pl.multiple_of(kt * 256, 256), 256)
            total = None
            for s in range(mb):
                nrm = (xs[s, :, feat].astype(F32) - stat[s, :, 0:1]) * stat[s, :, 1:2]
                h = (nrm * gain[:, feat] + shift[:, feat]).astype(BF16)
                term = dot(h, right[s], TN)
                total = term if total is None else total + term
            out[feat] = total.astype(BF16)

        return body

    acc_gain[...] = jnp.zeros_like(acc_gain)
    acc_bu[...] = jnp.zeros_like(acc_bu)
    acc_bq[...] = jnp.zeros_like(acc_bq)

    m_rs = [SeqScatter(at, part.at[s], m_sib.at[s], m_in.at[s], tok, [r.at[s] for r in (ms_s, ms_r, mu_s, mu_r, md_s, md_r)]) for s in range(mb)]
    t_rs = [SeqScatter(at, ep.at[s], t_sib.at[s], t_in.at[s], tok, [r.at[s] for r in (ts_s, ts_r, tu_s, tu_r, td_s, td_r)]) for s in range(mb)]
    rows_p = n * rows_w

    def plane_rows(ref, p):
        return ref.at[pl.ds(pl.multiple_of(p * rows_p, rows_p), rows_p)]

    wq1 = Exchange(at, "dp", lambda p: plane_rows(dwq, p), lambda s: wq_in.at[s], gq1s, gq1r)
    wu1 = Exchange(at, "dp", lambda p: plane_rows(dwu, p), lambda s: wu_in.at[s], gu1s, gu1r)
    wd1 = Exchange(at, "dp", lambda p: dwd.at[pl.ds(pl.multiple_of(p * rows_d, rows_d), rows_d)], lambda s: wd_in.at[s], gd_s, gd_r)
    wo1 = Exchange(at, "dp", lambda p: dwo, lambda s: wo_in.at[s], go1s, go1r)
    gv1 = Exchange(at, "dp", lambda p: vsum, lambda s: vin.at[s], gv1s, gv1r)
    wq2 = Exchange(at, "ctx", lambda p: wq_st.at[p], lambda s: dwq_out.at[s], gq2s, gq2r)
    wu2 = Exchange(at, "ctx", lambda p: wu_st.at[p], lambda s: dwu_out.at[s], gu2s, gu2r)
    gv2 = Exchange(at, "ctx", lambda p: vin.at[at.dp], lambda s: dv_out.at[s], gv2s, gv2r)

    def plane_sum(mine, buf):
        total = mine.astype(F32)
        for j in range(1, ndp):
            total = total + buf[lax.rem(at.dp + j, ndp)].astype(F32)
        return total

    def columns_on(first_hop, second_hop, mine, buf, stage, out):
        first_hop.wait_recv()
        total = plane_sum(plane_rows(mine, at.dp)[...], buf).astype(BF16)
        stage[...] = total.reshape(stage.shape)
        second_hop.start()
        out[at.c] = stage[at.c]

    def out_back(b, c):
        return remote(dwo.at[pl.ds(b * rows_w, rows_w)], dwo_out, go2s.at[b], go2r, at.dp, c)

    def starts(rs, zs):
        def event():
            for z in zs:
                rs.cross(z).start()

        return event

    def finish_mixed(s):
        m_rs[s].total(own)
        mixed_out[s] = (xs[s, own_rows].astype(F32) + own[...] + bo[...]).astype(BF16)

    def finish_grad(s):
        t_rs[s].total(own)
        e = own[...]
        nrm = normed_of(s, own_rows)
        inner = e - jnp.mean(e, axis=-1, keepdims=True) - nrm * jnp.mean(e * nrm, axis=-1, keepdims=True)
        grad_out[s] = (gs[s, own_rows].astype(F32) + stat[s, own_rows, 1:2] * inner).astype(BF16)

    x_ag[0].land()
    plane_w.wait_recv()
    blocks(nz, forward_one(0), {0: [lambda: x_ag[1].step(1), c_ag[0].start], 2: [lambda: x_ag[1].step(2)]})
    for i in range(nz):
        attend(0, i)
    x_ag[1].step(3)

    @pl.when(at.dp == first)
    def _():
        for b in range(ndp):
            src = lax.rem(at.c * ndp + b, n)

            @pl.when(src != at.c)
            def _():
                out_rows(b, at.c).wait_recv()

            @pl.when(src == at.c)
            def _():
                own_out.wait()

        plane_o.start()

    plane_d.wait_recv()

    @pl.when(at.dp != first)
    def _():
        plane_o.copy(first, first).wait_recv()

    blocks(nz, project(0))
    starts(m_rs[0], range(nz))()
    x_ag[1].land()
    c_ag[0].step(1)
    blocks(nz, forward_one(1), {0: [lambda: m_rs[0].step(0), c_ag[1].start], 1: [lambda: c_ag[0].step(2)], 2: [lambda: m_rs[0].step(1)], 3: [lambda: c_ag[0].step(3)]})
    for i in range(nz):
        attend(1, i)
    m_rs[0].step(2)
    blocks(nz, project(1))
    starts(m_rs[1], range(nz))()
    c_ag[1].step(1)
    c_ag[0].land()
    blocks(nz, backward_ffn(0), {0: [lambda: m_rs[1].step(0)], 1: [lambda: c_ag[1].step(2)], 2: [lambda: m_rs[1].step(1)], 3: [lambda: c_ag[1].step(3), lambda: finish_mixed(0)]})
    for i in reversed(range(nz)):
        attend_back(0, i)
        t_rs[0].cross(i).start()
    m_rs[1].step(2)
    c_ag[1].land()
    blocks(nz, backward_ffn(1), {0: [lambda: t_rs[0].step(0)], 2: [lambda: t_rs[0].step(1)], 3: [lambda: finish_mixed(1)]})
    blocks(width // 256, weight_cols(dwu, g2, s2, gp))
    wu1.start()

    def down_rows(kt):
        feat = pl.ds(pl.multiple_of(kt * 256, 256), 256)
        total = None
        for s in range(mb):
            term = dot(hid[s, :, feat], gs[s], TN)
            total = term if total is None else total + term
        dwd[feat] = total.astype(BF16)

    blocks(fu // 256, down_rows)
    wd1.start()
    t_rs[0].step(2)
    for i in reversed(range(nz)):
        attend_back(1, i)
        t_rs[1].cross(i).start()
    t_rs[1].step(0)
    total = None
    for s in range(mb):
        term = dot(ctx[s], gs[s], TN)
        total = term if total is None else total + term
    dwo[...] = total.astype(BF16)

    @pl.when(at.dp != first)
    def _():
        wo1.copy(first, at.dp).start()

    blocks(width // 256, weight_cols(dwq, g1, s1, dqkv))
    wq1.start()
    t_rs[1].step(1)
    vsum[...] = jnp.zeros_like(vsum)
    vsum[0:1, 0:384] = jnp.sum(acc_bq[0], axis=0, keepdims=True)
    vsum[1:2, 0:fu] = jnp.sum(acc_bu[0], axis=0, keepdims=True)
    for r in range(5):
        vsum[2 + r : 3 + r] = jnp.sum(acc_gain[r], axis=0, keepdims=True)
    gv1.start()
    columns_on(wu1, wu2, dwu, wu_in, wu_st, dwu_out)
    t_rs[1].step(2)
    gv1.wait_recv()
    vin[at.dp] = plane_sum(vsum[...], vin)
    gv2.start()
    dv_out[at.c] = vin[at.dp]
    wd1.wait_recv()
    dwd_out[...] = plane_sum(dwd[pl.ds(pl.multiple_of(at.dp * rows_d, rows_d), rows_d)], wd_in)
    finish_grad(0)

    @pl.when(at.dp == first)
    def _():
        wo1.wait_recv()
        dwo[...] = plane_sum(dwo[...], wo_in).astype(BF16)
        for b in range(ndp):
            owner = lax.rem(at.c * ndp + b, n)

            @pl.when(owner != at.c)
            def _():
                out_back(b, owner).start()

            @pl.when(owner == at.c)
            def _():
                dwo_out[...] = dwo[pl.ds(b * rows_w, rows_w)]

    columns_on(wq1, wq2, dwq, wq_in, wq_st, dwq_out)
    finish_grad(1)

    @pl.when(heads_of != at.c)
    def _():
        out_back(slot, at.c).wait_recv()
        out_rows(slot, heads_of).wait_send()

    @pl.when((heads_of == at.c) & (at.dp != first))
    def _():
        own_out.wait()

    @pl.when(at.dp == first)
    def _():
        plane_o.wait_send()
        for b in range(ndp):
            owner = lax.rem(at.c * ndp + b, n)

            @pl.when(owner != at.c)
            def _():
                out_back(b, owner).wait_send()

    @pl.when(at.dp != first)
    def _():
        wo1.copy(first, at.dp).wait_send()

    for part_ in (wq2, wu2, gv2):
        part_.wait_recv()
    for part_ in (cols, vec1, plane_w, plane_v, plane_d, wq1, wu1, wd1, gv1, wq2, wu2, gv2):
        part_.wait_send()
    for s in range(mb):
        x_ag[s].drain()
        c_ag[s].drain()
        m_rs[s].drain()
        t_rs[s].drain()


def fused_layer(ndp, n, dims, tok, cot, wp, wd, wo, vec, seg, cosine, sine):
    mb, tk, width, seq, heads, rows_w, rows_d = dims
    nz, block, fu = n // 2, 2 * tk, ndp * rows_d
    every = ndp * n
    dma = pltpu.SemaphoreType.DMA
    vm = pltpu.VMEM
    vmem = pl.BlockSpec(memory_space=pltpu.VMEM)
    slots = gather_slots(nz)
    scratch = [
        vm((mb, seq, width), BF16), vm((mb, seq, width), BF16),
        vm((ndp, n, rows_w, 384 + fu), BF16), vm((ndp, rows_d, width), BF16), vm((ndp, rows_w, width), BF16),
        vm((ndp, n, 16, 128), F32), vm((8, seq), F32), vm((seq, 8), F32), vm((seq, 128), F32), vm((seq, 128), F32),
        vm((1, width), F32), vm((1, width), F32), vm((1, width), F32), vm((1, width), F32), vm((1, width), F32),
        vm((1, 384), F32), vm((1, fu), F32),
        vm((mb, seq, 384), BF16), vm((mb, seq, fu), BF16), vm((mb, seq, fu), BF16), vm((mb, seq, 2), F32),
        vm((mb, seq, 128), BF16), vm((mb, seq, width), BF16), vm((mb, seq, width), BF16),
        vm((mb, seq, 128), BF16), vm((mb, seq, 384), BF16), vm((seq, 128), F32), vm((seq, 128), F32),
        vm((5, 8, width), F32), vm((1, 8, fu), F32), vm((1, 8, 384), F32),
        vm((mb, nz, tk, width), BF16), vm((mb, nz + 1, tk, width), BF16), vm((mb, nz, tk, width), BF16), vm((mb, nz + 1, tk, width), BF16),
        vm((width, 384), BF16), vm((width, fu), BF16), vm((fu, width), BF16), vm((128, width), BF16),
        vm((ndp, n * rows_w, 384), BF16), vm((ndp, n * rows_w, fu), BF16), vm((ndp, rows_d, width), BF16), vm((ndp, 128, width), BF16),
        vm((8, width), F32), vm((ndp, 8, width), F32), vm((n, rows_w, 384), BF16), vm((n, rows_w, fu), BF16),
        vm((tk, width), F32),
    ] + [vm((mb, heads, block, block * (i + 1)), BF16) for i in range(nz)]
    per_seq = [dma((mb, slots)), dma((mb, n))]
    sems = per_seq * 2 + [dma((n,)), dma((n,)), dma((ndp,)), dma((ndp,)), dma((n,)), dma((n,)), dma((ndp,)), dma((ndp,)), dma((ndp,)), dma((ndp,))]
    sems += [dma, dma((ndp,)), dma((ndp,)), dma((ndp,))]
    sems += [dma((mb, nz))] * 12
    sems += [dma((ndp,)), dma((ndp,)), dma((n,)), dma((n,))] * 2 + [dma((ndp,)), dma((ndp,))]
    sems += [dma((ndp,)), dma((ndp,)), dma((ndp,)), dma, dma((ndp,)), dma((ndp,)), dma((n,)), dma((n,)), dma((9,))]
    return pl.pallas_call(
        partial(fused_kernel, ndp, n, dims),
        out_shape=(
            jax.ShapeDtypeStruct((mb, tk, width), BF16),
            jax.ShapeDtypeStruct((mb, tk, width), BF16),
            jax.ShapeDtypeStruct((n, rows_w, 384), BF16),
            jax.ShapeDtypeStruct((n, rows_w, fu), BF16),
            jax.ShapeDtypeStruct((rows_d, width), F32),
            jax.ShapeDtypeStruct((rows_w, width), BF16),
            jax.ShapeDtypeStruct((n, 8, width), F32),
        ),
        in_specs=[ANY] * 9,
        out_specs=[vmem] * 7,
        scratch_shapes=scratch + sems,
        compiler_params=pltpu.CompilerParams(collective_id=5, has_side_effects=True, vmem_limit_bytes=63 * MIB),
    )(tok, cot, wp, wd, wo, vec, seg, cosine, sine)


def rotary_lanes(seq):
    half = ROT // 2
    inverse = (np.float32(10000.0) ** (-(np.float32(2.0) * np.arange(half, dtype=np.float32)) / np.float32(ROT))).astype(np.float32)
    angles = (np.arange(seq, dtype=np.float32)[:, None] * inverse[None, :]).astype(np.float32)
    cosine = np.ones((seq, HEAD), np.float32)
    sine = np.zeros((seq, HEAD), np.float32)
    cosine[:, :half] = cosine[:, half:ROT] = np.cos(angles)
    sine[:, :half] = -np.sin(angles)
    sine[:, half:ROT] = np.sin(angles)
    return np.tile(cosine, (1, 128 // HEAD)), np.tile(sine, (1, 128 // HEAD))


def fused_device(ndp, n, tokens, cotangent, segments, w_qkv, b_qkv, w_out, b_out, w_up, b_up, w_down, b_down, g1, s1, g2, s2):
    tok, mb, width = tokens.shape
    seq = segments.shape[1]
    hc = width // n
    rows_w, rows_d = w_qkv.shape[0], w_down.shape[0]
    fu = ndp * rows_d
    c, dp = lax.axis_index("ctx"), lax.axis_index("dp")
    toks, cot = jnp.transpose(tokens, (1, 0, 2)), jnp.transpose(cotangent, (1, 0, 2))
    qkv_cols = w_qkv.reshape(rows_w, 3, n, hc).transpose(2, 0, 1, 3).reshape(n, rows_w, 3 * hc)
    up_cols = w_up.reshape(rows_w, ndp, n, rows_d).transpose(2, 0, 1, 3).reshape(n, rows_w, fu)
    wp = jnp.concatenate([qkv_cols, up_cols], axis=2)
    units = jnp.concatenate([b_qkv, b_out, b_up, b_down, g1, s1, g2, s2]).astype(F32).reshape(-1, rows_w)
    vec = jnp.pad(jnp.tile(units, (1, 128 // rows_w)), ((0, 16 - units.shape[0]), (0, 0)))
    seg = jnp.pad(segments.astype(F32), ((0, 8 - mb), (0, 0)))
    cosine, sine = rotary_lanes(seq)
    dims = (mb, tok, width, seq, hc // HEAD, rows_w, rows_d)
    mixed, t_grad, dwq, dwu, dwd, dwo, dv = fused_layer(
        ndp, n, dims, toks, cot, wp, w_down, w_out, vec, seg, jnp.asarray(cosine), jnp.asarray(sine)
    )
    index = dp * n + c
    g_qkv = dwq.reshape(n, rows_w, 3, hc).transpose(1, 2, 0, 3).reshape(rows_w, 3 * width).astype(F32)
    g_up = dwu.reshape(n, rows_w, ndp, rows_d).transpose(1, 2, 0, 3).reshape(rows_w, -1).astype(F32)
    size = b_qkv.shape[0]
    g_bq = lax.dynamic_slice_in_dim(dv[:, 0, : 3 * hc].reshape(n, 3, hc).transpose(1, 0, 2).reshape(-1), index * size, size)
    own = lax.dynamic_index_in_dim(dv, c, 0, keepdims=False)
    g_bu = lax.dynamic_slice_in_dim(own[1], dp * rows_d, rows_d)
    four = lax.dynamic_slice_in_dim(jnp.sum(dv[:, 2:6], axis=0), index * rows_w, rows_w, axis=1)
    g_b = lax.dynamic_slice_in_dim(own[6], index * rows_w, rows_w)
    return (
        jnp.transpose(mixed, (1, 0, 2)),
        jnp.transpose(t_grad, (1, 0, 2)),
        g_qkv,
        g_bq,
        dwo.astype(F32),
        g_b,
        g_up,
        g_bu,
        dwd,
        g_b,
        four[0],
        four[1],
        four[2],
        four[3],
    )


def rotary_tables(seq):
    half_rot = ROT // 2
    inverse = 10000.0 ** (-(2.0 * jnp.arange(half_rot, dtype=F32)) / ROT)
    angles = jnp.arange(seq, dtype=jnp.int32).astype(F32)[:, None] * inverse[None, :]
    angles = jnp.concatenate([angles, angles], axis=-1)
    return (jnp.cos(angles)[None, :, None, :], jnp.sin(angles)[None, :, None, :])


def rotate(values, cosine, sine, back=False):
    half_rot = ROT // 2
    lead = values[..., :ROT]
    if back:
        u = lead * sine
        turned = jnp.concatenate([u[..., half_rot:], -u[..., :half_rot]], axis=-1)
        return jnp.concatenate([lead * cosine + turned, values[..., ROT:]], axis=-1)
    turned = jnp.concatenate([-lead[..., half_rot:], lead[..., :half_rot]], axis=-1)
    return jnp.concatenate([lead * cosine + turned * sine, values[..., ROT:]], axis=-1)


def per_device(ndp, n, tokens, cotangent, segments, w_qkv, b_qkv, w_out, b_out, w_up, b_up, w_down, b_down, g1, s1, g2, s2):
    tok, mb, width = tokens.shape
    seq = segments.shape[1]
    heads_all = width // HEAD
    hc = width // n
    heads = hc // HEAD
    rows_w = w_qkv.shape[0]
    rows_d = w_down.shape[0]
    fu = ndp * rows_d
    c = lax.axis_index("ctx")
    dp = lax.axis_index("dp")
    scale = HEAD ** (-0.5)

    cot = jnp.transpose(cotangent, (1, 0, 2))
    toks = jnp.transpose(tokens, (1, 0, 2))
    qkv_cols = w_qkv.reshape(rows_w, 3, n, hc).transpose(2, 0, 1, 3).reshape(n, rows_w, 3 * hc)
    up_cols = w_up.reshape(rows_w, ndp, n, rows_d).transpose(2, 0, 1, 3).reshape(n, rows_w, fu)
    wp = jnp.concatenate([qkv_cols, up_cols], axis=2)
    shard_vecs = (b_qkv, b_out, b_up, b_down, g1, s1, g2, s2)
    sizes = [v.shape[0] for v in shard_vecs]
    vec = jnp.concatenate(shard_vecs)
    lanes = 128
    per_vec = 16 * lanes
    vec = jnp.pad(vec, (0, per_vec - vec.shape[0])).reshape(16, lanes)
    x, g, w, wd, wo, vecs = gather_all(ndp, n, toks, cot, wp, w_down, w_out, vec)
    w = w.reshape(width, 3 * hc + fu)
    wq, wu = w[:, : 3 * hc], w[:, 3 * hc :]
    wd = wd.reshape(fu, width)
    wo = wo.reshape(hc, width)
    flat = vecs.reshape(ndp * n, per_vec).astype(F32)
    starts = [sum(sizes[:i]) for i in range(len(sizes))]
    full = [flat[:, s : s + z].reshape(-1) for s, z in zip(starts, sizes)]
    bq_all, bo, bu_all, bd, gain1, shift1, gain2, shift2 = full
    bq = lax.dynamic_index_in_dim(bq_all.reshape(3, n, hc), c, 1, keepdims=False).reshape(3 * hc)
    bu = lax.dynamic_index_in_dim(bu_all.reshape(ndp, n, rows_d), c, 1, keepdims=False).reshape(fu)

    xf = x.reshape(mb * seq, width).astype(F32)
    gl = g.reshape(mb * seq, width)
    mean = jnp.mean(xf, axis=-1, keepdims=True)
    cen = xf - mean
    rstd = lax.rsqrt(jnp.mean(cen * cen, axis=-1, keepdims=True) + 1e-05)
    normed = cen * rstd
    h1 = (normed * gain1 + shift1).astype(BF16)
    h2 = (normed * gain2 + shift2).astype(BF16)
    joined = (dot(h1, wq) + bq).reshape(mb, seq, 3, heads, HEAD)
    cosine, sine = rotary_tables(seq)
    q = rotate(joined[:, :, 0], cosine, sine).astype(BF16)
    k = rotate(joined[:, :, 1], cosine, sine).astype(BF16)
    v = joined[:, :, 2].astype(BF16)
    pos = jnp.arange(seq, dtype=jnp.int32)
    same = (segments[:, None, :] == segments[:, :, None]) & (segments[:, :, None] > 0)
    allow = (same & (pos[None, None, :] <= pos[None, :, None])) | (pos[None, None, :] == pos[None, :, None])
    scores = jnp.einsum("sqhd,skhd->shqk", q, k, preferred_element_type=F32) * scale
    scores = jnp.where(allow[:, None], scores, -1e30)
    top = jnp.max(scores, axis=-1, keepdims=True)
    e = jnp.exp(scores - top)
    probs = e / jnp.sum(e, axis=-1, keepdims=True)
    pl_low = probs.astype(BF16)
    ctx_f = jnp.einsum("shqk,skhd->sqhd", pl_low, v, preferred_element_type=F32)
    ctx = ctx_f.astype(BF16).reshape(mb * seq, hc)
    act = dot(h2, wu) + bu
    hidden = jax.nn.gelu(act, approximate=False).astype(BF16)
    part = (dot(ctx, wo) + dot(hidden, wd)).astype(BF16).reshape(mb, seq, width)
    mixed_sum = scatter_ctx(ndp, n, part, 1)
    mixed = (toks.astype(F32) + mixed_sum + bo + bd).astype(BF16)

    gf = gl.astype(F32)
    d_wd = dot(hidden, gl, ((0,), (0,)))
    d_wo = dot(ctx, gl, ((0,), (0,)))
    d_hidden = dot(gl, wd, ((1,), (1,)))
    _, pull = jax.vjp(partial(jax.nn.gelu, approximate=False), act)
    d_act = pull(d_hidden)[0].astype(BF16)
    d_wu = dot(h2, d_act, ((0,), (0,)))
    d_bu = jnp.sum(d_act.astype(F32), axis=0)
    d_h2 = dot(d_act, wu, ((1,), (1,)))
    d_ctx = dot(gl, wo, ((1,), (1,))).astype(BF16).reshape(mb, seq, heads, HEAD)
    d_probs = jnp.einsum("sqhd,skhd->shqk", d_ctx, v, preferred_element_type=F32)
    delta = jnp.sum(probs * d_probs, axis=-1, keepdims=True)
    d_scores = jnp.where(allow[:, None], probs * (d_probs - delta), 0.0).astype(BF16)
    d_q = jnp.einsum("shqk,skhd->sqhd", d_scores, k, preferred_element_type=F32) * scale
    d_k = jnp.einsum("shqk,sqhd->skhd", d_scores, q, preferred_element_type=F32) * scale
    d_v = jnp.einsum("shqk,sqhd->skhd", pl_low, d_ctx, preferred_element_type=F32)
    d_q = rotate(d_q, cosine, sine, True)
    d_k = rotate(d_k, cosine, sine, True)
    d_qkv = jnp.stack([d_q, d_k, d_v], axis=2).astype(BF16).reshape(mb * seq, 3 * hc)
    d_wq = dot(h1, d_qkv, ((0,), (0,)))
    d_bq = jnp.sum(d_qkv.astype(F32), axis=0)
    d_h1 = dot(d_qkv, wq, ((1,), (1,)))
    e_sum = (d_h1 * gain1 + d_h2 * gain2).astype(BF16).reshape(mb, seq, width)
    e_own = scatter_ctx(ndp, n, e_sum, 2)
    own_x = toks.astype(F32)
    o_mean = jnp.mean(own_x, axis=-1, keepdims=True)
    o_cen = own_x - o_mean
    o_rstd = lax.rsqrt(jnp.mean(o_cen * o_cen, axis=-1, keepdims=True) + 1e-05)
    o_n = o_cen * o_rstd
    t_grad = o_rstd * (e_own - jnp.mean(e_own, axis=-1, keepdims=True) - o_n * jnp.mean(e_own * o_n, axis=-1, keepdims=True))
    tokens_grad = (cot.astype(F32) + t_grad).astype(BF16)

    rows = [
        jnp.pad(d_bq, (0, width - 3 * hc)),
        jnp.pad(d_bu, (0, width - fu)),
        jnp.sum(d_h1 * normed, axis=0),
        jnp.sum(d_h1, axis=0),
        jnp.sum(d_h2 * normed, axis=0),
        jnp.sum(d_h2, axis=0),
        jnp.sum(gf, axis=0),
        jnp.zeros((width,), F32),
    ]
    dwp = jnp.concatenate([d_wq, d_wu], axis=1).astype(BF16).reshape(ndp, n, rows_w, 3 * hc + fu)
    dw, dwd, dwo, dv = grads_all(
        ndp, n, dwp, d_wd.astype(BF16).reshape(ndp, rows_d, width), d_wo.astype(BF16).reshape(ndp, rows_w, width), jnp.stack(rows)
    )
    index = dp * n + c
    g_qkv = dw[:, :, : 3 * hc].reshape(n, rows_w, 3, hc).transpose(1, 2, 0, 3).reshape(rows_w, 3 * width).astype(F32)
    g_up = dw[:, :, 3 * hc :].reshape(n, rows_w, ndp, rows_d).transpose(1, 2, 0, 3).reshape(rows_w, -1).astype(F32)
    g_bq = lax.dynamic_slice_in_dim(dv[:, 0, : 3 * hc].reshape(n, 3, hc).transpose(1, 0, 2).reshape(-1), index * sizes[0], sizes[0])
    own = lax.dynamic_index_in_dim(dv, c, 0, keepdims=False)
    g_bu = lax.dynamic_slice_in_dim(own[1], dp * rows_d, rows_d)
    four = lax.dynamic_slice_in_dim(jnp.sum(dv[:, 2:6], axis=0), index * rows_w, rows_w, axis=1)
    g_b = lax.dynamic_slice_in_dim(own[6], index * rows_w, rows_w)
    return (
        jnp.transpose(mixed, (1, 0, 2)),
        jnp.transpose(tokens_grad, (1, 0, 2)),
        g_qkv,
        g_bq,
        dwo.astype(F32),
        g_b,
        g_up,
        g_bu,
        dwd,
        g_b,
        four[0],
        four[1],
        four[2],
        four[3],
    )


def program(ndp, n, *args):
    tokens, w_qkv, w_down = args[0], args[3], args[9]
    rows_w = w_qkv.shape[0]
    whole_tiles = rows_w % 16 == 0 and tokens.shape[2] // n == 128 and w_down.shape[0] == 128 and tokens.shape[0] % 16 == 0
    return (fused_device if whole_tiles else per_device)(ndp, n, *args)


def solution(mesh):
    every = ("dp", "ctx")
    mat, vec, act = P(every, None), P(every), P("ctx", "dp", None)
    placed = (act, act, P("dp", None), mat, vec, mat, vec, mat, vec, mat, vec, vec, vec, vec, vec)
    return jax.shard_map(
        partial(program, mesh.shape["dp"], mesh.shape["ctx"]),
        mesh=mesh,
        in_specs=placed,
        out_specs=(act, act, mat, vec, mat, vec, mat, vec, mat, vec, vec, vec, vec, vec),
        check_vma=False,
    )
```

```python
from functools import partial

import jax
import jax.numpy as jnp
import numpy as np
from jax import lax
from jax.experimental import pallas as pl
from jax.experimental.pallas import tpu as pltpu
from jax.sharding import PartitionSpec as P

HEAD = 64
ROT = 16
MIB = 1 << 20
MESH = pl.DeviceIdType.MESH
ANY = pl.BlockSpec(memory_space=pl.ANY)
F32 = jnp.float32
BF16 = jnp.bfloat16


class Place:
    def __init__(self, ndp, n):
        self.ndp, self.n, self.nz = ndp, n, n // 2
        self.dp = lax.axis_index("dp")
        self.c = lax.axis_index("ctx")
        self.z = self.c // 2
        self.core = lax.rem(self.c, 2)
        self.sib = self.c + 1 - 2 * self.core
        self.has_up = self.z + 1 < self.nz
        self.has_down = self.z > 0
        self.px = self.dp + 1 - 2 * lax.rem(self.dp, 2)
        self.py = lax.rem(self.dp + 2, 4)
        self.diag = 3 - self.dp
        index, back = self.dp * n + self.c, self.c * ndp + self.dp
        self.rows_dp, self.rows_c = lax.rem(index, ndp), index // ndp
        self.from_dp, self.from_c = back // n, lax.rem(back, n)
        self.moves = index != back

    def barrier(self, ctx_all, dp_all, rows=False):
        bar = pltpu.get_barrier_semaphore()
        count = 0
        if rows:
            count = count + 2 * self.moves.astype(jnp.int32)

            @pl.when(self.moves)
            def _():
                pl.semaphore_signal(bar, inc=1, device_id=(self.rows_dp, self.rows_c), device_id_type=MESH)
                pl.semaphore_signal(bar, inc=1, device_id=(self.from_dp, self.from_c), device_id_type=MESH)

        if ctx_all:
            for j in range(1, self.n):
                peer = lax.rem(self.c + j, self.n)
                pl.semaphore_signal(bar, inc=1, device_id=(self.dp, peer), device_id_type=MESH)
                count += 1
        else:
            pl.semaphore_signal(bar, inc=1, device_id=(self.dp, self.sib), device_id_type=MESH)
            count += 1
            for ok, peer in ((self.has_up, self.c + 2), (self.has_down, self.c - 2)):

                @pl.when(ok)
                def _():
                    pl.semaphore_signal(bar, inc=1, device_id=(self.dp, peer), device_id_type=MESH)

        if dp_all:
            for j in range(1, self.ndp):
                peer = lax.rem(self.dp + j, self.ndp)
                pl.semaphore_signal(bar, inc=1, device_id=(peer, self.c), device_id_type=MESH)
                count += 1
        if not ctx_all:
            count = count + self.has_up.astype(jnp.int32) + self.has_down.astype(jnp.int32)
        pl.semaphore_wait(bar, count)


def remote(src, dst, send, recv, dp, c):
    return pltpu.make_async_remote_copy(
        src_ref=src,
        dst_ref=dst,
        send_sem=send,
        recv_sem=recv,
        device_id=(dp, c),
        device_id_type=MESH,
    )


class Gather:
    def __init__(self, at, src, dst, tok, sends, recvs):
        self.at, self.src, self.dst, self.tok, self.sends, self.recvs = at, src, dst, tok, sends, recvs

    def rows(self, c):
        return self.dst.at[:, pl.ds(pl.multiple_of(c * self.tok, self.tok), self.tok)]

    def copy(self, block, slot, c, src=None):
        at = self.at
        src = self.rows(block) if src is None else src
        return remote(src, self.rows(block), self.sends.at[slot], self.recvs.at[block], at.dp, c)

    def start(self):
        at = self.at

        @pl.when(at.has_up)
        def _():
            self.copy(at.c, 0, at.c + 2, self.src).start()

        @pl.when(at.has_down)
        def _():
            self.copy(at.c, 1, at.c - 2, self.src).start()

        self.copy(at.c, 2, at.sib, self.src).start()

    def step(self, k):
        at = self.at
        low, high = at.c - 2 * k, at.c + 2 * k

        @pl.when(at.z >= k)
        def _():
            self.copy(low, 0, at.c).wait_recv()

            @pl.when(at.has_up)
            def _():
                self.copy(low, 3 * k, at.c + 2).start()

            self.copy(low, 3 * k + 2, at.sib).start()

        @pl.when(at.z + k < at.nz)
        def _():
            self.copy(high, 0, at.c).wait_recv()

            @pl.when(at.has_down)
            def _():
                self.copy(high, 3 * k + 1, at.c - 2).start()

            self.copy(high, 3 * at.nz + k, at.sib).start()

    def finish(self):
        at = self.at
        for z in range(at.nz):
            self.copy(2 * z + 1 - at.core, 0, at.c).wait_recv()
        self.copy(at.c, 2, at.sib, self.src).wait_send()
        for k in range(at.nz):

            @pl.when((at.z >= k) & at.has_up)
            def _():
                self.copy(at.c, 3 * k, at.c).wait_send()

            @pl.when((at.z + k < at.nz) & at.has_down)
            def _():
                self.copy(at.c, 3 * k + 1, at.c).wait_send()

            if k:

                @pl.when(at.z >= k)
                def _():
                    self.copy(at.c, 3 * k + 2, at.c).wait_send()

                @pl.when(at.z + k < at.nz)
                def _():
                    self.copy(at.c, 3 * at.nz + k, at.c).wait_send()


def gather_slots(nz):
    return 4 * nz


class Exchange:
    def __init__(self, at, axis, src, dst, sends, recvs):
        self.at, self.axis, self.src, self.dst, self.sends, self.recvs = at, axis, src, dst, sends, recvs
        self.me, self.count = (at.c, at.n) if axis == "ctx" else (at.dp, at.ndp)

    def copy(self, peer, sender):
        at = self.at
        to = (at.dp, peer) if self.axis == "ctx" else (peer, at.c)
        return remote(self.src(peer), self.dst(sender), self.sends.at[peer], self.recvs.at[sender], *to)

    def start(self):
        for j in range(1, self.count):
            self.copy(lax.rem(self.me + j, self.count), self.me).start()

    def wait_recv(self):
        for j in range(1, self.count):
            peer = lax.rem(self.me + j, self.count)
            self.copy(peer, peer).wait_recv()

    def wait_send(self):
        for j in range(1, self.count):
            peer = lax.rem(self.me + j, self.count)
            self.copy(peer, self.me).wait_send()


def gather_kernel(ndp, n, tok_ref, cot_ref, wp_ref, wd_ref, wo_ref, vec_ref, x_out, g_out, w_out, wd_out, wo_out, vec_out, *sems):
    at = Place(ndp, n)
    tok = tok_ref.shape[1]
    (x_send, x_recv, g_send, g_recv, w1s, w1r, w2s, w2r, v1s, v1r, v2s, v2r, ds, dr, o1s, o1r, o2s, o2r, local) = sems
    at.barrier(True, True)
    own = (
        pltpu.make_async_copy(wp_ref.at[at.c], w_out.at[at.dp, at.c], local.at[0]),
        pltpu.make_async_copy(vec_ref, vec_out.at[at.dp, at.c], local.at[1]),
        pltpu.make_async_copy(wd_ref, wd_out.at[at.dp], local.at[2]),
        pltpu.make_async_copy(tok_ref, x_out.at[:, pl.ds(pl.multiple_of(at.c * tok, tok), tok)], local.at[3]),
        pltpu.make_async_copy(cot_ref, g_out.at[:, pl.ds(pl.multiple_of(at.c * tok, tok), tok)], local.at[4]),
    )
    for copy in own:
        copy.start()
    down_w = Exchange(at, "dp", lambda p: wd_ref, lambda s: wd_out.at[s], ds, dr)
    cols = Exchange(at, "ctx", lambda p: wp_ref.at[p], lambda s: w_out.at[at.dp, s], w1s, w1r)
    vecs = Exchange(at, "ctx", lambda p: vec_ref, lambda s: vec_out.at[at.dp, s], v1s, v1r)
    plane_w = Exchange(at, "dp", lambda p: w_out.at[at.dp], lambda s: w_out.at[s], w2s, w2r)
    plane_v = Exchange(at, "dp", lambda p: vec_out.at[at.dp], lambda s: vec_out.at[s], v2s, v2r)
    plane_o = Exchange(at, "dp", lambda p: wo_out, lambda s: wo_out, o2s, o2r)
    cols.start()
    vecs.start()
    index = at.dp * n + at.c
    heads_of, slot = index // ndp, lax.rem(index, ndp)

    def out_rows(b, c):
        return remote(wo_ref, wo_out.at[b], o1s, o1r.at[b], at.dp, c)

    @pl.when(heads_of != at.c)
    def _():
        out_rows(slot, heads_of).start()

    own_rows = pltpu.make_async_copy(wo_ref, wo_out.at[slot], local.at[5])

    @pl.when(heads_of == at.c)
    def _():
        own_rows.start()

    down_w.start()
    x_ag = Gather(at, tok_ref, x_out, tok, x_send, x_recv)
    g_ag = Gather(at, cot_ref, g_out, tok, g_send, g_recv)
    x_ag.start()
    own[0].wait()
    cols.wait_recv()
    plane_w.start()
    own[1].wait()
    vecs.wait_recv()
    plane_v.start()
    first = at.c * ndp // n

    @pl.when(at.dp == first)
    def _():
        for b in range(ndp):
            src = lax.rem(at.c * ndp + b, n)

            @pl.when(src != at.c)
            def _():
                out_rows(b, at.c).wait_recv()

            @pl.when(src == at.c)
            def _():
                own_rows.wait()

        plane_o.start()

    for k in range(1, at.nz):
        x_ag.step(k)
        if k == 1:
            g_ag.start()
    for k in range(1, at.nz):
        g_ag.step(k)
    x_ag.finish()
    g_ag.finish()

    @pl.when(heads_of != at.c)
    def _():
        out_rows(slot, heads_of).wait_send()

    @pl.when((heads_of == at.c) & (at.dp != first))
    def _():
        own_rows.wait()

    @pl.when(at.dp == first)
    def _():
        plane_o.wait_send()

    @pl.when(at.dp != first)
    def _():
        plane_o.copy(first, first).wait_recv()

    for copy in own[2:]:
        copy.wait()
    for part in (down_w, plane_w, plane_v):
        part.wait_recv()
    for part in (down_w, cols, vecs, plane_w, plane_v):
        part.wait_send()


def gather_all(ndp, n, tok, cot, wp, wd, wo, vec):
    mb, rows, width = tok.shape
    dma = pltpu.SemaphoreType.DMA
    slots = gather_slots(n // 2)
    return pl.pallas_call(
        partial(gather_kernel, ndp, n),
        out_shape=(
            jax.ShapeDtypeStruct((mb, rows * n, width), BF16),
            jax.ShapeDtypeStruct((mb, rows * n, width), BF16),
            jax.ShapeDtypeStruct((ndp,) + wp.shape, BF16),
            jax.ShapeDtypeStruct((ndp,) + wd.shape, BF16),
            jax.ShapeDtypeStruct((ndp,) + wo.shape, BF16),
            jax.ShapeDtypeStruct((ndp, n) + vec.shape, vec.dtype),
        ),
        in_specs=[ANY] * 6,
        out_specs=[ANY] * 6,
        scratch_shapes=[
            dma((slots,)), dma((n,)), dma((slots,)), dma((n,)),
            dma((n,)), dma((n,)), dma((ndp,)), dma((ndp,)),
            dma((n,)), dma((n,)), dma((ndp,)), dma((ndp,)),
            dma((ndp,)), dma((ndp,)),
            dma, dma((ndp,)), dma((ndp,)), dma((ndp,)),
            dma((6,)),
        ],
        compiler_params=pltpu.CompilerParams(collective_id=0, has_side_effects=True),
    )(tok, cot, wp, wd, wo, vec)


class Scatter:
    def __init__(self, at, part, out, sib_buf, low_buf, high_buf, stage, tok, sems):
        self.at, self.part, self.out, self.tok = at, part, out, tok
        self.sib_buf, self.low_buf, self.high_buf, self.stage = sib_buf, low_buf, high_buf, stage
        self.s_send, self.s_recv, self.up_send, self.up_recv, self.dn_send, self.dn_recv = sems

    def rows(self, c):
        return pl.ds(pl.multiple_of(c * self.tok, self.tok), self.tok)

    def cross(self, z):
        at = self.at
        src = self.part.at[:, self.rows(2 * z + 1 - at.core)]
        return remote(src, self.sib_buf.at[z], self.s_send.at[z], self.s_recv.at[z], at.dp, at.sib)

    def up(self, z):
        at = self.at
        return remote(self.stage.at[z], self.low_buf.at[z], self.up_send.at[z], self.up_recv.at[z], at.dp, at.c + 2)

    def down(self, z):
        at = self.at
        return remote(self.stage.at[z], self.high_buf.at[z], self.dn_send.at[z], self.dn_recv.at[z], at.dp, at.c - 2)

    def order(self):
        nz = self.at.nz
        for i in range(nz):
            yield nz - 1 - i
            if i != nz - 1 - i:
                pass

    def start(self):
        for i in range(self.at.nz):
            self.cross(i).start()

    def chip_sum(self, z):
        at = self.at
        mine = self.part[:, self.rows(2 * z + at.core)].astype(F32)
        return mine + self.sib_buf[z].astype(F32)

    def step(self, i):
        at = self.at
        up_z, dn_z = at.nz - 1 - i, i

        @pl.when(up_z > at.z)
        def _():
            self.cross(up_z).wait_recv()
            self.stage[up_z] = self.chip_sum(up_z).astype(BF16)

            @pl.when(at.has_down)
            def _():
                self.up(up_z).wait_recv()
                self.stage[up_z] = (self.stage[up_z].astype(F32) + self.low_buf[up_z].astype(F32)).astype(BF16)

            self.up(up_z).start()

        @pl.when(dn_z < at.z)
        def _():
            self.cross(dn_z).wait_recv()
            self.stage[dn_z] = self.chip_sum(dn_z).astype(BF16)

            @pl.when(at.has_up)
            def _():
                self.down(dn_z).wait_recv()
                self.stage[dn_z] = (self.stage[dn_z].astype(F32) + self.high_buf[dn_z].astype(F32)).astype(BF16)

            self.down(dn_z).start()

    def finish(self):
        at = self.at
        self.cross(at.z).wait_recv()
        self.out[...] = self.chip_sum(at.z)

        @pl.when(at.has_down)
        def _():
            self.up(at.z).wait_recv()
            self.out[...] += self.low_buf[at.z].astype(F32)

        @pl.when(at.has_up)
        def _():
            self.down(at.z).wait_recv()
            self.out[...] += self.high_buf[at.z].astype(F32)

        for z in range(at.nz):
            self.cross(z).wait_send()

            @pl.when(z > at.z)
            def _():
                self.up(z).wait_send()

            @pl.when(z < at.z)
            def _():
                self.down(z).wait_send()


def scatter_kernel(ndp, n, part_ref, out_ref, sib_buf, low_buf, high_buf, stage, *sems):
    at = Place(ndp, n)
    at.barrier(False, False)
    work = Scatter(at, part_ref, out_ref, sib_buf, low_buf, high_buf, stage, out_ref.shape[1], sems)
    work.start()
    for i in range(at.nz - 1):
        work.step(i)
    work.finish()


def scatter_ctx(ndp, n, part, collective):
    mb, seq, width = part.shape
    nz, tok = n // 2, seq // n
    dma = pltpu.SemaphoreType.DMA
    buf = pltpu.VMEM((nz, mb, tok, width), BF16)
    vmem = pl.BlockSpec(memory_space=pltpu.VMEM)
    return pl.pallas_call(
        partial(scatter_kernel, ndp, n),
        out_shape=jax.ShapeDtypeStruct((mb, tok, width), F32),
        in_specs=[vmem],
        out_specs=vmem,
        scratch_shapes=[buf, buf, buf, buf] + [dma((nz,))] * 6,
        compiler_params=pltpu.CompilerParams(collective_id=collective, has_side_effects=True, vmem_limit_bytes=48 * MIB),
    )(part)


def grads_kernel(ndp, n, wp_ref, wd_ref, wo_ref, v_ref, w_out, wd_out, wo_out, v_out, wbuf, wsum, dbuf, obuf, osum, vbuf, vsum, *sems):
    at = Place(ndp, n)
    (w1s, w1r, ds, dr, o1s, o1r, v1s, v1r, w2s, w2r, v2s, v2r, o2s, o2r, local) = sems
    at.barrier(True, True)
    first = at.c * ndp // n
    w1 = Exchange(at, "dp", lambda p: wp_ref.at[p], lambda s: wbuf.at[s], w1s, w1r)
    d1 = Exchange(at, "dp", lambda p: wd_ref.at[p], lambda s: dbuf.at[s], ds, dr)
    v1 = Exchange(at, "dp", lambda p: v_ref, lambda s: vbuf.at[s], v1s, v1r)
    o1 = Exchange(at, "dp", lambda p: wo_ref, lambda s: obuf.at[s], o1s, o1r)
    w1.start()
    v1.start()

    @pl.when(at.dp != first)
    def _():
        o1.copy(first, at.dp).start()

    d1.start()

    def total(ref, mine, get):
        ref[...] = mine
        for j in range(1, ndp):
            ref[...] += get(lax.rem(at.dp + j, ndp)).astype(F32)

    w1.wait_recv()
    total(wsum, wp_ref[at.dp].astype(F32), lambda s: wbuf[s])
    wbuf[at.dp] = wsum[...].astype(BF16)
    w2 = Exchange(at, "ctx", lambda p: wbuf.at[at.dp, p], lambda s: w_out.at[s], w2s, w2r)
    w2.start()
    w_out[at.c] = wbuf[at.dp, at.c]
    v1.wait_recv()
    total(vsum, v_ref[...], lambda s: vbuf[s])
    v2 = Exchange(at, "ctx", lambda p: vsum, lambda s: v_out.at[s], v2s, v2r)
    v2.start()
    v_out[at.c] = vsum[...]

    index = at.dp * n + at.c
    heads_of, slot = index // ndp, lax.rem(index, ndp)

    def out_rows(b, c):
        return remote(osum.at[b], wo_out, o2s.at[b], o2r, at.dp, c)

    @pl.when(at.dp == first)
    def _():
        o1.wait_recv()
        rows = wo_ref[...].astype(F32)
        for j in range(1, ndp):
            rows += obuf[lax.rem(at.dp + j, ndp)].astype(F32)
        osum[...] = rows.astype(BF16)
        for b in range(ndp):
            owner = lax.rem(at.c * ndp + b, n)

            @pl.when(owner != at.c)
            def _():
                out_rows(b, owner).start()

            @pl.when(owner == at.c)
            def _():
                wo_out[...] = osum[b]

    d1.wait_recv()
    total(wd_out, wd_ref[at.dp].astype(F32), lambda s: dbuf[s])

    @pl.when(heads_of != at.c)
    def _():
        out_rows(slot, at.c).wait_recv()

    w2.wait_recv()
    v2.wait_recv()
    for part in (w1, v1, d1, w2, v2):
        part.wait_send()

    @pl.when(at.dp != first)
    def _():
        o1.copy(first, at.dp).wait_send()

    @pl.when(at.dp == first)
    def _():
        for b in range(ndp):
            owner = lax.rem(at.c * ndp + b, n)

            @pl.when(owner != at.c)
            def _():
                out_rows(b, owner).wait_send()


def grads_all(ndp, n, wp, wd, wo, v):
    dma = pltpu.SemaphoreType.DMA
    vmem = pl.BlockSpec(memory_space=pltpu.VMEM)
    return pl.pallas_call(
        partial(grads_kernel, ndp, n),
        out_shape=(
            jax.ShapeDtypeStruct(wp.shape[1:], BF16),
            jax.ShapeDtypeStruct(wd.shape[1:], F32),
            jax.ShapeDtypeStruct(wo.shape[1:], BF16),
            jax.ShapeDtypeStruct((n,) + v.shape, F32),
        ),
        in_specs=[vmem] * 4,
        out_specs=[vmem] * 4,
        scratch_shapes=[
            pltpu.VMEM(wp.shape, BF16),
            pltpu.VMEM(wp.shape[1:], F32),
            pltpu.VMEM(wd.shape, BF16),
            pltpu.VMEM((ndp,) + wo.shape, BF16),
            pltpu.VMEM(wo.shape, BF16),
            pltpu.VMEM((ndp,) + v.shape, F32),
            pltpu.VMEM(v.shape, F32),
            dma((ndp,)), dma((ndp,)), dma((ndp,)), dma((ndp,)), dma((ndp,)), dma((ndp,)), dma((ndp,)), dma((ndp,)),
            dma((n,)), dma((n,)), dma((n,)), dma((n,)), dma((ndp,)), dma,
            dma((1,)),
        ],
        compiler_params=pltpu.CompilerParams(collective_id=3, has_side_effects=True, vmem_limit_bytes=48 * MIB),
    )(wp, wd, wo, v)


def dot(a, b, dims=((1,), (0,))):
    return lax.dot_general(a, b, (dims, ((), ())), preferred_element_type=F32)


NT = ((1,), (1,))
TN = ((0,), (0,))


class SeqGather:
    def __init__(self, at, src, dst, tok, sends, recvs):
        self.at, self.src, self.dst, self.tok, self.sends, self.recvs = at, src, dst, tok, sends, recvs

    def rows(self, c):
        return self.dst.at[pl.ds(pl.multiple_of(c * self.tok, self.tok), self.tok)]

    def copy(self, block, slot, c, src=None):
        src = self.rows(block) if src is None else src
        return remote(src, self.rows(block), self.sends.at[slot], self.recvs.at[block], self.at.dp, c)

    def start(self):
        at = self.at

        @pl.when(at.has_up)
        def _():
            self.copy(at.c, 0, at.c + 2, self.src).start()

        @pl.when(at.has_down)
        def _():
            self.copy(at.c, 1, at.c - 2, self.src).start()

        self.copy(at.c, 2, at.sib, self.src).start()

    def step(self, k):
        at = self.at
        low, high = at.c - 2 * k, at.c + 2 * k

        @pl.when(at.z >= k)
        def _():
            self.copy(low, 0, at.c).wait_recv()

            @pl.when(at.has_up)
            def _():
                self.copy(low, 3 * k, at.c + 2).start()

            self.copy(low, 3 * k + 2, at.sib).start()

        @pl.when(at.z + k < at.nz)
        def _():
            self.copy(high, 0, at.c).wait_recv()

            @pl.when(at.has_down)
            def _():
                self.copy(high, 3 * k + 1, at.c - 2).start()

            self.copy(high, 3 * at.nz + k, at.sib).start()

    def land(self):
        at = self.at
        for z in range(at.nz):
            self.copy(2 * z + 1 - at.core, 0, at.c).wait_recv()

    def drain(self):
        at = self.at
        self.copy(at.c, 2, at.sib, self.src).wait_send()
        for k in range(at.nz):

            @pl.when((at.z >= k) & at.has_up)
            def _():
                self.copy(at.c, 3 * k, at.c).wait_send()

            @pl.when((at.z + k < at.nz) & at.has_down)
            def _():
                self.copy(at.c, 3 * k + 1, at.c).wait_send()

            if k:

                @pl.when(at.z >= k)
                def _():
                    self.copy(at.c, 3 * k + 2, at.c).wait_send()

                @pl.when(at.z + k < at.nz)
                def _():
                    self.copy(at.c, 3 * at.nz + k, at.c).wait_send()


class SeqScatter:
    def __init__(self, at, part, sib_buf, in_buf, tok, sems):
        self.at, self.part, self.sib_buf, self.in_buf, self.tok = at, part, sib_buf, in_buf, tok
        self.s_send, self.s_recv, self.up_send, self.up_recv, self.dn_send, self.dn_recv = sems

    def rows(self, c):
        return pl.ds(pl.multiple_of(c * self.tok, self.tok), self.tok)

    def cross(self, z):
        at = self.at
        src = self.part.at[self.rows(2 * z + 1 - at.core)]
        return remote(src, self.sib_buf.at[z], self.s_send.at[z], self.s_recv.at[z], at.dp, at.sib)

    def up(self, z):
        at = self.at
        return remote(self.sib_buf.at[z], self.in_buf.at[z], self.up_send.at[z], self.up_recv.at[z], at.dp, at.c + 2)

    def down(self, z, sender=None):
        at = self.at
        slot = jnp.where(z == (at.z - 1 if sender is None else sender - 1), at.nz, z)
        return remote(self.sib_buf.at[z], self.in_buf.at[slot], self.dn_send.at[z], self.dn_recv.at[z], at.dp, at.c - 2)

    def chip_sum(self, z):
        mine = self.part[self.rows(2 * z + self.at.core)].astype(F32)
        return mine + self.sib_buf[z].astype(F32)

    def step(self, t):
        self.step_up(t)
        self.step_down(t)

    def step_up(self, t):
        at = self.at
        z = at.nz - 1 - t + at.z

        @pl.when(at.z <= t)
        def _():
            self.cross(z).wait_recv()

            @pl.when(at.has_down)
            def _():
                self.up(z).wait_recv()
                self.sib_buf[z] = (self.chip_sum(z) + self.in_buf[z].astype(F32)).astype(BF16)

            @pl.when(jnp.logical_not(at.has_down))
            def _():
                self.sib_buf[z] = self.chip_sum(z).astype(BF16)

            self.up(z).start()

    def step_down(self, t):
        at = self.at
        z = t - (at.nz - 1 - at.z)

        @pl.when(z >= 0)
        def _():
            self.cross(z).wait_recv()

            @pl.when(at.has_up)
            def _():
                self.down(z, at.z + 1).wait_recv()
                self.sib_buf[z] = (self.chip_sum(z) + self.in_buf[z].astype(F32)).astype(BF16)

            @pl.when(jnp.logical_not(at.has_up))
            def _():
                self.sib_buf[z] = self.chip_sum(z).astype(BF16)

            self.down(z).start()

    def total(self, acc):
        at = self.at
        self.cross(at.z).wait_recv()
        acc[...] = self.chip_sum(at.z)

        @pl.when(at.has_down)
        def _():
            self.up(at.z).wait_recv()
            acc[...] += self.in_buf[at.z].astype(F32)

        @pl.when(at.has_up)
        def _():
            self.down(at.z, at.z + 1).wait_recv()
            acc[...] += self.in_buf[at.nz].astype(F32)

    def drain(self):
        at = self.at
        for z in range(at.nz):
            self.cross(z).wait_send()

            @pl.when(z > at.z)
            def _():
                self.up(z).wait_send()

            @pl.when(z < at.z)
            def _():
                self.down(z).wait_send()


class PlaneGather:
    def __init__(self, at, part, sends, recvs):
        self.at, self.part, self.sends, self.recvs = at, part, sends, recvs

    def copy(self, p, h, i, to):
        return remote(self.part(p, h), self.part(p, h), self.sends.at[i], self.recvs.at[i], to, self.at.c)

    def start(self):
        at = self.at
        for h in (0, 1):
            self.copy(at.dp, h, h, at.px).start()
            self.copy(at.dp, 1 - h, 3 - h, at.py).start()

    def forward(self):
        at = self.at
        self.copy(at.px, 0, 0, at.px).wait_recv()
        self.copy(at.px, 0, 4, at.py).start()
        self.copy(at.py, 1, 3, at.py).wait_recv()
        self.copy(at.py, 1, 5, at.px).start()

    def land(self):
        at = self.at
        self.copy(at.px, 1, 1, at.px).wait_recv()
        self.copy(at.py, 0, 2, at.py).wait_recv()
        self.copy(at.diag, 0, 4, at.py).wait_recv()
        self.copy(at.diag, 1, 5, at.px).wait_recv()

    def drain(self):
        at = self.at
        for h in (0, 1):
            self.copy(at.dp, h, h, at.px).wait_send()
            self.copy(at.dp, h, 2 + h, at.py).wait_send()
        self.copy(at.px, 0, 4, at.py).wait_send()
        self.copy(at.py, 1, 5, at.px).wait_send()


class PlaneReduce:
    def __init__(self, at, part, via_x, via_y, from_x, from_y, sends, recvs):
        self.at, self.part, self.sends, self.recvs = at, part, sends, recvs
        self.via_x, self.via_y, self.from_x, self.from_y = via_x, via_y, from_x, from_y

    def copy(self, i):
        at = self.at
        src, dst, to = (
            (lambda: self.part(at.diag, 1), self.via_x, at.px),
            (lambda: self.part(at.diag, 0), self.via_y, at.py),
            (lambda: self.part(at.px, 1), self.from_x(1), at.px),
            (lambda: self.part(at.py, 0), self.from_y(0), at.py),
            (lambda: self.part(at.py, 1), self.from_y(1), at.py),
            (lambda: self.part(at.px, 0), self.from_x(0), at.px),
        )[i]
        return remote(src(), dst, self.sends.at[i], self.recvs.at[i], to, at.c)

    def start(self):
        for i in range(4):
            self.copy(i).start()

    def combine(self):
        at = self.at
        for i, via, p, h in ((0, self.via_x, at.py, 1), (1, self.via_y, at.px, 0)):
            self.copy(i).wait_recv()
            ref = self.part(p, h)
            ref[...] = (ref[...].astype(F32) + via[...].astype(F32)).astype(BF16)
            self.copy(4 + i).start()

    def total(self, h):
        for i in ((5, 3), (2, 4))[h]:
            self.copy(i).wait_recv()
        return self.part(self.at.dp, h)[...].astype(F32) + self.from_x(h)[...].astype(F32) + self.from_y(h)[...].astype(F32)

    def drain(self):
        for i in range(6):
            self.copy(i).wait_send()


def blocks(count, body, hooks=None):
    hooks = hooks or {}

    def one(i, carry):
        body(i)
        for index, events in hooks.items():

            @pl.when(i == index)
            def _():
                for event in events:
                    event()

        return carry

    lax.fori_loop(0, count, one, 0)


def fused_kernel(ndp, n, dims, *refs):
    mb, tok, width, seq, heads, rows_w, rows_d = dims
    nz, block, every = n // 2, 2 * tok, ndp * n
    fu = ndp * rows_d
    (tok_ref, cot_ref, wp_ref, wd_ref, wo_ref, vec_ref, seg_ref, cos_ref, sin_ref) = refs[:9]
    (mixed_out, grad_out, dwq_out, dwu_out, dwd_out, dwo_out, dv_out) = refs[9:16]
    (xs, gs, ws, wdo, vecs, segs, seg_col, cos_t, sin_t, g1, s1, g2, s2, bo, bq, bu, qkv, hid, gp, stat, ctx, part, ep, dctx, dqkv,
     dk, dv, acc_gain, acc_bu, acc_bq, m_sib, m_in, t_sib, t_in, dwq, dwu, dwdo, q_via, q_from, u_via, u_from, d_via, d_from, vsum, vin, wq_st, wu_st,
     own, dwo_st) = refs[16:65]
    probs = refs[65 : 65 + nz]
    (x_s, x_r, c_s, c_r, w1s, w1r, w2s, w2r, v1s, v1r, v2s, v2r, d_s, d_r, o1s, o1r,
     ms_s, ms_r, mu_s, mu_r, md_s, md_r, ts_s, ts_r, tu_s, tu_r, td_s, td_r,
     gq1s, gq1r, gq2s, gq2r, gu1s, gu1r, gu2s, gu2r, gd_s, gd_r, go2s, go2r, gv1s, gv1r, gv2s, gv2r, local) = refs[65 + nz :]
    at = Place(ndp, n)
    at.barrier(True, True, True)
    own_rows = pl.ds(pl.multiple_of(at.c * tok, tok), tok)

    cols = Exchange(at, "ctx", lambda p: wp_ref.at[p], lambda s: ws.at[at.dp, s], w1s, w1r)
    vec1 = Exchange(at, "ctx", lambda p: vec_ref, lambda s: vecs.at[at.dp, s], v1s, v1r)
    plane_w = PlaneGather(at, lambda p, h: ws.at[p, pl.ds(h * (n // 2), n // 2)], w2s, w2r)
    plane_v = Exchange(at, "dp", lambda p: vecs.at[at.dp], lambda s: vecs.at[s], v2s, v2r)
    rows_do = rows_d + rows_w
    plane_d = PlaneGather(at, lambda p, h: wdo.at[p, pl.ds(h * (rows_do // 2), rows_do // 2)], d_s, d_r)
    x_ag = [SeqGather(at, tok_ref.at[s], xs.at[s], tok, x_s.at[s], x_r.at[s]) for s in range(mb)]
    c_ag = [SeqGather(at, cot_ref.at[s], gs.at[s], tok, c_s.at[s], c_r.at[s]) for s in range(mb)]
    copies = [
        pltpu.make_async_copy(wp_ref.at[at.c], ws.at[at.dp, at.c], local.at[0]),
        pltpu.make_async_copy(vec_ref, vecs.at[at.dp, at.c], local.at[1]),
        pltpu.make_async_copy(wd_ref, wdo.at[at.dp, pl.ds(0, rows_d)], local.at[2]),
        pltpu.make_async_copy(seg_ref, segs, local.at[3]),
        pltpu.make_async_copy(cos_ref, cos_t, local.at[4]),
        pltpu.make_async_copy(sin_ref, sin_t, local.at[5]),
        pltpu.make_async_copy(tok_ref, xs.at[:, own_rows], local.at[6]),
        pltpu.make_async_copy(cot_ref, gs.at[:, own_rows], local.at[7]),
    ]
    out_rows = remote(wo_ref, wdo.at[at.rows_dp, pl.ds(rows_d, rows_w)], o1s, o1r, at.rows_dp, at.rows_c)
    out_mine = remote(wo_ref, wdo.at[at.dp, pl.ds(rows_d, rows_w)], o1s, o1r, at.rows_dp, at.rows_c)
    own_out = pltpu.make_async_copy(wo_ref, wdo.at[at.dp, pl.ds(rows_d, rows_w)], local.at[8])
    cols.start()
    vec1.start()

    @pl.when(at.moves)
    def _():
        out_rows.start()

    @pl.when(jnp.logical_not(at.moves))
    def _():
        own_out.start()

    for copy in copies:
        copy.start()
    x_ag[0].start()
    for copy in copies:
        copy.wait()
    vec1.wait_recv()
    plane_v.start()
    cols.wait_recv()
    plane_w.start()
    x_ag[0].step(1)
    x_ag[1].start()
    plane_w.forward()

    @pl.when(at.moves)
    def _():
        out_mine.wait_recv()

    @pl.when(jnp.logical_not(at.moves))
    def _():
        own_out.wait()

    plane_d.start()
    x_ag[0].step(2)
    plane_v.wait_recv()

    lane = lax.broadcasted_iota(jnp.int32, (16, 128), 1)
    per = 128 // rows_w
    for q in range(width // 128):
        piece = vecs[(per * q) // n, (per * q) % n]
        for u in range(1, per):
            d = per * q + u
            piece = jnp.where(lane >= u * rows_w, vecs[d // n, d % n], piece)
        span = pl.ds(q * 128, 128)
        bo[:, span] = piece[3:4] + piece[8:9]
        for ref, r in ((g1, 9), (s1, 10), (g2, 11), (s2, 12)):
            ref[:, span] = piece[r : r + 1]
    lane1 = lax.broadcasted_iota(jnp.int32, (1, 128), 1)
    for d in range(ndp):
        rows = vecs[d, at.c]
        piece = rows[4:5]
        for u in range(1, per):
            piece = jnp.where(lane1 >= u * rows_w, rows[4 + u : 5 + u], piece)
        bu[:, pl.ds(d * 128, 128)] = piece
    for p in range(3):
        piece = None
        for u in range(per):
            t = (p * width + at.c * 128) // rows_w + u
            d, r = t // 3, lax.rem(t, 3)
            rows = vecs[d // n, lax.rem(d, n)]
            row = jnp.where(r == 0, rows[0:1], jnp.where(r == 1, rows[1:2], rows[2:3]))
            piece = row if piece is None else jnp.where(lane1 >= u * rows_w, row, piece)
        bq[:, pl.ds(p * 128, 128)] = piece
    seg_t = jnp.transpose(segs[...])
    seg_col[...] = jnp.where(seg_t == 0.0, -1.0, seg_t)

    lanes = lax.broadcasted_iota(jnp.int32, (1, 128), 1)
    in_head = [(lanes >= h * HEAD) & (lanes < (h + 1) * HEAD) for h in range(heads)]
    low_half = (lanes & (HEAD - 1)) < ROT // 2
    w_q = lambda: ws[:, :, :, :384].reshape(width, 384)
    w_u = lambda: ws[:, :, :, 384:].reshape(width, fu)
    w_d = lambda: wdo[:, 0:rows_d].reshape(fu, width)
    w_o = lambda: wdo[:, rows_d:].reshape(128, width)

    def rows_of(i):
        return pl.ds(pl.multiple_of(i * block, block), block)

    def turn(u, rows, sign):
        turned = jnp.where(low_half, pltpu.roll(u, 128 - ROT // 2, 1), pltpu.roll(u, ROT // 2, 1))
        if sign > 0:
            return u * cos_t[rows] + turned * sin_t[rows]
        return u * cos_t[rows] - turned * sin_t[rows]

    def normed_of(s, rows):
        return (xs[s, rows].astype(F32) - stat[s, rows, 0:1]) * stat[s, rows, 1:2]

    def forward_one(s):
        def body(i):
            rows = rows_of(i)
            x = xs[s, rows].astype(F32)
            mean = jnp.mean(x, axis=-1, keepdims=True)
            cen = x - mean
            rstd = lax.rsqrt(jnp.mean(cen * cen, axis=-1, keepdims=True) + 1e-05)
            stat[s, rows, 0:1] = mean
            stat[s, rows, 1:2] = rstd
            nrm = cen * rstd
            h1 = (nrm * g1[...] + s1[...]).astype(BF16)
            joined = dot(h1, w_q()) + bq[...]
            qkv[s, rows, 0:128] = (turn(joined[:, 0:128], rows, 1).astype(BF16).astype(F32) * (HEAD ** (-0.5))).astype(BF16)
            qkv[s, rows, 128:256] = turn(joined[:, 128:256], rows, 1).astype(BF16)
            qkv[s, rows, 256:384] = joined[:, 256:384].astype(BF16)
            h2 = (nrm * g2[...] + s2[...]).astype(BF16)
            act = dot(h2, w_u()) + bu[...]
            cdf = 0.5 + 0.5 * lax.erf(act * (0.5 ** 0.5))
            hid[s, rows] = (act * cdf).astype(BF16)
            gp[s, rows] = (cdf + act * (jnp.exp(-0.5 * act * act) * 0.3989422804014327)).astype(BF16)

        return body

    def attend(s, i):
        rows = pl.ds(i * block, block)
        keys = (i + 1) * block
        q_pos = lax.broadcasted_iota(jnp.int32, (block, keys), 0) + i * block
        k_pos = lax.broadcasted_iota(jnp.int32, (block, keys), 1)
        same = segs[s : s + 1, 0:keys] == seg_col[rows, s : s + 1]
        allow = (same & (k_pos <= q_pos)) | (k_pos == q_pos)
        q, k, v = qkv[s, rows, 0:128], qkv[s, 0:keys, 128:256], qkv[s, 0:keys, 256:384]
        out = None
        for h in range(heads):
            scores = dot(jnp.where(in_head[h], q, jnp.zeros_like(q)), k, NT)
            scores = jnp.where(allow, scores, -1e30)
            e = jnp.exp(scores - jnp.max(scores, axis=-1, keepdims=True))
            p = (e * (1.0 / jnp.sum(e, axis=-1, keepdims=True))).astype(BF16)
            probs[i][s, h] = p
            o = dot(p, v)
            out = o if out is None else jnp.where(in_head[h], o, out)
        ctx[s, rows] = out.astype(BF16)

    def project(s):
        def body(i):
            rows = rows_of(i)
            both = dot(ctx[s, rows], w_o()) + dot(hid[s, rows], w_d())
            part[s, rows] = both.astype(BF16)

        return body

    def fold(ref, row, value):
        count, cols_ = value.shape
        ref[row, :, 0:cols_] += jnp.sum(value.reshape(count // 8, 8, cols_), axis=0)

    def backward_ffn(s):
        def body(i):
            rows = rows_of(i)
            g = gs[s, rows]
            dctx[s, rows] = dot(g, w_o(), NT).astype(BF16)
            d_act = (dot(g, w_d(), NT) * gp[s, rows].astype(F32)).astype(BF16)
            gp[s, rows] = d_act
            fold(acc_gain, 4, g.astype(F32))
            fold(acc_bu, 0, d_act.astype(F32))
            d_h = dot(d_act, w_u(), NT)
            fold(acc_gain, 2, d_h * normed_of(s, rows))
            fold(acc_gain, 3, d_h)
            ep[s, rows] = (d_h * g2[...]).astype(BF16)

        return body

    def attend_back(s, i):
        rows = pl.ds(i * block, block)
        keys = (i + 1) * block
        span = pl.ds(0, keys)
        q, k, v = qkv[s, rows, 0:128], qkv[s, span, 128:256], qkv[s, span, 256:384]
        d_c = dctx[s, rows]
        zero = jnp.zeros_like(q)
        d_q = None
        for h in range(heads):
            p = probs[i][s, h]
            d_h = jnp.where(in_head[h], d_c, zero)
            d_p = dot(d_h, v, NT)
            p_f = p.astype(F32)
            delta = jnp.sum(p_f * d_p, axis=-1, keepdims=True)
            d_s = (p_f * (d_p - delta)).astype(BF16)
            o = dot(d_s, k)
            d_q = o if d_q is None else jnp.where(in_head[h], o, d_q)
            d_k = dot(d_s, jnp.where(in_head[h], q, zero), TN)
            d_v = dot(p, d_h, TN)
            if i == nz - 1 and h == 0:
                dk[...] = d_k
                dv[...] = d_v
            else:
                dk[span] += d_k
                dv[span] += d_v
        d_q = turn(d_q, rows, -1) * (HEAD ** (-0.5))
        d_all = jnp.concatenate([d_q, turn(dk[rows], rows, -1), dv[rows]], axis=1).astype(BF16)
        dqkv[s, rows] = d_all
        fold(acc_bq, 0, d_all.astype(F32))
        d_n = dot(d_all, w_q(), NT)
        fold(acc_gain, 0, d_n * normed_of(s, rows))
        fold(acc_gain, 1, d_n)
        ep[s, rows] = (d_n * g1[...] + ep[s, rows].astype(F32)).astype(BF16)

    def weight_cols(out, gain, shift, right):
        def body(kt):
            feat = pl.ds(pl.multiple_of(kt * 256, 256), 256)
            total = None
            for s in range(mb):
                nrm = (xs[s, :, feat].astype(F32) - stat[s, :, 0:1]) * stat[s, :, 1:2]
                h = (nrm * gain[:, feat] + shift[:, feat]).astype(BF16)
                term = dot(h, right[s], TN)
                total = term if total is None else total + term
            out[feat] = total.astype(BF16)

        return body

    acc_gain[...] = jnp.zeros_like(acc_gain)
    acc_bu[...] = jnp.zeros_like(acc_bu)
    acc_bq[...] = jnp.zeros_like(acc_bq)

    m_rs = [SeqScatter(at, part.at[s], m_sib.at[s], m_in.at[s], tok, [r.at[s] for r in (ms_s, ms_r, mu_s, mu_r, md_s, md_r)]) for s in range(mb)]
    t_rs = [SeqScatter(at, ep.at[s], t_sib.at[s], t_in.at[s], tok, [r.at[s] for r in (ts_s, ts_r, tu_s, tu_r, td_s, td_r)]) for s in range(mb)]
    rows_p = n * rows_w

    def col_halves(ref):
        return lambda p, h: ref.at[pl.ds(pl.multiple_of(p * rows_p + h * (rows_p // 2), rows_p // 2), rows_p // 2)]

    def halves(ref, i, size):
        return lambda h: ref.at[i, pl.ds(h * size, size)]

    half = rows_p // 2
    wq1 = PlaneReduce(at, col_halves(dwq), q_via.at[0], q_via.at[1], halves(q_from, 0, half), halves(q_from, 1, half), gq1s, gq1r)
    wu1 = PlaneReduce(at, col_halves(dwu), u_via.at[0], u_via.at[1], halves(u_from, 0, half), halves(u_from, 1, half), gu1s, gu1r)
    half_do = rows_do // 2
    wd1 = PlaneReduce(at, lambda p, h: dwdo.at[p, pl.ds(h * half_do, half_do)], d_via.at[0], d_via.at[1],
                      halves(d_from, 0, half_do), halves(d_from, 1, half_do), gd_s, gd_r)
    gv1 = Exchange(at, "dp", lambda p: vsum, lambda s: vin.at[s], gv1s, gv1r)
    wq2 = Exchange(at, "ctx", lambda p: wq_st.at[p], lambda s: dwq_out.at[s], gq2s, gq2r)
    wu2 = Exchange(at, "ctx", lambda p: wu_st.at[p], lambda s: dwu_out.at[s], gu2s, gu2r)
    gv2 = Exchange(at, "ctx", lambda p: vin.at[at.dp], lambda s: dv_out.at[s], gv2s, gv2r)
    out_back = remote(dwo_st, dwo_out, go2s, go2r, at.from_dp, at.from_c)

    def columns_on(first_hop, second_hop, stage, out):
        for h in (0, 1):
            total = first_hop.total(h).astype(BF16)
            stage[pl.ds(h * (n // 2), n // 2)] = total.reshape((n // 2,) + stage.shape[1:])
        second_hop.start()
        out[at.c] = stage[at.c]

    def down_out():
        low, high = wd1.total(0), wd1.total(1)
        dwd_out[pl.ds(0, half_do)] = low
        dwd_out[pl.ds(half_do, rows_d - half_do)] = high[0 : rows_d - half_do]
        rows = high[rows_d - half_do :].astype(BF16)

        @pl.when(at.moves)
        def _():
            dwo_st[...] = rows
            out_back.start()

        @pl.when(jnp.logical_not(at.moves))
        def _():
            dwo_out[...] = rows

    def starts(rs, zs):
        def event():
            for z in zs:
                rs.cross(z).start()

        return event

    def finish_mixed(s):
        m_rs[s].total(own)
        mixed_out[s] = (xs[s, own_rows].astype(F32) + own[...] + bo[...]).astype(BF16)

    def finish_grad(s):
        t_rs[s].total(own)
        e = own[...]
        nrm = normed_of(s, own_rows)
        inner = e - jnp.mean(e, axis=-1, keepdims=True) - nrm * jnp.mean(e * nrm, axis=-1, keepdims=True)
        grad_out[s] = (gs[s, own_rows].astype(F32) + stat[s, own_rows, 1:2] * inner).astype(BF16)

    def down_rows(kt):
        feat = pl.ds(pl.multiple_of(kt * 256, 256), 256)
        total = None
        for s in range(mb):
            term = dot(hid[s, :, feat], gs[s], TN)
            total = term if total is None else total + term
        dwdo[pl.ds(kt * (256 // rows_d), 256 // rows_d), 0:rows_d] = total.astype(BF16).reshape(256 // rows_d, rows_d, width)

    def out_grad():
        total = None
        for s in range(mb):
            term = dot(ctx[s], gs[s], TN)
            total = term if total is None else total + term
        dwdo[:, rows_d:] = total.astype(BF16).reshape(ndp, rows_w, width)

    x_ag[0].step(3)
    plane_w.land()
    x_ag[0].land()
    blocks(nz, forward_one(0), {1: [plane_d.forward], 3: [lambda: x_ag[1].step(1), c_ag[0].start]})
    for i in range(nz):
        attend(0, i)
    x_ag[1].step(2)
    plane_d.land()
    blocks(nz, project(0))
    starts(m_rs[0], range(nz))()
    m_rs[0].step(0)
    x_ag[1].step(3)
    x_ag[1].land()
    blocks(nz, forward_one(1), {3: [lambda: c_ag[0].step(1), c_ag[1].start]})
    m_rs[0].step(1)
    for i in range(nz):
        attend(1, i)
    c_ag[0].step(2)
    blocks(nz, project(1))
    starts(m_rs[1], range(nz))()
    m_rs[0].step(2)
    m_rs[1].step(0)
    c_ag[0].step(3)
    c_ag[0].land()
    blocks(nz, backward_ffn(0), {3: [lambda: c_ag[1].step(1)]})
    m_rs[1].step(1)
    for i in reversed(range(nz)):
        attend_back(0, i)
        t_rs[0].cross(i).start()
        if i == 2:
            c_ag[1].step(2)
    m_rs[1].step(2)
    t_rs[0].step(0)
    finish_mixed(0)
    c_ag[1].step(3)
    c_ag[1].land()
    blocks(nz, backward_ffn(1), {3: [lambda: t_rs[0].step(1)]})
    blocks(width // 256, weight_cols(dwu, g2, s2, gp))
    wu1.start()
    finish_mixed(1)
    t_rs[0].step(2)
    blocks(fu // 256, down_rows)
    out_grad()
    wu1.combine()
    wd1.start()
    for i in reversed(range(nz)):
        attend_back(1, i)
        t_rs[1].cross(i).start()
        if i == 3:
            wd1.combine()
    t_rs[1].step(0)
    columns_on(wu1, wu2, wu_st, dwu_out)
    blocks(width // 256, weight_cols(dwq, g1, s1, dqkv))
    wq1.start()
    t_rs[1].step(1)
    vsum[...] = jnp.zeros_like(vsum)
    vsum[0:1, 0:384] = jnp.sum(acc_bq[0], axis=0, keepdims=True)
    vsum[1:2, 0:fu] = jnp.sum(acc_bu[0], axis=0, keepdims=True)
    for r in range(5):
        vsum[2 + r : 3 + r] = jnp.sum(acc_gain[r], axis=0, keepdims=True)
    gv1.start()
    wq1.combine()
    down_out()
    t_rs[1].step(2)
    gv1.wait_recv()
    total = vsum[...]
    for j in range(1, ndp):
        total = total + vin[lax.rem(at.dp + j, ndp)]
    vin[at.dp] = total
    gv2.start()
    dv_out[at.c] = vin[at.dp]
    finish_grad(0)
    columns_on(wq1, wq2, wq_st, dwq_out)
    finish_grad(1)

    @pl.when(at.moves)
    def _():
        out_rows.wait_send()
        out_back.wait()

    for part_ in (wq2, wu2, gv2):
        part_.wait_recv()
    for part_ in (cols, vec1, plane_v, gv1, wq2, wu2, gv2):
        part_.wait_send()
    for part_ in (plane_w, plane_d, wq1, wu1, wd1):
        part_.drain()
    for s in range(mb):
        x_ag[s].drain()
        c_ag[s].drain()
        m_rs[s].drain()
        t_rs[s].drain()


def fused_layer(ndp, n, dims, tok, cot, wp, wd, wo, vec, seg, cosine, sine):
    mb, tk, width, seq, heads, rows_w, rows_d = dims
    nz, block, fu = n // 2, 2 * tk, ndp * rows_d
    rows_do, rows_p = rows_d + rows_w, n * rows_w
    dma = pltpu.SemaphoreType.DMA
    vm = pltpu.VMEM
    vmem = pl.BlockSpec(memory_space=pltpu.VMEM)
    slots = gather_slots(nz)
    scratch = [
        vm((mb, seq, width), BF16), vm((mb, seq, width), BF16),
        vm((ndp, n, rows_w, 384 + fu), BF16), vm((ndp, rows_d + rows_w, width), BF16),
        vm((ndp, n, 16, 128), F32), vm((8, seq), F32), vm((seq, 8), F32), vm((seq, 128), F32), vm((seq, 128), F32),
        vm((1, width), F32), vm((1, width), F32), vm((1, width), F32), vm((1, width), F32), vm((1, width), F32),
        vm((1, 384), F32), vm((1, fu), F32),
        vm((mb, seq, 384), BF16), vm((mb, seq, fu), BF16), vm((mb, seq, fu), BF16), vm((mb, seq, 2), F32),
        vm((mb, seq, 128), BF16), vm((mb, seq, width), BF16), vm((mb, seq, width), BF16),
        vm((mb, seq, 128), BF16), vm((mb, seq, 384), BF16), vm((seq, 128), F32), vm((seq, 128), F32),
        vm((5, 8, width), F32), vm((1, 8, fu), F32), vm((1, 8, 384), F32),
        vm((mb, nz, tk, width), BF16), vm((mb, nz + 1, tk, width), BF16), vm((mb, nz, tk, width), BF16), vm((mb, nz + 1, tk, width), BF16),
        vm((width, 384), BF16), vm((width, fu), BF16), vm((ndp, rows_do, width), BF16),
        vm((2, rows_p // 2, 384), BF16), vm((2, rows_p, 384), BF16), vm((2, rows_p // 2, fu), BF16), vm((2, rows_p, fu), BF16),
        vm((2, rows_do // 2, width), BF16), vm((2, rows_do, width), BF16),
        vm((8, width), F32), vm((ndp, 8, width), F32), vm((n, rows_w, 384), BF16), vm((n, rows_w, fu), BF16),
        vm((tk, width), F32), vm((rows_w, width), BF16),
    ] + [vm((mb, heads, block, block * (i + 1)), BF16) for i in range(nz)]
    per_seq = [dma((mb, slots)), dma((mb, n))]
    to_ctx, to_dp, plane = [dma((n,))] * 2, [dma((ndp,))] * 2, [dma((6,))] * 2
    sems = per_seq * 2 + to_ctx + plane + to_ctx + to_dp + plane + [dma, dma]
    sems += [dma((mb, nz))] * 12
    sems += (plane + to_ctx) * 2 + plane + [dma, dma] + to_dp + to_ctx + [dma((9,))]
    return pl.pallas_call(
        partial(fused_kernel, ndp, n, dims),
        out_shape=(
            jax.ShapeDtypeStruct((mb, tk, width), BF16),
            jax.ShapeDtypeStruct((mb, tk, width), BF16),
            jax.ShapeDtypeStruct((n, rows_w, 384), BF16),
            jax.ShapeDtypeStruct((n, rows_w, fu), BF16),
            jax.ShapeDtypeStruct((rows_d, width), F32),
            jax.ShapeDtypeStruct((rows_w, width), BF16),
            jax.ShapeDtypeStruct((n, 8, width), F32),
        ),
        in_specs=[ANY] * 9,
        out_specs=[vmem] * 7,
        scratch_shapes=scratch + sems,
        compiler_params=pltpu.CompilerParams(collective_id=5, has_side_effects=True, vmem_limit_bytes=63 * MIB),
    )(tok, cot, wp, wd, wo, vec, seg, cosine, sine)


def rotary_lanes(seq):
    half = ROT // 2
    inverse = (np.float32(10000.0) ** (-(np.float32(2.0) * np.arange(half, dtype=np.float32)) / np.float32(ROT))).astype(np.float32)
    angles = (np.arange(seq, dtype=np.float32)[:, None] * inverse[None, :]).astype(np.float32)
    cosine = np.ones((seq, HEAD), np.float32)
    sine = np.zeros((seq, HEAD), np.float32)
    cosine[:, :half] = cosine[:, half:ROT] = np.cos(angles)
    sine[:, :half] = -np.sin(angles)
    sine[:, half:ROT] = np.sin(angles)
    return np.tile(cosine, (1, 128 // HEAD)), np.tile(sine, (1, 128 // HEAD))


def fused_device(ndp, n, tokens, cotangent, segments, w_qkv, b_qkv, w_out, b_out, w_up, b_up, w_down, b_down, g1, s1, g2, s2):
    tok, mb, width = tokens.shape
    seq = segments.shape[1]
    hc = width // n
    rows_w, rows_d = w_qkv.shape[0], w_down.shape[0]
    fu = ndp * rows_d
    c, dp = lax.axis_index("ctx"), lax.axis_index("dp")
    toks, cot = jnp.transpose(tokens, (1, 0, 2)), jnp.transpose(cotangent, (1, 0, 2))
    qkv_cols = w_qkv.reshape(rows_w, 3, n, hc).transpose(2, 0, 1, 3).reshape(n, rows_w, 3 * hc)
    up_cols = w_up.reshape(rows_w, ndp, n, rows_d).transpose(2, 0, 1, 3).reshape(n, rows_w, fu)
    wp = jnp.concatenate([qkv_cols, up_cols], axis=2)
    units = jnp.concatenate([b_qkv, b_out, b_up, b_down, g1, s1, g2, s2]).astype(F32).reshape(-1, rows_w)
    vec = jnp.pad(jnp.tile(units, (1, 128 // rows_w)), ((0, 16 - units.shape[0]), (0, 0)))
    seg = jnp.pad(segments.astype(F32), ((0, 8 - mb), (0, 0)))
    cosine, sine = rotary_lanes(seq)
    dims = (mb, tok, width, seq, hc // HEAD, rows_w, rows_d)
    mixed, t_grad, dwq, dwu, dwd, dwo, dv = fused_layer(
        ndp, n, dims, toks, cot, wp, w_down, w_out, vec, seg, jnp.asarray(cosine), jnp.asarray(sine)
    )
    index = dp * n + c
    g_qkv = dwq.reshape(n, rows_w, 3, hc).transpose(1, 2, 0, 3).reshape(rows_w, 3 * width).astype(F32)
    g_up = dwu.reshape(n, rows_w, ndp, rows_d).transpose(1, 2, 0, 3).reshape(rows_w, -1).astype(F32)
    size = b_qkv.shape[0]
    g_bq = lax.dynamic_slice_in_dim(dv[:, 0, : 3 * hc].reshape(n, 3, hc).transpose(1, 0, 2).reshape(-1), index * size, size)
    own = lax.dynamic_index_in_dim(dv, c, 0, keepdims=False)
    g_bu = lax.dynamic_slice_in_dim(own[1], dp * rows_d, rows_d)
    four = lax.dynamic_slice_in_dim(jnp.sum(dv[:, 2:6], axis=0), index * rows_w, rows_w, axis=1)
    g_b = lax.dynamic_slice_in_dim(own[6], index * rows_w, rows_w)
    return (
        jnp.transpose(mixed, (1, 0, 2)),
        jnp.transpose(t_grad, (1, 0, 2)),
        g_qkv,
        g_bq,
        dwo.astype(F32),
        g_b,
        g_up,
        g_bu,
        dwd,
        g_b,
        four[0],
        four[1],
        four[2],
        four[3],
    )


def rotary_tables(seq):
    half_rot = ROT // 2
    inverse = 10000.0 ** (-(2.0 * jnp.arange(half_rot, dtype=F32)) / ROT)
    angles = jnp.arange(seq, dtype=jnp.int32).astype(F32)[:, None] * inverse[None, :]
    angles = jnp.concatenate([angles, angles], axis=-1)
    return (jnp.cos(angles)[None, :, None, :], jnp.sin(angles)[None, :, None, :])


def rotate(values, cosine, sine, back=False):
    half_rot = ROT // 2
    lead = values[..., :ROT]
    if back:
        u = lead * sine
        turned = jnp.concatenate([u[..., half_rot:], -u[..., :half_rot]], axis=-1)
        return jnp.concatenate([lead * cosine + turned, values[..., ROT:]], axis=-1)
    turned = jnp.concatenate([-lead[..., half_rot:], lead[..., :half_rot]], axis=-1)
    return jnp.concatenate([lead * cosine + turned * sine, values[..., ROT:]], axis=-1)


def per_device(ndp, n, tokens, cotangent, segments, w_qkv, b_qkv, w_out, b_out, w_up, b_up, w_down, b_down, g1, s1, g2, s2):
    tok, mb, width = tokens.shape
    seq = segments.shape[1]
    heads_all = width // HEAD
    hc = width // n
    heads = hc // HEAD
    rows_w = w_qkv.shape[0]
    rows_d = w_down.shape[0]
    fu = ndp * rows_d
    c = lax.axis_index("ctx")
    dp = lax.axis_index("dp")
    scale = HEAD ** (-0.5)

    cot = jnp.transpose(cotangent, (1, 0, 2))
    toks = jnp.transpose(tokens, (1, 0, 2))
    qkv_cols = w_qkv.reshape(rows_w, 3, n, hc).transpose(2, 0, 1, 3).reshape(n, rows_w, 3 * hc)
    up_cols = w_up.reshape(rows_w, ndp, n, rows_d).transpose(2, 0, 1, 3).reshape(n, rows_w, fu)
    wp = jnp.concatenate([qkv_cols, up_cols], axis=2)
    shard_vecs = (b_qkv, b_out, b_up, b_down, g1, s1, g2, s2)
    sizes = [v.shape[0] for v in shard_vecs]
    vec = jnp.concatenate(shard_vecs)
    lanes = 128
    per_vec = 16 * lanes
    vec = jnp.pad(vec, (0, per_vec - vec.shape[0])).reshape(16, lanes)
    x, g, w, wd, wo, vecs = gather_all(ndp, n, toks, cot, wp, w_down, w_out, vec)
    w = w.reshape(width, 3 * hc + fu)
    wq, wu = w[:, : 3 * hc], w[:, 3 * hc :]
    wd = wd.reshape(fu, width)
    wo = wo.reshape(hc, width)
    flat = vecs.reshape(ndp * n, per_vec).astype(F32)
    starts = [sum(sizes[:i]) for i in range(len(sizes))]
    full = [flat[:, s : s + z].reshape(-1) for s, z in zip(starts, sizes)]
    bq_all, bo, bu_all, bd, gain1, shift1, gain2, shift2 = full
    bq = lax.dynamic_index_in_dim(bq_all.reshape(3, n, hc), c, 1, keepdims=False).reshape(3 * hc)
    bu = lax.dynamic_index_in_dim(bu_all.reshape(ndp, n, rows_d), c, 1, keepdims=False).reshape(fu)

    xf = x.reshape(mb * seq, width).astype(F32)
    gl = g.reshape(mb * seq, width)
    mean = jnp.mean(xf, axis=-1, keepdims=True)
    cen = xf - mean
    rstd = lax.rsqrt(jnp.mean(cen * cen, axis=-1, keepdims=True) + 1e-05)
    normed = cen * rstd
    h1 = (normed * gain1 + shift1).astype(BF16)
    h2 = (normed * gain2 + shift2).astype(BF16)
    joined = (dot(h1, wq) + bq).reshape(mb, seq, 3, heads, HEAD)
    cosine, sine = rotary_tables(seq)
    q = rotate(joined[:, :, 0], cosine, sine).astype(BF16)
    k = rotate(joined[:, :, 1], cosine, sine).astype(BF16)
    v = joined[:, :, 2].astype(BF16)
    pos = jnp.arange(seq, dtype=jnp.int32)
    same = (segments[:, None, :] == segments[:, :, None]) & (segments[:, :, None] > 0)
    allow = (same & (pos[None, None, :] <= pos[None, :, None])) | (pos[None, None, :] == pos[None, :, None])
    scores = jnp.einsum("sqhd,skhd->shqk", q, k, preferred_element_type=F32) * scale
    scores = jnp.where(allow[:, None], scores, -1e30)
    top = jnp.max(scores, axis=-1, keepdims=True)
    e = jnp.exp(scores - top)
    probs = e / jnp.sum(e, axis=-1, keepdims=True)
    pl_low = probs.astype(BF16)
    ctx_f = jnp.einsum("shqk,skhd->sqhd", pl_low, v, preferred_element_type=F32)
    ctx = ctx_f.astype(BF16).reshape(mb * seq, hc)
    act = dot(h2, wu) + bu
    hidden = jax.nn.gelu(act, approximate=False).astype(BF16)
    part = (dot(ctx, wo) + dot(hidden, wd)).astype(BF16).reshape(mb, seq, width)
    mixed_sum = scatter_ctx(ndp, n, part, 1)
    mixed = (toks.astype(F32) + mixed_sum + bo + bd).astype(BF16)

    gf = gl.astype(F32)
    d_wd = dot(hidden, gl, ((0,), (0,)))
    d_wo = dot(ctx, gl, ((0,), (0,)))
    d_hidden = dot(gl, wd, ((1,), (1,)))
    _, pull = jax.vjp(partial(jax.nn.gelu, approximate=False), act)
    d_act = pull(d_hidden)[0].astype(BF16)
    d_wu = dot(h2, d_act, ((0,), (0,)))
    d_bu = jnp.sum(d_act.astype(F32), axis=0)
    d_h2 = dot(d_act, wu, ((1,), (1,)))
    d_ctx = dot(gl, wo, ((1,), (1,))).astype(BF16).reshape(mb, seq, heads, HEAD)
    d_probs = jnp.einsum("sqhd,skhd->shqk", d_ctx, v, preferred_element_type=F32)
    delta = jnp.sum(probs * d_probs, axis=-1, keepdims=True)
    d_scores = jnp.where(allow[:, None], probs * (d_probs - delta), 0.0).astype(BF16)
    d_q = jnp.einsum("shqk,skhd->sqhd", d_scores, k, preferred_element_type=F32) * scale
    d_k = jnp.einsum("shqk,sqhd->skhd", d_scores, q, preferred_element_type=F32) * scale
    d_v = jnp.einsum("shqk,sqhd->skhd", pl_low, d_ctx, preferred_element_type=F32)
    d_q = rotate(d_q, cosine, sine, True)
    d_k = rotate(d_k, cosine, sine, True)
    d_qkv = jnp.stack([d_q, d_k, d_v], axis=2).astype(BF16).reshape(mb * seq, 3 * hc)
    d_wq = dot(h1, d_qkv, ((0,), (0,)))
    d_bq = jnp.sum(d_qkv.astype(F32), axis=0)
    d_h1 = dot(d_qkv, wq, ((1,), (1,)))
    e_sum = (d_h1 * gain1 + d_h2 * gain2).astype(BF16).reshape(mb, seq, width)
    e_own = scatter_ctx(ndp, n, e_sum, 2)
    own_x = toks.astype(F32)
    o_mean = jnp.mean(own_x, axis=-1, keepdims=True)
    o_cen = own_x - o_mean
    o_rstd = lax.rsqrt(jnp.mean(o_cen * o_cen, axis=-1, keepdims=True) + 1e-05)
    o_n = o_cen * o_rstd
    t_grad = o_rstd * (e_own - jnp.mean(e_own, axis=-1, keepdims=True) - o_n * jnp.mean(e_own * o_n, axis=-1, keepdims=True))
    tokens_grad = (cot.astype(F32) + t_grad).astype(BF16)

    rows = [
        jnp.pad(d_bq, (0, width - 3 * hc)),
        jnp.pad(d_bu, (0, width - fu)),
        jnp.sum(d_h1 * normed, axis=0),
        jnp.sum(d_h1, axis=0),
        jnp.sum(d_h2 * normed, axis=0),
        jnp.sum(d_h2, axis=0),
        jnp.sum(gf, axis=0),
        jnp.zeros((width,), F32),
    ]
    dwp = jnp.concatenate([d_wq, d_wu], axis=1).astype(BF16).reshape(ndp, n, rows_w, 3 * hc + fu)
    dw, dwd, dwo, dv = grads_all(
        ndp, n, dwp, d_wd.astype(BF16).reshape(ndp, rows_d, width), d_wo.astype(BF16).reshape(ndp, rows_w, width), jnp.stack(rows)
    )
    index = dp * n + c
    g_qkv = dw[:, :, : 3 * hc].reshape(n, rows_w, 3, hc).transpose(1, 2, 0, 3).reshape(rows_w, 3 * width).astype(F32)
    g_up = dw[:, :, 3 * hc :].reshape(n, rows_w, ndp, rows_d).transpose(1, 2, 0, 3).reshape(rows_w, -1).astype(F32)
    g_bq = lax.dynamic_slice_in_dim(dv[:, 0, : 3 * hc].reshape(n, 3, hc).transpose(1, 0, 2).reshape(-1), index * sizes[0], sizes[0])
    own = lax.dynamic_index_in_dim(dv, c, 0, keepdims=False)
    g_bu = lax.dynamic_slice_in_dim(own[1], dp * rows_d, rows_d)
    four = lax.dynamic_slice_in_dim(jnp.sum(dv[:, 2:6], axis=0), index * rows_w, rows_w, axis=1)
    g_b = lax.dynamic_slice_in_dim(own[6], index * rows_w, rows_w)
    return (
        jnp.transpose(mixed, (1, 0, 2)),
        jnp.transpose(tokens_grad, (1, 0, 2)),
        g_qkv,
        g_bq,
        dwo.astype(F32),
        g_b,
        g_up,
        g_bu,
        dwd,
        g_b,
        four[0],
        four[1],
        four[2],
        four[3],
    )


def program(ndp, n, *args):
    tokens, w_qkv, w_down = args[0], args[3], args[9]
    rows_w = w_qkv.shape[0]
    whole_tiles = ndp == 4 and rows_w % 16 == 0 and tokens.shape[2] // n == 128 and w_down.shape[0] == 128 and tokens.shape[0] % 16 == 0
    return (fused_device if whole_tiles else per_device)(ndp, n, *args)


def solution(mesh):
    every = ("dp", "ctx")
    mat, vec, act = P(every, None), P(every), P("ctx", "dp", None)
    placed = (act, act, P("dp", None), mat, vec, mat, vec, mat, vec, mat, vec, vec, vec, vec, vec)
    return jax.shard_map(
        partial(program, mesh.shape["dp"], mesh.shape["ctx"]),
        mesh=mesh,
        in_specs=placed,
        out_specs=(act, act, mat, vec, mat, vec, mat, vec, mat, vec, vec, vec, vec, vec),
        check_vma=False,
    )
```

```python
from functools import partial

import jax
import jax.numpy as jnp
import numpy as np
from jax import lax
from jax.experimental import pallas as pl
from jax.experimental.pallas import tpu as pltpu
from jax.sharding import PartitionSpec as P

HEAD = 64
ROT = 16
MIB = 1 << 20
PIECES = 2
MESH = pl.DeviceIdType.MESH
ANY = pl.BlockSpec(memory_space=pl.ANY)
F32 = jnp.float32
BF16 = jnp.bfloat16


class Place:
    def __init__(self, ndp, n):
        self.ndp, self.n, self.nz = ndp, n, n // 2
        self.dp = lax.axis_index("dp")
        self.c = lax.axis_index("ctx")
        self.z = self.c // 2
        self.core = lax.rem(self.c, 2)
        self.sib = self.c + 1 - 2 * self.core
        self.has_up = self.z + 1 < self.nz
        self.has_down = self.z > 0
        self.px = self.dp + 1 - 2 * lax.rem(self.dp, 2)
        self.py = lax.rem(self.dp + 2, 4)
        self.diag = 3 - self.dp
        index, back = self.dp * n + self.c, self.c * ndp + self.dp
        self.rows_dp, self.rows_c = lax.rem(index, ndp), index // ndp
        self.from_dp, self.from_c = back // n, lax.rem(back, n)
        self.moves = index != back

    def barrier(self, ctx_all, dp_all, rows=False):
        bar = pltpu.get_barrier_semaphore()
        count = 0
        if rows:
            count = count + 2 * self.moves.astype(jnp.int32)

            @pl.when(self.moves)
            def _():
                pl.semaphore_signal(bar, inc=1, device_id=(self.rows_dp, self.rows_c), device_id_type=MESH)
                pl.semaphore_signal(bar, inc=1, device_id=(self.from_dp, self.from_c), device_id_type=MESH)

        if ctx_all:
            for j in range(1, self.n):
                peer = lax.rem(self.c + j, self.n)
                pl.semaphore_signal(bar, inc=1, device_id=(self.dp, peer), device_id_type=MESH)
                count += 1
        else:
            pl.semaphore_signal(bar, inc=1, device_id=(self.dp, self.sib), device_id_type=MESH)
            count += 1
            for ok, peer in ((self.has_up, self.c + 2), (self.has_down, self.c - 2)):

                @pl.when(ok)
                def _():
                    pl.semaphore_signal(bar, inc=1, device_id=(self.dp, peer), device_id_type=MESH)

        if dp_all:
            for j in range(1, self.ndp):
                peer = lax.rem(self.dp + j, self.ndp)
                pl.semaphore_signal(bar, inc=1, device_id=(peer, self.c), device_id_type=MESH)
                count += 1
        if not ctx_all:
            count = count + self.has_up.astype(jnp.int32) + self.has_down.astype(jnp.int32)
        pl.semaphore_wait(bar, count)


def remote(src, dst, send, recv, dp, c):
    return pltpu.make_async_remote_copy(
        src_ref=src,
        dst_ref=dst,
        send_sem=send,
        recv_sem=recv,
        device_id=(dp, c),
        device_id_type=MESH,
    )


class Gather:
    def __init__(self, at, src, dst, tok, sends, recvs):
        self.at, self.src, self.dst, self.tok, self.sends, self.recvs = at, src, dst, tok, sends, recvs

    def rows(self, c):
        return self.dst.at[:, pl.ds(pl.multiple_of(c * self.tok, self.tok), self.tok)]

    def copy(self, block, slot, c, src=None):
        at = self.at
        src = self.rows(block) if src is None else src
        return remote(src, self.rows(block), self.sends.at[slot], self.recvs.at[block], at.dp, c)

    def start(self):
        at = self.at

        @pl.when(at.has_up)
        def _():
            self.copy(at.c, 0, at.c + 2, self.src).start()

        @pl.when(at.has_down)
        def _():
            self.copy(at.c, 1, at.c - 2, self.src).start()

        self.copy(at.c, 2, at.sib, self.src).start()

    def step(self, k):
        at = self.at
        low, high = at.c - 2 * k, at.c + 2 * k

        @pl.when(at.z >= k)
        def _():
            self.copy(low, 0, at.c).wait_recv()

            @pl.when(at.has_up)
            def _():
                self.copy(low, 3 * k, at.c + 2).start()

            self.copy(low, 3 * k + 2, at.sib).start()

        @pl.when(at.z + k < at.nz)
        def _():
            self.copy(high, 0, at.c).wait_recv()

            @pl.when(at.has_down)
            def _():
                self.copy(high, 3 * k + 1, at.c - 2).start()

            self.copy(high, 3 * at.nz + k, at.sib).start()

    def finish(self):
        at = self.at
        for z in range(at.nz):
            self.copy(2 * z + 1 - at.core, 0, at.c).wait_recv()
        self.copy(at.c, 2, at.sib, self.src).wait_send()
        for k in range(at.nz):

            @pl.when((at.z >= k) & at.has_up)
            def _():
                self.copy(at.c, 3 * k, at.c).wait_send()

            @pl.when((at.z + k < at.nz) & at.has_down)
            def _():
                self.copy(at.c, 3 * k + 1, at.c).wait_send()

            if k:

                @pl.when(at.z >= k)
                def _():
                    self.copy(at.c, 3 * k + 2, at.c).wait_send()

                @pl.when(at.z + k < at.nz)
                def _():
                    self.copy(at.c, 3 * at.nz + k, at.c).wait_send()


def gather_slots(nz):
    return 4 * nz


class Exchange:
    def __init__(self, at, axis, src, dst, sends, recvs):
        self.at, self.axis, self.src, self.dst, self.sends, self.recvs = at, axis, src, dst, sends, recvs
        self.me, self.count = (at.c, at.n) if axis == "ctx" else (at.dp, at.ndp)

    def copy(self, peer, sender):
        at = self.at
        to = (at.dp, peer) if self.axis == "ctx" else (peer, at.c)
        return remote(self.src(peer), self.dst(sender), self.sends.at[peer], self.recvs.at[sender], *to)

    def start(self):
        for j in range(1, self.count):
            self.copy(lax.rem(self.me + j, self.count), self.me).start()

    def wait_recv(self):
        for j in range(1, self.count):
            peer = lax.rem(self.me + j, self.count)
            self.copy(peer, peer).wait_recv()

    def wait_send(self):
        for j in range(1, self.count):
            peer = lax.rem(self.me + j, self.count)
            self.copy(peer, self.me).wait_send()


def gather_kernel(ndp, n, tok_ref, cot_ref, wp_ref, wd_ref, wo_ref, vec_ref, x_out, g_out, w_out, wd_out, wo_out, vec_out, *sems):
    at = Place(ndp, n)
    tok = tok_ref.shape[1]
    (x_send, x_recv, g_send, g_recv, w1s, w1r, w2s, w2r, v1s, v1r, v2s, v2r, ds, dr, o1s, o1r, o2s, o2r, local) = sems
    at.barrier(True, True)
    own = (
        pltpu.make_async_copy(wp_ref.at[at.c], w_out.at[at.dp, at.c], local.at[0]),
        pltpu.make_async_copy(vec_ref, vec_out.at[at.dp, at.c], local.at[1]),
        pltpu.make_async_copy(wd_ref, wd_out.at[at.dp], local.at[2]),
        pltpu.make_async_copy(tok_ref, x_out.at[:, pl.ds(pl.multiple_of(at.c * tok, tok), tok)], local.at[3]),
        pltpu.make_async_copy(cot_ref, g_out.at[:, pl.ds(pl.multiple_of(at.c * tok, tok), tok)], local.at[4]),
    )
    for copy in own:
        copy.start()
    down_w = Exchange(at, "dp", lambda p: wd_ref, lambda s: wd_out.at[s], ds, dr)
    cols = Exchange(at, "ctx", lambda p: wp_ref.at[p], lambda s: w_out.at[at.dp, s], w1s, w1r)
    vecs = Exchange(at, "ctx", lambda p: vec_ref, lambda s: vec_out.at[at.dp, s], v1s, v1r)
    plane_w = Exchange(at, "dp", lambda p: w_out.at[at.dp], lambda s: w_out.at[s], w2s, w2r)
    plane_v = Exchange(at, "dp", lambda p: vec_out.at[at.dp], lambda s: vec_out.at[s], v2s, v2r)
    plane_o = Exchange(at, "dp", lambda p: wo_out, lambda s: wo_out, o2s, o2r)
    cols.start()
    vecs.start()
    index = at.dp * n + at.c
    heads_of, slot = index // ndp, lax.rem(index, ndp)

    def out_rows(b, c):
        return remote(wo_ref, wo_out.at[b], o1s, o1r.at[b], at.dp, c)

    @pl.when(heads_of != at.c)
    def _():
        out_rows(slot, heads_of).start()

    own_rows = pltpu.make_async_copy(wo_ref, wo_out.at[slot], local.at[5])

    @pl.when(heads_of == at.c)
    def _():
        own_rows.start()

    down_w.start()
    x_ag = Gather(at, tok_ref, x_out, tok, x_send, x_recv)
    g_ag = Gather(at, cot_ref, g_out, tok, g_send, g_recv)
    x_ag.start()
    own[0].wait()
    cols.wait_recv()
    plane_w.start()
    own[1].wait()
    vecs.wait_recv()
    plane_v.start()
    first = at.c * ndp // n

    @pl.when(at.dp == first)
    def _():
        for b in range(ndp):
            src = lax.rem(at.c * ndp + b, n)

            @pl.when(src != at.c)
            def _():
                out_rows(b, at.c).wait_recv()

            @pl.when(src == at.c)
            def _():
                own_rows.wait()

        plane_o.start()

    for k in range(1, at.nz):
        x_ag.step(k)
        if k == 1:
            g_ag.start()
    for k in range(1, at.nz):
        g_ag.step(k)
    x_ag.finish()
    g_ag.finish()

    @pl.when(heads_of != at.c)
    def _():
        out_rows(slot, heads_of).wait_send()

    @pl.when((heads_of == at.c) & (at.dp != first))
    def _():
        own_rows.wait()

    @pl.when(at.dp == first)
    def _():
        plane_o.wait_send()

    @pl.when(at.dp != first)
    def _():
        plane_o.copy(first, first).wait_recv()

    for copy in own[2:]:
        copy.wait()
    for part in (down_w, plane_w, plane_v):
        part.wait_recv()
    for part in (down_w, cols, vecs, plane_w, plane_v):
        part.wait_send()


def gather_all(ndp, n, tok, cot, wp, wd, wo, vec):
    mb, rows, width = tok.shape
    dma = pltpu.SemaphoreType.DMA
    slots = gather_slots(n // 2)
    return pl.pallas_call(
        partial(gather_kernel, ndp, n),
        out_shape=(
            jax.ShapeDtypeStruct((mb, rows * n, width), BF16),
            jax.ShapeDtypeStruct((mb, rows * n, width), BF16),
            jax.ShapeDtypeStruct((ndp,) + wp.shape, BF16),
            jax.ShapeDtypeStruct((ndp,) + wd.shape, BF16),
            jax.ShapeDtypeStruct((ndp,) + wo.shape, BF16),
            jax.ShapeDtypeStruct((ndp, n) + vec.shape, vec.dtype),
        ),
        in_specs=[ANY] * 6,
        out_specs=[ANY] * 6,
        scratch_shapes=[
            dma((slots,)), dma((n,)), dma((slots,)), dma((n,)),
            dma((n,)), dma((n,)), dma((ndp,)), dma((ndp,)),
            dma((n,)), dma((n,)), dma((ndp,)), dma((ndp,)),
            dma((ndp,)), dma((ndp,)),
            dma, dma((ndp,)), dma((ndp,)), dma((ndp,)),
            dma((6,)),
        ],
        compiler_params=pltpu.CompilerParams(collective_id=0, has_side_effects=True),
    )(tok, cot, wp, wd, wo, vec)


class Scatter:
    def __init__(self, at, part, out, sib_buf, low_buf, high_buf, stage, tok, sems):
        self.at, self.part, self.out, self.tok = at, part, out, tok
        self.sib_buf, self.low_buf, self.high_buf, self.stage = sib_buf, low_buf, high_buf, stage
        self.s_send, self.s_recv, self.up_send, self.up_recv, self.dn_send, self.dn_recv = sems

    def rows(self, c):
        return pl.ds(pl.multiple_of(c * self.tok, self.tok), self.tok)

    def cross(self, z):
        at = self.at
        src = self.part.at[:, self.rows(2 * z + 1 - at.core)]
        return remote(src, self.sib_buf.at[z], self.s_send.at[z], self.s_recv.at[z], at.dp, at.sib)

    def up(self, z):
        at = self.at
        return remote(self.stage.at[z], self.low_buf.at[z], self.up_send.at[z], self.up_recv.at[z], at.dp, at.c + 2)

    def down(self, z):
        at = self.at
        return remote(self.stage.at[z], self.high_buf.at[z], self.dn_send.at[z], self.dn_recv.at[z], at.dp, at.c - 2)

    def order(self):
        nz = self.at.nz
        for i in range(nz):
            yield nz - 1 - i
            if i != nz - 1 - i:
                pass

    def start(self):
        for i in range(self.at.nz):
            self.cross(i).start()

    def chip_sum(self, z):
        at = self.at
        mine = self.part[:, self.rows(2 * z + at.core)].astype(F32)
        return mine + self.sib_buf[z].astype(F32)

    def step(self, i):
        at = self.at
        up_z, dn_z = at.nz - 1 - i, i

        @pl.when(up_z > at.z)
        def _():
            self.cross(up_z).wait_recv()
            self.stage[up_z] = self.chip_sum(up_z).astype(BF16)

            @pl.when(at.has_down)
            def _():
                self.up(up_z).wait_recv()
                self.stage[up_z] = (self.stage[up_z].astype(F32) + self.low_buf[up_z].astype(F32)).astype(BF16)

            self.up(up_z).start()

        @pl.when(dn_z < at.z)
        def _():
            self.cross(dn_z).wait_recv()
            self.stage[dn_z] = self.chip_sum(dn_z).astype(BF16)

            @pl.when(at.has_up)
            def _():
                self.down(dn_z).wait_recv()
                self.stage[dn_z] = (self.stage[dn_z].astype(F32) + self.high_buf[dn_z].astype(F32)).astype(BF16)

            self.down(dn_z).start()

    def finish(self):
        at = self.at
        self.cross(at.z).wait_recv()
        self.out[...] = self.chip_sum(at.z)

        @pl.when(at.has_down)
        def _():
            self.up(at.z).wait_recv()
            self.out[...] += self.low_buf[at.z].astype(F32)

        @pl.when(at.has_up)
        def _():
            self.down(at.z).wait_recv()
            self.out[...] += self.high_buf[at.z].astype(F32)

        for z in range(at.nz):
            self.cross(z).wait_send()

            @pl.when(z > at.z)
            def _():
                self.up(z).wait_send()

            @pl.when(z < at.z)
            def _():
                self.down(z).wait_send()


def scatter_kernel(ndp, n, part_ref, out_ref, sib_buf, low_buf, high_buf, stage, *sems):
    at = Place(ndp, n)
    at.barrier(False, False)
    work = Scatter(at, part_ref, out_ref, sib_buf, low_buf, high_buf, stage, out_ref.shape[1], sems)
    work.start()
    for i in range(at.nz - 1):
        work.step(i)
    work.finish()


def scatter_ctx(ndp, n, part, collective):
    mb, seq, width = part.shape
    nz, tok = n // 2, seq // n
    dma = pltpu.SemaphoreType.DMA
    buf = pltpu.VMEM((nz, mb, tok, width), BF16)
    vmem = pl.BlockSpec(memory_space=pltpu.VMEM)
    return pl.pallas_call(
        partial(scatter_kernel, ndp, n),
        out_shape=jax.ShapeDtypeStruct((mb, tok, width), F32),
        in_specs=[vmem],
        out_specs=vmem,
        scratch_shapes=[buf, buf, buf, buf] + [dma((nz,))] * 6,
        compiler_params=pltpu.CompilerParams(collective_id=collective, has_side_effects=True, vmem_limit_bytes=48 * MIB),
    )(part)


def grads_kernel(ndp, n, wp_ref, wd_ref, wo_ref, v_ref, w_out, wd_out, wo_out, v_out, wbuf, wsum, dbuf, obuf, osum, vbuf, vsum, *sems):
    at = Place(ndp, n)
    (w1s, w1r, ds, dr, o1s, o1r, v1s, v1r, w2s, w2r, v2s, v2r, o2s, o2r, local) = sems
    at.barrier(True, True)
    first = at.c * ndp // n
    w1 = Exchange(at, "dp", lambda p: wp_ref.at[p], lambda s: wbuf.at[s], w1s, w1r)
    d1 = Exchange(at, "dp", lambda p: wd_ref.at[p], lambda s: dbuf.at[s], ds, dr)
    v1 = Exchange(at, "dp", lambda p: v_ref, lambda s: vbuf.at[s], v1s, v1r)
    o1 = Exchange(at, "dp", lambda p: wo_ref, lambda s: obuf.at[s], o1s, o1r)
    w1.start()
    v1.start()

    @pl.when(at.dp != first)
    def _():
        o1.copy(first, at.dp).start()

    d1.start()

    def total(ref, mine, get):
        ref[...] = mine
        for j in range(1, ndp):
            ref[...] += get(lax.rem(at.dp + j, ndp)).astype(F32)

    w1.wait_recv()
    total(wsum, wp_ref[at.dp].astype(F32), lambda s: wbuf[s])
    wbuf[at.dp] = wsum[...].astype(BF16)
    w2 = Exchange(at, "ctx", lambda p: wbuf.at[at.dp, p], lambda s: w_out.at[s], w2s, w2r)
    w2.start()
    w_out[at.c] = wbuf[at.dp, at.c]
    v1.wait_recv()
    total(vsum, v_ref[...], lambda s: vbuf[s])
    v2 = Exchange(at, "ctx", lambda p: vsum, lambda s: v_out.at[s], v2s, v2r)
    v2.start()
    v_out[at.c] = vsum[...]

    index = at.dp * n + at.c
    heads_of, slot = index // ndp, lax.rem(index, ndp)

    def out_rows(b, c):
        return remote(osum.at[b], wo_out, o2s.at[b], o2r, at.dp, c)

    @pl.when(at.dp == first)
    def _():
        o1.wait_recv()
        rows = wo_ref[...].astype(F32)
        for j in range(1, ndp):
            rows += obuf[lax.rem(at.dp + j, ndp)].astype(F32)
        osum[...] = rows.astype(BF16)
        for b in range(ndp):
            owner = lax.rem(at.c * ndp + b, n)

            @pl.when(owner != at.c)
            def _():
                out_rows(b, owner).start()

            @pl.when(owner == at.c)
            def _():
                wo_out[...] = osum[b]

    d1.wait_recv()
    total(wd_out, wd_ref[at.dp].astype(F32), lambda s: dbuf[s])

    @pl.when(heads_of != at.c)
    def _():
        out_rows(slot, at.c).wait_recv()

    w2.wait_recv()
    v2.wait_recv()
    for part in (w1, v1, d1, w2, v2):
        part.wait_send()

    @pl.when(at.dp != first)
    def _():
        o1.copy(first, at.dp).wait_send()

    @pl.when(at.dp == first)
    def _():
        for b in range(ndp):
            owner = lax.rem(at.c * ndp + b, n)

            @pl.when(owner != at.c)
            def _():
                out_rows(b, owner).wait_send()


def grads_all(ndp, n, wp, wd, wo, v):
    dma = pltpu.SemaphoreType.DMA
    vmem = pl.BlockSpec(memory_space=pltpu.VMEM)
    return pl.pallas_call(
        partial(grads_kernel, ndp, n),
        out_shape=(
            jax.ShapeDtypeStruct(wp.shape[1:], BF16),
            jax.ShapeDtypeStruct(wd.shape[1:], F32),
            jax.ShapeDtypeStruct(wo.shape[1:], BF16),
            jax.ShapeDtypeStruct((n,) + v.shape, F32),
        ),
        in_specs=[vmem] * 4,
        out_specs=[vmem] * 4,
        scratch_shapes=[
            pltpu.VMEM(wp.shape, BF16),
            pltpu.VMEM(wp.shape[1:], F32),
            pltpu.VMEM(wd.shape, BF16),
            pltpu.VMEM((ndp,) + wo.shape, BF16),
            pltpu.VMEM(wo.shape, BF16),
            pltpu.VMEM((ndp,) + v.shape, F32),
            pltpu.VMEM(v.shape, F32),
            dma((ndp,)), dma((ndp,)), dma((ndp,)), dma((ndp,)), dma((ndp,)), dma((ndp,)), dma((ndp,)), dma((ndp,)),
            dma((n,)), dma((n,)), dma((n,)), dma((n,)), dma((ndp,)), dma,
            dma((1,)),
        ],
        compiler_params=pltpu.CompilerParams(collective_id=3, has_side_effects=True, vmem_limit_bytes=48 * MIB),
    )(wp, wd, wo, v)


def dot(a, b, dims=((1,), (0,))):
    return lax.dot_general(a, b, (dims, ((), ())), preferred_element_type=F32)


NT = ((1,), (1,))
TN = ((0,), (0,))


class SeqGather:
    def __init__(self, at, src, dst, tok, first, size, sends, recvs):
        self.at, self.dst, self.tok, self.first, self.size, self.sends, self.recvs = at, dst, tok, first, size, sends, recvs
        self.src = src.at[pl.ds(first, size)]

    def rows(self, c):
        return self.dst.at[pl.ds(pl.multiple_of(c * self.tok + self.first, self.size), self.size)]

    def copy(self, block, slot, c, src=None):
        src = self.rows(block) if src is None else src
        return remote(src, self.rows(block), self.sends.at[slot], self.recvs.at[block], self.at.dp, c)

    def start(self):
        at = self.at

        @pl.when(at.has_up)
        def _():
            self.copy(at.c, 0, at.c + 2, self.src).start()

        @pl.when(at.has_down)
        def _():
            self.copy(at.c, 1, at.c - 2, self.src).start()

        self.copy(at.c, 2, at.sib, self.src).start()

    def step(self, k):
        at = self.at
        low, high = at.c - 2 * k, at.c + 2 * k

        @pl.when(at.z >= k)
        def _():
            self.copy(low, 0, at.c).wait_recv()

            @pl.when(at.has_up)
            def _():
                self.copy(low, 3 * k, at.c + 2).start()

            self.copy(low, 3 * k + 2, at.sib).start()

        @pl.when(at.z + k < at.nz)
        def _():
            self.copy(high, 0, at.c).wait_recv()

            @pl.when(at.has_down)
            def _():
                self.copy(high, 3 * k + 1, at.c - 2).start()

            self.copy(high, 3 * at.nz + k, at.sib).start()

    def land(self):
        for z in range(self.at.nz):
            self.land_chip(z)

    def land_chip(self, z):
        self.copy(2 * z + 1 - self.at.core, 0, self.at.c).wait_recv()


    def drain(self):
        at = self.at
        self.copy(at.c, 2, at.sib, self.src).wait_send()
        for k in range(at.nz):

            @pl.when((at.z >= k) & at.has_up)
            def _():
                self.copy(at.c, 3 * k, at.c).wait_send()

            @pl.when((at.z + k < at.nz) & at.has_down)
            def _():
                self.copy(at.c, 3 * k + 1, at.c).wait_send()

            if k:

                @pl.when(at.z >= k)
                def _():
                    self.copy(at.c, 3 * k + 2, at.c).wait_send()

                @pl.when(at.z + k < at.nz)
                def _():
                    self.copy(at.c, 3 * at.nz + k, at.c).wait_send()


class Pieces:
    def __init__(self, pieces):
        self.pieces = pieces

    def each(self, name, *args):
        for piece in self.pieces:
            getattr(piece, name)(*args)

    def start(self):
        self.each("start")

    def step(self, k):
        self.each("step", k)

    def land(self):
        self.each("land")

    def drain(self):
        self.each("drain")

    def take(self, k, body):
        at = self.pieces[0].at

        def one(t, carry):
            z = at.z - k + 2 * k * t

            @pl.when((z >= 0) & (z < at.nz))
            def _():
                self.each("land_chip", z)
                body(z)

            return carry

        lax.fori_loop(0, 2 if k else 1, one, 0)


class SeqScatter:
    def __init__(self, at, part, sib_buf, in_buf, tok, first, size, sems):
        self.at, self.part, self.tok, self.first, self.size = at, part, tok, first, size
        self.sib_buf, self.in_buf = sib_buf.at[:, pl.ds(first, size)], in_buf.at[:, pl.ds(first, size)]
        self.s_send, self.s_recv, self.up_send, self.up_recv, self.dn_send, self.dn_recv = sems

    def rows(self, c):
        return pl.ds(pl.multiple_of(c * self.tok + self.first, self.size), self.size)

    def cross(self, z):
        at = self.at
        src = self.part.at[self.rows(2 * z + 1 - at.core)]
        return remote(src, self.sib_buf.at[z], self.s_send.at[z], self.s_recv.at[z], at.dp, at.sib)

    def up(self, z):
        at = self.at
        return remote(self.sib_buf.at[z], self.in_buf.at[z], self.up_send.at[z], self.up_recv.at[z], at.dp, at.c + 2)

    def down(self, z, sender=None):
        at = self.at
        slot = jnp.where(z == (at.z - 1 if sender is None else sender - 1), at.nz, z)
        return remote(self.sib_buf.at[z], self.in_buf.at[slot], self.dn_send.at[z], self.dn_recv.at[z], at.dp, at.c - 2)

    def chip_sum(self, z):
        mine = self.part[self.rows(2 * z + self.at.core)].astype(F32)
        return mine + self.sib_buf[z].astype(F32)

    def step(self, t):
        self.step_up(t)
        self.step_down(t)

    def step_up(self, t):
        self.lead_up(t)
        self.follow_up(t)

    def lead_up(self, t):
        at = self.at
        z = at.nz - 1 - t

        @pl.when(at.z == 0)
        def _():
            self.cross(z).wait_recv()
            self.sib_buf[z] = self.chip_sum(z).astype(BF16)
            self.up(z).start()

    def follow_up(self, t):
        at = self.at
        z = at.nz - 1 - t + at.z

        @pl.when((at.z <= t) & at.has_down)
        def _():
            self.cross(z).wait_recv()
            self.up(z).wait_recv()
            self.sib_buf[z] = (self.chip_sum(z) + self.in_buf[z].astype(F32)).astype(BF16)
            self.up(z).start()

    def step_down(self, t):
        self.lead_down(t)
        self.follow_down(t)

    def lead_down(self, t):
        at = self.at

        @pl.when(at.z == at.nz - 1)
        def _():
            self.cross(t).wait_recv()
            self.sib_buf[t] = self.chip_sum(t).astype(BF16)
            self.down(t).start()

    def follow_down(self, t):
        at = self.at
        z = t - (at.nz - 1 - at.z)

        @pl.when((z >= 0) & at.has_up)
        def _():
            self.cross(z).wait_recv()
            self.down(z, at.z + 1).wait_recv()
            self.sib_buf[z] = (self.chip_sum(z) + self.in_buf[z].astype(F32)).astype(BF16)
            self.down(z).start()

    def total(self, acc):
        at = self.at
        acc = acc.at[pl.ds(self.first, self.size)]
        self.cross(at.z).wait_recv()
        acc[...] = self.chip_sum(at.z)

        @pl.when(at.has_down)
        def _():
            self.up(at.z).wait_recv()
            acc[...] += self.in_buf[at.z].astype(F32)

        @pl.when(at.has_up)
        def _():
            self.down(at.z, at.z + 1).wait_recv()
            acc[...] += self.in_buf[at.nz].astype(F32)

    def drain(self):
        at = self.at
        for z in range(at.nz):
            self.cross(z).wait_send()

            @pl.when(z > at.z)
            def _():
                self.up(z).wait_send()

            @pl.when(z < at.z)
            def _():
                self.down(z).wait_send()


class ScatterPieces(Pieces):
    def cross(self, z):
        return Pieces([piece.cross(z) for piece in self.pieces])

    def lead_up(self, t):
        self.each("lead_up", t)

    def lead_down(self, t):
        self.each("lead_down", t)

    def follow(self, t):
        for piece in self.pieces:
            piece.follow_up(t)
            piece.follow_down(t)

    def step(self, t):
        for piece in self.pieces:
            piece.step_up(t)
            piece.step_down(t)

    def total(self, acc):
        self.each("total", acc)


class PlaneGather:
    def __init__(self, at, part, sends, recvs):
        self.at, self.part, self.sends, self.recvs = at, part, sends, recvs

    def copy(self, p, h, i, to):
        return remote(self.part(p, h), self.part(p, h), self.sends.at[i], self.recvs.at[i], to, self.at.c)

    def start(self):
        at = self.at
        for h in (0, 1):
            self.copy(at.dp, h, h, at.px).start()
            self.copy(at.dp, 1 - h, 3 - h, at.py).start()

    def forward(self):
        at = self.at
        self.copy(at.px, 0, 0, at.px).wait_recv()
        self.copy(at.px, 0, 4, at.py).start()
        self.copy(at.py, 1, 3, at.py).wait_recv()
        self.copy(at.py, 1, 5, at.px).start()

    def land(self):
        at = self.at
        self.copy(at.px, 1, 1, at.px).wait_recv()
        self.copy(at.py, 0, 2, at.py).wait_recv()
        self.copy(at.diag, 0, 4, at.py).wait_recv()
        self.copy(at.diag, 1, 5, at.px).wait_recv()

    def drain(self):
        at = self.at
        for h in (0, 1):
            self.copy(at.dp, h, h, at.px).wait_send()
            self.copy(at.dp, h, 2 + h, at.py).wait_send()
        self.copy(at.px, 0, 4, at.py).wait_send()
        self.copy(at.py, 1, 5, at.px).wait_send()


class PlaneReduce:
    def __init__(self, at, part, via_x, via_y, from_x, from_y, sends, recvs):
        self.at, self.part, self.sends, self.recvs = at, part, sends, recvs
        self.via_x, self.via_y, self.from_x, self.from_y = via_x, via_y, from_x, from_y

    def copy(self, i):
        at = self.at
        src, dst, to = (
            (lambda: self.part(at.diag, 1), self.via_x, at.px),
            (lambda: self.part(at.diag, 0), self.via_y, at.py),
            (lambda: self.part(at.px, 1), self.from_x(1), at.px),
            (lambda: self.part(at.py, 0), self.from_y(0), at.py),
            (lambda: self.part(at.py, 1), self.from_y(1), at.py),
            (lambda: self.part(at.px, 0), self.from_x(0), at.px),
        )[i]
        return remote(src(), dst, self.sends.at[i], self.recvs.at[i], to, at.c)

    def start(self):
        for i in range(4):
            self.copy(i).start()

    def combine(self):
        at = self.at
        for i, via, p, h in ((0, self.via_x, at.py, 1), (1, self.via_y, at.px, 0)):
            self.copy(i).wait_recv()
            ref = self.part(p, h)
            ref[...] = (ref[...].astype(F32) + via[...].astype(F32)).astype(BF16)
            self.copy(4 + i).start()

    def total(self, h):
        for i in ((5, 3), (2, 4))[h]:
            self.copy(i).wait_recv()
        return self.part(self.at.dp, h)[...].astype(F32) + self.from_x(h)[...].astype(F32) + self.from_y(h)[...].astype(F32)

    def drain(self):
        for i in range(6):
            self.copy(i).wait_send()


def blocks(count, body, hooks=None):
    hooks = hooks or {}

    def one(i, carry):
        body(i)
        for index, events in hooks.items():

            @pl.when(i == index)
            def _():
                for event in events:
                    event()

        return carry

    lax.fori_loop(0, count, one, 0)


def fused_kernel(ndp, n, dims, *refs):
    mb, tok, width, seq, heads, rows_w, rows_d = dims
    nz, block, every = n // 2, 2 * tok, ndp * n
    fu = ndp * rows_d
    (tok_ref, cot_ref, rq_ref, ru_ref, wd_ref, wo_ref, vec_ref, seg_ref, cos_ref, sin_ref) = refs[:10]
    (mixed_out, grad_out, qkv_out, up_out, dwd_out, dwo_out, vec_out) = refs[10:17]
    (xs, gs, ws, wdo, vecs, segs, seg_col, cos_t, sin_t, g1, s1, g2, s2, bo, bq, bu, qkv, hid, gp, stat, ctx, part, ep, dctx, dqkv,
     dk, dv, acc_gain, acc_bu, acc_bq, m_sib, m_in, t_sib, t_in, dwq, dwu, dwdo, q_via, q_from, u_via, u_from, d_via, d_from, vsum, vin, wq_st, wu_st,
     own, dwo_st, vsum_all, v_st, seg_i, raw_q, raw_u, wp_st, wq_rx, wu_rx, v_rx) = refs[17:75]
    probs = refs[75 : 75 + nz]
    (x_s, x_r, c_s, c_r, w1s, w1r, w2s, w2r, v1s, v1r, v2s, v2r, d_s, d_r, o1s, o1r,
     ms_s, ms_r, mu_s, mu_r, md_s, md_r, ts_s, ts_r, tu_s, tu_r, td_s, td_r,
     gq1s, gq1r, gq2s, gq2r, gu1s, gu1r, gu2s, gu2r, gd_s, gd_r, go2s, go2r, gv1s, gv1r, gv2s, gv2r, local) = refs[75 + nz :]
    at = Place(ndp, n)
    at.barrier(True, True, True)
    own_rows = pl.ds(pl.multiple_of(at.c * tok, tok), tok)

    cols = Exchange(at, "ctx", lambda p: wp_st.at[p], lambda s: ws.at[at.dp, s], w1s, w1r)
    vec1 = Exchange(at, "ctx", lambda p: vec_ref, lambda s: vecs.at[at.dp, s], v1s, v1r)
    plane_w = PlaneGather(at, lambda p, h: ws.at[p, pl.ds(h * (n // 2), n // 2)], w2s, w2r)
    plane_v = Exchange(at, "dp", lambda p: vecs.at[at.dp], lambda s: vecs.at[s], v2s, v2r)
    rows_do = rows_d + rows_w
    plane_d = PlaneGather(at, lambda p, h: wdo.at[p, pl.ds(h * (rows_do // 2), rows_do // 2)], d_s, d_r)
    size = tok // PIECES

    def gather(src, dst, sends, recvs):
        return Pieces([SeqGather(at, src, dst, tok, h * size, size, sends.at[h], recvs.at[h]) for h in range(PIECES)])

    x_ag = [gather(tok_ref.at[s], xs.at[s], x_s.at[s], x_r.at[s]) for s in range(mb)]
    c_ag = [gather(cot_ref.at[s], gs.at[s], c_s.at[s], c_r.at[s]) for s in range(mb)]
    copies = [
        pltpu.make_async_copy(rq_ref, raw_q, local.at[0]),
        pltpu.make_async_copy(ru_ref, raw_u, local.at[9]),
        pltpu.make_async_copy(vec_ref, vecs.at[at.dp, at.c], local.at[1]),
        pltpu.make_async_copy(wd_ref, wdo.at[at.dp, pl.ds(0, rows_d)], local.at[2]),
        pltpu.make_async_copy(seg_ref, seg_i, local.at[3]),
        pltpu.make_async_copy(cos_ref, cos_t, local.at[4]),
        pltpu.make_async_copy(sin_ref, sin_t, local.at[5]),
        pltpu.make_async_copy(tok_ref, xs.at[:, own_rows], local.at[6]),
        pltpu.make_async_copy(cot_ref, gs.at[:, own_rows], local.at[7]),
    ]
    out_rows = remote(wo_ref, wdo.at[at.rows_dp, pl.ds(rows_d, rows_w)], o1s, o1r, at.rows_dp, at.rows_c)
    out_mine = remote(wo_ref, wdo.at[at.dp, pl.ds(rows_d, rows_w)], o1s, o1r, at.rows_dp, at.rows_c)
    own_out = pltpu.make_async_copy(wo_ref, wdo.at[at.dp, pl.ds(rows_d, rows_w)], local.at[8])
    for copy in copies:
        copy.start()
    vec1.start()

    @pl.when(at.moves)
    def _():
        out_rows.start()

    @pl.when(jnp.logical_not(at.moves))
    def _():
        own_out.start()

    copies[0].wait()
    copies[1].wait()
    for p in range(n):
        for part_ in range(3):
            wp_st[p, :, part_ * 128 : (part_ + 1) * 128] = raw_q[:, part_ * width + p * 128 : part_ * width + (p + 1) * 128]
        for d in range(ndp):
            wp_st[p, :, 384 + d * rows_d : 384 + (d + 1) * rows_d] = raw_u[:, (d * n + p) * rows_d : (d * n + p + 1) * rows_d]
    cols.start()
    ws[at.dp, at.c] = wp_st[at.c]
    for copy in copies[2:]:
        copy.wait()
    segs[...] = jnp.zeros_like(segs)
    segs[0:mb] = seg_i[...].astype(F32)
    cols.wait_recv()
    plane_w.start()
    x_ag[0].start()
    vec1.wait_recv()
    plane_v.start()
    plane_w.forward()
    x_ag[0].step(1)

    @pl.when(at.moves)
    def _():
        out_mine.wait_recv()

    @pl.when(jnp.logical_not(at.moves))
    def _():
        own_out.wait()

    plane_v.wait_recv()

    lane = lax.broadcasted_iota(jnp.int32, (16, 128), 1)
    per = 128 // rows_w
    for q in range(width // 128):
        piece = vecs[(per * q) // n, (per * q) % n]
        for u in range(1, per):
            d = per * q + u
            piece = jnp.where(lane >= u * rows_w, vecs[d // n, d % n], piece)
        span = pl.ds(q * 128, 128)
        bo[:, span] = piece[3:4] + piece[8:9]
        for ref, r in ((g1, 9), (s1, 10), (g2, 11), (s2, 12)):
            ref[:, span] = piece[r : r + 1]
    lane1 = lax.broadcasted_iota(jnp.int32, (1, 128), 1)
    for d in range(ndp):
        rows = vecs[d, at.c]
        piece = rows[4:5]
        for u in range(1, per):
            piece = jnp.where(lane1 >= u * rows_w, rows[4 + u : 5 + u], piece)
        bu[:, pl.ds(d * 128, 128)] = piece
    for p in range(3):
        piece = None
        for u in range(per):
            t = (p * width + at.c * 128) // rows_w + u
            d, r = t // 3, lax.rem(t, 3)
            rows = vecs[d // n, lax.rem(d, n)]
            row = jnp.where(r == 0, rows[0:1], jnp.where(r == 1, rows[1:2], rows[2:3]))
            piece = row if piece is None else jnp.where(lane1 >= u * rows_w, row, piece)
        bq[:, pl.ds(p * 128, 128)] = piece
    seg_t = jnp.transpose(segs[...])
    seg_col[...] = jnp.where(seg_t == 0.0, -1.0, seg_t)

    lanes = lax.broadcasted_iota(jnp.int32, (1, 128), 1)
    in_head = [(lanes >= h * HEAD) & (lanes < (h + 1) * HEAD) for h in range(heads)]
    low_half = (lanes & (HEAD - 1)) < ROT // 2
    w_q = lambda: ws[:, :, :, :384].reshape(width, 384)
    w_u = lambda: ws[:, :, :, 384:].reshape(width, fu)
    w_d = lambda: wdo[:, 0:rows_d].reshape(fu, width)
    w_o = lambda: wdo[:, rows_d:].reshape(128, width)

    def rows_of(i):
        return pl.ds(pl.multiple_of(i * block, block), block)

    def turn(u, rows, sign):
        turned = jnp.where(low_half, pltpu.roll(u, 128 - ROT // 2, 1), pltpu.roll(u, ROT // 2, 1))
        if sign > 0:
            return u * cos_t[rows] + turned * sin_t[rows]
        return u * cos_t[rows] - turned * sin_t[rows]

    def normed_of(s, rows):
        return (xs[s, rows].astype(F32) - stat[s, rows, 0:1]) * stat[s, rows, 1:2]

    def forward_one(s):
        def body(i):
            rows = rows_of(i)
            x = xs[s, rows].astype(F32)
            mean = jnp.mean(x, axis=-1, keepdims=True)
            cen = x - mean
            rstd = lax.rsqrt(jnp.mean(cen * cen, axis=-1, keepdims=True) + 1e-05)
            stat[s, rows, 0:1] = mean
            stat[s, rows, 1:2] = rstd
            nrm = cen * rstd
            h1 = (nrm * g1[...] + s1[...]).astype(BF16)
            joined = dot(h1, w_q()) + bq[...]
            qkv[s, rows, 0:128] = (turn(joined[:, 0:128], rows, 1).astype(BF16).astype(F32) * (HEAD ** (-0.5))).astype(BF16)
            qkv[s, rows, 128:256] = turn(joined[:, 128:256], rows, 1).astype(BF16)
            qkv[s, rows, 256:384] = joined[:, 256:384].astype(BF16)
            h2 = (nrm * g2[...] + s2[...]).astype(BF16)
            act = dot(h2, w_u()) + bu[...]
            cdf = 0.5 + 0.5 * lax.erf(act * (0.5 ** 0.5))
            hid[s, rows] = (act * cdf).astype(BF16)
            gp[s, rows] = (cdf + act * (jnp.exp(-0.5 * act * act) * 0.3989422804014327)).astype(BF16)

        return body

    def attend(s, i):
        rows = pl.ds(i * block, block)
        keys = (i + 1) * block
        q_pos = lax.broadcasted_iota(jnp.int32, (block, keys), 0) + i * block
        k_pos = lax.broadcasted_iota(jnp.int32, (block, keys), 1)
        same = segs[s : s + 1, 0:keys] == seg_col[rows, s : s + 1]
        allow = (same & (k_pos <= q_pos)) | (k_pos == q_pos)
        q, k, v = qkv[s, rows, 0:128], qkv[s, 0:keys, 128:256], qkv[s, 0:keys, 256:384]
        out = None
        for h in range(heads):
            scores = dot(jnp.where(in_head[h], q, jnp.zeros_like(q)), k, NT)
            scores = jnp.where(allow, scores, -1e30)
            e = jnp.exp(scores - jnp.max(scores, axis=-1, keepdims=True))
            p = (e * (1.0 / jnp.sum(e, axis=-1, keepdims=True))).astype(BF16)
            probs[i][h] = p
            o = dot(p, v)
            out = o if out is None else jnp.where(in_head[h], o, out)
        ctx[s, rows] = out.astype(BF16)

    def project(s):
        def body(i):
            rows = rows_of(i)
            both = dot(ctx[s, rows], w_o()) + dot(hid[s, rows], w_d())
            part[s, rows] = both.astype(BF16)

        return body

    def fold(ref, row, value):
        count, cols_ = value.shape
        ref[row, :, 0:cols_] += jnp.sum(value.reshape(count // 8, 8, cols_), axis=0)

    def backward_ffn(s):
        def body(i):
            rows = rows_of(i)
            g = gs[s, rows]
            dctx[s, rows] = dot(g, w_o(), NT).astype(BF16)
            d_act = (dot(g, w_d(), NT) * gp[s, rows].astype(F32)).astype(BF16)
            gp[s, rows] = d_act
            fold(acc_gain, 4, g.astype(F32))
            fold(acc_bu, 0, d_act.astype(F32))
            d_h = dot(d_act, w_u(), NT)
            fold(acc_gain, 2, d_h * normed_of(s, rows))
            fold(acc_gain, 3, d_h)
            ep[s, rows] = (d_h * g2[...]).astype(BF16)

        return body

    def attend_back(s, i):
        rows = pl.ds(i * block, block)
        keys = (i + 1) * block
        span = pl.ds(0, keys)
        q, k, v = qkv[s, rows, 0:128], qkv[s, span, 128:256], qkv[s, span, 256:384]
        d_c = dctx[s, rows]
        zero = jnp.zeros_like(q)
        d_q = None
        for h in range(heads):
            p = probs[i][h]
            d_h = jnp.where(in_head[h], d_c, zero)
            d_p = dot(d_h, v, NT)
            p_f = p.astype(F32)
            delta = jnp.sum(p_f * d_p, axis=-1, keepdims=True)
            d_s = (p_f * (d_p - delta)).astype(BF16)
            o = dot(d_s, k)
            d_q = o if d_q is None else jnp.where(in_head[h], o, d_q)
            d_k = dot(d_s, jnp.where(in_head[h], q, zero), TN)
            d_v = dot(p, d_h, TN)
            if i == nz - 1 and h == 0:
                dk[...] = d_k
                dv[...] = d_v
            else:
                dk[span] += d_k
                dv[span] += d_v
        d_q = turn(d_q, rows, -1) * (HEAD ** (-0.5))
        d_all = jnp.concatenate([d_q, turn(dk[rows], rows, -1), dv[rows]], axis=1).astype(BF16)
        dqkv[s, rows] = d_all
        fold(acc_bq, 0, d_all.astype(F32))
        d_n = dot(d_all, w_q(), NT)
        fold(acc_gain, 0, d_n * normed_of(s, rows))
        fold(acc_gain, 1, d_n)
        ep[s, rows] = (d_n * g1[...] + ep[s, rows].astype(F32)).astype(BF16)

    def put(ref, rows, s, total):
        if s:
            total = total + ref[rows].astype(F32).reshape(total.shape)
        ref[rows] = total.astype(BF16).reshape(ref[rows].shape)

    def weight_cols(s, out, gain, shift, right):
        def body(kt):
            feat = pl.ds(pl.multiple_of(kt * 256, 256), 256)
            nrm = (xs[s, :, feat].astype(F32) - stat[s, :, 0:1]) * stat[s, :, 1:2]
            h = (nrm * gain[:, feat] + shift[:, feat]).astype(BF16)
            put(out, feat, s, dot(h, right[s], TN))

        return body

    acc_gain[...] = jnp.zeros_like(acc_gain)
    acc_bu[...] = jnp.zeros_like(acc_bu)
    acc_bq[...] = jnp.zeros_like(acc_bq)

    def scatter(part_, sib_, in_, sems_):
        return ScatterPieces([SeqScatter(at, part_, sib_, in_, tok, h * size, size, [r.at[h] for r in sems_]) for h in range(PIECES)])

    m_rs = [scatter(part.at[s], m_sib.at[s], m_in.at[s], [r.at[s] for r in (ms_s, ms_r, mu_s, mu_r, md_s, md_r)]) for s in range(mb)]
    t_rs = [scatter(ep.at[s], t_sib.at[s], t_in.at[s], [r.at[s] for r in (ts_s, ts_r, tu_s, tu_r, td_s, td_r)]) for s in range(mb)]
    rows_p = n * rows_w

    def col_halves(ref):
        return lambda p, h: ref.at[pl.ds(pl.multiple_of(p * rows_p + h * (rows_p // 2), rows_p // 2), rows_p // 2)]

    def halves(ref, i, size):
        return lambda h: ref.at[i, pl.ds(h * size, size)]

    half = rows_p // 2
    wq1 = PlaneReduce(at, col_halves(dwq), q_via.at[0], q_via.at[1], halves(q_from, 0, half), halves(q_from, 1, half), gq1s, gq1r)
    wu1 = PlaneReduce(at, col_halves(dwu), u_via.at[0], u_via.at[1], halves(u_from, 0, half), halves(u_from, 1, half), gu1s, gu1r)
    half_do = rows_do // 2
    wd1 = PlaneReduce(at, lambda p, h: dwdo.at[p, pl.ds(h * half_do, half_do)], d_via.at[0], d_via.at[1],
                      halves(d_from, 0, half_do), halves(d_from, 1, half_do), gd_s, gd_r)
    gv1 = Exchange(at, "dp", lambda p: vsum, lambda s: vin.at[s], gv1s, gv1r)
    wq2 = Exchange(at, "ctx", lambda p: wq_st.at[p], lambda s: wq_rx.at[s], gq2s, gq2r)
    wu2 = Exchange(at, "ctx", lambda p: wu_st.at[p], lambda s: wu_rx.at[s], gu2s, gu2r)
    gv2 = Exchange(at, "ctx", lambda p: v_st.at[p], lambda s: v_rx.at[s], gv2s, gv2r)
    out_back = remote(dwo_st, dwo_out, go2s, go2r, at.from_dp, at.from_c)

    def columns_on(first_hop, second_hop, stage, out):
        for h in (0, 1):
            total = first_hop.total(h).astype(BF16)
            stage[pl.ds(h * (n // 2), n // 2)] = total.reshape((n // 2,) + stage.shape[1:])
        second_hop.start()
        out[at.c] = stage[at.c]

    def down_out():
        low, high = wd1.total(0), wd1.total(1)
        dwd_out[pl.ds(0, half_do)] = low
        dwd_out[pl.ds(half_do, rows_d - half_do)] = high[0 : rows_d - half_do]
        rows = high[rows_d - half_do :].astype(BF16)

        @pl.when(at.moves)
        def _():
            dwo_st[...] = rows
            out_back.start()

        @pl.when(jnp.logical_not(at.moves))
        def _():
            dwo_out[...] = rows

    def vectors_out():
        mine = v_rx[at.c]
        index = at.dp * n + at.c
        start = index * (3 * rows_w)
        shift, tile = lax.rem(start, 128), start // 128

        def tile_of(t):
            rows = v_rx[lax.rem(t, n)]
            third = t // n
            return jnp.where(third == 0, rows[8:9], jnp.where(third == 1, rows[9:10], rows[10:11]))

        low, high = tile_of(tile), tile_of(jnp.minimum(tile + 1, 3 * n - 1))
        both = low
        for u in range(1, 128 // rows_w):
            off = u * rows_w
            moved = jnp.where(lane1 < 128 - off, pltpu.roll(low, 128 - off, 1), pltpu.roll(high, 128 - off, 1))
            both = jnp.where(shift == off, moved, both)
        place = lax.rem(index * rows_w, 128)
        base = v_rx[0, 0:8]
        for p in range(1, n):
            base = base + v_rx[p, 0:8]
        row = lax.broadcasted_iota(jnp.int32, (8, 128), 0)
        base = jnp.where(row < 6, base, mine[0:8])
        out = base
        for u in range(1, 128 // rows_w):
            out = jnp.where(place == u * rows_w, pltpu.roll(base, 128 - u * rows_w, 1), out)
        vec_out[...] = out
        vec_out[0:1] = both
        vec_out[1:2] = mine[11:12]
        vec_out[7:8] = out[6:7]

    def starts(rs, zs):
        def event():
            for z in zs:
                rs.cross(z).start()

        return event

    def finish_mixed(s):
        m_rs[s].total(own)
        mixed_out[s] = (xs[s, own_rows].astype(F32) + own[...] + bo[...]).astype(BF16)

    def finish_grad(s):
        t_rs[s].total(own)
        e = own[...]
        nrm = normed_of(s, own_rows)
        inner = e - jnp.mean(e, axis=-1, keepdims=True) - nrm * jnp.mean(e * nrm, axis=-1, keepdims=True)
        grad_out[s] = (gs[s, own_rows].astype(F32) + stat[s, own_rows, 1:2] * inner).astype(BF16)

    def down_rows(s):
        def body(kt):
            feat = pl.ds(pl.multiple_of(kt * 256, 256), 256)
            total = dot(hid[s, :, feat], gs[s], TN).reshape(256 // rows_d, rows_d, width)
            mine = dwdo.at[pl.ds(kt * (256 // rows_d), 256 // rows_d), pl.ds(0, rows_d)]
            if s:
                total = total + mine[...].astype(F32)
            mine[...] = total.astype(BF16)

        return body

    def out_grad(s):
        total = dot(ctx[s], gs[s], TN).reshape(ndp, rows_w, width)
        mine = dwdo.at[:, pl.ds(rows_d, rows_w)]
        if s:
            total = total + mine[...].astype(F32)
        mine[...] = total.astype(BF16)

    x_ag[0].step(2)
    c_ag[0].start()
    plane_d.start()
    x_ag[0].step(3)
    plane_w.land()
    x_ag[0].land()
    blocks(nz, forward_one(0), {3: [lambda: c_ag[0].step(1)]})
    plane_d.forward()
    for i in range(nz):
        attend(0, i)
        if i == 2:
            c_ag[0].step(2)
            x_ag[1].start()
    plane_d.land()
    blocks(nz, project(0))
    starts(m_rs[0], range(nz))()
    m_rs[0].step(0)
    c_ag[0].step(3)
    c_ag[0].land()
    blocks(nz, backward_ffn(0), {2: [lambda: x_ag[1].step(1), c_ag[1].start]})
    m_rs[0].step(1)
    for i in reversed(range(nz)):
        attend_back(0, i)
        t_rs[0].cross(i).start()
        if i == 2:
            x_ag[1].step(2)
    t_rs[0].step(0)
    blocks(width // 256, weight_cols(0, dwu, g2, s2, gp))
    x_ag[1].step(3)
    x_ag[1].land()
    blocks(nz, forward_one(1), {0: [lambda: c_ag[1].step(1)]})
    for i in range(nz):
        attend(1, i)
        if i == 1:
            c_ag[1].step(2)
    m_rs[0].step(2)
    t_rs[0].step(1)
    blocks(nz, project(1))
    starts(m_rs[1], range(nz))()
    m_rs[1].step(0)
    blocks(width // 256, weight_cols(0, dwq, g1, s1, dqkv))
    blocks(fu // 256, down_rows(0))
    out_grad(0)
    back = backward_ffn(1)
    for k in range(nz):
        if k == nz - 1:
            c_ag[1].step(k)
            t_rs[0].step(2)
        c_ag[1].take(k, back)
    m_rs[1].step(1)
    blocks(width // 256, weight_cols(1, dwu, g2, s2, gp))
    wu1.start()
    for i in reversed(range(nz)):
        attend_back(1, i)
        t_rs[1].cross(i).start()
        if i == 2:
            m_rs[1].step(2)
        if i < nz - 1:
            t_rs[1].lead_up(nz - 2 - i)
        if i == 1:
            wu1.combine()
    for t in range(nz - 1):
        t_rs[1].lead_down(t)
    blocks(width // 256, weight_cols(1, dwq, g1, s1, dqkv))
    wq1.start()
    vsum[...] = jnp.zeros_like(vsum)
    vsum[0:1, 0:384] = jnp.sum(acc_bq[0], axis=0, keepdims=True)
    vsum[1:2, 0:fu] = jnp.sum(acc_bu[0], axis=0, keepdims=True)
    for r in range(5):
        vsum[2 + r : 3 + r] = jnp.sum(acc_gain[r], axis=0, keepdims=True)
    gv1.start()
    columns_on(wu1, wu2, wu_st, wu_rx)
    blocks(fu // 256, down_rows(1))
    out_grad(1)
    t_rs[1].follow(1)
    wq1.combine()
    wd1.start()
    finish_mixed(0)
    finish_mixed(1)
    finish_grad(0)
    columns_on(wq1, wq2, wq_st, wq_rx)
    t_rs[1].follow(2)
    gv1.wait_recv()
    total = vsum[...]
    for j in range(1, ndp):
        total = total + vin[lax.rem(at.dp + j, ndp)]
    vsum_all[...] = total
    for p in range(n):
        v_st[p, 0:8] = vsum_all[:, pl.ds(pl.multiple_of((at.dp * n + p) * rows_w // 128 * 128, 128), 128)]
        for r in range(3):
            v_st[p, 8 + r : 9 + r] = total[0:1, r * 128 : (r + 1) * 128]
        v_st[p, 11:12] = vsum_all[1:2, pl.ds(pl.multiple_of(at.dp * rows_d, 128), 128)]
        v_st[p, 12:16] = jnp.zeros((4, 128), F32)
    gv2.start()
    v_rx[at.c] = v_st[at.c]
    wd1.combine()
    finish_grad(1)
    down_out()

    @pl.when(at.moves)
    def _():
        out_rows.wait_send()
        out_back.wait()

    wu2.wait_recv()
    for p in range(n):
        for d in range(ndp):
            up_out[:, (d * n + p) * rows_d : (d * n + p + 1) * rows_d] = wu_rx[p, :, d * rows_d : (d + 1) * rows_d]
    gv2.wait_recv()
    vectors_out()
    wq2.wait_recv()
    for p in range(n):
        for part_ in range(3):
            qkv_out[:, part_ * width + p * 128 : part_ * width + (p + 1) * 128] = wq_rx[p, :, part_ * 128 : (part_ + 1) * 128]
    for part_ in (cols, vec1, plane_v, gv1, wq2, wu2, gv2):
        part_.wait_send()
    for part_ in (plane_w, plane_d, wq1, wu1, wd1):
        part_.drain()
    for s in range(mb):
        x_ag[s].drain()
        c_ag[s].drain()
        m_rs[s].drain()
        t_rs[s].drain()


def fused_layer(ndp, n, dims, tok, cot, rq, ru, wd, wo, vec, seg, cosine, sine):
    mb, tk, width, seq, heads, rows_w, rows_d = dims
    nz, block, fu = n // 2, 2 * tk, ndp * rows_d
    rows_do, rows_p = rows_d + rows_w, n * rows_w
    dma = pltpu.SemaphoreType.DMA
    vm = pltpu.VMEM
    vmem = pl.BlockSpec(memory_space=pltpu.VMEM)
    slots = gather_slots(nz)
    scratch = [
        vm((mb, seq, width), BF16), vm((mb, seq, width), BF16),
        vm((ndp, n, rows_w, 384 + fu), BF16), vm((ndp, rows_d + rows_w, width), BF16),
        vm((ndp, n, 16, 128), F32), vm((8, seq), F32), vm((seq, 8), F32), vm((seq, 128), F32), vm((seq, 128), F32),
        vm((1, width), F32), vm((1, width), F32), vm((1, width), F32), vm((1, width), F32), vm((1, width), F32),
        vm((1, 384), F32), vm((1, fu), F32),
        vm((mb, seq, 384), BF16), vm((mb, seq, fu), BF16), vm((mb, seq, fu), BF16), vm((mb, seq, 2), F32),
        vm((mb, seq, 128), BF16), vm((mb, seq, width), BF16), vm((mb, seq, width), BF16),
        vm((mb, seq, 128), BF16), vm((mb, seq, 384), BF16), vm((seq, 128), F32), vm((seq, 128), F32),
        vm((5, 8, width), F32), vm((1, 8, fu), F32), vm((1, 8, 384), F32),
        vm((mb, nz, tk, width), BF16), vm((mb, nz + 1, tk, width), BF16), vm((mb, nz, tk, width), BF16), vm((mb, nz + 1, tk, width), BF16),
        vm((width, 384), BF16), vm((width, fu), BF16), vm((ndp, rows_do, width), BF16),
        vm((2, rows_p // 2, 384), BF16), vm((2, rows_p, 384), BF16), vm((2, rows_p // 2, fu), BF16), vm((2, rows_p, fu), BF16),
        vm((2, rows_do // 2, width), BF16), vm((2, rows_do, width), BF16),
        vm((8, width), F32), vm((ndp, 8, width), F32), vm((n, rows_w, 384), BF16), vm((n, rows_w, fu), BF16),
        vm((tk, width), F32), vm((rows_w, width), BF16),
        vm((8, width), F32), vm((n, 16, 128), F32),
        vm((mb, seq), jnp.int32), vm((rows_w, 3 * width), BF16), vm((rows_w, n * fu), BF16), vm((n, rows_w, 384 + fu), BF16),
        vm((n, rows_w, 384), BF16), vm((n, rows_w, fu), BF16), vm((n, 16, 128), F32),
    ] + [vm((heads, block, block * (i + 1)), BF16) for i in range(nz)]
    per_seq = [dma((mb, PIECES, slots)), dma((mb, PIECES, n))]
    to_ctx, to_dp, plane = [dma((n,))] * 2, [dma((ndp,))] * 2, [dma((6,))] * 2
    sems = per_seq * 2 + to_ctx + plane + to_ctx + to_dp + plane + [dma, dma]
    sems += [dma((mb, PIECES, nz))] * 12
    sems += (plane + to_ctx) * 2 + plane + [dma, dma] + to_dp + to_ctx + [dma((10,))]
    return pl.pallas_call(
        partial(fused_kernel, ndp, n, dims),
        out_shape=(
            jax.ShapeDtypeStruct((mb, tk, width), BF16),
            jax.ShapeDtypeStruct((mb, tk, width), BF16),
            jax.ShapeDtypeStruct((rows_w, 3 * width), BF16),
            jax.ShapeDtypeStruct((rows_w, n * fu), BF16),
            jax.ShapeDtypeStruct((rows_d, width), F32),
            jax.ShapeDtypeStruct((rows_w, width), BF16),
            jax.ShapeDtypeStruct((8, 128), F32),
        ),
        in_specs=[ANY] * 10,
        out_specs=[vmem] * 7,
        scratch_shapes=scratch + sems,
        compiler_params=pltpu.CompilerParams(collective_id=5, has_side_effects=True, vmem_limit_bytes=63 * MIB),
    )(tok, cot, rq, ru, wd, wo, vec, seg, cosine, sine)


def rotary_lanes(seq):
    half = ROT // 2
    inverse = (np.float32(10000.0) ** (-(np.float32(2.0) * np.arange(half, dtype=np.float32)) / np.float32(ROT))).astype(np.float32)
    angles = (np.arange(seq, dtype=np.float32)[:, None] * inverse[None, :]).astype(np.float32)
    cosine = np.ones((seq, HEAD), np.float32)
    sine = np.zeros((seq, HEAD), np.float32)
    cosine[:, :half] = cosine[:, half:ROT] = np.cos(angles)
    sine[:, :half] = -np.sin(angles)
    sine[:, half:ROT] = np.sin(angles)
    return np.tile(cosine, (1, 128 // HEAD)), np.tile(sine, (1, 128 // HEAD))


def fused_device(ndp, n, tokens, cotangent, segments, w_qkv, b_qkv, w_out, b_out, w_up, b_up, w_down, b_down, g1, s1, g2, s2):
    tok, mb, width = tokens.shape
    seq = segments.shape[1]
    hc = width // n
    rows_w, rows_d = w_qkv.shape[0], w_down.shape[0]
    toks, cot = jnp.transpose(tokens, (1, 0, 2)), jnp.transpose(cotangent, (1, 0, 2))
    toks, cot, small = lax.optimization_barrier((toks, cot, (b_qkv, b_out, b_up, b_down, g1, s1, g2, s2)))
    units = jnp.concatenate(small).astype(F32).reshape(-1, rows_w)
    vec = jnp.pad(jnp.tile(units, (1, 128 // rows_w)), ((0, 16 - units.shape[0]), (0, 0)))
    cosine, sine = rotary_lanes(seq)
    dims = (mb, tok, width, seq, hc // HEAD, rows_w, rows_d)
    mixed, t_grad, d_qkv, d_up, dwd, dwo, dv = fused_layer(
        ndp, n, dims, toks, cot, w_qkv, w_up, w_down, w_out, vec, segments, jnp.asarray(cosine), jnp.asarray(sine)
    )
    one = lambda r: dv[r, :rows_w]
    return (
        jnp.transpose(mixed, (1, 0, 2)),
        jnp.transpose(t_grad, (1, 0, 2)),
        d_qkv.astype(F32),
        dv[0, : b_qkv.shape[0]],
        dwo.astype(F32),
        one(6),
        d_up.astype(F32),
        dv[1, :rows_d],
        dwd,
        one(7),
        one(2),
        one(3),
        one(4),
        one(5),
    )


def rotary_tables(seq):
    half_rot = ROT // 2
    inverse = 10000.0 ** (-(2.0 * jnp.arange(half_rot, dtype=F32)) / ROT)
    angles = jnp.arange(seq, dtype=jnp.int32).astype(F32)[:, None] * inverse[None, :]
    angles = jnp.concatenate([angles, angles], axis=-1)
    return (jnp.cos(angles)[None, :, None, :], jnp.sin(angles)[None, :, None, :])


def rotate(values, cosine, sine, back=False):
    half_rot = ROT // 2
    lead = values[..., :ROT]
    if back:
        u = lead * sine
        turned = jnp.concatenate([u[..., half_rot:], -u[..., :half_rot]], axis=-1)
        return jnp.concatenate([lead * cosine + turned, values[..., ROT:]], axis=-1)
    turned = jnp.concatenate([-lead[..., half_rot:], lead[..., :half_rot]], axis=-1)
    return jnp.concatenate([lead * cosine + turned * sine, values[..., ROT:]], axis=-1)


def per_device(ndp, n, tokens, cotangent, segments, w_qkv, b_qkv, w_out, b_out, w_up, b_up, w_down, b_down, g1, s1, g2, s2):
    tok, mb, width = tokens.shape
    seq = segments.shape[1]
    heads_all = width // HEAD
    hc = width // n
    heads = hc // HEAD
    rows_w = w_qkv.shape[0]
    rows_d = w_down.shape[0]
    fu = ndp * rows_d
    c = lax.axis_index("ctx")
    dp = lax.axis_index("dp")
    scale = HEAD ** (-0.5)

    cot = jnp.transpose(cotangent, (1, 0, 2))
    toks = jnp.transpose(tokens, (1, 0, 2))
    qkv_cols = w_qkv.reshape(rows_w, 3, n, hc).transpose(2, 0, 1, 3).reshape(n, rows_w, 3 * hc)
    up_cols = w_up.reshape(rows_w, ndp, n, rows_d).transpose(2, 0, 1, 3).reshape(n, rows_w, fu)
    wp = jnp.concatenate([qkv_cols, up_cols], axis=2)
    shard_vecs = (b_qkv, b_out, b_up, b_down, g1, s1, g2, s2)
    sizes = [v.shape[0] for v in shard_vecs]
    vec = jnp.concatenate(shard_vecs)
    lanes = 128
    per_vec = 16 * lanes
    vec = jnp.pad(vec, (0, per_vec - vec.shape[0])).reshape(16, lanes)
    x, g, w, wd, wo, vecs = gather_all(ndp, n, toks, cot, wp, w_down, w_out, vec)
    w = w.reshape(width, 3 * hc + fu)
    wq, wu = w[:, : 3 * hc], w[:, 3 * hc :]
    wd = wd.reshape(fu, width)
    wo = wo.reshape(hc, width)
    flat = vecs.reshape(ndp * n, per_vec).astype(F32)
    starts = [sum(sizes[:i]) for i in range(len(sizes))]
    full = [flat[:, s : s + z].reshape(-1) for s, z in zip(starts, sizes)]
    bq_all, bo, bu_all, bd, gain1, shift1, gain2, shift2 = full
    bq = lax.dynamic_index_in_dim(bq_all.reshape(3, n, hc), c, 1, keepdims=False).reshape(3 * hc)
    bu = lax.dynamic_index_in_dim(bu_all.reshape(ndp, n, rows_d), c, 1, keepdims=False).reshape(fu)

    xf = x.reshape(mb * seq, width).astype(F32)
    gl = g.reshape(mb * seq, width)
    mean = jnp.mean(xf, axis=-1, keepdims=True)
    cen = xf - mean
    rstd = lax.rsqrt(jnp.mean(cen * cen, axis=-1, keepdims=True) + 1e-05)
    normed = cen * rstd
    h1 = (normed * gain1 + shift1).astype(BF16)
    h2 = (normed * gain2 + shift2).astype(BF16)
    joined = (dot(h1, wq) + bq).reshape(mb, seq, 3, heads, HEAD)
    cosine, sine = rotary_tables(seq)
    q = rotate(joined[:, :, 0], cosine, sine).astype(BF16)
    k = rotate(joined[:, :, 1], cosine, sine).astype(BF16)
    v = joined[:, :, 2].astype(BF16)
    pos = jnp.arange(seq, dtype=jnp.int32)
    same = (segments[:, None, :] == segments[:, :, None]) & (segments[:, :, None] > 0)
    allow = (same & (pos[None, None, :] <= pos[None, :, None])) | (pos[None, None, :] == pos[None, :, None])
    scores = jnp.einsum("sqhd,skhd->shqk", q, k, preferred_element_type=F32) * scale
    scores = jnp.where(allow[:, None], scores, -1e30)
    top = jnp.max(scores, axis=-1, keepdims=True)
    e = jnp.exp(scores - top)
    probs = e / jnp.sum(e, axis=-1, keepdims=True)
    pl_low = probs.astype(BF16)
    ctx_f = jnp.einsum("shqk,skhd->sqhd", pl_low, v, preferred_element_type=F32)
    ctx = ctx_f.astype(BF16).reshape(mb * seq, hc)
    act = dot(h2, wu) + bu
    hidden = jax.nn.gelu(act, approximate=False).astype(BF16)
    part = (dot(ctx, wo) + dot(hidden, wd)).astype(BF16).reshape(mb, seq, width)
    mixed_sum = scatter_ctx(ndp, n, part, 1)
    mixed = (toks.astype(F32) + mixed_sum + bo + bd).astype(BF16)

    gf = gl.astype(F32)
    d_wd = dot(hidden, gl, ((0,), (0,)))
    d_wo = dot(ctx, gl, ((0,), (0,)))
    d_hidden = dot(gl, wd, ((1,), (1,)))
    _, pull = jax.vjp(partial(jax.nn.gelu, approximate=False), act)
    d_act = pull(d_hidden)[0].astype(BF16)
    d_wu = dot(h2, d_act, ((0,), (0,)))
    d_bu = jnp.sum(d_act.astype(F32), axis=0)
    d_h2 = dot(d_act, wu, ((1,), (1,)))
    d_ctx = dot(gl, wo, ((1,), (1,))).astype(BF16).reshape(mb, seq, heads, HEAD)
    d_probs = jnp.einsum("sqhd,skhd->shqk", d_ctx, v, preferred_element_type=F32)
    delta = jnp.sum(probs * d_probs, axis=-1, keepdims=True)
    d_scores = jnp.where(allow[:, None], probs * (d_probs - delta), 0.0).astype(BF16)
    d_q = jnp.einsum("shqk,skhd->sqhd", d_scores, k, preferred_element_type=F32) * scale
    d_k = jnp.einsum("shqk,sqhd->skhd", d_scores, q, preferred_element_type=F32) * scale
    d_v = jnp.einsum("shqk,sqhd->skhd", pl_low, d_ctx, preferred_element_type=F32)
    d_q = rotate(d_q, cosine, sine, True)
    d_k = rotate(d_k, cosine, sine, True)
    d_qkv = jnp.stack([d_q, d_k, d_v], axis=2).astype(BF16).reshape(mb * seq, 3 * hc)
    d_wq = dot(h1, d_qkv, ((0,), (0,)))
    d_bq = jnp.sum(d_qkv.astype(F32), axis=0)
    d_h1 = dot(d_qkv, wq, ((1,), (1,)))
    e_sum = (d_h1 * gain1 + d_h2 * gain2).astype(BF16).reshape(mb, seq, width)
    e_own = scatter_ctx(ndp, n, e_sum, 2)
    own_x = toks.astype(F32)
    o_mean = jnp.mean(own_x, axis=-1, keepdims=True)
    o_cen = own_x - o_mean
    o_rstd = lax.rsqrt(jnp.mean(o_cen * o_cen, axis=-1, keepdims=True) + 1e-05)
    o_n = o_cen * o_rstd
    t_grad = o_rstd * (e_own - jnp.mean(e_own, axis=-1, keepdims=True) - o_n * jnp.mean(e_own * o_n, axis=-1, keepdims=True))
    tokens_grad = (cot.astype(F32) + t_grad).astype(BF16)

    rows = [
        jnp.pad(d_bq, (0, width - 3 * hc)),
        jnp.pad(d_bu, (0, width - fu)),
        jnp.sum(d_h1 * normed, axis=0),
        jnp.sum(d_h1, axis=0),
        jnp.sum(d_h2 * normed, axis=0),
        jnp.sum(d_h2, axis=0),
        jnp.sum(gf, axis=0),
        jnp.zeros((width,), F32),
    ]
    dwp = jnp.concatenate([d_wq, d_wu], axis=1).astype(BF16).reshape(ndp, n, rows_w, 3 * hc + fu)
    dw, dwd, dwo, dv = grads_all(
        ndp, n, dwp, d_wd.astype(BF16).reshape(ndp, rows_d, width), d_wo.astype(BF16).reshape(ndp, rows_w, width), jnp.stack(rows)
    )
    index = dp * n + c
    g_qkv = dw[:, :, : 3 * hc].reshape(n, rows_w, 3, hc).transpose(1, 2, 0, 3).reshape(rows_w, 3 * width).astype(F32)
    g_up = dw[:, :, 3 * hc :].reshape(n, rows_w, ndp, rows_d).transpose(1, 2, 0, 3).reshape(rows_w, -1).astype(F32)
    g_bq = lax.dynamic_slice_in_dim(dv[:, 0, : 3 * hc].reshape(n, 3, hc).transpose(1, 0, 2).reshape(-1), index * sizes[0], sizes[0])
    own = lax.dynamic_index_in_dim(dv, c, 0, keepdims=False)
    g_bu = lax.dynamic_slice_in_dim(own[1], dp * rows_d, rows_d)
    four = lax.dynamic_slice_in_dim(jnp.sum(dv[:, 2:6], axis=0), index * rows_w, rows_w, axis=1)
    g_b = lax.dynamic_slice_in_dim(own[6], index * rows_w, rows_w)
    return (
        jnp.transpose(mixed, (1, 0, 2)),
        jnp.transpose(tokens_grad, (1, 0, 2)),
        g_qkv,
        g_bq,
        dwo.astype(F32),
        g_b,
        g_up,
        g_bu,
        dwd,
        g_b,
        four[0],
        four[1],
        four[2],
        four[3],
    )


def program(ndp, n, *args):
    tokens, w_qkv, w_down = args[0], args[3], args[9]
    rows_w = w_qkv.shape[0]
    whole_tiles = ndp == 4 and rows_w % 16 == 0 and tokens.shape[2] // n == 128 and w_down.shape[0] == 128 and tokens.shape[0] % 16 == 0
    return (fused_device if whole_tiles else per_device)(ndp, n, *args)


def solution(mesh):
    every = ("dp", "ctx")
    mat, vec, act = P(every, None), P(every), P("ctx", "dp", None)
    placed = (act, act, P("dp", None), mat, vec, mat, vec, mat, vec, mat, vec, vec, vec, vec, vec)
    return jax.shard_map(
        partial(program, mesh.shape["dp"], mesh.shape["ctx"]),
        mesh=mesh,
        in_specs=placed,
        out_specs=(act, act, mat, vec, mat, vec, mat, vec, mat, vec, vec, vec, vec, vec),
        check_vma=False,
    )
```

```python
from functools import partial

import jax
import jax.numpy as jnp
import numpy as np
from jax import lax
from jax.experimental import pallas as pl
from jax.experimental.pallas import tpu as pltpu
from jax.sharding import PartitionSpec as P

HEAD = 64
ROT = 16
MIB = 1 << 20
CUT_TOKENS, CUT_COTANGENT, CUT_MIXED, CUT_GRAD = (2, 1), (1, 1), (1, 1), (1, 2)
MESH = pl.DeviceIdType.MESH
ANY = pl.BlockSpec(memory_space=pl.ANY)
F32 = jnp.float32
BF16 = jnp.bfloat16


class Place:
    def __init__(self, ndp, n):
        self.ndp, self.n, self.nz = ndp, n, n // 2
        self.dp = lax.axis_index("dp")
        self.c = lax.axis_index("ctx")
        self.z = self.c // 2
        self.core = lax.rem(self.c, 2)
        self.sib = self.c + 1 - 2 * self.core
        self.has_up = self.z + 1 < self.nz
        self.has_down = self.z > 0
        self.px = self.dp + 1 - 2 * lax.rem(self.dp, 2)
        self.py = lax.rem(self.dp + 2, 4)
        self.diag = 3 - self.dp
        index, back = self.dp * n + self.c, self.c * ndp + self.dp
        self.rows_dp, self.rows_c = lax.rem(index, ndp), index // ndp
        self.from_dp, self.from_c = back // n, lax.rem(back, n)
        self.moves = index != back

    def barrier(self, ctx_all, dp_all, rows=False):
        bar = pltpu.get_barrier_semaphore()
        count = 0
        if rows:
            count = count + 2 * self.moves.astype(jnp.int32)

            @pl.when(self.moves)
            def _():
                pl.semaphore_signal(bar, inc=1, device_id=(self.rows_dp, self.rows_c), device_id_type=MESH)
                pl.semaphore_signal(bar, inc=1, device_id=(self.from_dp, self.from_c), device_id_type=MESH)

        if ctx_all:
            for j in range(1, self.n):
                peer = lax.rem(self.c + j, self.n)
                pl.semaphore_signal(bar, inc=1, device_id=(self.dp, peer), device_id_type=MESH)
                count += 1
        else:
            pl.semaphore_signal(bar, inc=1, device_id=(self.dp, self.sib), device_id_type=MESH)
            count += 1
            for ok, peer in ((self.has_up, self.c + 2), (self.has_down, self.c - 2)):

                @pl.when(ok)
                def _():
                    pl.semaphore_signal(bar, inc=1, device_id=(self.dp, peer), device_id_type=MESH)

        if dp_all:
            for j in range(1, self.ndp):
                peer = lax.rem(self.dp + j, self.ndp)
                pl.semaphore_signal(bar, inc=1, device_id=(peer, self.c), device_id_type=MESH)
                count += 1
        if not ctx_all:
            count = count + self.has_up.astype(jnp.int32) + self.has_down.astype(jnp.int32)
        pl.semaphore_wait(bar, count)


def remote(src, dst, send, recv, dp, c):
    return pltpu.make_async_remote_copy(
        src_ref=src,
        dst_ref=dst,
        send_sem=send,
        recv_sem=recv,
        device_id=(dp, c),
        device_id_type=MESH,
    )


class Gather:
    def __init__(self, at, src, dst, tok, sends, recvs):
        self.at, self.src, self.dst, self.tok, self.sends, self.recvs = at, src, dst, tok, sends, recvs

    def rows(self, c):
        return self.dst.at[:, pl.ds(pl.multiple_of(c * self.tok, self.tok), self.tok)]

    def copy(self, block, slot, c, src=None):
        at = self.at
        src = self.rows(block) if src is None else src
        return remote(src, self.rows(block), self.sends.at[slot], self.recvs.at[block], at.dp, c)

    def start(self):
        at = self.at

        @pl.when(at.has_up)
        def _():
            self.copy(at.c, 0, at.c + 2, self.src).start()

        @pl.when(at.has_down)
        def _():
            self.copy(at.c, 1, at.c - 2, self.src).start()

        self.copy(at.c, 2, at.sib, self.src).start()

    def step(self, k):
        at = self.at
        low, high = at.c - 2 * k, at.c + 2 * k

        @pl.when(at.z >= k)
        def _():
            self.copy(low, 0, at.c).wait_recv()

            @pl.when(at.has_up)
            def _():
                self.copy(low, 3 * k, at.c + 2).start()

            self.copy(low, 3 * k + 2, at.sib).start()

        @pl.when(at.z + k < at.nz)
        def _():
            self.copy(high, 0, at.c).wait_recv()

            @pl.when(at.has_down)
            def _():
                self.copy(high, 3 * k + 1, at.c - 2).start()

            self.copy(high, 3 * at.nz + k, at.sib).start()

    def finish(self):
        at = self.at
        for z in range(at.nz):
            self.copy(2 * z + 1 - at.core, 0, at.c).wait_recv()
        self.copy(at.c, 2, at.sib, self.src).wait_send()
        for k in range(at.nz):

            @pl.when((at.z >= k) & at.has_up)
            def _():
                self.copy(at.c, 3 * k, at.c).wait_send()

            @pl.when((at.z + k < at.nz) & at.has_down)
            def _():
                self.copy(at.c, 3 * k + 1, at.c).wait_send()

            if k:

                @pl.when(at.z >= k)
                def _():
                    self.copy(at.c, 3 * k + 2, at.c).wait_send()

                @pl.when(at.z + k < at.nz)
                def _():
                    self.copy(at.c, 3 * at.nz + k, at.c).wait_send()


def gather_slots(nz):
    return 4 * nz


class Exchange:
    def __init__(self, at, axis, src, dst, sends, recvs):
        self.at, self.axis, self.src, self.dst, self.sends, self.recvs = at, axis, src, dst, sends, recvs
        self.me, self.count = (at.c, at.n) if axis == "ctx" else (at.dp, at.ndp)

    def copy(self, peer, sender):
        at = self.at
        to = (at.dp, peer) if self.axis == "ctx" else (peer, at.c)
        return remote(self.src(peer), self.dst(sender), self.sends.at[peer], self.recvs.at[sender], *to)

    def start(self):
        for j in range(1, self.count):
            self.copy(lax.rem(self.me + j, self.count), self.me).start()

    def wait_recv(self):
        for j in range(1, self.count):
            peer = lax.rem(self.me + j, self.count)
            self.copy(peer, peer).wait_recv()

    def wait_send(self):
        for j in range(1, self.count):
            peer = lax.rem(self.me + j, self.count)
            self.copy(peer, self.me).wait_send()


def gather_kernel(ndp, n, tok_ref, cot_ref, wp_ref, wd_ref, wo_ref, vec_ref, x_out, g_out, w_out, wd_out, wo_out, vec_out, *sems):
    at = Place(ndp, n)
    tok = tok_ref.shape[1]
    (x_send, x_recv, g_send, g_recv, w1s, w1r, w2s, w2r, v1s, v1r, v2s, v2r, ds, dr, o1s, o1r, o2s, o2r, local) = sems
    at.barrier(True, True)
    own = (
        pltpu.make_async_copy(wp_ref.at[at.c], w_out.at[at.dp, at.c], local.at[0]),
        pltpu.make_async_copy(vec_ref, vec_out.at[at.dp, at.c], local.at[1]),
        pltpu.make_async_copy(wd_ref, wd_out.at[at.dp], local.at[2]),
        pltpu.make_async_copy(tok_ref, x_out.at[:, pl.ds(pl.multiple_of(at.c * tok, tok), tok)], local.at[3]),
        pltpu.make_async_copy(cot_ref, g_out.at[:, pl.ds(pl.multiple_of(at.c * tok, tok), tok)], local.at[4]),
    )
    for copy in own:
        copy.start()
    down_w = Exchange(at, "dp", lambda p: wd_ref, lambda s: wd_out.at[s], ds, dr)
    cols = Exchange(at, "ctx", lambda p: wp_ref.at[p], lambda s: w_out.at[at.dp, s], w1s, w1r)
    vecs = Exchange(at, "ctx", lambda p: vec_ref, lambda s: vec_out.at[at.dp, s], v1s, v1r)
    plane_w = Exchange(at, "dp", lambda p: w_out.at[at.dp], lambda s: w_out.at[s], w2s, w2r)
    plane_v = Exchange(at, "dp", lambda p: vec_out.at[at.dp], lambda s: vec_out.at[s], v2s, v2r)
    plane_o = Exchange(at, "dp", lambda p: wo_out, lambda s: wo_out, o2s, o2r)
    cols.start()
    vecs.start()
    index = at.dp * n + at.c
    heads_of, slot = index // ndp, lax.rem(index, ndp)

    def out_rows(b, c):
        return remote(wo_ref, wo_out.at[b], o1s, o1r.at[b], at.dp, c)

    @pl.when(heads_of != at.c)
    def _():
        out_rows(slot, heads_of).start()

    own_rows = pltpu.make_async_copy(wo_ref, wo_out.at[slot], local.at[5])

    @pl.when(heads_of == at.c)
    def _():
        own_rows.start()

    down_w.start()
    x_ag = Gather(at, tok_ref, x_out, tok, x_send, x_recv)
    g_ag = Gather(at, cot_ref, g_out, tok, g_send, g_recv)
    x_ag.start()
    own[0].wait()
    cols.wait_recv()
    plane_w.start()
    own[1].wait()
    vecs.wait_recv()
    plane_v.start()
    first = at.c * ndp // n

    @pl.when(at.dp == first)
    def _():
        for b in range(ndp):
            src = lax.rem(at.c * ndp + b, n)

            @pl.when(src != at.c)
            def _():
                out_rows(b, at.c).wait_recv()

            @pl.when(src == at.c)
            def _():
                own_rows.wait()

        plane_o.start()

    for k in range(1, at.nz):
        x_ag.step(k)
        if k == 1:
            g_ag.start()
    for k in range(1, at.nz):
        g_ag.step(k)
    x_ag.finish()
    g_ag.finish()

    @pl.when(heads_of != at.c)
    def _():
        out_rows(slot, heads_of).wait_send()

    @pl.when((heads_of == at.c) & (at.dp != first))
    def _():
        own_rows.wait()

    @pl.when(at.dp == first)
    def _():
        plane_o.wait_send()

    @pl.when(at.dp != first)
    def _():
        plane_o.copy(first, first).wait_recv()

    for copy in own[2:]:
        copy.wait()
    for part in (down_w, plane_w, plane_v):
        part.wait_recv()
    for part in (down_w, cols, vecs, plane_w, plane_v):
        part.wait_send()


def gather_all(ndp, n, tok, cot, wp, wd, wo, vec):
    mb, rows, width = tok.shape
    dma = pltpu.SemaphoreType.DMA
    slots = gather_slots(n // 2)
    return pl.pallas_call(
        partial(gather_kernel, ndp, n),
        out_shape=(
            jax.ShapeDtypeStruct((mb, rows * n, width), BF16),
            jax.ShapeDtypeStruct((mb, rows * n, width), BF16),
            jax.ShapeDtypeStruct((ndp,) + wp.shape, BF16),
            jax.ShapeDtypeStruct((ndp,) + wd.shape, BF16),
            jax.ShapeDtypeStruct((ndp,) + wo.shape, BF16),
            jax.ShapeDtypeStruct((ndp, n) + vec.shape, vec.dtype),
        ),
        in_specs=[ANY] * 6,
        out_specs=[ANY] * 6,
        scratch_shapes=[
            dma((slots,)), dma((n,)), dma((slots,)), dma((n,)),
            dma((n,)), dma((n,)), dma((ndp,)), dma((ndp,)),
            dma((n,)), dma((n,)), dma((ndp,)), dma((ndp,)),
            dma((ndp,)), dma((ndp,)),
            dma, dma((ndp,)), dma((ndp,)), dma((ndp,)),
            dma((6,)),
        ],
        compiler_params=pltpu.CompilerParams(collective_id=0, has_side_effects=True),
    )(tok, cot, wp, wd, wo, vec)


class Scatter:
    def __init__(self, at, part, out, sib_buf, low_buf, high_buf, stage, tok, sems):
        self.at, self.part, self.out, self.tok = at, part, out, tok
        self.sib_buf, self.low_buf, self.high_buf, self.stage = sib_buf, low_buf, high_buf, stage
        self.s_send, self.s_recv, self.up_send, self.up_recv, self.dn_send, self.dn_recv = sems

    def rows(self, c):
        return pl.ds(pl.multiple_of(c * self.tok, self.tok), self.tok)

    def cross(self, z):
        at = self.at
        src = self.part.at[:, self.rows(2 * z + 1 - at.core)]
        return remote(src, self.sib_buf.at[z], self.s_send.at[z], self.s_recv.at[z], at.dp, at.sib)

    def up(self, z):
        at = self.at
        return remote(self.stage.at[z], self.low_buf.at[z], self.up_send.at[z], self.up_recv.at[z], at.dp, at.c + 2)

    def down(self, z):
        at = self.at
        return remote(self.stage.at[z], self.high_buf.at[z], self.dn_send.at[z], self.dn_recv.at[z], at.dp, at.c - 2)

    def order(self):
        nz = self.at.nz
        for i in range(nz):
            yield nz - 1 - i
            if i != nz - 1 - i:
                pass

    def start(self):
        for i in range(self.at.nz):
            self.cross(i).start()

    def chip_sum(self, z):
        at = self.at
        mine = self.part[:, self.rows(2 * z + at.core)].astype(F32)
        return mine + self.sib_buf[z].astype(F32)

    def step(self, i):
        at = self.at
        up_z, dn_z = at.nz - 1 - i, i

        @pl.when(up_z > at.z)
        def _():
            self.cross(up_z).wait_recv()
            self.stage[up_z] = self.chip_sum(up_z).astype(BF16)

            @pl.when(at.has_down)
            def _():
                self.up(up_z).wait_recv()
                self.stage[up_z] = (self.stage[up_z].astype(F32) + self.low_buf[up_z].astype(F32)).astype(BF16)

            self.up(up_z).start()

        @pl.when(dn_z < at.z)
        def _():
            self.cross(dn_z).wait_recv()
            self.stage[dn_z] = self.chip_sum(dn_z).astype(BF16)

            @pl.when(at.has_up)
            def _():
                self.down(dn_z).wait_recv()
                self.stage[dn_z] = (self.stage[dn_z].astype(F32) + self.high_buf[dn_z].astype(F32)).astype(BF16)

            self.down(dn_z).start()

    def finish(self):
        at = self.at
        self.cross(at.z).wait_recv()
        self.out[...] = self.chip_sum(at.z)

        @pl.when(at.has_down)
        def _():
            self.up(at.z).wait_recv()
            self.out[...] += self.low_buf[at.z].astype(F32)

        @pl.when(at.has_up)
        def _():
            self.down(at.z).wait_recv()
            self.out[...] += self.high_buf[at.z].astype(F32)

        for z in range(at.nz):
            self.cross(z).wait_send()

            @pl.when(z > at.z)
            def _():
                self.up(z).wait_send()

            @pl.when(z < at.z)
            def _():
                self.down(z).wait_send()


def scatter_kernel(ndp, n, part_ref, out_ref, sib_buf, low_buf, high_buf, stage, *sems):
    at = Place(ndp, n)
    at.barrier(False, False)
    work = Scatter(at, part_ref, out_ref, sib_buf, low_buf, high_buf, stage, out_ref.shape[1], sems)
    work.start()
    for i in range(at.nz - 1):
        work.step(i)
    work.finish()


def scatter_ctx(ndp, n, part, collective):
    mb, seq, width = part.shape
    nz, tok = n // 2, seq // n
    dma = pltpu.SemaphoreType.DMA
    buf = pltpu.VMEM((nz, mb, tok, width), BF16)
    vmem = pl.BlockSpec(memory_space=pltpu.VMEM)
    return pl.pallas_call(
        partial(scatter_kernel, ndp, n),
        out_shape=jax.ShapeDtypeStruct((mb, tok, width), F32),
        in_specs=[vmem],
        out_specs=vmem,
        scratch_shapes=[buf, buf, buf, buf] + [dma((nz,))] * 6,
        compiler_params=pltpu.CompilerParams(collective_id=collective, has_side_effects=True, vmem_limit_bytes=48 * MIB),
    )(part)


def grads_kernel(ndp, n, wp_ref, wd_ref, wo_ref, v_ref, w_out, wd_out, wo_out, v_out, wbuf, wsum, dbuf, obuf, osum, vbuf, vsum, *sems):
    at = Place(ndp, n)
    (w1s, w1r, ds, dr, o1s, o1r, v1s, v1r, w2s, w2r, v2s, v2r, o2s, o2r, local) = sems
    at.barrier(True, True)
    first = at.c * ndp // n
    w1 = Exchange(at, "dp", lambda p: wp_ref.at[p], lambda s: wbuf.at[s], w1s, w1r)
    d1 = Exchange(at, "dp", lambda p: wd_ref.at[p], lambda s: dbuf.at[s], ds, dr)
    v1 = Exchange(at, "dp", lambda p: v_ref, lambda s: vbuf.at[s], v1s, v1r)
    o1 = Exchange(at, "dp", lambda p: wo_ref, lambda s: obuf.at[s], o1s, o1r)
    w1.start()
    v1.start()

    @pl.when(at.dp != first)
    def _():
        o1.copy(first, at.dp).start()

    d1.start()

    def total(ref, mine, get):
        ref[...] = mine
        for j in range(1, ndp):
            ref[...] += get(lax.rem(at.dp + j, ndp)).astype(F32)

    w1.wait_recv()
    total(wsum, wp_ref[at.dp].astype(F32), lambda s: wbuf[s])
    wbuf[at.dp] = wsum[...].astype(BF16)
    w2 = Exchange(at, "ctx", lambda p: wbuf.at[at.dp, p], lambda s: w_out.at[s], w2s, w2r)
    w2.start()
    w_out[at.c] = wbuf[at.dp, at.c]
    v1.wait_recv()
    total(vsum, v_ref[...], lambda s: vbuf[s])
    v2 = Exchange(at, "ctx", lambda p: vsum, lambda s: v_out.at[s], v2s, v2r)
    v2.start()
    v_out[at.c] = vsum[...]

    index = at.dp * n + at.c
    heads_of, slot = index // ndp, lax.rem(index, ndp)

    def out_rows(b, c):
        return remote(osum.at[b], wo_out, o2s.at[b], o2r, at.dp, c)

    @pl.when(at.dp == first)
    def _():
        o1.wait_recv()
        rows = wo_ref[...].astype(F32)
        for j in range(1, ndp):
            rows += obuf[lax.rem(at.dp + j, ndp)].astype(F32)
        osum[...] = rows.astype(BF16)
        for b in range(ndp):
            owner = lax.rem(at.c * ndp + b, n)

            @pl.when(owner != at.c)
            def _():
                out_rows(b, owner).start()

            @pl.when(owner == at.c)
            def _():
                wo_out[...] = osum[b]

    d1.wait_recv()
    total(wd_out, wd_ref[at.dp].astype(F32), lambda s: dbuf[s])

    @pl.when(heads_of != at.c)
    def _():
        out_rows(slot, at.c).wait_recv()

    w2.wait_recv()
    v2.wait_recv()
    for part in (w1, v1, d1, w2, v2):
        part.wait_send()

    @pl.when(at.dp != first)
    def _():
        o1.copy(first, at.dp).wait_send()

    @pl.when(at.dp == first)
    def _():
        for b in range(ndp):
            owner = lax.rem(at.c * ndp + b, n)

            @pl.when(owner != at.c)
            def _():
                out_rows(b, owner).wait_send()


def grads_all(ndp, n, wp, wd, wo, v):
    dma = pltpu.SemaphoreType.DMA
    vmem = pl.BlockSpec(memory_space=pltpu.VMEM)
    return pl.pallas_call(
        partial(grads_kernel, ndp, n),
        out_shape=(
            jax.ShapeDtypeStruct(wp.shape[1:], BF16),
            jax.ShapeDtypeStruct(wd.shape[1:], F32),
            jax.ShapeDtypeStruct(wo.shape[1:], BF16),
            jax.ShapeDtypeStruct((n,) + v.shape, F32),
        ),
        in_specs=[vmem] * 4,
        out_specs=[vmem] * 4,
        scratch_shapes=[
            pltpu.VMEM(wp.shape, BF16),
            pltpu.VMEM(wp.shape[1:], F32),
            pltpu.VMEM(wd.shape, BF16),
            pltpu.VMEM((ndp,) + wo.shape, BF16),
            pltpu.VMEM(wo.shape, BF16),
            pltpu.VMEM((ndp,) + v.shape, F32),
            pltpu.VMEM(v.shape, F32),
            dma((ndp,)), dma((ndp,)), dma((ndp,)), dma((ndp,)), dma((ndp,)), dma((ndp,)), dma((ndp,)), dma((ndp,)),
            dma((n,)), dma((n,)), dma((n,)), dma((n,)), dma((ndp,)), dma,
            dma((1,)),
        ],
        compiler_params=pltpu.CompilerParams(collective_id=3, has_side_effects=True, vmem_limit_bytes=48 * MIB),
    )(wp, wd, wo, v)


def dot(a, b, dims=((1,), (0,))):
    return lax.dot_general(a, b, (dims, ((), ())), preferred_element_type=F32)


NT = ((1,), (1,))
TN = ((0,), (0,))


class SeqGather:
    def __init__(self, at, dst, tok, first, size, sends, recvs):
        self.at, self.dst, self.tok, self.first, self.size, self.sends, self.recvs = at, dst, tok, first, size, sends, recvs

    def rows(self, c):
        return self.dst.at[pl.ds(pl.multiple_of(c * self.tok + self.first, self.size), self.size)]

    def copy(self, block, slot, c):
        return remote(self.rows(block), self.rows(block), self.sends.at[slot], self.recvs.at[block], self.at.dp, c)

    def up_slot(self, k):
        return k

    def down_slot(self, k):
        return self.at.nz - 1 + k

    def side_slot(self, k):
        return 2 * (self.at.nz - 1) + k

    def start(self):
        at = self.at

        @pl.when(at.has_up)
        def _():
            self.copy(at.c, self.up_slot(0), at.c + 2).start()

        @pl.when(at.has_down)
        def _():
            self.copy(at.c, self.down_slot(0), at.c - 2).start()

        self.copy(at.c, self.side_slot(0), at.sib).start()

    def step(self, k):
        at = self.at
        low, high = at.c - 2 * k, at.c + 2 * k

        @pl.when(at.z >= k)
        def _():
            self.copy(low, 0, at.c).wait_recv()

            @pl.when(at.has_up)
            def _():
                self.copy(low, self.up_slot(k), at.c + 2).start()

            self.copy(low, self.side_slot(k), at.sib).start()

        @pl.when(at.z + k < at.nz)
        def _():
            self.copy(high, 0, at.c).wait_recv()

            @pl.when(at.has_down)
            def _():
                self.copy(high, self.down_slot(k), at.c - 2).start()

            self.copy(high, self.side_slot(at.z + k), at.sib).start()

    def land(self):
        for z in range(self.at.nz):
            self.land_chip(z)

    def land_chip(self, z):
        self.copy(2 * z + 1 - self.at.core, 0, self.at.c).wait_recv()


    def drain(self):
        at = self.at
        for k in range(at.nz):
            self.copy(at.c, self.side_slot(k), at.c).wait_send()
            if k == at.nz - 1:
                continue

            @pl.when((at.z >= k) & at.has_up)
            def _():
                self.copy(at.c, self.up_slot(k), at.c).wait_send()

            @pl.when((at.z + k < at.nz) & at.has_down)
            def _():
                self.copy(at.c, self.down_slot(k), at.c).wait_send()


class Pieces:
    def __init__(self, pieces):
        self.pieces = pieces

    def each(self, name, *args):
        for piece in self.pieces:
            getattr(piece, name)(*args)

    def start(self):
        self.each("start")

    def step(self, k):
        self.each("step", k)

    def land(self):
        self.each("land")

    def drain(self):
        self.each("drain")

    def take(self, k, body):
        at = self.pieces[0].at

        def one(t, carry):
            z = at.z - k + 2 * k * t

            @pl.when((z >= 0) & (z < at.nz))
            def _():
                self.each("land_chip", z)
                body(z)

            return carry

        lax.fori_loop(0, 2 if k else 1, one, 0)


class SeqScatter:
    def __init__(self, at, part, sib_buf, in_buf, tok, first, size, sems):
        self.at, self.part, self.tok, self.first, self.size = at, part, tok, first, size
        self.sib_buf, self.in_buf = sib_buf.at[:, pl.ds(first, size)], in_buf.at[:, pl.ds(first, size)]
        self.s_send, self.s_recv, self.up_send, self.up_recv, self.dn_send, self.dn_recv = sems

    def rows(self, c):
        return pl.ds(pl.multiple_of(c * self.tok + self.first, self.size), self.size)

    def cross(self, z):
        at = self.at
        src = self.part.at[self.rows(2 * z + 1 - at.core)]
        return remote(src, self.sib_buf.at[z], self.s_send.at[z], self.s_recv.at[z], at.dp, at.sib)

    def up(self, z):
        at = self.at
        return remote(self.sib_buf.at[z], self.in_buf.at[z], self.up_send.at[z], self.up_recv.at[z], at.dp, at.c + 2)

    def down(self, z, sender=None):
        at = self.at
        slot = jnp.where(z == (at.z - 1 if sender is None else sender - 1), at.nz, z)
        return remote(self.sib_buf.at[z], self.in_buf.at[slot], self.dn_send.at[z], self.dn_recv.at[z], at.dp, at.c - 2)

    def chip_sum(self, z):
        mine = self.part[self.rows(2 * z + self.at.core)].astype(F32)
        return mine + self.sib_buf[z].astype(F32)

    def step(self, t):
        self.step_up(t)
        self.step_down(t)

    def step_up(self, t):
        self.lead_up(t)
        self.follow_up(t)

    def lead_up(self, t):
        at = self.at
        z = at.nz - 1 - t

        @pl.when(at.z == 0)
        def _():
            self.cross(z).wait_recv()
            self.sib_buf[z] = self.chip_sum(z).astype(BF16)
            self.up(z).start()

    def follow_up(self, t):
        at = self.at
        z = at.nz - 1 - t + at.z

        @pl.when((at.z <= t) & at.has_down)
        def _():
            self.cross(z).wait_recv()
            self.up(z).wait_recv()
            self.sib_buf[z] = (self.chip_sum(z) + self.in_buf[z].astype(F32)).astype(BF16)
            self.up(z).start()

    def step_down(self, t):
        self.lead_down(t)
        self.follow_down(t)

    def lead_down(self, t):
        at = self.at

        @pl.when(at.z == at.nz - 1)
        def _():
            self.cross(t).wait_recv()
            self.sib_buf[t] = self.chip_sum(t).astype(BF16)
            self.down(t).start()

    def follow_down(self, t):
        at = self.at
        z = t - (at.nz - 1 - at.z)

        @pl.when((z >= 0) & at.has_up)
        def _():
            self.cross(z).wait_recv()
            self.down(z, at.z + 1).wait_recv()
            self.sib_buf[z] = (self.chip_sum(z) + self.in_buf[z].astype(F32)).astype(BF16)
            self.down(z).start()

    def total(self, acc):
        at = self.at
        acc = acc.at[pl.ds(self.first, self.size)]
        self.cross(at.z).wait_recv()
        acc[...] = self.chip_sum(at.z)

        @pl.when(at.has_down)
        def _():
            self.up(at.z).wait_recv()
            acc[...] += self.in_buf[at.z].astype(F32)

        @pl.when(at.has_up)
        def _():
            self.down(at.z, at.z + 1).wait_recv()
            acc[...] += self.in_buf[at.nz].astype(F32)

    def drain(self):
        at = self.at
        for z in range(at.nz):
            self.cross(z).wait_send()

            @pl.when(z > at.z)
            def _():
                self.up(z).wait_send()

            @pl.when(z < at.z)
            def _():
                self.down(z).wait_send()


class ScatterPieces(Pieces):
    def cross(self, z):
        return Pieces([piece.cross(z) for piece in self.pieces])

    def lead_up(self, t):
        self.each("lead_up", t)

    def lead_down(self, t):
        self.each("lead_down", t)

    def follow(self, t):
        for piece in self.pieces:
            piece.follow_up(t)
            piece.follow_down(t)

    def step(self, t):
        for piece in self.pieces:
            piece.step_up(t)
            piece.step_down(t)

    def total(self, acc):
        self.each("total", acc)


class PlaneGather:
    def __init__(self, at, part, sends, recvs):
        self.at, self.part, self.sends, self.recvs = at, part, sends, recvs

    def copy(self, p, h, i, to):
        return remote(self.part(p, h), self.part(p, h), self.sends.at[i], self.recvs.at[i], to, self.at.c)

    def start(self):
        at = self.at
        for h in (0, 1):
            self.copy(at.dp, h, h, at.px).start()
            self.copy(at.dp, 1 - h, 3 - h, at.py).start()

    def forward(self):
        at = self.at
        self.copy(at.px, 0, 0, at.px).wait_recv()
        self.copy(at.px, 0, 4, at.py).start()
        self.copy(at.py, 1, 3, at.py).wait_recv()
        self.copy(at.py, 1, 5, at.px).start()

    def land(self):
        at = self.at
        self.copy(at.px, 1, 1, at.px).wait_recv()
        self.copy(at.py, 0, 2, at.py).wait_recv()
        self.copy(at.diag, 0, 4, at.py).wait_recv()
        self.copy(at.diag, 1, 5, at.px).wait_recv()

    def drain(self):
        at = self.at
        for h in (0, 1):
            self.copy(at.dp, h, h, at.px).wait_send()
            self.copy(at.dp, h, 2 + h, at.py).wait_send()
        self.copy(at.px, 0, 4, at.py).wait_send()
        self.copy(at.py, 1, 5, at.px).wait_send()


class PlaneReduce:
    def __init__(self, at, part, via_x, via_y, from_x, from_y, sends, recvs):
        self.at, self.part, self.sends, self.recvs = at, part, sends, recvs
        self.via_x, self.via_y, self.from_x, self.from_y = via_x, via_y, from_x, from_y

    def copy(self, i):
        at = self.at
        src, dst, to = (
            (lambda: self.part(at.diag, 1), self.via_x, at.px),
            (lambda: self.part(at.diag, 0), self.via_y, at.py),
            (lambda: self.part(at.px, 1), self.from_x(1), at.px),
            (lambda: self.part(at.py, 0), self.from_y(0), at.py),
            (lambda: self.part(at.py, 1), self.from_y(1), at.py),
            (lambda: self.part(at.px, 0), self.from_x(0), at.px),
        )[i]
        return remote(src(), dst, self.sends.at[i], self.recvs.at[i], to, at.c)

    def start(self):
        for i in range(4):
            self.copy(i).start()

    def combine(self):
        at = self.at
        for i, via, p, h in ((0, self.via_x, at.py, 1), (1, self.via_y, at.px, 0)):
            self.copy(i).wait_recv()
            ref = self.part(p, h)
            ref[...] = (ref[...].astype(F32) + via[...].astype(F32)).astype(BF16)
            self.copy(4 + i).start()

    def total(self, h):
        for i in ((5, 3), (2, 4))[h]:
            self.copy(i).wait_recv()
        return self.part(self.at.dp, h)[...].astype(F32) + self.from_x(h)[...].astype(F32) + self.from_y(h)[...].astype(F32)

    def drain(self):
        for i in range(6):
            self.copy(i).wait_send()


def blocks(count, body, hooks=None):
    hooks = hooks or {}

    def one(i, carry):
        body(i)
        for index, events in hooks.items():

            @pl.when(i == index)
            def _():
                for event in events:
                    event()

        return carry

    lax.fori_loop(0, count, one, 0)


def fused_kernel(ndp, n, dims, *refs):
    mb, tok, width, seq, heads, rows_w, rows_d = dims
    nz, block, every = n // 2, 2 * tok, ndp * n
    fu = ndp * rows_d
    (tok_ref, cot_ref, rq_ref, ru_ref, wd_ref, wo_ref, vec_ref, seg_ref, cos_ref, sin_ref) = refs[:10]
    (mixed_out, grad_out, qkv_out, up_out, dwd_out, dwo_out, vec_out) = refs[10:17]
    (xs, gs, ws, wdo, vecs, segs, seg_col, cos_t, sin_t, g1, s1, g2, s2, bo, bq, bu, qkv, hid, gp, stat, ctx, part, ep, dctx, dqkv,
     dk, dv, acc_gain, acc_bu, acc_bq, m_sib, m_in, t_sib, t_in, dwq, dwu, dwdo, q_via, q_from, u_via, u_from, d_via, d_from, vsum, vin, wq_st, wu_st,
     own, dwo_st, vsum_all, v_st, seg_i, wp_st, wq_rx, wu_rx, v_rx, h1_all, h2_all) = refs[17:75]
    probs = refs[75 : 75 + nz]
    (x_s, x_r, c_s, c_r, w1s, w1r, w2s, w2r, v1s, v1r, v2s, v2r, d_s, d_r, o1s, o1r,
     ms_s, ms_r, mu_s, mu_r, md_s, md_r, ts_s, ts_r, tu_s, tu_r, td_s, td_r,
     gq1s, gq1r, gq2s, gq2r, gu1s, gu1r, gu2s, gu2r, gd_s, gd_r, go2s, go2r, gv1s, gv1r, gv2s, gv2r, local) = refs[75 + nz :]
    at = Place(ndp, n)
    at.barrier(True, True, True)
    raw_q, raw_u, raw_t, raw_c = qkv_out, up_out, mixed_out, grad_out
    own_rows = pl.ds(pl.multiple_of(at.c * tok, tok), tok)

    cols = Exchange(at, "ctx", lambda p: wp_st.at[p], lambda s: ws.at[at.dp, s], w1s, w1r)
    vec1 = Exchange(at, "ctx", lambda p: vec_ref, lambda s: vecs.at[at.dp, s], v1s, v1r)
    plane_w = PlaneGather(at, lambda p, h: ws.at[p, pl.ds(h * (n // 2), n // 2)], w2s, w2r)
    plane_v = Exchange(at, "dp", lambda p: vecs.at[at.dp], lambda s: vecs.at[s], v2s, v2r)
    rows_do = rows_d + rows_w
    plane_d = PlaneGather(at, lambda p, h: wdo.at[p, pl.ds(h * (rows_do // 2), rows_do // 2)], d_s, d_r)
    def gather(dst, sends, recvs, counts, s):
        size, first = tok // counts[s], sum(counts[:s])
        return Pieces([SeqGather(at, dst.at[s], tok, h * size, size, sends.at[first + h], recvs.at[first + h]) for h in range(counts[s])])

    x_ag = [gather(xs, x_s, x_r, CUT_TOKENS, s) for s in range(mb)]
    c_ag = [gather(gs, c_s, c_r, CUT_COTANGENT, s) for s in range(mb)]
    copies = [
        pltpu.make_async_copy(rq_ref, raw_q, local.at[0]),
        pltpu.make_async_copy(ru_ref, raw_u, local.at[9]),
        pltpu.make_async_copy(vec_ref, vecs.at[at.dp, at.c], local.at[1]),
        pltpu.make_async_copy(wd_ref, wdo.at[at.dp, pl.ds(0, rows_d)], local.at[2]),
        pltpu.make_async_copy(seg_ref, seg_i, local.at[3]),
        pltpu.make_async_copy(cos_ref, cos_t, local.at[4]),
        pltpu.make_async_copy(sin_ref, sin_t, local.at[5]),
        pltpu.make_async_copy(tok_ref, raw_t, local.at[6]),
        pltpu.make_async_copy(cot_ref, raw_c, local.at[7]),
    ]
    out_rows = remote(wo_ref, wdo.at[at.rows_dp, pl.ds(rows_d, rows_w)], o1s, o1r, at.rows_dp, at.rows_c)
    out_mine = remote(wo_ref, wdo.at[at.dp, pl.ds(rows_d, rows_w)], o1s, o1r, at.rows_dp, at.rows_c)
    own_out = pltpu.make_async_copy(wo_ref, wdo.at[at.dp, pl.ds(rows_d, rows_w)], local.at[8])
    for copy in copies:
        copy.start()
    vec1.start()

    @pl.when(at.moves)
    def _():
        out_rows.start()

    @pl.when(jnp.logical_not(at.moves))
    def _():
        own_out.start()

    copies[0].wait()
    copies[1].wait()
    for p in range(n):
        for part_ in range(3):
            wp_st[p, :, part_ * 128 : (part_ + 1) * 128] = raw_q[:, part_ * width + p * 128 : part_ * width + (p + 1) * 128]
        for d in range(ndp):
            wp_st[p, :, 384 + d * rows_d : 384 + (d + 1) * rows_d] = raw_u[:, (d * n + p) * rows_d : (d * n + p + 1) * rows_d]
    cols.start()
    ws[at.dp, at.c] = wp_st[at.c]
    for copy in copies[2:]:
        copy.wait()
    for s in range(mb):
        xs[s, own_rows] = raw_t[:, s, :]
        gs[s, own_rows] = raw_c[:, s, :]
    segs[...] = jnp.zeros_like(segs)
    segs[0:mb] = seg_i[...]
    cols.wait_recv()
    plane_w.start()
    x_ag[0].start()
    vec1.wait_recv()
    plane_v.start()
    x_ag[0].step(1)
    plane_w.forward()
    x_ag[0].step(2)
    c_ag[0].start()

    @pl.when(at.moves)
    def _():
        out_mine.wait_recv()

    @pl.when(jnp.logical_not(at.moves))
    def _():
        own_out.wait()

    plane_d.start()
    plane_v.wait_recv()

    lane = lax.broadcasted_iota(jnp.int32, (16, 128), 1)
    per = 128 // rows_w
    for q in range(width // 128):
        piece = vecs[(per * q) // n, (per * q) % n]
        for u in range(1, per):
            d = per * q + u
            piece = jnp.where(lane >= u * rows_w, vecs[d // n, d % n], piece)
        span = pl.ds(q * 128, 128)
        bo[:, span] = piece[3:4] + piece[8:9]
        for ref, r in ((g1, 9), (s1, 10), (g2, 11), (s2, 12)):
            ref[:, span] = piece[r : r + 1]
    lane1 = lax.broadcasted_iota(jnp.int32, (1, 128), 1)
    for d in range(ndp):
        rows = vecs[d, at.c]
        piece = rows[4:5]
        for u in range(1, per):
            piece = jnp.where(lane1 >= u * rows_w, rows[4 + u : 5 + u], piece)
        bu[:, pl.ds(d * 128, 128)] = piece
    for p in range(3):
        piece = None
        for u in range(per):
            t = (p * width + at.c * 128) // rows_w + u
            d, r = t // 3, lax.rem(t, 3)
            rows = vecs[d // n, lax.rem(d, n)]
            row = jnp.where(r == 0, rows[0:1], jnp.where(r == 1, rows[1:2], rows[2:3]))
            piece = row if piece is None else jnp.where(lane1 >= u * rows_w, row, piece)
        bq[:, pl.ds(p * 128, 128)] = piece
    seg_t = jnp.transpose(segs[...])
    seg_col[...] = jnp.where(seg_t == 0.0, -1.0, seg_t)

    lanes = lax.broadcasted_iota(jnp.int32, (1, 128), 1)
    in_head = [(lanes >= h * HEAD) & (lanes < (h + 1) * HEAD) for h in range(heads)]
    low_half = (lanes & (HEAD - 1)) < ROT // 2
    w_q = lambda: ws[:, :, :, :384].reshape(width, 384)
    w_u = lambda: ws[:, :, :, 384:].reshape(width, fu)
    w_d = lambda: wdo[:, 0:rows_d].reshape(fu, width)
    w_o = lambda: wdo[:, rows_d:].reshape(128, width)

    def rows_of(i):
        return pl.ds(pl.multiple_of(i * block, block), block)

    def turn(u, rows, sign):
        turned = jnp.where(low_half, pltpu.roll(u, 128 - ROT // 2, 1), pltpu.roll(u, ROT // 2, 1))
        if sign > 0:
            return u * cos_t[rows] + turned * sin_t[rows]
        return u * cos_t[rows] - turned * sin_t[rows]

    def normed_of(s, rows):
        return (xs[s, rows].astype(F32) - stat[s, rows, 0:1]) * stat[s, rows, 1:2]

    def forward_one(s):
        def body(i):
            rows = rows_of(i)
            x = xs[s, rows].astype(F32)
            mean = jnp.mean(x, axis=-1, keepdims=True)
            cen = x - mean
            rstd = lax.rsqrt(jnp.mean(cen * cen, axis=-1, keepdims=True) + 1e-05)
            stat[s, rows, 0:1] = mean
            stat[s, rows, 1:2] = rstd
            nrm = cen * rstd
            h1 = (nrm * g1[...] + s1[...]).astype(BF16)
            h1_all[s, rows] = h1
            joined = dot(h1, w_q()) + bq[...]
            qkv[s, rows, 0:128] = (turn(joined[:, 0:128], rows, 1).astype(BF16).astype(F32) * (HEAD ** (-0.5))).astype(BF16)
            qkv[s, rows, 128:256] = turn(joined[:, 128:256], rows, 1).astype(BF16)
            qkv[s, rows, 256:384] = joined[:, 256:384].astype(BF16)
            h2 = (nrm * g2[...] + s2[...]).astype(BF16)
            h2_all[rows] = h2
            act = dot(h2, w_u()) + bu[...]
            cdf = 0.5 + 0.5 * lax.erf(act * (0.5 ** 0.5))
            hid[s, rows] = (act * cdf).astype(BF16)
            gp[rows] = (cdf + act * (jnp.exp(-0.5 * act * act) * 0.3989422804014327)).astype(BF16)

        return body

    def attend(s, i):
        rows = pl.ds(i * block, block)
        keys = (i + 1) * block
        q_pos = lax.broadcasted_iota(jnp.int32, (block, keys), 0) + i * block
        k_pos = lax.broadcasted_iota(jnp.int32, (block, keys), 1)
        same = segs[s : s + 1, 0:keys] == seg_col[rows, s : s + 1]
        allow = (same & (k_pos <= q_pos)) | (k_pos == q_pos)
        q, k, v = qkv[s, rows, 0:128], qkv[s, 0:keys, 128:256], qkv[s, 0:keys, 256:384]
        out = None
        for h in range(heads):
            scores = dot(jnp.where(in_head[h], q, jnp.zeros_like(q)), k, NT)
            scores = jnp.where(allow, scores, -1e30)
            e = jnp.exp(scores - jnp.max(scores, axis=-1, keepdims=True))
            p = (e * (1.0 / jnp.sum(e, axis=-1, keepdims=True))).astype(BF16)
            probs[i][h] = p
            o = dot(p, v)
            out = o if out is None else jnp.where(in_head[h], o, out)
        ctx[s, rows] = out.astype(BF16)

    def project(s):
        def body(i):
            rows = rows_of(i)
            both = dot(ctx[s, rows], w_o()) + dot(hid[s, rows], w_d())
            part[s, rows] = both.astype(BF16)

        return body

    def fold(ref, row, value):
        count, cols_ = value.shape
        ref[row, :, 0:cols_] += jnp.sum(value.reshape(count // 8, 8, cols_), axis=0)

    def backward_ffn(s):
        def body(i):
            rows = rows_of(i)
            g = gs[s, rows]
            dctx[s, rows] = dot(g, w_o(), NT).astype(BF16)
            d_act = (dot(g, w_d(), NT) * gp[rows].astype(F32)).astype(BF16)
            gp[rows] = d_act
            fold(acc_gain, 4, g.astype(F32))
            fold(acc_bu, 0, d_act.astype(F32))
            d_h = dot(d_act, w_u(), NT)
            fold(acc_gain, 2, d_h * normed_of(s, rows))
            fold(acc_gain, 3, d_h)
            ep[s, rows] = (d_h * g2[...]).astype(BF16)

        return body

    def attend_back(s, i):
        rows = pl.ds(i * block, block)
        keys = (i + 1) * block
        span = pl.ds(0, keys)
        q, k, v = qkv[s, rows, 0:128], qkv[s, span, 128:256], qkv[s, span, 256:384]
        d_c = dctx[s, rows]
        zero = jnp.zeros_like(q)
        d_q = None
        for h in range(heads):
            p = probs[i][h]
            d_h = jnp.where(in_head[h], d_c, zero)
            d_p = dot(d_h, v, NT)
            p_f = p.astype(F32)
            delta = jnp.sum(p_f * d_p, axis=-1, keepdims=True)
            d_s = (p_f * (d_p - delta)).astype(BF16)
            o = dot(d_s, k)
            d_q = o if d_q is None else jnp.where(in_head[h], o, d_q)
            d_k = dot(jnp.where(in_head[h], q, zero), d_s, TN)
            d_v = dot(d_h, p, TN)
            if i == nz - 1 and h == 0:
                dk[...] = d_k
                dv[...] = d_v
            else:
                dk[:, span] += d_k
                dv[:, span] += d_v
        d_q = turn(d_q, rows, -1) * (HEAD ** (-0.5))
        d_k, d_v = jnp.transpose(dk[:, rows]), jnp.transpose(dv[:, rows])
        d_all = jnp.concatenate([d_q, turn(d_k, rows, -1), d_v], axis=1).astype(BF16)
        dqkv[s, rows] = d_all
        fold(acc_bq, 0, d_all.astype(F32))
        d_n = dot(d_all, w_q(), NT)
        fold(acc_gain, 0, d_n * normed_of(s, rows))
        fold(acc_gain, 1, d_n)
        ep[s, rows] = (d_n * g1[...] + ep[s, rows].astype(F32)).astype(BF16)

    def put(ref, rows, s, total):
        if s:
            total = total + ref[rows].astype(F32).reshape(total.shape)
        ref[rows] = total.astype(BF16).reshape(ref[rows].shape)

    def weight_cols(s, out, left, right):
        def body(kt):
            feat = pl.ds(pl.multiple_of(kt * 256, 256), 256)
            put(out, feat, s, dot(left[:, feat], right[...], TN))

        return body

    acc_gain[...] = jnp.zeros_like(acc_gain)
    acc_bu[...] = jnp.zeros_like(acc_bu)
    acc_bq[...] = jnp.zeros_like(acc_bq)

    def scatter(part_, sib_, in_, sems_, counts, s):
        size, first = tok // counts[s], sum(counts[:s])
        return ScatterPieces([SeqScatter(at, part_.at[s], sib_.at[s], in_.at[s], tok, h * size, size, [r.at[first + h] for r in sems_]) for h in range(counts[s])])

    m_rs = [scatter(part, m_sib, m_in, (ms_s, ms_r, mu_s, mu_r, md_s, md_r), CUT_MIXED, s) for s in range(mb)]
    t_rs = [scatter(ep, t_sib, t_in, (ts_s, ts_r, tu_s, tu_r, td_s, td_r), CUT_GRAD, s) for s in range(mb)]
    rows_p = n * rows_w

    def col_halves(ref):
        return lambda p, h: ref.at[pl.ds(pl.multiple_of(p * rows_p + h * (rows_p // 2), rows_p // 2), rows_p // 2)]

    def halves(ref, i, size):
        return lambda h: ref.at[i, pl.ds(h * size, size)]

    half = rows_p // 2
    wq1 = PlaneReduce(at, col_halves(dwq), q_via.at[0], q_via.at[1], halves(q_from, 0, half), halves(q_from, 1, half), gq1s, gq1r)
    wu1 = PlaneReduce(at, col_halves(dwu), u_via.at[0], u_via.at[1], halves(u_from, 0, half), halves(u_from, 1, half), gu1s, gu1r)
    half_do = rows_do // 2
    wd1 = PlaneReduce(at, lambda p, h: dwdo.at[p, pl.ds(h * half_do, half_do)], d_via.at[0], d_via.at[1],
                      halves(d_from, 0, half_do), halves(d_from, 1, half_do), gd_s, gd_r)
    gv1 = Exchange(at, "dp", lambda p: vsum, lambda s: vin.at[s], gv1s, gv1r)
    wq2 = Exchange(at, "ctx", lambda p: wq_st.at[p], lambda s: wq_rx.at[s], gq2s, gq2r)
    wu2 = Exchange(at, "ctx", lambda p: wu_st.at[p], lambda s: wu_rx.at[s], gu2s, gu2r)
    gv2 = Exchange(at, "ctx", lambda p: v_st.at[p], lambda s: v_rx.at[s], gv2s, gv2r)
    out_back = remote(dwo_st, dwo_out, go2s, go2r, at.from_dp, at.from_c)

    def columns_on(first_hop, second_hop, stage, out):
        for h in (0, 1):
            total = first_hop.total(h).astype(BF16)
            stage[pl.ds(h * (n // 2), n // 2)] = total.reshape((n // 2,) + stage.shape[1:])
        second_hop.start()
        out[at.c] = stage[at.c]

    def down_out():
        low, high = wd1.total(0), wd1.total(1)
        dwd_out[pl.ds(0, half_do)] = low
        dwd_out[pl.ds(half_do, rows_d - half_do)] = high[0 : rows_d - half_do]
        rows = high[rows_d - half_do :].astype(BF16)

        @pl.when(at.moves)
        def _():
            dwo_st[...] = rows
            out_back.start()

        @pl.when(jnp.logical_not(at.moves))
        def _():
            dwo_out[...] = rows

    def vectors_out():
        mine = v_rx[at.c]
        index = at.dp * n + at.c
        start = index * (3 * rows_w)
        shift, tile = lax.rem(start, 128), start // 128

        def tile_of(t):
            rows = v_rx[lax.rem(t, n)]
            third = t // n
            return jnp.where(third == 0, rows[8:9], jnp.where(third == 1, rows[9:10], rows[10:11]))

        low, high = tile_of(tile), tile_of(jnp.minimum(tile + 1, 3 * n - 1))
        both = low
        for u in range(1, 128 // rows_w):
            off = u * rows_w
            moved = jnp.where(lane1 < 128 - off, pltpu.roll(low, 128 - off, 1), pltpu.roll(high, 128 - off, 1))
            both = jnp.where(shift == off, moved, both)
        place = lax.rem(index * rows_w, 128)
        base = v_rx[0, 0:8]
        for p in range(1, n):
            base = base + v_rx[p, 0:8]
        row = lax.broadcasted_iota(jnp.int32, (8, 128), 0)
        base = jnp.where(row < 6, base, mine[0:8])
        out = base
        for u in range(1, 128 // rows_w):
            out = jnp.where(place == u * rows_w, pltpu.roll(base, 128 - u * rows_w, 1), out)
        vec_out[...] = out
        vec_out[0:1] = both
        vec_out[1:2] = mine[11:12]
        vec_out[7:8] = out[6:7]

    def starts(rs, zs):
        def event():
            for z in zs:
                rs.cross(z).start()

        return event

    def finish_mixed(s):
        m_rs[s].total(own)
        mixed_out[:, s, :] = (xs[s, own_rows].astype(F32) + own[...] + bo[...]).astype(BF16)

    def finish_grad(s):
        t_rs[s].total(own)
        e = own[...]
        nrm = normed_of(s, own_rows)
        inner = e - jnp.mean(e, axis=-1, keepdims=True) - nrm * jnp.mean(e * nrm, axis=-1, keepdims=True)
        grad_out[:, s, :] = (gs[s, own_rows].astype(F32) + stat[s, own_rows, 1:2] * inner).astype(BF16)

    def down_rows(s):
        def body(kt):
            feat = pl.ds(pl.multiple_of(kt * 256, 256), 256)
            total = dot(hid[s, :, feat], gs[s], TN).reshape(256 // rows_d, rows_d, width)
            mine = dwdo.at[pl.ds(kt * (256 // rows_d), 256 // rows_d), pl.ds(0, rows_d)]
            if s:
                total = total + mine[...].astype(F32)
            mine[...] = total.astype(BF16)

        return body

    def out_grad(s):
        total = dot(ctx[s], gs[s], TN).reshape(ndp, rows_w, width)
        mine = dwdo.at[:, pl.ds(rows_d, rows_w)]
        if s:
            total = total + mine[...].astype(F32)
        mine[...] = total.astype(BF16)

    x_ag[0].step(3)
    plane_w.land()
    x_ag[0].land()
    blocks(nz, forward_one(0), {3: [lambda: c_ag[0].step(1), x_ag[1].start]})
    plane_d.forward()
    for i in range(nz):
        attend(0, i)
    c_ag[0].step(2)
    plane_d.land()
    blocks(nz, project(0))
    starts(m_rs[0], range(nz))()
    m_rs[0].step(0)
    back = backward_ffn(0)
    c_ag[0].take(0, back)
    x_ag[1].step(1)
    c_ag[1].start()
    c_ag[0].take(1, back)
    c_ag[0].take(2, back)
    c_ag[0].step(3)
    c_ag[0].take(3, back)
    m_rs[0].step(1)
    for i in reversed(range(nz)):
        attend_back(0, i)
        t_rs[0].cross(i).start()
        if i == 3:
            x_ag[1].step(2)
        if i == 1:
            m_rs[0].step(2)
    t_rs[0].step(0)
    blocks(width // 256, weight_cols(0, dwu, h2_all, gp))
    ahead = forward_one(1)
    x_ag[1].take(0, ahead)
    c_ag[1].step(1)
    x_ag[1].take(1, ahead)
    x_ag[1].take(2, ahead)
    x_ag[1].step(3)
    x_ag[1].take(3, ahead)
    t_rs[0].step(1)
    for i in range(nz):
        attend(1, i)
        if i == 2:
            c_ag[1].step(2)
    blocks(nz, project(1))
    starts(m_rs[1], range(nz))()
    m_rs[1].step(0)
    t_rs[0].step(2)
    blocks(width // 256, weight_cols(0, dwq, h1_all.at[0], dqkv.at[0]))
    blocks(fu // 256, down_rows(0))
    out_grad(0)
    back = backward_ffn(1)
    c_ag[1].take(0, back)
    c_ag[1].take(1, back)
    m_rs[1].step(1)
    c_ag[1].take(2, back)
    c_ag[1].step(3)
    c_ag[1].take(3, back)
    blocks(width // 256, weight_cols(1, dwu, h2_all, gp))
    wu1.start()
    for i in reversed(range(nz)):
        attend_back(1, i)
        t_rs[1].cross(i).start()
        if i < nz - 1:
            t_rs[1].lead_up(nz - 2 - i)
        if i == 1:
            wu1.combine()
            m_rs[1].step(2)
    for t in range(nz - 1):
        t_rs[1].lead_down(t)
    blocks(width // 256, weight_cols(1, dwq, h1_all.at[1], dqkv.at[1]))
    wq1.start()
    vsum[...] = jnp.zeros_like(vsum)
    vsum[0:1, 0:384] = jnp.sum(acc_bq[0], axis=0, keepdims=True)
    vsum[1:2, 0:fu] = jnp.sum(acc_bu[0], axis=0, keepdims=True)
    for r in range(5):
        vsum[2 + r : 3 + r] = jnp.sum(acc_gain[r], axis=0, keepdims=True)
    gv1.start()
    columns_on(wu1, wu2, wu_st, wu_rx)
    blocks(fu // 256, down_rows(1))
    out_grad(1)
    t_rs[1].follow(1)
    wq1.combine()
    wd1.start()
    finish_mixed(0)
    finish_mixed(1)
    finish_grad(0)
    columns_on(wq1, wq2, wq_st, wq_rx)
    t_rs[1].follow(2)
    gv1.wait_recv()
    total = vsum[...]
    for j in range(1, ndp):
        total = total + vin[lax.rem(at.dp + j, ndp)]
    vsum_all[...] = total
    for p in range(n):
        v_st[p, 0:8] = vsum_all[:, pl.ds(pl.multiple_of((at.dp * n + p) * rows_w // 128 * 128, 128), 128)]
        for r in range(3):
            v_st[p, 8 + r : 9 + r] = total[0:1, r * 128 : (r + 1) * 128]
        v_st[p, 11:12] = vsum_all[1:2, pl.ds(pl.multiple_of(at.dp * rows_d, 128), 128)]
        v_st[p, 12:16] = jnp.zeros((4, 128), F32)
    gv2.start()
    v_rx[at.c] = v_st[at.c]
    wd1.combine()
    finish_grad(1)
    down_out()

    @pl.when(at.moves)
    def _():
        out_rows.wait_send()
        out_back.wait()

    wu2.wait_recv()
    for p in range(n):
        for d in range(ndp):
            up_out[:, (d * n + p) * rows_d : (d * n + p + 1) * rows_d] = wu_rx[p, :, d * rows_d : (d + 1) * rows_d]
    gv2.wait_recv()
    vectors_out()
    wq2.wait_recv()
    for p in range(n):
        for part_ in range(3):
            qkv_out[:, part_ * width + p * 128 : part_ * width + (p + 1) * 128] = wq_rx[p, :, part_ * 128 : (part_ + 1) * 128]
    for part_ in (cols, vec1, plane_v, gv1, wq2, wu2, gv2):
        part_.wait_send()
    for part_ in (plane_w, plane_d, wq1, wu1, wd1):
        part_.drain()
    for s in range(mb):
        x_ag[s].drain()
        c_ag[s].drain()
        m_rs[s].drain()
        t_rs[s].drain()


def fused_layer(ndp, n, dims, tok, cot, rq, ru, wd, wo, vec, seg, cosine, sine):
    mb, tk, width, seq, heads, rows_w, rows_d = dims
    nz, block, fu = n // 2, 2 * tk, ndp * rows_d
    rows_do, rows_p = rows_d + rows_w, n * rows_w
    dma = pltpu.SemaphoreType.DMA
    vm = pltpu.VMEM
    vmem = pl.BlockSpec(memory_space=pltpu.VMEM)
    slots = gather_slots(nz)
    scratch = [
        vm((mb, seq, width), BF16), vm((mb, seq, width), BF16),
        vm((ndp, n, rows_w, 384 + fu), BF16), vm((ndp, rows_d + rows_w, width), BF16),
        vm((ndp, n, 16, 128), F32), vm((8, seq), F32), vm((seq, 8), F32), vm((seq, 128), F32), vm((seq, 128), F32),
        vm((1, width), F32), vm((1, width), F32), vm((1, width), F32), vm((1, width), F32), vm((1, width), F32),
        vm((1, 384), F32), vm((1, fu), F32),
        vm((mb, seq, 384), BF16), vm((mb, seq, fu), BF16), vm((seq, fu), BF16), vm((mb, seq, 2), F32),
        vm((mb, seq, 128), BF16), vm((mb, seq, width), BF16), vm((mb, seq, width), BF16),
        vm((mb, seq, 128), BF16), vm((mb, seq, 384), BF16), vm((128, seq), F32), vm((128, seq), F32),
        vm((5, 8, width), F32), vm((1, 8, fu), F32), vm((1, 8, 384), F32),
        vm((mb, nz, tk, width), BF16), vm((mb, nz + 1, tk, width), BF16), vm((mb, nz, tk, width), BF16), vm((mb, nz + 1, tk, width), BF16),
        vm((width, 384), BF16), vm((width, fu), BF16), vm((ndp, rows_do, width), BF16),
        vm((2, rows_p // 2, 384), BF16), vm((2, rows_p, 384), BF16), vm((2, rows_p // 2, fu), BF16), vm((2, rows_p, fu), BF16),
        vm((2, rows_do // 2, width), BF16), vm((2, rows_do, width), BF16),
        vm((8, width), F32), vm((ndp, 8, width), F32), vm((n, rows_w, 384), BF16), vm((n, rows_w, fu), BF16),
        vm((tk, width), F32), vm((rows_w, width), BF16),
        vm((8, width), F32), vm((n, 16, 128), F32),
        vm((mb, seq), F32), vm((n, rows_w, 384 + fu), BF16),
        vm((n, rows_w, 384), BF16), vm((n, rows_w, fu), BF16), vm((n, 16, 128), F32),
        vm((mb, seq, width), BF16), vm((seq, width), BF16),
    ] + [vm((heads, block, block * (i + 1)), BF16) for i in range(nz)]
    per_seq = [dma((sum(cuts), size)) for cuts in (CUT_TOKENS, CUT_COTANGENT) for size in (3 * nz - 2, n)]
    to_ctx, to_dp, plane = [dma((n,))] * 2, [dma((ndp,))] * 2, [dma((6,))] * 2
    sems = per_seq + to_ctx + plane + to_ctx + to_dp + plane + [dma, dma]
    sems += [dma((sum(CUT_MIXED), nz))] * 6 + [dma((sum(CUT_GRAD), nz))] * 6
    sems += (plane + to_ctx) * 2 + plane + [dma, dma] + to_dp + to_ctx + [dma((10,))]
    return pl.pallas_call(
        partial(fused_kernel, ndp, n, dims),
        out_shape=(
            jax.ShapeDtypeStruct((tk, mb, width), BF16),
            jax.ShapeDtypeStruct((tk, mb, width), BF16),
            jax.ShapeDtypeStruct((rows_w, 3 * width), BF16),
            jax.ShapeDtypeStruct((rows_w, n * fu), BF16),
            jax.ShapeDtypeStruct((rows_d, width), F32),
            jax.ShapeDtypeStruct((rows_w, width), BF16),
            jax.ShapeDtypeStruct((8, 128), F32),
        ),
        in_specs=[ANY] * 10,
        out_specs=[vmem] * 7,
        scratch_shapes=scratch + sems,
        compiler_params=pltpu.CompilerParams(collective_id=5, has_side_effects=True, vmem_limit_bytes=63 * MIB),
    )(tok, cot, rq, ru, wd, wo, vec, seg, cosine, sine)


def rotary_lanes(seq):
    half = ROT // 2
    inverse = (np.float32(10000.0) ** (-(np.float32(2.0) * np.arange(half, dtype=np.float32)) / np.float32(ROT))).astype(np.float32)
    angles = (np.arange(seq, dtype=np.float32)[:, None] * inverse[None, :]).astype(np.float32)
    cosine = np.ones((seq, HEAD), np.float32)
    sine = np.zeros((seq, HEAD), np.float32)
    cosine[:, :half] = cosine[:, half:ROT] = np.cos(angles)
    sine[:, :half] = -np.sin(angles)
    sine[:, half:ROT] = np.sin(angles)
    return np.tile(cosine, (1, 128 // HEAD)), np.tile(sine, (1, 128 // HEAD))


def fused_device(ndp, n, tokens, cotangent, segments, w_qkv, b_qkv, w_out, b_out, w_up, b_up, w_down, b_down, g1, s1, g2, s2):
    tok, mb, width = tokens.shape
    seq = segments.shape[1]
    hc = width // n
    rows_w, rows_d = w_qkv.shape[0], w_down.shape[0]
    seg_f = segments.astype(F32)
    seg_f, small = lax.optimization_barrier((seg_f, (b_qkv, b_out, b_up, b_down, g1, s1, g2, s2)))
    units = jnp.concatenate(small).astype(F32).reshape(-1, rows_w)
    vec = jnp.pad(jnp.tile(units, (1, 128 // rows_w)), ((0, 16 - units.shape[0]), (0, 0)))
    cosine, sine = rotary_lanes(seq)
    dims = (mb, tok, width, seq, hc // HEAD, rows_w, rows_d)
    mixed, t_grad, d_qkv, d_up, dwd, dwo, dv = fused_layer(
        ndp, n, dims, tokens, cotangent, w_qkv, w_up, w_down, w_out, vec, seg_f, jnp.asarray(cosine), jnp.asarray(sine)
    )
    one = lambda r: dv[r, :rows_w]
    return (
        mixed,
        t_grad,
        d_qkv.astype(F32),
        dv[0, : b_qkv.shape[0]],
        dwo.astype(F32),
        one(6),
        d_up.astype(F32),
        dv[1, :rows_d],
        dwd,
        one(7),
        one(2),
        one(3),
        one(4),
        one(5),
    )


def rotary_tables(seq):
    half_rot = ROT // 2
    inverse = 10000.0 ** (-(2.0 * jnp.arange(half_rot, dtype=F32)) / ROT)
    angles = jnp.arange(seq, dtype=jnp.int32).astype(F32)[:, None] * inverse[None, :]
    angles = jnp.concatenate([angles, angles], axis=-1)
    return (jnp.cos(angles)[None, :, None, :], jnp.sin(angles)[None, :, None, :])


def rotate(values, cosine, sine, back=False):
    half_rot = ROT // 2
    lead = values[..., :ROT]
    if back:
        u = lead * sine
        turned = jnp.concatenate([u[..., half_rot:], -u[..., :half_rot]], axis=-1)
        return jnp.concatenate([lead * cosine + turned, values[..., ROT:]], axis=-1)
    turned = jnp.concatenate([-lead[..., half_rot:], lead[..., :half_rot]], axis=-1)
    return jnp.concatenate([lead * cosine + turned * sine, values[..., ROT:]], axis=-1)


def per_device(ndp, n, tokens, cotangent, segments, w_qkv, b_qkv, w_out, b_out, w_up, b_up, w_down, b_down, g1, s1, g2, s2):
    tok, mb, width = tokens.shape
    seq = segments.shape[1]
    heads_all = width // HEAD
    hc = width // n
    heads = hc // HEAD
    rows_w = w_qkv.shape[0]
    rows_d = w_down.shape[0]
    fu = ndp * rows_d
    c = lax.axis_index("ctx")
    dp = lax.axis_index("dp")
    scale = HEAD ** (-0.5)

    cot = jnp.transpose(cotangent, (1, 0, 2))
    toks = jnp.transpose(tokens, (1, 0, 2))
    qkv_cols = w_qkv.reshape(rows_w, 3, n, hc).transpose(2, 0, 1, 3).reshape(n, rows_w, 3 * hc)
    up_cols = w_up.reshape(rows_w, ndp, n, rows_d).transpose(2, 0, 1, 3).reshape(n, rows_w, fu)
    wp = jnp.concatenate([qkv_cols, up_cols], axis=2)
    shard_vecs = (b_qkv, b_out, b_up, b_down, g1, s1, g2, s2)
    sizes = [v.shape[0] for v in shard_vecs]
    vec = jnp.concatenate(shard_vecs)
    lanes = 128
    per_vec = 16 * lanes
    vec = jnp.pad(vec, (0, per_vec - vec.shape[0])).reshape(16, lanes)
    x, g, w, wd, wo, vecs = gather_all(ndp, n, toks, cot, wp, w_down, w_out, vec)
    w = w.reshape(width, 3 * hc + fu)
    wq, wu = w[:, : 3 * hc], w[:, 3 * hc :]
    wd = wd.reshape(fu, width)
    wo = wo.reshape(hc, width)
    flat = vecs.reshape(ndp * n, per_vec).astype(F32)
    starts = [sum(sizes[:i]) for i in range(len(sizes))]
    full = [flat[:, s : s + z].reshape(-1) for s, z in zip(starts, sizes)]
    bq_all, bo, bu_all, bd, gain1, shift1, gain2, shift2 = full
    bq = lax.dynamic_index_in_dim(bq_all.reshape(3, n, hc), c, 1, keepdims=False).reshape(3 * hc)
    bu = lax.dynamic_index_in_dim(bu_all.reshape(ndp, n, rows_d), c, 1, keepdims=False).reshape(fu)

    xf = x.reshape(mb * seq, width).astype(F32)
    gl = g.reshape(mb * seq, width)
    mean = jnp.mean(xf, axis=-1, keepdims=True)
    cen = xf - mean
    rstd = lax.rsqrt(jnp.mean(cen * cen, axis=-1, keepdims=True) + 1e-05)
    normed = cen * rstd
    h1 = (normed * gain1 + shift1).astype(BF16)
    h2 = (normed * gain2 + shift2).astype(BF16)
    joined = (dot(h1, wq) + bq).reshape(mb, seq, 3, heads, HEAD)
    cosine, sine = rotary_tables(seq)
    q = rotate(joined[:, :, 0], cosine, sine).astype(BF16)
    k = rotate(joined[:, :, 1], cosine, sine).astype(BF16)
    v = joined[:, :, 2].astype(BF16)
    pos = jnp.arange(seq, dtype=jnp.int32)
    same = (segments[:, None, :] == segments[:, :, None]) & (segments[:, :, None] > 0)
    allow = (same & (pos[None, None, :] <= pos[None, :, None])) | (pos[None, None, :] == pos[None, :, None])
    scores = jnp.einsum("sqhd,skhd->shqk", q, k, preferred_element_type=F32) * scale
    scores = jnp.where(allow[:, None], scores, -1e30)
    top = jnp.max(scores, axis=-1, keepdims=True)
    e = jnp.exp(scores - top)
    probs = e / jnp.sum(e, axis=-1, keepdims=True)
    pl_low = probs.astype(BF16)
    ctx_f = jnp.einsum("shqk,skhd->sqhd", pl_low, v, preferred_element_type=F32)
    ctx = ctx_f.astype(BF16).reshape(mb * seq, hc)
    act = dot(h2, wu) + bu
    hidden = jax.nn.gelu(act, approximate=False).astype(BF16)
    part = (dot(ctx, wo) + dot(hidden, wd)).astype(BF16).reshape(mb, seq, width)
    mixed_sum = scatter_ctx(ndp, n, part, 1)
    mixed = (toks.astype(F32) + mixed_sum + bo + bd).astype(BF16)

    gf = gl.astype(F32)
    d_wd = dot(hidden, gl, ((0,), (0,)))
    d_wo = dot(ctx, gl, ((0,), (0,)))
    d_hidden = dot(gl, wd, ((1,), (1,)))
    _, pull = jax.vjp(partial(jax.nn.gelu, approximate=False), act)
    d_act = pull(d_hidden)[0].astype(BF16)
    d_wu = dot(h2, d_act, ((0,), (0,)))
    d_bu = jnp.sum(d_act.astype(F32), axis=0)
    d_h2 = dot(d_act, wu, ((1,), (1,)))
    d_ctx = dot(gl, wo, ((1,), (1,))).astype(BF16).reshape(mb, seq, heads, HEAD)
    d_probs = jnp.einsum("sqhd,skhd->shqk", d_ctx, v, preferred_element_type=F32)
    delta = jnp.sum(probs * d_probs, axis=-1, keepdims=True)
    d_scores = jnp.where(allow[:, None], probs * (d_probs - delta), 0.0).astype(BF16)
    d_q = jnp.einsum("shqk,skhd->sqhd", d_scores, k, preferred_element_type=F32) * scale
    d_k = jnp.einsum("shqk,sqhd->skhd", d_scores, q, preferred_element_type=F32) * scale
    d_v = jnp.einsum("shqk,sqhd->skhd", pl_low, d_ctx, preferred_element_type=F32)
    d_q = rotate(d_q, cosine, sine, True)
    d_k = rotate(d_k, cosine, sine, True)
    d_qkv = jnp.stack([d_q, d_k, d_v], axis=2).astype(BF16).reshape(mb * seq, 3 * hc)
    d_wq = dot(h1, d_qkv, ((0,), (0,)))
    d_bq = jnp.sum(d_qkv.astype(F32), axis=0)
    d_h1 = dot(d_qkv, wq, ((1,), (1,)))
    e_sum = (d_h1 * gain1 + d_h2 * gain2).astype(BF16).reshape(mb, seq, width)
    e_own = scatter_ctx(ndp, n, e_sum, 2)
    own_x = toks.astype(F32)
    o_mean = jnp.mean(own_x, axis=-1, keepdims=True)
    o_cen = own_x - o_mean
    o_rstd = lax.rsqrt(jnp.mean(o_cen * o_cen, axis=-1, keepdims=True) + 1e-05)
    o_n = o_cen * o_rstd
    t_grad = o_rstd * (e_own - jnp.mean(e_own, axis=-1, keepdims=True) - o_n * jnp.mean(e_own * o_n, axis=-1, keepdims=True))
    tokens_grad = (cot.astype(F32) + t_grad).astype(BF16)

    rows = [
        jnp.pad(d_bq, (0, width - 3 * hc)),
        jnp.pad(d_bu, (0, width - fu)),
        jnp.sum(d_h1 * normed, axis=0),
        jnp.sum(d_h1, axis=0),
        jnp.sum(d_h2 * normed, axis=0),
        jnp.sum(d_h2, axis=0),
        jnp.sum(gf, axis=0),
        jnp.zeros((width,), F32),
    ]
    dwp = jnp.concatenate([d_wq, d_wu], axis=1).astype(BF16).reshape(ndp, n, rows_w, 3 * hc + fu)
    dw, dwd, dwo, dv = grads_all(
        ndp, n, dwp, d_wd.astype(BF16).reshape(ndp, rows_d, width), d_wo.astype(BF16).reshape(ndp, rows_w, width), jnp.stack(rows)
    )
    index = dp * n + c
    g_qkv = dw[:, :, : 3 * hc].reshape(n, rows_w, 3, hc).transpose(1, 2, 0, 3).reshape(rows_w, 3 * width).astype(F32)
    g_up = dw[:, :, 3 * hc :].reshape(n, rows_w, ndp, rows_d).transpose(1, 2, 0, 3).reshape(rows_w, -1).astype(F32)
    g_bq = lax.dynamic_slice_in_dim(dv[:, 0, : 3 * hc].reshape(n, 3, hc).transpose(1, 0, 2).reshape(-1), index * sizes[0], sizes[0])
    own = lax.dynamic_index_in_dim(dv, c, 0, keepdims=False)
    g_bu = lax.dynamic_slice_in_dim(own[1], dp * rows_d, rows_d)
    four = lax.dynamic_slice_in_dim(jnp.sum(dv[:, 2:6], axis=0), index * rows_w, rows_w, axis=1)
    g_b = lax.dynamic_slice_in_dim(own[6], index * rows_w, rows_w)
    return (
        jnp.transpose(mixed, (1, 0, 2)),
        jnp.transpose(tokens_grad, (1, 0, 2)),
        g_qkv,
        g_bq,
        dwo.astype(F32),
        g_b,
        g_up,
        g_bu,
        dwd,
        g_b,
        four[0],
        four[1],
        four[2],
        four[3],
    )


def program(ndp, n, *args):
    tokens, w_qkv, w_down = args[0], args[3], args[9]
    rows_w = w_qkv.shape[0]
    whole_tiles = ndp == 4 and rows_w % 16 == 0 and tokens.shape[2] // n == 128 and w_down.shape[0] == 128 and tokens.shape[0] % 16 == 0
    return (fused_device if whole_tiles else per_device)(ndp, n, *args)


def solution(mesh):
    every = ("dp", "ctx")
    mat, vec, act = P(every, None), P(every), P("ctx", "dp", None)
    placed = (act, act, P("dp", None), mat, vec, mat, vec, mat, vec, mat, vec, vec, vec, vec, vec)
    return jax.shard_map(
        partial(program, mesh.shape["dp"], mesh.shape["ctx"]),
        mesh=mesh,
        in_specs=placed,
        out_specs=(act, act, mat, vec, mat, vec, mat, vec, mat, vec, vec, vec, vec, vec),
        check_vma=False,
    )
```

```python
from functools import partial

import jax
import jax.numpy as jnp
import numpy as np
from jax import lax
from jax.experimental import pallas as pl
from jax.experimental.pallas import tpu as pltpu
from jax.sharding import PartitionSpec as P

HEAD = 64
ROT = 16
MIB = 1 << 20
CUT_TOKENS, CUT_COTANGENT, CUT_MIXED, CUT_GRAD = (2, 1), (1, 1), (1, 1), (1, 2)
MESH = pl.DeviceIdType.MESH
ANY = pl.BlockSpec(memory_space=pl.ANY)
F32 = jnp.float32
BF16 = jnp.bfloat16


class Place:
    def __init__(self, ndp, n):
        self.ndp, self.n, self.nz = ndp, n, n // 2
        self.dp = lax.axis_index("dp")
        self.c = lax.axis_index("ctx")
        self.z = self.c // 2
        self.core = lax.rem(self.c, 2)
        self.sib = self.c + 1 - 2 * self.core
        self.has_up = self.z + 1 < self.nz
        self.has_down = self.z > 0
        self.px = self.dp + 1 - 2 * lax.rem(self.dp, 2)
        self.py = lax.rem(self.dp + 2, 4)
        self.diag = 3 - self.dp
        index, back = self.dp * n + self.c, self.c * ndp + self.dp
        self.rows_dp, self.rows_c = lax.rem(index, ndp), index // ndp
        self.from_dp, self.from_c = back // n, lax.rem(back, n)
        self.moves = index != back

    def barrier(self, ctx_all, dp_all, rows=False):
        bar = pltpu.get_barrier_semaphore()
        count = 0
        if rows:
            count = count + 2 * self.moves.astype(jnp.int32)

            @pl.when(self.moves)
            def _():
                pl.semaphore_signal(bar, inc=1, device_id=(self.rows_dp, self.rows_c), device_id_type=MESH)
                pl.semaphore_signal(bar, inc=1, device_id=(self.from_dp, self.from_c), device_id_type=MESH)

        if ctx_all:
            for j in range(1, self.n):
                peer = lax.rem(self.c + j, self.n)
                pl.semaphore_signal(bar, inc=1, device_id=(self.dp, peer), device_id_type=MESH)
                count += 1
        else:
            pl.semaphore_signal(bar, inc=1, device_id=(self.dp, self.sib), device_id_type=MESH)
            count += 1
            for ok, peer in ((self.has_up, self.c + 2), (self.has_down, self.c - 2)):

                @pl.when(ok)
                def _():
                    pl.semaphore_signal(bar, inc=1, device_id=(self.dp, peer), device_id_type=MESH)

        if dp_all:
            for j in range(1, self.ndp):
                peer = lax.rem(self.dp + j, self.ndp)
                pl.semaphore_signal(bar, inc=1, device_id=(peer, self.c), device_id_type=MESH)
                count += 1
        if not ctx_all:
            count = count + self.has_up.astype(jnp.int32) + self.has_down.astype(jnp.int32)
        pl.semaphore_wait(bar, count)


def remote(src, dst, send, recv, dp, c):
    return pltpu.make_async_remote_copy(
        src_ref=src,
        dst_ref=dst,
        send_sem=send,
        recv_sem=recv,
        device_id=(dp, c),
        device_id_type=MESH,
    )


class Gather:
    def __init__(self, at, src, dst, tok, sends, recvs):
        self.at, self.src, self.dst, self.tok, self.sends, self.recvs = at, src, dst, tok, sends, recvs

    def rows(self, c):
        return self.dst.at[:, pl.ds(pl.multiple_of(c * self.tok, self.tok), self.tok)]

    def copy(self, block, slot, c, src=None):
        at = self.at
        src = self.rows(block) if src is None else src
        return remote(src, self.rows(block), self.sends.at[slot], self.recvs.at[block], at.dp, c)

    def start(self):
        at = self.at

        @pl.when(at.has_up)
        def _():
            self.copy(at.c, 0, at.c + 2, self.src).start()

        @pl.when(at.has_down)
        def _():
            self.copy(at.c, 1, at.c - 2, self.src).start()

        self.copy(at.c, 2, at.sib, self.src).start()

    def step(self, k):
        at = self.at
        low, high = at.c - 2 * k, at.c + 2 * k

        @pl.when(at.z >= k)
        def _():
            self.copy(low, 0, at.c).wait_recv()

            @pl.when(at.has_up)
            def _():
                self.copy(low, 3 * k, at.c + 2).start()

            self.copy(low, 3 * k + 2, at.sib).start()

        @pl.when(at.z + k < at.nz)
        def _():
            self.copy(high, 0, at.c).wait_recv()

            @pl.when(at.has_down)
            def _():
                self.copy(high, 3 * k + 1, at.c - 2).start()

            self.copy(high, 3 * at.nz + k, at.sib).start()

    def finish(self):
        at = self.at
        for z in range(at.nz):
            self.copy(2 * z + 1 - at.core, 0, at.c).wait_recv()
        self.copy(at.c, 2, at.sib, self.src).wait_send()
        for k in range(at.nz):

            @pl.when((at.z >= k) & at.has_up)
            def _():
                self.copy(at.c, 3 * k, at.c).wait_send()

            @pl.when((at.z + k < at.nz) & at.has_down)
            def _():
                self.copy(at.c, 3 * k + 1, at.c).wait_send()

            if k:

                @pl.when(at.z >= k)
                def _():
                    self.copy(at.c, 3 * k + 2, at.c).wait_send()

                @pl.when(at.z + k < at.nz)
                def _():
                    self.copy(at.c, 3 * at.nz + k, at.c).wait_send()


def gather_slots(nz):
    return 4 * nz


class Exchange:
    def __init__(self, at, axis, src, dst, sends, recvs):
        self.at, self.axis, self.src, self.dst, self.sends, self.recvs = at, axis, src, dst, sends, recvs
        self.me, self.count = (at.c, at.n) if axis == "ctx" else (at.dp, at.ndp)

    def copy(self, peer, sender):
        at = self.at
        to = (at.dp, peer) if self.axis == "ctx" else (peer, at.c)
        return remote(self.src(peer), self.dst(sender), self.sends.at[peer], self.recvs.at[sender], *to)

    def start(self):
        for j in range(1, self.count):
            self.copy(lax.rem(self.me + j, self.count), self.me).start()

    def wait_recv(self):
        for j in range(1, self.count):
            peer = lax.rem(self.me + j, self.count)
            self.copy(peer, peer).wait_recv()

    def wait_send(self):
        for j in range(1, self.count):
            peer = lax.rem(self.me + j, self.count)
            self.copy(peer, self.me).wait_send()


def gather_kernel(ndp, n, tok_ref, cot_ref, wp_ref, wd_ref, wo_ref, vec_ref, x_out, g_out, w_out, wd_out, wo_out, vec_out, *sems):
    at = Place(ndp, n)
    tok = tok_ref.shape[1]
    (x_send, x_recv, g_send, g_recv, w1s, w1r, w2s, w2r, v1s, v1r, v2s, v2r, ds, dr, o1s, o1r, o2s, o2r, local) = sems
    at.barrier(True, True)
    own = (
        pltpu.make_async_copy(wp_ref.at[at.c], w_out.at[at.dp, at.c], local.at[0]),
        pltpu.make_async_copy(vec_ref, vec_out.at[at.dp, at.c], local.at[1]),
        pltpu.make_async_copy(wd_ref, wd_out.at[at.dp], local.at[2]),
        pltpu.make_async_copy(tok_ref, x_out.at[:, pl.ds(pl.multiple_of(at.c * tok, tok), tok)], local.at[3]),
        pltpu.make_async_copy(cot_ref, g_out.at[:, pl.ds(pl.multiple_of(at.c * tok, tok), tok)], local.at[4]),
    )
    for copy in own:
        copy.start()
    down_w = Exchange(at, "dp", lambda p: wd_ref, lambda s: wd_out.at[s], ds, dr)
    cols = Exchange(at, "ctx", lambda p: wp_ref.at[p], lambda s: w_out.at[at.dp, s], w1s, w1r)
    vecs = Exchange(at, "ctx", lambda p: vec_ref, lambda s: vec_out.at[at.dp, s], v1s, v1r)
    plane_w = Exchange(at, "dp", lambda p: w_out.at[at.dp], lambda s: w_out.at[s], w2s, w2r)
    plane_v = Exchange(at, "dp", lambda p: vec_out.at[at.dp], lambda s: vec_out.at[s], v2s, v2r)
    plane_o = Exchange(at, "dp", lambda p: wo_out, lambda s: wo_out, o2s, o2r)
    cols.start()
    vecs.start()
    index = at.dp * n + at.c
    heads_of, slot = index // ndp, lax.rem(index, ndp)

    def out_rows(b, c):
        return remote(wo_ref, wo_out.at[b], o1s, o1r.at[b], at.dp, c)

    @pl.when(heads_of != at.c)
    def _():
        out_rows(slot, heads_of).start()

    own_rows = pltpu.make_async_copy(wo_ref, wo_out.at[slot], local.at[5])

    @pl.when(heads_of == at.c)
    def _():
        own_rows.start()

    down_w.start()
    x_ag = Gather(at, tok_ref, x_out, tok, x_send, x_recv)
    g_ag = Gather(at, cot_ref, g_out, tok, g_send, g_recv)
    x_ag.start()
    own[0].wait()
    cols.wait_recv()
    plane_w.start()
    own[1].wait()
    vecs.wait_recv()
    plane_v.start()
    first = at.c * ndp // n

    @pl.when(at.dp == first)
    def _():
        for b in range(ndp):
            src = lax.rem(at.c * ndp + b, n)

            @pl.when(src != at.c)
            def _():
                out_rows(b, at.c).wait_recv()

            @pl.when(src == at.c)
            def _():
                own_rows.wait()

        plane_o.start()

    for k in range(1, at.nz):
        x_ag.step(k)
        if k == 1:
            g_ag.start()
    for k in range(1, at.nz):
        g_ag.step(k)
    x_ag.finish()
    g_ag.finish()

    @pl.when(heads_of != at.c)
    def _():
        out_rows(slot, heads_of).wait_send()

    @pl.when((heads_of == at.c) & (at.dp != first))
    def _():
        own_rows.wait()

    @pl.when(at.dp == first)
    def _():
        plane_o.wait_send()

    @pl.when(at.dp != first)
    def _():
        plane_o.copy(first, first).wait_recv()

    for copy in own[2:]:
        copy.wait()
    for part in (down_w, plane_w, plane_v):
        part.wait_recv()
    for part in (down_w, cols, vecs, plane_w, plane_v):
        part.wait_send()


def gather_all(ndp, n, tok, cot, wp, wd, wo, vec):
    mb, rows, width = tok.shape
    dma = pltpu.SemaphoreType.DMA
    slots = gather_slots(n // 2)
    return pl.pallas_call(
        partial(gather_kernel, ndp, n),
        out_shape=(
            jax.ShapeDtypeStruct((mb, rows * n, width), BF16),
            jax.ShapeDtypeStruct((mb, rows * n, width), BF16),
            jax.ShapeDtypeStruct((ndp,) + wp.shape, BF16),
            jax.ShapeDtypeStruct((ndp,) + wd.shape, BF16),
            jax.ShapeDtypeStruct((ndp,) + wo.shape, BF16),
            jax.ShapeDtypeStruct((ndp, n) + vec.shape, vec.dtype),
        ),
        in_specs=[ANY] * 6,
        out_specs=[ANY] * 6,
        scratch_shapes=[
            dma((slots,)), dma((n,)), dma((slots,)), dma((n,)),
            dma((n,)), dma((n,)), dma((ndp,)), dma((ndp,)),
            dma((n,)), dma((n,)), dma((ndp,)), dma((ndp,)),
            dma((ndp,)), dma((ndp,)),
            dma, dma((ndp,)), dma((ndp,)), dma((ndp,)),
            dma((6,)),
        ],
        compiler_params=pltpu.CompilerParams(collective_id=0, has_side_effects=True),
    )(tok, cot, wp, wd, wo, vec)


class Scatter:
    def __init__(self, at, part, out, sib_buf, low_buf, high_buf, stage, tok, sems):
        self.at, self.part, self.out, self.tok = at, part, out, tok
        self.sib_buf, self.low_buf, self.high_buf, self.stage = sib_buf, low_buf, high_buf, stage
        self.s_send, self.s_recv, self.up_send, self.up_recv, self.dn_send, self.dn_recv = sems

    def rows(self, c):
        return pl.ds(pl.multiple_of(c * self.tok, self.tok), self.tok)

    def cross(self, z):
        at = self.at
        src = self.part.at[:, self.rows(2 * z + 1 - at.core)]
        return remote(src, self.sib_buf.at[z], self.s_send.at[z], self.s_recv.at[z], at.dp, at.sib)

    def up(self, z):
        at = self.at
        return remote(self.stage.at[z], self.low_buf.at[z], self.up_send.at[z], self.up_recv.at[z], at.dp, at.c + 2)

    def down(self, z):
        at = self.at
        return remote(self.stage.at[z], self.high_buf.at[z], self.dn_send.at[z], self.dn_recv.at[z], at.dp, at.c - 2)

    def order(self):
        nz = self.at.nz
        for i in range(nz):
            yield nz - 1 - i
            if i != nz - 1 - i:
                pass

    def start(self):
        for i in range(self.at.nz):
            self.cross(i).start()

    def chip_sum(self, z):
        at = self.at
        mine = self.part[:, self.rows(2 * z + at.core)].astype(F32)
        return mine + self.sib_buf[z].astype(F32)

    def step(self, i):
        at = self.at
        up_z, dn_z = at.nz - 1 - i, i

        @pl.when(up_z > at.z)
        def _():
            self.cross(up_z).wait_recv()
            self.stage[up_z] = self.chip_sum(up_z).astype(BF16)

            @pl.when(at.has_down)
            def _():
                self.up(up_z).wait_recv()
                self.stage[up_z] = (self.stage[up_z].astype(F32) + self.low_buf[up_z].astype(F32)).astype(BF16)

            self.up(up_z).start()

        @pl.when(dn_z < at.z)
        def _():
            self.cross(dn_z).wait_recv()
            self.stage[dn_z] = self.chip_sum(dn_z).astype(BF16)

            @pl.when(at.has_up)
            def _():
                self.down(dn_z).wait_recv()
                self.stage[dn_z] = (self.stage[dn_z].astype(F32) + self.high_buf[dn_z].astype(F32)).astype(BF16)

            self.down(dn_z).start()

    def finish(self):
        at = self.at
        self.cross(at.z).wait_recv()
        self.out[...] = self.chip_sum(at.z)

        @pl.when(at.has_down)
        def _():
            self.up(at.z).wait_recv()
            self.out[...] += self.low_buf[at.z].astype(F32)

        @pl.when(at.has_up)
        def _():
            self.down(at.z).wait_recv()
            self.out[...] += self.high_buf[at.z].astype(F32)

        for z in range(at.nz):
            self.cross(z).wait_send()

            @pl.when(z > at.z)
            def _():
                self.up(z).wait_send()

            @pl.when(z < at.z)
            def _():
                self.down(z).wait_send()


def scatter_kernel(ndp, n, part_ref, out_ref, sib_buf, low_buf, high_buf, stage, *sems):
    at = Place(ndp, n)
    at.barrier(False, False)
    work = Scatter(at, part_ref, out_ref, sib_buf, low_buf, high_buf, stage, out_ref.shape[1], sems)
    work.start()
    for i in range(at.nz - 1):
        work.step(i)
    work.finish()


def scatter_ctx(ndp, n, part, collective):
    mb, seq, width = part.shape
    nz, tok = n // 2, seq // n
    dma = pltpu.SemaphoreType.DMA
    buf = pltpu.VMEM((nz, mb, tok, width), BF16)
    vmem = pl.BlockSpec(memory_space=pltpu.VMEM)
    return pl.pallas_call(
        partial(scatter_kernel, ndp, n),
        out_shape=jax.ShapeDtypeStruct((mb, tok, width), F32),
        in_specs=[vmem],
        out_specs=vmem,
        scratch_shapes=[buf, buf, buf, buf] + [dma((nz,))] * 6,
        compiler_params=pltpu.CompilerParams(collective_id=collective, has_side_effects=True, vmem_limit_bytes=48 * MIB),
    )(part)


def grads_kernel(ndp, n, wp_ref, wd_ref, wo_ref, v_ref, w_out, wd_out, wo_out, v_out, wbuf, wsum, dbuf, obuf, osum, vbuf, vsum, *sems):
    at = Place(ndp, n)
    (w1s, w1r, ds, dr, o1s, o1r, v1s, v1r, w2s, w2r, v2s, v2r, o2s, o2r, local) = sems
    at.barrier(True, True)
    first = at.c * ndp // n
    w1 = Exchange(at, "dp", lambda p: wp_ref.at[p], lambda s: wbuf.at[s], w1s, w1r)
    d1 = Exchange(at, "dp", lambda p: wd_ref.at[p], lambda s: dbuf.at[s], ds, dr)
    v1 = Exchange(at, "dp", lambda p: v_ref, lambda s: vbuf.at[s], v1s, v1r)
    o1 = Exchange(at, "dp", lambda p: wo_ref, lambda s: obuf.at[s], o1s, o1r)
    w1.start()
    v1.start()

    @pl.when(at.dp != first)
    def _():
        o1.copy(first, at.dp).start()

    d1.start()

    def total(ref, mine, get):
        ref[...] = mine
        for j in range(1, ndp):
            ref[...] += get(lax.rem(at.dp + j, ndp)).astype(F32)

    w1.wait_recv()
    total(wsum, wp_ref[at.dp].astype(F32), lambda s: wbuf[s])
    wbuf[at.dp] = wsum[...].astype(BF16)
    w2 = Exchange(at, "ctx", lambda p: wbuf.at[at.dp, p], lambda s: w_out.at[s], w2s, w2r)
    w2.start()
    w_out[at.c] = wbuf[at.dp, at.c]
    v1.wait_recv()
    total(vsum, v_ref[...], lambda s: vbuf[s])
    v2 = Exchange(at, "ctx", lambda p: vsum, lambda s: v_out.at[s], v2s, v2r)
    v2.start()
    v_out[at.c] = vsum[...]

    index = at.dp * n + at.c
    heads_of, slot = index // ndp, lax.rem(index, ndp)

    def out_rows(b, c):
        return remote(osum.at[b], wo_out, o2s.at[b], o2r, at.dp, c)

    @pl.when(at.dp == first)
    def _():
        o1.wait_recv()
        rows = wo_ref[...].astype(F32)
        for j in range(1, ndp):
            rows += obuf[lax.rem(at.dp + j, ndp)].astype(F32)
        osum[...] = rows.astype(BF16)
        for b in range(ndp):
            owner = lax.rem(at.c * ndp + b, n)

            @pl.when(owner != at.c)
            def _():
                out_rows(b, owner).start()

            @pl.when(owner == at.c)
            def _():
                wo_out[...] = osum[b]

    d1.wait_recv()
    total(wd_out, wd_ref[at.dp].astype(F32), lambda s: dbuf[s])

    @pl.when(heads_of != at.c)
    def _():
        out_rows(slot, at.c).wait_recv()

    w2.wait_recv()
    v2.wait_recv()
    for part in (w1, v1, d1, w2, v2):
        part.wait_send()

    @pl.when(at.dp != first)
    def _():
        o1.copy(first, at.dp).wait_send()

    @pl.when(at.dp == first)
    def _():
        for b in range(ndp):
            owner = lax.rem(at.c * ndp + b, n)

            @pl.when(owner != at.c)
            def _():
                out_rows(b, owner).wait_send()


def grads_all(ndp, n, wp, wd, wo, v):
    dma = pltpu.SemaphoreType.DMA
    vmem = pl.BlockSpec(memory_space=pltpu.VMEM)
    return pl.pallas_call(
        partial(grads_kernel, ndp, n),
        out_shape=(
            jax.ShapeDtypeStruct(wp.shape[1:], BF16),
            jax.ShapeDtypeStruct(wd.shape[1:], F32),
            jax.ShapeDtypeStruct(wo.shape[1:], BF16),
            jax.ShapeDtypeStruct((n,) + v.shape, F32),
        ),
        in_specs=[vmem] * 4,
        out_specs=[vmem] * 4,
        scratch_shapes=[
            pltpu.VMEM(wp.shape, BF16),
            pltpu.VMEM(wp.shape[1:], F32),
            pltpu.VMEM(wd.shape, BF16),
            pltpu.VMEM((ndp,) + wo.shape, BF16),
            pltpu.VMEM(wo.shape, BF16),
            pltpu.VMEM((ndp,) + v.shape, F32),
            pltpu.VMEM(v.shape, F32),
            dma((ndp,)), dma((ndp,)), dma((ndp,)), dma((ndp,)), dma((ndp,)), dma((ndp,)), dma((ndp,)), dma((ndp,)),
            dma((n,)), dma((n,)), dma((n,)), dma((n,)), dma((ndp,)), dma,
            dma((1,)),
        ],
        compiler_params=pltpu.CompilerParams(collective_id=3, has_side_effects=True, vmem_limit_bytes=48 * MIB),
    )(wp, wd, wo, v)


def dot(a, b, dims=((1,), (0,))):
    return lax.dot_general(a, b, (dims, ((), ())), preferred_element_type=F32)


NT = ((1,), (1,))
TN = ((0,), (0,))


class SeqGather:
    def __init__(self, at, dst, tok, first, size, sends, recvs):
        self.at, self.dst, self.tok, self.first, self.size, self.sends, self.recvs = at, dst, tok, first, size, sends, recvs

    def rows(self, c):
        return self.dst.at[pl.ds(pl.multiple_of(c * self.tok + self.first, self.size), self.size)]

    def copy(self, block, slot, c):
        return remote(self.rows(block), self.rows(block), self.sends.at[slot], self.recvs.at[block], self.at.dp, c)

    def up_slot(self, k):
        return k

    def down_slot(self, k):
        return self.at.nz - 1 + k

    def side_slot(self, k):
        return 2 * (self.at.nz - 1) + k

    def start(self):
        at = self.at

        @pl.when(at.has_up)
        def _():
            self.copy(at.c, self.up_slot(0), at.c + 2).start()

        @pl.when(at.has_down)
        def _():
            self.copy(at.c, self.down_slot(0), at.c - 2).start()

        self.copy(at.c, self.side_slot(0), at.sib).start()

    def step(self, k):
        at = self.at
        low, high = at.c - 2 * k, at.c + 2 * k

        @pl.when(at.z >= k)
        def _():
            self.copy(low, 0, at.c).wait_recv()

            @pl.when(at.has_up)
            def _():
                self.copy(low, self.up_slot(k), at.c + 2).start()

            self.copy(low, self.side_slot(k), at.sib).start()

        @pl.when(at.z + k < at.nz)
        def _():
            self.copy(high, 0, at.c).wait_recv()

            @pl.when(at.has_down)
            def _():
                self.copy(high, self.down_slot(k), at.c - 2).start()

            self.copy(high, self.side_slot(at.z + k), at.sib).start()

    def land(self):
        for z in range(self.at.nz):
            self.land_chip(z)

    def land_chip(self, z):
        self.copy(2 * z + 1 - self.at.core, 0, self.at.c).wait_recv()


    def drain(self):
        at = self.at
        for k in range(at.nz):
            self.copy(at.c, self.side_slot(k), at.c).wait_send()
            if k == at.nz - 1:
                continue

            @pl.when((at.z >= k) & at.has_up)
            def _():
                self.copy(at.c, self.up_slot(k), at.c).wait_send()

            @pl.when((at.z + k < at.nz) & at.has_down)
            def _():
                self.copy(at.c, self.down_slot(k), at.c).wait_send()


class Pieces:
    def __init__(self, pieces):
        self.pieces = pieces

    def each(self, name, *args):
        for piece in self.pieces:
            getattr(piece, name)(*args)

    def start(self):
        self.each("start")

    def step(self, k):
        self.each("step", k)

    def land(self):
        self.each("land")

    def drain(self):
        self.each("drain")

    def take(self, k, body):
        at = self.pieces[0].at

        def one(t, carry):
            z = at.z - k + 2 * k * t

            @pl.when((z >= 0) & (z < at.nz))
            def _():
                self.each("land_chip", z)
                body(z)

            return carry

        lax.fori_loop(0, 2 if k else 1, one, 0)


class SeqScatter:
    def __init__(self, at, part, sib_buf, in_buf, tok, first, size, sems):
        self.at, self.part, self.tok, self.first, self.size = at, part, tok, first, size
        self.sib_buf, self.in_buf = sib_buf.at[:, pl.ds(first, size)], in_buf.at[:, pl.ds(first, size)]
        self.s_send, self.s_recv, self.up_send, self.up_recv, self.dn_send, self.dn_recv = sems

    def rows(self, c):
        return pl.ds(pl.multiple_of(c * self.tok + self.first, self.size), self.size)

    def cross(self, z):
        at = self.at
        src = self.part.at[self.rows(2 * z + 1 - at.core)]
        return remote(src, self.sib_buf.at[z], self.s_send.at[z], self.s_recv.at[z], at.dp, at.sib)

    def up(self, z):
        at = self.at
        return remote(self.sib_buf.at[z], self.in_buf.at[z], self.up_send.at[z], self.up_recv.at[z], at.dp, at.c + 2)

    def down(self, z, sender=None):
        at = self.at
        slot = jnp.where(z == (at.z - 1 if sender is None else sender - 1), at.nz, z)
        return remote(self.sib_buf.at[z], self.in_buf.at[slot], self.dn_send.at[z], self.dn_recv.at[z], at.dp, at.c - 2)

    def chip_sum(self, z):
        mine = self.part[self.rows(2 * z + self.at.core)].astype(F32)
        return mine + self.sib_buf[z].astype(F32)

    def step(self, t):
        self.step_up(t)
        self.step_down(t)

    def step_up(self, t):
        self.lead_up(t)
        self.follow_up(t)

    def lead_up(self, t):
        at = self.at
        z = at.nz - 1 - t

        @pl.when(at.z == 0)
        def _():
            self.cross(z).wait_recv()
            self.sib_buf[z] = self.chip_sum(z).astype(BF16)
            self.up(z).start()

    def follow_up(self, t):
        at = self.at
        z = at.nz - 1 - t + at.z

        @pl.when((at.z <= t) & at.has_down)
        def _():
            self.cross(z).wait_recv()
            self.up(z).wait_recv()
            self.sib_buf[z] = (self.chip_sum(z) + self.in_buf[z].astype(F32)).astype(BF16)
            self.up(z).start()

    def step_down(self, t):
        self.lead_down(t)
        self.follow_down(t)

    def lead_down(self, t):
        at = self.at

        @pl.when(at.z == at.nz - 1)
        def _():
            self.cross(t).wait_recv()
            self.sib_buf[t] = self.chip_sum(t).astype(BF16)
            self.down(t).start()

    def follow_down(self, t):
        at = self.at
        z = t - (at.nz - 1 - at.z)

        @pl.when((z >= 0) & at.has_up)
        def _():
            self.cross(z).wait_recv()
            self.down(z, at.z + 1).wait_recv()
            self.sib_buf[z] = (self.chip_sum(z) + self.in_buf[z].astype(F32)).astype(BF16)
            self.down(z).start()

    def total(self, acc):
        at = self.at
        acc = acc.at[pl.ds(self.first, self.size)]
        self.cross(at.z).wait_recv()
        acc[...] = self.chip_sum(at.z)

        @pl.when(at.has_down)
        def _():
            self.up(at.z).wait_recv()
            acc[...] += self.in_buf[at.z].astype(F32)

        @pl.when(at.has_up)
        def _():
            self.down(at.z, at.z + 1).wait_recv()
            acc[...] += self.in_buf[at.nz].astype(F32)

    def drain(self):
        at = self.at
        for z in range(at.nz):
            self.cross(z).wait_send()

            @pl.when(z > at.z)
            def _():
                self.up(z).wait_send()

            @pl.when(z < at.z)
            def _():
                self.down(z).wait_send()


class ScatterPieces(Pieces):
    def cross(self, z):
        return Pieces([piece.cross(z) for piece in self.pieces])

    def lead_up(self, t):
        self.each("lead_up", t)

    def lead_down(self, t):
        self.each("lead_down", t)

    def lead(self):
        for t in range(self.pieces[0].at.nz - 1):
            self.lead_up(t)
            self.lead_down(t)

    def follow(self, t):
        for piece in self.pieces:
            piece.follow_up(t)
            piece.follow_down(t)

    def step(self, t):
        for piece in self.pieces:
            piece.step_up(t)
            piece.step_down(t)

    def total(self, acc):
        self.each("total", acc)


class PlaneGather:
    def __init__(self, at, part, sends, recvs):
        self.at, self.part, self.sends, self.recvs = at, part, sends, recvs

    def copy(self, p, h, i, to):
        return remote(self.part(p, h), self.part(p, h), self.sends.at[i], self.recvs.at[i], to, self.at.c)

    def start(self):
        at = self.at
        for h in (0, 1):
            self.copy(at.dp, h, h, at.px).start()
            self.copy(at.dp, 1 - h, 3 - h, at.py).start()

    def forward(self):
        at = self.at
        self.copy(at.px, 0, 0, at.px).wait_recv()
        self.copy(at.px, 0, 4, at.py).start()
        self.copy(at.py, 1, 3, at.py).wait_recv()
        self.copy(at.py, 1, 5, at.px).start()

    def land(self):
        at = self.at
        self.copy(at.px, 1, 1, at.px).wait_recv()
        self.copy(at.py, 0, 2, at.py).wait_recv()
        self.copy(at.diag, 0, 4, at.py).wait_recv()
        self.copy(at.diag, 1, 5, at.px).wait_recv()

    def drain(self):
        at = self.at
        for h in (0, 1):
            self.copy(at.dp, h, h, at.px).wait_send()
            self.copy(at.dp, h, 2 + h, at.py).wait_send()
        self.copy(at.px, 0, 4, at.py).wait_send()
        self.copy(at.py, 1, 5, at.px).wait_send()


class PlaneReduce:
    def __init__(self, at, part, via_x, via_y, from_x, from_y, sends, recvs):
        self.at, self.part, self.sends, self.recvs = at, part, sends, recvs
        self.via_x, self.via_y, self.from_x, self.from_y = via_x, via_y, from_x, from_y

    def copy(self, i):
        at = self.at
        src, dst, to = (
            (lambda: self.part(at.diag, 1), self.via_x, at.px),
            (lambda: self.part(at.diag, 0), self.via_y, at.py),
            (lambda: self.part(at.px, 1), self.from_x(1), at.px),
            (lambda: self.part(at.py, 0), self.from_y(0), at.py),
            (lambda: self.part(at.py, 1), self.from_y(1), at.py),
            (lambda: self.part(at.px, 0), self.from_x(0), at.px),
        )[i]
        return remote(src(), dst, self.sends.at[i], self.recvs.at[i], to, at.c)

    def start(self):
        for i in range(4):
            self.copy(i).start()

    def combine(self):
        at = self.at
        for i, via, p, h in ((0, self.via_x, at.py, 1), (1, self.via_y, at.px, 0)):
            self.copy(i).wait_recv()
            ref = self.part(p, h)
            ref[...] = (ref[...].astype(F32) + via[...].astype(F32)).astype(BF16)
            self.copy(4 + i).start()

    def total(self, h):
        for i in ((5, 3), (2, 4))[h]:
            self.copy(i).wait_recv()
        return self.part(self.at.dp, h)[...].astype(F32) + self.from_x(h)[...].astype(F32) + self.from_y(h)[...].astype(F32)

    def drain(self):
        for i in range(6):
            self.copy(i).wait_send()


def blocks(count, body, hooks=None):
    hooks = hooks or {}

    def one(i, carry):
        body(i)
        for index, events in hooks.items():

            @pl.when(i == index)
            def _():
                for event in events:
                    event()

        return carry

    lax.fori_loop(0, count, one, 0)


def fused_kernel(ndp, n, dims, *refs):
    mb, tok, width, seq, heads, rows_w, rows_d = dims
    nz, block, every = n // 2, 2 * tok, ndp * n
    fu = ndp * rows_d
    (tok_ref, cot_ref, rq_ref, ru_ref, wd_ref, wo_ref, vec_ref, seg_ref, cos_ref, sin_ref) = refs[:10]
    (mixed_out, grad_out, qkv_out, up_out, dwd_out, dwo_out, vec_out) = refs[10:17]
    (xs, gs, ws, wdo, vecs, segs, seg_col, cos_t, sin_t, g1, s1, g2, s2, bo, bq, bu, qkv, hid, gp, stat, ctx, part, ep, dctx, dqkv,
     dk, dv, acc_gain, acc_bu, acc_bq, m_sib, m_in, t_sib, t_in, dwq, dwu, dwdo, q_via, q_from, u_via, u_from, d_via, d_from, vsum, vin, wq_st, wu_st,
     own, dwo_st, vsum_all, v_st, seg_i, wp_st, wq_rx, wu_rx, v_rx, h1_all, h2_all) = refs[17:75]
    probs = refs[75 : 75 + nz]
    (x_s, x_r, c_s, c_r, w1s, w1r, w2s, w2r, v1s, v1r, v2s, v2r, d_s, d_r, o1s, o1r,
     ms_s, ms_r, mu_s, mu_r, md_s, md_r, ts_s, ts_r, tu_s, tu_r, td_s, td_r,
     gq1s, gq1r, gq2s, gq2r, gu1s, gu1r, gu2s, gu2r, gd_s, gd_r, go2s, go2r, gv1s, gv1r, gv2s, gv2r, local) = refs[75 + nz :]
    at = Place(ndp, n)
    at.barrier(True, True, True)
    raw_q, raw_u, raw_t, raw_c = qkv_out, up_out, mixed_out, grad_out
    own_rows = pl.ds(pl.multiple_of(at.c * tok, tok), tok)

    cols = Exchange(at, "ctx", lambda p: wp_st.at[p], lambda s: ws.at[at.dp, s], w1s, w1r)
    vec1 = Exchange(at, "ctx", lambda p: vec_ref, lambda s: vecs.at[at.dp, s], v1s, v1r)
    plane_w = PlaneGather(at, lambda p, h: ws.at[p, pl.ds(h * (n // 2), n // 2)], w2s, w2r)
    plane_v = Exchange(at, "dp", lambda p: vecs.at[at.dp], lambda s: vecs.at[s], v2s, v2r)
    rows_do = rows_d + rows_w
    plane_d = PlaneGather(at, lambda p, h: wdo.at[p, pl.ds(h * (rows_do // 2), rows_do // 2)], d_s, d_r)
    def gather(dst, sends, recvs, counts, s):
        size, first = tok // counts[s], sum(counts[:s])
        return Pieces([SeqGather(at, dst.at[s], tok, h * size, size, sends.at[first + h], recvs.at[first + h]) for h in range(counts[s])])

    x_ag = [gather(xs, x_s, x_r, CUT_TOKENS, s) for s in range(mb)]
    c_ag = [gather(gs, c_s, c_r, CUT_COTANGENT, s) for s in range(mb)]
    copies = [
        pltpu.make_async_copy(rq_ref, raw_q, local.at[0]),
        pltpu.make_async_copy(ru_ref, raw_u, local.at[9]),
        pltpu.make_async_copy(vec_ref, vecs.at[at.dp, at.c], local.at[1]),
        pltpu.make_async_copy(wd_ref, wdo.at[at.dp, pl.ds(0, rows_d)], local.at[2]),
        pltpu.make_async_copy(seg_ref, seg_i, local.at[3]),
        pltpu.make_async_copy(cos_ref, cos_t, local.at[4]),
        pltpu.make_async_copy(sin_ref, sin_t, local.at[5]),
        pltpu.make_async_copy(tok_ref, raw_t, local.at[6]),
        pltpu.make_async_copy(cot_ref, raw_c, local.at[7]),
    ]
    out_rows = remote(wo_ref, wdo.at[at.rows_dp, pl.ds(rows_d, rows_w)], o1s, o1r, at.rows_dp, at.rows_c)
    out_mine = remote(wo_ref, wdo.at[at.dp, pl.ds(rows_d, rows_w)], o1s, o1r, at.rows_dp, at.rows_c)
    own_out = pltpu.make_async_copy(wo_ref, wdo.at[at.dp, pl.ds(rows_d, rows_w)], local.at[8])
    for copy in copies:
        copy.start()
    vec1.start()

    @pl.when(at.moves)
    def _():
        out_rows.start()

    @pl.when(jnp.logical_not(at.moves))
    def _():
        own_out.start()

    copies[0].wait()
    copies[1].wait()
    for p in range(n):
        for part_ in range(3):
            wp_st[p, :, part_ * 128 : (part_ + 1) * 128] = raw_q[:, part_ * width + p * 128 : part_ * width + (p + 1) * 128]
        for d in range(ndp):
            wp_st[p, :, 384 + d * rows_d : 384 + (d + 1) * rows_d] = raw_u[:, (d * n + p) * rows_d : (d * n + p + 1) * rows_d]
    cols.start()
    ws[at.dp, at.c] = wp_st[at.c]
    for copy in copies[2:]:
        copy.wait()
    for s in range(mb):
        xs[s, own_rows] = raw_t[:, s, :]
        gs[s, own_rows] = raw_c[:, s, :]
    segs[...] = jnp.zeros_like(segs)
    segs[0:mb] = seg_i[...]
    cols.wait_recv()
    plane_w.start()
    x_ag[0].start()
    vec1.wait_recv()
    plane_v.start()
    x_ag[0].step(1)
    plane_w.forward()
    x_ag[0].step(2)
    c_ag[0].start()

    @pl.when(at.moves)
    def _():
        out_mine.wait_recv()

    @pl.when(jnp.logical_not(at.moves))
    def _():
        own_out.wait()

    plane_d.start()
    plane_v.wait_recv()

    lane = lax.broadcasted_iota(jnp.int32, (16, 128), 1)
    per = 128 // rows_w
    for q in range(width // 128):
        piece = vecs[(per * q) // n, (per * q) % n]
        for u in range(1, per):
            d = per * q + u
            piece = jnp.where(lane >= u * rows_w, vecs[d // n, d % n], piece)
        span = pl.ds(q * 128, 128)
        bo[:, span] = piece[3:4] + piece[8:9]
        for ref, r in ((g1, 9), (s1, 10), (g2, 11), (s2, 12)):
            ref[:, span] = piece[r : r + 1]
    lane1 = lax.broadcasted_iota(jnp.int32, (1, 128), 1)
    for d in range(ndp):
        rows = vecs[d, at.c]
        piece = rows[4:5]
        for u in range(1, per):
            piece = jnp.where(lane1 >= u * rows_w, rows[4 + u : 5 + u], piece)
        bu[:, pl.ds(d * 128, 128)] = piece
    for p in range(3):
        piece = None
        for u in range(per):
            t = (p * width + at.c * 128) // rows_w + u
            d, r = t // 3, lax.rem(t, 3)
            rows = vecs[d // n, lax.rem(d, n)]
            row = jnp.where(r == 0, rows[0:1], jnp.where(r == 1, rows[1:2], rows[2:3]))
            piece = row if piece is None else jnp.where(lane1 >= u * rows_w, row, piece)
        bq[:, pl.ds(p * 128, 128)] = piece
    seg_t = jnp.transpose(segs[...])
    seg_col[...] = jnp.where(seg_t == 0.0, -1.0, seg_t)

    lanes = lax.broadcasted_iota(jnp.int32, (1, 128), 1)
    in_head = [(lanes >= h * HEAD) & (lanes < (h + 1) * HEAD) for h in range(heads)]
    low_half = (lanes & (HEAD - 1)) < ROT // 2
    w_q = lambda: ws[:, :, :, :384].reshape(width, 384)
    w_u = lambda: ws[:, :, :, 384:].reshape(width, fu)
    w_d = lambda: wdo[:, 0:rows_d].reshape(fu, width)
    w_o = lambda: wdo[:, rows_d:].reshape(128, width)

    def rows_of(i):
        return pl.ds(pl.multiple_of(i * block, block), block)

    def turn(u, rows, sign):
        turned = jnp.where(low_half, pltpu.roll(u, 128 - ROT // 2, 1), pltpu.roll(u, ROT // 2, 1))
        if sign > 0:
            return u * cos_t[rows] + turned * sin_t[rows]
        return u * cos_t[rows] - turned * sin_t[rows]

    def normed_of(s, rows):
        return (xs[s, rows].astype(F32) - stat[s, rows, 0:1]) * stat[s, rows, 1:2]

    def forward_one(s):
        def body(i):
            rows = rows_of(i)
            x = xs[s, rows].astype(F32)
            mean = jnp.mean(x, axis=-1, keepdims=True)
            cen = x - mean
            rstd = lax.rsqrt(jnp.mean(cen * cen, axis=-1, keepdims=True) + 1e-05)
            stat[s, rows, 0:1] = mean
            stat[s, rows, 1:2] = rstd
            nrm = cen * rstd
            h1 = (nrm * g1[...] + s1[...]).astype(BF16)
            h1_all[s, rows] = h1
            joined = dot(h1, w_q()) + bq[...]
            qkv[s, rows, 0:128] = (turn(joined[:, 0:128], rows, 1).astype(BF16).astype(F32) * (HEAD ** (-0.5))).astype(BF16)
            qkv[s, rows, 128:256] = turn(joined[:, 128:256], rows, 1).astype(BF16)
            qkv[s, rows, 256:384] = joined[:, 256:384].astype(BF16)
            h2 = (nrm * g2[...] + s2[...]).astype(BF16)
            h2_all[rows] = h2
            act = dot(h2, w_u()) + bu[...]
            cdf = 0.5 + 0.5 * lax.erf(act * (0.5 ** 0.5))
            hid[s, rows] = (act * cdf).astype(BF16)
            gp[rows] = (cdf + act * (jnp.exp(-0.5 * act * act) * 0.3989422804014327)).astype(BF16)

        return body

    def attend(s, i):
        rows = pl.ds(i * block, block)
        keys = (i + 1) * block
        q_pos = lax.broadcasted_iota(jnp.int32, (block, keys), 0) + i * block
        k_pos = lax.broadcasted_iota(jnp.int32, (block, keys), 1)
        same = segs[s : s + 1, 0:keys] == seg_col[rows, s : s + 1]
        allow = (same & (k_pos <= q_pos)) | (k_pos == q_pos)
        q, k, v = qkv[s, rows, 0:128], qkv[s, 0:keys, 128:256], qkv[s, 0:keys, 256:384]
        out = None
        for h in range(heads):
            scores = dot(jnp.where(in_head[h], q, jnp.zeros_like(q)), k, NT)
            scores = jnp.where(allow, scores, -1e30)
            e = jnp.exp(scores - jnp.max(scores, axis=-1, keepdims=True))
            p = (e * (1.0 / jnp.sum(e, axis=-1, keepdims=True))).astype(BF16)
            probs[i][h] = p
            o = dot(p, v)
            out = o if out is None else jnp.where(in_head[h], o, out)
        ctx[s, rows] = out.astype(BF16)

    def project(s):
        def body(i):
            rows = rows_of(i)
            both = dot(ctx[s, rows], w_o()) + dot(hid[s, rows], w_d())
            part[s, rows] = both.astype(BF16)

        return body

    def fold(ref, row, value):
        count, cols_ = value.shape
        ref[row, :, 0:cols_] += jnp.sum(value.reshape(count // 8, 8, cols_), axis=0)

    def backward_ffn(s):
        def body(i):
            rows = rows_of(i)
            g = gs[s, rows]
            dctx[s, rows] = dot(g, w_o(), NT).astype(BF16)
            d_act = (dot(g, w_d(), NT) * gp[rows].astype(F32)).astype(BF16)
            gp[rows] = d_act
            fold(acc_gain, 4, g.astype(F32))
            fold(acc_bu, 0, d_act.astype(F32))
            d_h = dot(d_act, w_u(), NT)
            fold(acc_gain, 2, d_h * normed_of(s, rows))
            fold(acc_gain, 3, d_h)
            ep[s, rows] = (d_h * g2[...]).astype(BF16)

        return body

    def attend_back(s, i):
        rows = pl.ds(i * block, block)
        keys = (i + 1) * block
        span = pl.ds(0, keys)
        q, k, v = qkv[s, rows, 0:128], qkv[s, span, 128:256], qkv[s, span, 256:384]
        d_c = dctx[s, rows]
        zero = jnp.zeros_like(q)
        d_q = None
        for h in range(heads):
            p = probs[i][h]
            d_h = jnp.where(in_head[h], d_c, zero)
            d_p = dot(d_h, v, NT)
            p_f = p.astype(F32)
            delta = jnp.sum(p_f * d_p, axis=-1, keepdims=True)
            d_s = (p_f * (d_p - delta)).astype(BF16)
            o = dot(d_s, k)
            d_q = o if d_q is None else jnp.where(in_head[h], o, d_q)
            d_k = dot(jnp.where(in_head[h], q, zero), d_s, TN)
            d_v = dot(d_h, p, TN)
            if i == nz - 1 and h == 0:
                dk[...] = d_k
                dv[...] = d_v
            else:
                dk[:, span] += d_k
                dv[:, span] += d_v
        d_q = turn(d_q, rows, -1) * (HEAD ** (-0.5))
        d_k, d_v = jnp.transpose(dk[:, rows]), jnp.transpose(dv[:, rows])
        d_all = jnp.concatenate([d_q, turn(d_k, rows, -1), d_v], axis=1).astype(BF16)
        dqkv[s, rows] = d_all
        fold(acc_bq, 0, d_all.astype(F32))
        d_n = dot(d_all, w_q(), NT)
        fold(acc_gain, 0, d_n * normed_of(s, rows))
        fold(acc_gain, 1, d_n)
        ep[s, rows] = (d_n * g1[...] + ep[s, rows].astype(F32)).astype(BF16)

    def put(ref, rows, s, total):
        if s:
            total = total + ref[rows].astype(F32).reshape(total.shape)
        ref[rows] = total.astype(BF16).reshape(ref[rows].shape)

    def weight_cols(s, out, left, right):
        def body(kt):
            feat = pl.ds(pl.multiple_of(kt * 256, 256), 256)
            put(out, feat, s, dot(left[:, feat], right[...], TN))

        return body

    acc_gain[...] = jnp.zeros_like(acc_gain)
    acc_bu[...] = jnp.zeros_like(acc_bu)
    acc_bq[...] = jnp.zeros_like(acc_bq)

    def scatter(part_, sib_, in_, sems_, counts, s):
        size, first = tok // counts[s], sum(counts[:s])
        return ScatterPieces([SeqScatter(at, part_.at[s], sib_.at[s], in_.at[s], tok, h * size, size, [r.at[first + h] for r in sems_]) for h in range(counts[s])])

    m_rs = [scatter(part, m_sib, m_in, (ms_s, ms_r, mu_s, mu_r, md_s, md_r), CUT_MIXED, s) for s in range(mb)]
    t_rs = [scatter(ep, t_sib, t_in, (ts_s, ts_r, tu_s, tu_r, td_s, td_r), CUT_GRAD, s) for s in range(mb)]
    rows_p = n * rows_w

    def col_halves(ref):
        return lambda p, h: ref.at[pl.ds(pl.multiple_of(p * rows_p + h * (rows_p // 2), rows_p // 2), rows_p // 2)]

    def halves(ref, i, size):
        return lambda h: ref.at[i, pl.ds(h * size, size)]

    half = rows_p // 2
    wq1 = PlaneReduce(at, col_halves(dwq), q_via.at[0], q_via.at[1], halves(q_from, 0, half), halves(q_from, 1, half), gq1s, gq1r)
    wu1 = PlaneReduce(at, col_halves(dwu), u_via.at[0], u_via.at[1], halves(u_from, 0, half), halves(u_from, 1, half), gu1s, gu1r)
    half_do = rows_do // 2
    wd1 = PlaneReduce(at, lambda p, h: dwdo.at[p, pl.ds(h * half_do, half_do)], d_via.at[0], d_via.at[1],
                      halves(d_from, 0, half_do), halves(d_from, 1, half_do), gd_s, gd_r)
    gv1 = Exchange(at, "dp", lambda p: vsum, lambda s: vin.at[s], gv1s, gv1r)
    wq2 = Exchange(at, "ctx", lambda p: wq_st.at[p], lambda s: wq_rx.at[s], gq2s, gq2r)
    wu2 = Exchange(at, "ctx", lambda p: wu_st.at[p], lambda s: wu_rx.at[s], gu2s, gu2r)
    gv2 = Exchange(at, "ctx", lambda p: v_st.at[p], lambda s: v_rx.at[s], gv2s, gv2r)
    out_back = remote(dwo_st, dwo_out, go2s, go2r, at.from_dp, at.from_c)

    def columns_on(first_hop, second_hop, stage, out):
        for h in (0, 1):
            total = first_hop.total(h).astype(BF16)
            stage[pl.ds(h * (n // 2), n // 2)] = total.reshape((n // 2,) + stage.shape[1:])
        second_hop.start()
        out[at.c] = stage[at.c]

    def down_out():
        low, high = wd1.total(0), wd1.total(1)
        dwd_out[pl.ds(0, half_do)] = low
        dwd_out[pl.ds(half_do, rows_d - half_do)] = high[0 : rows_d - half_do]
        rows = high[rows_d - half_do :].astype(BF16)

        @pl.when(at.moves)
        def _():
            dwo_st[...] = rows
            out_back.start()

        @pl.when(jnp.logical_not(at.moves))
        def _():
            dwo_out[...] = rows

    def vectors_out():
        mine = v_rx[at.c]
        index = at.dp * n + at.c
        start = index * (3 * rows_w)
        shift, tile = lax.rem(start, 128), start // 128

        def tile_of(t):
            rows = v_rx[lax.rem(t, n)]
            third = t // n
            return jnp.where(third == 0, rows[8:9], jnp.where(third == 1, rows[9:10], rows[10:11]))

        low, high = tile_of(tile), tile_of(jnp.minimum(tile + 1, 3 * n - 1))
        both = low
        for u in range(1, 128 // rows_w):
            off = u * rows_w
            moved = jnp.where(lane1 < 128 - off, pltpu.roll(low, 128 - off, 1), pltpu.roll(high, 128 - off, 1))
            both = jnp.where(shift == off, moved, both)
        place = lax.rem(index * rows_w, 128)
        base = v_rx[0, 0:8]
        for p in range(1, n):
            base = base + v_rx[p, 0:8]
        row = lax.broadcasted_iota(jnp.int32, (8, 128), 0)
        base = jnp.where(row < 6, base, mine[0:8])
        out = base
        for u in range(1, 128 // rows_w):
            out = jnp.where(place == u * rows_w, pltpu.roll(base, 128 - u * rows_w, 1), out)
        vec_out[...] = out
        vec_out[0:1] = both
        vec_out[1:2] = mine[11:12]
        vec_out[7:8] = out[6:7]

    def starts(rs, zs):
        def event():
            for z in zs:
                rs.cross(z).start()

        return event

    def finish_mixed(s):
        m_rs[s].total(own)
        mixed_out[:, s, :] = (xs[s, own_rows].astype(F32) + own[...] + bo[...]).astype(BF16)

    def finish_grad(s):
        t_rs[s].total(own)
        e = own[...]
        nrm = normed_of(s, own_rows)
        inner = e - jnp.mean(e, axis=-1, keepdims=True) - nrm * jnp.mean(e * nrm, axis=-1, keepdims=True)
        grad_out[:, s, :] = (gs[s, own_rows].astype(F32) + stat[s, own_rows, 1:2] * inner).astype(BF16)

    def down_rows(s):
        def body(kt):
            feat = pl.ds(pl.multiple_of(kt * 256, 256), 256)
            total = dot(hid[s, :, feat], gs[s], TN).reshape(256 // rows_d, rows_d, width)
            mine = dwdo.at[pl.ds(kt * (256 // rows_d), 256 // rows_d), pl.ds(0, rows_d)]
            if s:
                total = total + mine[...].astype(F32)
            mine[...] = total.astype(BF16)

        return body

    def out_grad(s):
        total = dot(ctx[s], gs[s], TN).reshape(ndp, rows_w, width)
        mine = dwdo.at[:, pl.ds(rows_d, rows_w)]
        if s:
            total = total + mine[...].astype(F32)
        mine[...] = total.astype(BF16)

    x_ag[0].step(3)
    plane_w.land()
    x_ag[0].land()
    blocks(nz, forward_one(0), {3: [lambda: c_ag[0].step(1), x_ag[1].start]})
    plane_d.forward()
    for i in range(nz):
        attend(0, i)
    c_ag[0].step(2)
    plane_d.land()
    blocks(nz, project(0))
    starts(m_rs[0], range(nz))()
    m_rs[0].step(0)
    back = backward_ffn(0)
    c_ag[0].take(0, back)
    x_ag[1].step(1)
    c_ag[1].start()
    c_ag[0].take(1, back)
    c_ag[0].take(2, back)
    c_ag[0].step(3)
    c_ag[0].take(3, back)
    m_rs[0].step(1)
    for i in reversed(range(nz)):
        attend_back(0, i)
        t_rs[0].cross(i).start()
        if i == 3:
            x_ag[1].step(2)
        if i == 1:
            m_rs[0].step(2)
    t_rs[0].step(0)
    blocks(width // 256, weight_cols(0, dwu, h2_all, gp))
    ahead = forward_one(1)
    x_ag[1].take(0, ahead)
    c_ag[1].step(1)
    x_ag[1].take(1, ahead)
    x_ag[1].take(2, ahead)
    x_ag[1].step(3)
    x_ag[1].take(3, ahead)
    t_rs[0].step(1)
    for i in range(nz):
        attend(1, i)
        if i == 2:
            c_ag[1].step(2)
    blocks(nz, project(1))
    starts(m_rs[1], range(nz))()
    m_rs[1].lead()
    t_rs[0].step(2)
    blocks(width // 256, weight_cols(0, dwq, h1_all.at[0], dqkv.at[0]))
    blocks(fu // 256, down_rows(0))
    out_grad(0)
    back = backward_ffn(1)
    c_ag[1].take(0, back)
    c_ag[1].take(1, back)
    m_rs[1].follow(1)
    c_ag[1].take(2, back)
    c_ag[1].step(3)
    c_ag[1].take(3, back)
    blocks(width // 256, weight_cols(1, dwu, h2_all, gp))
    wu1.start()
    for i in reversed(range(nz)):
        attend_back(1, i)
        t_rs[1].cross(i).start()
        if i < nz - 1:
            t_rs[1].lead_up(nz - 2 - i)
        if i == 1:
            wu1.combine()
            m_rs[1].follow(2)
    for t in range(nz - 1):
        t_rs[1].lead_down(t)
    blocks(width // 256, weight_cols(1, dwq, h1_all.at[1], dqkv.at[1]))
    wq1.start()
    vsum[...] = jnp.zeros_like(vsum)
    vsum[0:1, 0:384] = jnp.sum(acc_bq[0], axis=0, keepdims=True)
    vsum[1:2, 0:fu] = jnp.sum(acc_bu[0], axis=0, keepdims=True)
    for r in range(5):
        vsum[2 + r : 3 + r] = jnp.sum(acc_gain[r], axis=0, keepdims=True)
    gv1.start()
    columns_on(wu1, wu2, wu_st, wu_rx)
    blocks(fu // 256, down_rows(1))
    out_grad(1)
    t_rs[1].follow(1)
    wq1.combine()
    wd1.start()
    finish_mixed(0)
    finish_mixed(1)
    finish_grad(0)
    columns_on(wq1, wq2, wq_st, wq_rx)
    t_rs[1].follow(2)
    gv1.wait_recv()
    total = vsum[...]
    for j in range(1, ndp):
        total = total + vin[lax.rem(at.dp + j, ndp)]
    vsum_all[...] = total
    for p in range(n):
        v_st[p, 0:8] = vsum_all[:, pl.ds(pl.multiple_of((at.dp * n + p) * rows_w // 128 * 128, 128), 128)]
        for r in range(3):
            v_st[p, 8 + r : 9 + r] = total[0:1, r * 128 : (r + 1) * 128]
        v_st[p, 11:12] = vsum_all[1:2, pl.ds(pl.multiple_of(at.dp * rows_d, 128), 128)]
        v_st[p, 12:16] = jnp.zeros((4, 128), F32)
    gv2.start()
    v_rx[at.c] = v_st[at.c]
    wd1.combine()
    finish_grad(1)
    down_out()

    @pl.when(at.moves)
    def _():
        out_rows.wait_send()
        out_back.wait()

    wu2.wait_recv()
    for p in range(n):
        for d in range(ndp):
            up_out[:, (d * n + p) * rows_d : (d * n + p + 1) * rows_d] = wu_rx[p, :, d * rows_d : (d + 1) * rows_d]
    gv2.wait_recv()
    vectors_out()
    wq2.wait_recv()
    for p in range(n):
        for part_ in range(3):
            qkv_out[:, part_ * width + p * 128 : part_ * width + (p + 1) * 128] = wq_rx[p, :, part_ * 128 : (part_ + 1) * 128]
    for part_ in (cols, vec1, plane_v, gv1, wq2, wu2, gv2):
        part_.wait_send()
    for part_ in (plane_w, plane_d, wq1, wu1, wd1):
        part_.drain()
    for s in range(mb):
        x_ag[s].drain()
        c_ag[s].drain()
        m_rs[s].drain()
        t_rs[s].drain()


def fused_layer(ndp, n, dims, tok, cot, rq, ru, wd, wo, vec, seg, cosine, sine):
    mb, tk, width, seq, heads, rows_w, rows_d = dims
    nz, block, fu = n // 2, 2 * tk, ndp * rows_d
    rows_do, rows_p = rows_d + rows_w, n * rows_w
    dma = pltpu.SemaphoreType.DMA
    vm = pltpu.VMEM
    vmem = pl.BlockSpec(memory_space=pltpu.VMEM)
    slots = gather_slots(nz)
    scratch = [
        vm((mb, seq, width), BF16), vm((mb, seq, width), BF16),
        vm((ndp, n, rows_w, 384 + fu), BF16), vm((ndp, rows_d + rows_w, width), BF16),
        vm((ndp, n, 16, 128), F32), vm((8, seq), F32), vm((seq, 8), F32), vm((seq, 128), F32), vm((seq, 128), F32),
        vm((1, width), F32), vm((1, width), F32), vm((1, width), F32), vm((1, width), F32), vm((1, width), F32),
        vm((1, 384), F32), vm((1, fu), F32),
        vm((mb, seq, 384), BF16), vm((mb, seq, fu), BF16), vm((seq, fu), BF16), vm((mb, seq, 2), F32),
        vm((mb, seq, 128), BF16), vm((mb, seq, width), BF16), vm((mb, seq, width), BF16),
        vm((mb, seq, 128), BF16), vm((mb, seq, 384), BF16), vm((128, seq), F32), vm((128, seq), F32),
        vm((5, 8, width), F32), vm((1, 8, fu), F32), vm((1, 8, 384), F32),
        vm((mb, nz, tk, width), BF16), vm((mb, nz + 1, tk, width), BF16), vm((mb, nz, tk, width), BF16), vm((mb, nz + 1, tk, width), BF16),
        vm((width, 384), BF16), vm((width, fu), BF16), vm((ndp, rows_do, width), BF16),
        vm((2, rows_p // 2, 384), BF16), vm((2, rows_p, 384), BF16), vm((2, rows_p // 2, fu), BF16), vm((2, rows_p, fu), BF16),
        vm((2, rows_do // 2, width), BF16), vm((2, rows_do, width), BF16),
        vm((8, width), F32), vm((ndp, 8, width), F32), vm((n, rows_w, 384), BF16), vm((n, rows_w, fu), BF16),
        vm((tk, width), F32), vm((rows_w, width), BF16),
        vm((8, width), F32), vm((n, 16, 128), F32),
        vm((mb, seq), F32), vm((n, rows_w, 384 + fu), BF16),
        vm((n, rows_w, 384), BF16), vm((n, rows_w, fu), BF16), vm((n, 16, 128), F32),
        vm((mb, seq, width), BF16), vm((seq, width), BF16),
    ] + [vm((heads, block, block * (i + 1)), BF16) for i in range(nz)]
    per_seq = [dma((sum(cuts), size)) for cuts in (CUT_TOKENS, CUT_COTANGENT) for size in (3 * nz - 2, n)]
    to_ctx, to_dp, plane = [dma((n,))] * 2, [dma((ndp,))] * 2, [dma((6,))] * 2
    sems = per_seq + to_ctx + plane + to_ctx + to_dp + plane + [dma, dma]
    sems += [dma((sum(CUT_MIXED), nz))] * 6 + [dma((sum(CUT_GRAD), nz))] * 6
    sems += (plane + to_ctx) * 2 + plane + [dma, dma] + to_dp + to_ctx + [dma((10,))]
    return pl.pallas_call(
        partial(fused_kernel, ndp, n, dims),
        out_shape=(
            jax.ShapeDtypeStruct((tk, mb, width), BF16),
            jax.ShapeDtypeStruct((tk, mb, width), BF16),
            jax.ShapeDtypeStruct((rows_w, 3 * width), BF16),
            jax.ShapeDtypeStruct((rows_w, n * fu), BF16),
            jax.ShapeDtypeStruct((rows_d, width), F32),
            jax.ShapeDtypeStruct((rows_w, width), BF16),
            jax.ShapeDtypeStruct((8, 128), F32),
        ),
        in_specs=[ANY] * 10,
        out_specs=[vmem] * 7,
        scratch_shapes=scratch + sems,
        compiler_params=pltpu.CompilerParams(collective_id=5, has_side_effects=True, vmem_limit_bytes=63 * MIB),
    )(tok, cot, rq, ru, wd, wo, vec, seg, cosine, sine)


def rotary_lanes(seq):
    half = ROT // 2
    inverse = (np.float32(10000.0) ** (-(np.float32(2.0) * np.arange(half, dtype=np.float32)) / np.float32(ROT))).astype(np.float32)
    angles = (np.arange(seq, dtype=np.float32)[:, None] * inverse[None, :]).astype(np.float32)
    cosine = np.ones((seq, HEAD), np.float32)
    sine = np.zeros((seq, HEAD), np.float32)
    cosine[:, :half] = cosine[:, half:ROT] = np.cos(angles)
    sine[:, :half] = -np.sin(angles)
    sine[:, half:ROT] = np.sin(angles)
    return np.tile(cosine, (1, 128 // HEAD)), np.tile(sine, (1, 128 // HEAD))


def fused_device(ndp, n, tokens, cotangent, segments, w_qkv, b_qkv, w_out, b_out, w_up, b_up, w_down, b_down, g1, s1, g2, s2):
    tok, mb, width = tokens.shape
    seq = segments.shape[1]
    hc = width // n
    rows_w, rows_d = w_qkv.shape[0], w_down.shape[0]
    seg_f = segments.astype(F32)
    seg_f, small = lax.optimization_barrier((seg_f, (b_qkv, b_out, b_up, b_down, g1, s1, g2, s2)))
    units = jnp.concatenate(small).astype(F32).reshape(-1, rows_w)
    vec = jnp.pad(jnp.tile(units, (1, 128 // rows_w)), ((0, 16 - units.shape[0]), (0, 0)))
    cosine, sine = rotary_lanes(seq)
    dims = (mb, tok, width, seq, hc // HEAD, rows_w, rows_d)
    mixed, t_grad, d_qkv, d_up, dwd, dwo, dv = fused_layer(
        ndp, n, dims, tokens, cotangent, w_qkv, w_up, w_down, w_out, vec, seg_f, jnp.asarray(cosine), jnp.asarray(sine)
    )
    one = lambda r: dv[r, :rows_w]
    return (
        mixed,
        t_grad,
        d_qkv.astype(F32),
        dv[0, : b_qkv.shape[0]],
        dwo.astype(F32),
        one(6),
        d_up.astype(F32),
        dv[1, :rows_d],
        dwd,
        one(7),
        one(2),
        one(3),
        one(4),
        one(5),
    )


def rotary_tables(seq):
    half_rot = ROT // 2
    inverse = 10000.0 ** (-(2.0 * jnp.arange(half_rot, dtype=F32)) / ROT)
    angles = jnp.arange(seq, dtype=jnp.int32).astype(F32)[:, None] * inverse[None, :]
    angles = jnp.concatenate([angles, angles], axis=-1)
    return (jnp.cos(angles)[None, :, None, :], jnp.sin(angles)[None, :, None, :])


def rotate(values, cosine, sine, back=False):
    half_rot = ROT // 2
    lead = values[..., :ROT]
    if back:
        u = lead * sine
        turned = jnp.concatenate([u[..., half_rot:], -u[..., :half_rot]], axis=-1)
        return jnp.concatenate([lead * cosine + turned, values[..., ROT:]], axis=-1)
    turned = jnp.concatenate([-lead[..., half_rot:], lead[..., :half_rot]], axis=-1)
    return jnp.concatenate([lead * cosine + turned * sine, values[..., ROT:]], axis=-1)


def per_device(ndp, n, tokens, cotangent, segments, w_qkv, b_qkv, w_out, b_out, w_up, b_up, w_down, b_down, g1, s1, g2, s2):
    tok, mb, width = tokens.shape
    seq = segments.shape[1]
    heads_all = width // HEAD
    hc = width // n
    heads = hc // HEAD
    rows_w = w_qkv.shape[0]
    rows_d = w_down.shape[0]
    fu = ndp * rows_d
    c = lax.axis_index("ctx")
    dp = lax.axis_index("dp")
    scale = HEAD ** (-0.5)

    cot = jnp.transpose(cotangent, (1, 0, 2))
    toks = jnp.transpose(tokens, (1, 0, 2))
    qkv_cols = w_qkv.reshape(rows_w, 3, n, hc).transpose(2, 0, 1, 3).reshape(n, rows_w, 3 * hc)
    up_cols = w_up.reshape(rows_w, ndp, n, rows_d).transpose(2, 0, 1, 3).reshape(n, rows_w, fu)
    wp = jnp.concatenate([qkv_cols, up_cols], axis=2)
    shard_vecs = (b_qkv, b_out, b_up, b_down, g1, s1, g2, s2)
    sizes = [v.shape[0] for v in shard_vecs]
    vec = jnp.concatenate(shard_vecs)
    lanes = 128
    per_vec = 16 * lanes
    vec = jnp.pad(vec, (0, per_vec - vec.shape[0])).reshape(16, lanes)
    x, g, w, wd, wo, vecs = gather_all(ndp, n, toks, cot, wp, w_down, w_out, vec)
    w = w.reshape(width, 3 * hc + fu)
    wq, wu = w[:, : 3 * hc], w[:, 3 * hc :]
    wd = wd.reshape(fu, width)
    wo = wo.reshape(hc, width)
    flat = vecs.reshape(ndp * n, per_vec).astype(F32)
    starts = [sum(sizes[:i]) for i in range(len(sizes))]
    full = [flat[:, s : s + z].reshape(-1) for s, z in zip(starts, sizes)]
    bq_all, bo, bu_all, bd, gain1, shift1, gain2, shift2 = full
    bq = lax.dynamic_index_in_dim(bq_all.reshape(3, n, hc), c, 1, keepdims=False).reshape(3 * hc)
    bu = lax.dynamic_index_in_dim(bu_all.reshape(ndp, n, rows_d), c, 1, keepdims=False).reshape(fu)

    xf = x.reshape(mb * seq, width).astype(F32)
    gl = g.reshape(mb * seq, width)
    mean = jnp.mean(xf, axis=-1, keepdims=True)
    cen = xf - mean
    rstd = lax.rsqrt(jnp.mean(cen * cen, axis=-1, keepdims=True) + 1e-05)
    normed = cen * rstd
    h1 = (normed * gain1 + shift1).astype(BF16)
    h2 = (normed * gain2 + shift2).astype(BF16)
    joined = (dot(h1, wq) + bq).reshape(mb, seq, 3, heads, HEAD)
    cosine, sine = rotary_tables(seq)
    q = rotate(joined[:, :, 0], cosine, sine).astype(BF16)
    k = rotate(joined[:, :, 1], cosine, sine).astype(BF16)
    v = joined[:, :, 2].astype(BF16)
    pos = jnp.arange(seq, dtype=jnp.int32)
    same = (segments[:, None, :] == segments[:, :, None]) & (segments[:, :, None] > 0)
    allow = (same & (pos[None, None, :] <= pos[None, :, None])) | (pos[None, None, :] == pos[None, :, None])
    scores = jnp.einsum("sqhd,skhd->shqk", q, k, preferred_element_type=F32) * scale
    scores = jnp.where(allow[:, None], scores, -1e30)
    top = jnp.max(scores, axis=-1, keepdims=True)
    e = jnp.exp(scores - top)
    probs = e / jnp.sum(e, axis=-1, keepdims=True)
    pl_low = probs.astype(BF16)
    ctx_f = jnp.einsum("shqk,skhd->sqhd", pl_low, v, preferred_element_type=F32)
    ctx = ctx_f.astype(BF16).reshape(mb * seq, hc)
    act = dot(h2, wu) + bu
    hidden = jax.nn.gelu(act, approximate=False).astype(BF16)
    part = (dot(ctx, wo) + dot(hidden, wd)).astype(BF16).reshape(mb, seq, width)
    mixed_sum = scatter_ctx(ndp, n, part, 1)
    mixed = (toks.astype(F32) + mixed_sum + bo + bd).astype(BF16)

    gf = gl.astype(F32)
    d_wd = dot(hidden, gl, ((0,), (0,)))
    d_wo = dot(ctx, gl, ((0,), (0,)))
    d_hidden = dot(gl, wd, ((1,), (1,)))
    _, pull = jax.vjp(partial(jax.nn.gelu, approximate=False), act)
    d_act = pull(d_hidden)[0].astype(BF16)
    d_wu = dot(h2, d_act, ((0,), (0,)))
    d_bu = jnp.sum(d_act.astype(F32), axis=0)
    d_h2 = dot(d_act, wu, ((1,), (1,)))
    d_ctx = dot(gl, wo, ((1,), (1,))).astype(BF16).reshape(mb, seq, heads, HEAD)
    d_probs = jnp.einsum("sqhd,skhd->shqk", d_ctx, v, preferred_element_type=F32)
    delta = jnp.sum(probs * d_probs, axis=-1, keepdims=True)
    d_scores = jnp.where(allow[:, None], probs * (d_probs - delta), 0.0).astype(BF16)
    d_q = jnp.einsum("shqk,skhd->sqhd", d_scores, k, preferred_element_type=F32) * scale
    d_k = jnp.einsum("shqk,sqhd->skhd", d_scores, q, preferred_element_type=F32) * scale
    d_v = jnp.einsum("shqk,sqhd->skhd", pl_low, d_ctx, preferred_element_type=F32)
    d_q = rotate(d_q, cosine, sine, True)
    d_k = rotate(d_k, cosine, sine, True)
    d_qkv = jnp.stack([d_q, d_k, d_v], axis=2).astype(BF16).reshape(mb * seq, 3 * hc)
    d_wq = dot(h1, d_qkv, ((0,), (0,)))
    d_bq = jnp.sum(d_qkv.astype(F32), axis=0)
    d_h1 = dot(d_qkv, wq, ((1,), (1,)))
    e_sum = (d_h1 * gain1 + d_h2 * gain2).astype(BF16).reshape(mb, seq, width)
    e_own = scatter_ctx(ndp, n, e_sum, 2)
    own_x = toks.astype(F32)
    o_mean = jnp.mean(own_x, axis=-1, keepdims=True)
    o_cen = own_x - o_mean
    o_rstd = lax.rsqrt(jnp.mean(o_cen * o_cen, axis=-1, keepdims=True) + 1e-05)
    o_n = o_cen * o_rstd
    t_grad = o_rstd * (e_own - jnp.mean(e_own, axis=-1, keepdims=True) - o_n * jnp.mean(e_own * o_n, axis=-1, keepdims=True))
    tokens_grad = (cot.astype(F32) + t_grad).astype(BF16)

    rows = [
        jnp.pad(d_bq, (0, width - 3 * hc)),
        jnp.pad(d_bu, (0, width - fu)),
        jnp.sum(d_h1 * normed, axis=0),
        jnp.sum(d_h1, axis=0),
        jnp.sum(d_h2 * normed, axis=0),
        jnp.sum(d_h2, axis=0),
        jnp.sum(gf, axis=0),
        jnp.zeros((width,), F32),
    ]
    dwp = jnp.concatenate([d_wq, d_wu], axis=1).astype(BF16).reshape(ndp, n, rows_w, 3 * hc + fu)
    dw, dwd, dwo, dv = grads_all(
        ndp, n, dwp, d_wd.astype(BF16).reshape(ndp, rows_d, width), d_wo.astype(BF16).reshape(ndp, rows_w, width), jnp.stack(rows)
    )
    index = dp * n + c
    g_qkv = dw[:, :, : 3 * hc].reshape(n, rows_w, 3, hc).transpose(1, 2, 0, 3).reshape(rows_w, 3 * width).astype(F32)
    g_up = dw[:, :, 3 * hc :].reshape(n, rows_w, ndp, rows_d).transpose(1, 2, 0, 3).reshape(rows_w, -1).astype(F32)
    g_bq = lax.dynamic_slice_in_dim(dv[:, 0, : 3 * hc].reshape(n, 3, hc).transpose(1, 0, 2).reshape(-1), index * sizes[0], sizes[0])
    own = lax.dynamic_index_in_dim(dv, c, 0, keepdims=False)
    g_bu = lax.dynamic_slice_in_dim(own[1], dp * rows_d, rows_d)
    four = lax.dynamic_slice_in_dim(jnp.sum(dv[:, 2:6], axis=0), index * rows_w, rows_w, axis=1)
    g_b = lax.dynamic_slice_in_dim(own[6], index * rows_w, rows_w)
    return (
        jnp.transpose(mixed, (1, 0, 2)),
        jnp.transpose(tokens_grad, (1, 0, 2)),
        g_qkv,
        g_bq,
        dwo.astype(F32),
        g_b,
        g_up,
        g_bu,
        dwd,
        g_b,
        four[0],
        four[1],
        four[2],
        four[3],
    )


def program(ndp, n, *args):
    tokens, w_qkv, w_down = args[0], args[3], args[9]
    rows_w = w_qkv.shape[0]
    whole_tiles = ndp == 4 and rows_w % 16 == 0 and tokens.shape[2] // n == 128 and w_down.shape[0] == 128 and tokens.shape[0] % 16 == 0
    return (fused_device if whole_tiles else per_device)(ndp, n, *args)


def solution(mesh):
    every = ("dp", "ctx")
    mat, vec, act = P(every, None), P(every), P("ctx", "dp", None)
    placed = (act, act, P("dp", None), mat, vec, mat, vec, mat, vec, mat, vec, vec, vec, vec, vec)
    return jax.shard_map(
        partial(program, mesh.shape["dp"], mesh.shape["ctx"]),
        mesh=mesh,
        in_specs=placed,
        out_specs=(act, act, mat, vec, mat, vec, mat, vec, mat, vec, vec, vec, vec, vec),
        check_vma=False,
    )
```

```python
from functools import partial

import jax
import jax.numpy as jnp
import numpy as np
from jax import lax
from jax.experimental import pallas as pl
from jax.experimental.pallas import tpu as pltpu
from jax.sharding import PartitionSpec as P

HEAD = 64
ROT = 16
MIB = 1 << 20
CUT_TOKENS, CUT_COTANGENT, CUT_MIXED, CUT_GRAD = (2, 1), (1, 1), (1, 1), (1, 2)
MESH = pl.DeviceIdType.MESH
ANY = pl.BlockSpec(memory_space=pl.ANY)
F32 = jnp.float32
BF16 = jnp.bfloat16


class Place:
    def __init__(self, ndp, n):
        self.ndp, self.n, self.nz = ndp, n, n // 2
        self.dp = lax.axis_index("dp")
        self.c = lax.axis_index("ctx")
        self.z = self.c // 2
        self.core = lax.rem(self.c, 2)
        self.sib = self.c + 1 - 2 * self.core
        self.has_up = self.z + 1 < self.nz
        self.has_down = self.z > 0
        self.px = self.dp + 1 - 2 * lax.rem(self.dp, 2)
        self.py = lax.rem(self.dp + 2, 4)
        self.diag = 3 - self.dp
        index, back = self.dp * n + self.c, self.c * ndp + self.dp
        self.rows_dp, self.rows_c = lax.rem(index, ndp), index // ndp
        self.from_dp, self.from_c = back // n, lax.rem(back, n)
        self.moves = index != back

    def barrier(self, ctx_all, dp_all, rows=False):
        bar = pltpu.get_barrier_semaphore()
        count = 0
        if rows:
            count = count + 2 * self.moves.astype(jnp.int32)

            @pl.when(self.moves)
            def _():
                pl.semaphore_signal(bar, inc=1, device_id=(self.rows_dp, self.rows_c), device_id_type=MESH)
                pl.semaphore_signal(bar, inc=1, device_id=(self.from_dp, self.from_c), device_id_type=MESH)

        if ctx_all:
            for j in range(1, self.n):
                peer = lax.rem(self.c + j, self.n)
                pl.semaphore_signal(bar, inc=1, device_id=(self.dp, peer), device_id_type=MESH)
                count += 1
        else:
            pl.semaphore_signal(bar, inc=1, device_id=(self.dp, self.sib), device_id_type=MESH)
            count += 1
            for ok, peer in ((self.has_up, self.c + 2), (self.has_down, self.c - 2)):

                @pl.when(ok)
                def _():
                    pl.semaphore_signal(bar, inc=1, device_id=(self.dp, peer), device_id_type=MESH)

        if dp_all:
            for j in range(1, self.ndp):
                peer = lax.rem(self.dp + j, self.ndp)
                pl.semaphore_signal(bar, inc=1, device_id=(peer, self.c), device_id_type=MESH)
                count += 1
        if not ctx_all:
            count = count + self.has_up.astype(jnp.int32) + self.has_down.astype(jnp.int32)
        pl.semaphore_wait(bar, count)


def remote(src, dst, send, recv, dp, c):
    return pltpu.make_async_remote_copy(
        src_ref=src,
        dst_ref=dst,
        send_sem=send,
        recv_sem=recv,
        device_id=(dp, c),
        device_id_type=MESH,
    )


class Gather:
    def __init__(self, at, src, dst, tok, sends, recvs):
        self.at, self.src, self.dst, self.tok, self.sends, self.recvs = at, src, dst, tok, sends, recvs

    def rows(self, c):
        return self.dst.at[:, pl.ds(pl.multiple_of(c * self.tok, self.tok), self.tok)]

    def copy(self, block, slot, c, src=None):
        at = self.at
        src = self.rows(block) if src is None else src
        return remote(src, self.rows(block), self.sends.at[slot], self.recvs.at[block], at.dp, c)

    def start(self):
        at = self.at

        @pl.when(at.has_up)
        def _():
            self.copy(at.c, 0, at.c + 2, self.src).start()

        @pl.when(at.has_down)
        def _():
            self.copy(at.c, 1, at.c - 2, self.src).start()

        self.copy(at.c, 2, at.sib, self.src).start()

    def step(self, k):
        at = self.at
        low, high = at.c - 2 * k, at.c + 2 * k

        @pl.when(at.z >= k)
        def _():
            self.copy(low, 0, at.c).wait_recv()

            @pl.when(at.has_up)
            def _():
                self.copy(low, 3 * k, at.c + 2).start()

            self.copy(low, 3 * k + 2, at.sib).start()

        @pl.when(at.z + k < at.nz)
        def _():
            self.copy(high, 0, at.c).wait_recv()

            @pl.when(at.has_down)
            def _():
                self.copy(high, 3 * k + 1, at.c - 2).start()

            self.copy(high, 3 * at.nz + k, at.sib).start()

    def finish(self):
        at = self.at
        for z in range(at.nz):
            self.copy(2 * z + 1 - at.core, 0, at.c).wait_recv()
        self.copy(at.c, 2, at.sib, self.src).wait_send()
        for k in range(at.nz):

            @pl.when((at.z >= k) & at.has_up)
            def _():
                self.copy(at.c, 3 * k, at.c).wait_send()

            @pl.when((at.z + k < at.nz) & at.has_down)
            def _():
                self.copy(at.c, 3 * k + 1, at.c).wait_send()

            if k:

                @pl.when(at.z >= k)
                def _():
                    self.copy(at.c, 3 * k + 2, at.c).wait_send()

                @pl.when(at.z + k < at.nz)
                def _():
                    self.copy(at.c, 3 * at.nz + k, at.c).wait_send()


def gather_slots(nz):
    return 4 * nz


class Exchange:
    def __init__(self, at, axis, src, dst, sends, recvs):
        self.at, self.axis, self.src, self.dst, self.sends, self.recvs = at, axis, src, dst, sends, recvs
        self.me, self.count = (at.c, at.n) if axis == "ctx" else (at.dp, at.ndp)

    def copy(self, peer, sender):
        at = self.at
        to = (at.dp, peer) if self.axis == "ctx" else (peer, at.c)
        return remote(self.src(peer), self.dst(sender), self.sends.at[peer], self.recvs.at[sender], *to)

    def start(self):
        for j in range(1, self.count):
            self.copy(lax.rem(self.me + j, self.count), self.me).start()

    def wait_recv(self):
        for j in range(1, self.count):
            peer = lax.rem(self.me + j, self.count)
            self.copy(peer, peer).wait_recv()

    def wait_send(self):
        for j in range(1, self.count):
            peer = lax.rem(self.me + j, self.count)
            self.copy(peer, self.me).wait_send()


def gather_kernel(ndp, n, tok_ref, cot_ref, wp_ref, wd_ref, wo_ref, vec_ref, x_out, g_out, w_out, wd_out, wo_out, vec_out, *sems):
    at = Place(ndp, n)
    tok = tok_ref.shape[1]
    (x_send, x_recv, g_send, g_recv, w1s, w1r, w2s, w2r, v1s, v1r, v2s, v2r, ds, dr, o1s, o1r, o2s, o2r, local) = sems
    at.barrier(True, True)
    own = (
        pltpu.make_async_copy(wp_ref.at[at.c], w_out.at[at.dp, at.c], local.at[0]),
        pltpu.make_async_copy(vec_ref, vec_out.at[at.dp, at.c], local.at[1]),
        pltpu.make_async_copy(wd_ref, wd_out.at[at.dp], local.at[2]),
        pltpu.make_async_copy(tok_ref, x_out.at[:, pl.ds(pl.multiple_of(at.c * tok, tok), tok)], local.at[3]),
        pltpu.make_async_copy(cot_ref, g_out.at[:, pl.ds(pl.multiple_of(at.c * tok, tok), tok)], local.at[4]),
    )
    for copy in own:
        copy.start()
    down_w = Exchange(at, "dp", lambda p: wd_ref, lambda s: wd_out.at[s], ds, dr)
    cols = Exchange(at, "ctx", lambda p: wp_ref.at[p], lambda s: w_out.at[at.dp, s], w1s, w1r)
    vecs = Exchange(at, "ctx", lambda p: vec_ref, lambda s: vec_out.at[at.dp, s], v1s, v1r)
    plane_w = Exchange(at, "dp", lambda p: w_out.at[at.dp], lambda s: w_out.at[s], w2s, w2r)
    plane_v = Exchange(at, "dp", lambda p: vec_out.at[at.dp], lambda s: vec_out.at[s], v2s, v2r)
    plane_o = Exchange(at, "dp", lambda p: wo_out, lambda s: wo_out, o2s, o2r)
    cols.start()
    vecs.start()
    index = at.dp * n + at.c
    heads_of, slot = index // ndp, lax.rem(index, ndp)

    def out_rows(b, c):
        return remote(wo_ref, wo_out.at[b], o1s, o1r.at[b], at.dp, c)

    @pl.when(heads_of != at.c)
    def _():
        out_rows(slot, heads_of).start()

    own_rows = pltpu.make_async_copy(wo_ref, wo_out.at[slot], local.at[5])

    @pl.when(heads_of == at.c)
    def _():
        own_rows.start()

    down_w.start()
    x_ag = Gather(at, tok_ref, x_out, tok, x_send, x_recv)
    g_ag = Gather(at, cot_ref, g_out, tok, g_send, g_recv)
    x_ag.start()
    own[0].wait()
    cols.wait_recv()
    plane_w.start()
    own[1].wait()
    vecs.wait_recv()
    plane_v.start()
    first = at.c * ndp // n

    @pl.when(at.dp == first)
    def _():
        for b in range(ndp):
            src = lax.rem(at.c * ndp + b, n)

            @pl.when(src != at.c)
            def _():
                out_rows(b, at.c).wait_recv()

            @pl.when(src == at.c)
            def _():
                own_rows.wait()

        plane_o.start()

    for k in range(1, at.nz):
        x_ag.step(k)
        if k == 1:
            g_ag.start()
    for k in range(1, at.nz):
        g_ag.step(k)
    x_ag.finish()
    g_ag.finish()

    @pl.when(heads_of != at.c)
    def _():
        out_rows(slot, heads_of).wait_send()

    @pl.when((heads_of == at.c) & (at.dp != first))
    def _():
        own_rows.wait()

    @pl.when(at.dp == first)
    def _():
        plane_o.wait_send()

    @pl.when(at.dp != first)
    def _():
        plane_o.copy(first, first).wait_recv()

    for copy in own[2:]:
        copy.wait()
    for part in (down_w, plane_w, plane_v):
        part.wait_recv()
    for part in (down_w, cols, vecs, plane_w, plane_v):
        part.wait_send()


def gather_all(ndp, n, tok, cot, wp, wd, wo, vec):
    mb, rows, width = tok.shape
    dma = pltpu.SemaphoreType.DMA
    slots = gather_slots(n // 2)
    return pl.pallas_call(
        partial(gather_kernel, ndp, n),
        out_shape=(
            jax.ShapeDtypeStruct((mb, rows * n, width), BF16),
            jax.ShapeDtypeStruct((mb, rows * n, width), BF16),
            jax.ShapeDtypeStruct((ndp,) + wp.shape, BF16),
            jax.ShapeDtypeStruct((ndp,) + wd.shape, BF16),
            jax.ShapeDtypeStruct((ndp,) + wo.shape, BF16),
            jax.ShapeDtypeStruct((ndp, n) + vec.shape, vec.dtype),
        ),
        in_specs=[ANY] * 6,
        out_specs=[ANY] * 6,
        scratch_shapes=[
            dma((slots,)), dma((n,)), dma((slots,)), dma((n,)),
            dma((n,)), dma((n,)), dma((ndp,)), dma((ndp,)),
            dma((n,)), dma((n,)), dma((ndp,)), dma((ndp,)),
            dma((ndp,)), dma((ndp,)),
            dma, dma((ndp,)), dma((ndp,)), dma((ndp,)),
            dma((6,)),
        ],
        compiler_params=pltpu.CompilerParams(collective_id=0, has_side_effects=True),
    )(tok, cot, wp, wd, wo, vec)


class Scatter:
    def __init__(self, at, part, out, sib_buf, low_buf, high_buf, stage, tok, sems):
        self.at, self.part, self.out, self.tok = at, part, out, tok
        self.sib_buf, self.low_buf, self.high_buf, self.stage = sib_buf, low_buf, high_buf, stage
        self.s_send, self.s_recv, self.up_send, self.up_recv, self.dn_send, self.dn_recv = sems

    def rows(self, c):
        return pl.ds(pl.multiple_of(c * self.tok, self.tok), self.tok)

    def cross(self, z):
        at = self.at
        src = self.part.at[:, self.rows(2 * z + 1 - at.core)]
        return remote(src, self.sib_buf.at[z], self.s_send.at[z], self.s_recv.at[z], at.dp, at.sib)

    def up(self, z):
        at = self.at
        return remote(self.stage.at[z], self.low_buf.at[z], self.up_send.at[z], self.up_recv.at[z], at.dp, at.c + 2)

    def down(self, z):
        at = self.at
        return remote(self.stage.at[z], self.high_buf.at[z], self.dn_send.at[z], self.dn_recv.at[z], at.dp, at.c - 2)

    def order(self):
        nz = self.at.nz
        for i in range(nz):
            yield nz - 1 - i
            if i != nz - 1 - i:
                pass

    def start(self):
        for i in range(self.at.nz):
            self.cross(i).start()

    def chip_sum(self, z):
        at = self.at
        mine = self.part[:, self.rows(2 * z + at.core)].astype(F32)
        return mine + self.sib_buf[z].astype(F32)

    def step(self, i):
        at = self.at
        up_z, dn_z = at.nz - 1 - i, i

        @pl.when(up_z > at.z)
        def _():
            self.cross(up_z).wait_recv()
            self.stage[up_z] = self.chip_sum(up_z).astype(BF16)

            @pl.when(at.has_down)
            def _():
                self.up(up_z).wait_recv()
                self.stage[up_z] = (self.stage[up_z].astype(F32) + self.low_buf[up_z].astype(F32)).astype(BF16)

            self.up(up_z).start()

        @pl.when(dn_z < at.z)
        def _():
            self.cross(dn_z).wait_recv()
            self.stage[dn_z] = self.chip_sum(dn_z).astype(BF16)

            @pl.when(at.has_up)
            def _():
                self.down(dn_z).wait_recv()
                self.stage[dn_z] = (self.stage[dn_z].astype(F32) + self.high_buf[dn_z].astype(F32)).astype(BF16)

            self.down(dn_z).start()

    def finish(self):
        at = self.at
        self.cross(at.z).wait_recv()
        self.out[...] = self.chip_sum(at.z)

        @pl.when(at.has_down)
        def _():
            self.up(at.z).wait_recv()
            self.out[...] += self.low_buf[at.z].astype(F32)

        @pl.when(at.has_up)
        def _():
            self.down(at.z).wait_recv()
            self.out[...] += self.high_buf[at.z].astype(F32)

        for z in range(at.nz):
            self.cross(z).wait_send()

            @pl.when(z > at.z)
            def _():
                self.up(z).wait_send()

            @pl.when(z < at.z)
            def _():
                self.down(z).wait_send()


def scatter_kernel(ndp, n, part_ref, out_ref, sib_buf, low_buf, high_buf, stage, *sems):
    at = Place(ndp, n)
    at.barrier(False, False)
    work = Scatter(at, part_ref, out_ref, sib_buf, low_buf, high_buf, stage, out_ref.shape[1], sems)
    work.start()
    for i in range(at.nz - 1):
        work.step(i)
    work.finish()


def scatter_ctx(ndp, n, part, collective):
    mb, seq, width = part.shape
    nz, tok = n // 2, seq // n
    dma = pltpu.SemaphoreType.DMA
    buf = pltpu.VMEM((nz, mb, tok, width), BF16)
    vmem = pl.BlockSpec(memory_space=pltpu.VMEM)
    return pl.pallas_call(
        partial(scatter_kernel, ndp, n),
        out_shape=jax.ShapeDtypeStruct((mb, tok, width), F32),
        in_specs=[vmem],
        out_specs=vmem,
        scratch_shapes=[buf, buf, buf, buf] + [dma((nz,))] * 6,
        compiler_params=pltpu.CompilerParams(collective_id=collective, has_side_effects=True, vmem_limit_bytes=48 * MIB),
    )(part)


def grads_kernel(ndp, n, wp_ref, wd_ref, wo_ref, v_ref, w_out, wd_out, wo_out, v_out, wbuf, wsum, dbuf, obuf, osum, vbuf, vsum, *sems):
    at = Place(ndp, n)
    (w1s, w1r, ds, dr, o1s, o1r, v1s, v1r, w2s, w2r, v2s, v2r, o2s, o2r, local) = sems
    at.barrier(True, True)
    first = at.c * ndp // n
    w1 = Exchange(at, "dp", lambda p: wp_ref.at[p], lambda s: wbuf.at[s], w1s, w1r)
    d1 = Exchange(at, "dp", lambda p: wd_ref.at[p], lambda s: dbuf.at[s], ds, dr)
    v1 = Exchange(at, "dp", lambda p: v_ref, lambda s: vbuf.at[s], v1s, v1r)
    o1 = Exchange(at, "dp", lambda p: wo_ref, lambda s: obuf.at[s], o1s, o1r)
    w1.start()
    v1.start()

    @pl.when(at.dp != first)
    def _():
        o1.copy(first, at.dp).start()

    d1.start()

    def total(ref, mine, get):
        ref[...] = mine
        for j in range(1, ndp):
            ref[...] += get(lax.rem(at.dp + j, ndp)).astype(F32)

    w1.wait_recv()
    total(wsum, wp_ref[at.dp].astype(F32), lambda s: wbuf[s])
    wbuf[at.dp] = wsum[...].astype(BF16)
    w2 = Exchange(at, "ctx", lambda p: wbuf.at[at.dp, p], lambda s: w_out.at[s], w2s, w2r)
    w2.start()
    w_out[at.c] = wbuf[at.dp, at.c]
    v1.wait_recv()
    total(vsum, v_ref[...], lambda s: vbuf[s])
    v2 = Exchange(at, "ctx", lambda p: vsum, lambda s: v_out.at[s], v2s, v2r)
    v2.start()
    v_out[at.c] = vsum[...]

    index = at.dp * n + at.c
    heads_of, slot = index // ndp, lax.rem(index, ndp)

    def out_rows(b, c):
        return remote(osum.at[b], wo_out, o2s.at[b], o2r, at.dp, c)

    @pl.when(at.dp == first)
    def _():
        o1.wait_recv()
        rows = wo_ref[...].astype(F32)
        for j in range(1, ndp):
            rows += obuf[lax.rem(at.dp + j, ndp)].astype(F32)
        osum[...] = rows.astype(BF16)
        for b in range(ndp):
            owner = lax.rem(at.c * ndp + b, n)

            @pl.when(owner != at.c)
            def _():
                out_rows(b, owner).start()

            @pl.when(owner == at.c)
            def _():
                wo_out[...] = osum[b]

    d1.wait_recv()
    total(wd_out, wd_ref[at.dp].astype(F32), lambda s: dbuf[s])

    @pl.when(heads_of != at.c)
    def _():
        out_rows(slot, at.c).wait_recv()

    w2.wait_recv()
    v2.wait_recv()
    for part in (w1, v1, d1, w2, v2):
        part.wait_send()

    @pl.when(at.dp != first)
    def _():
        o1.copy(first, at.dp).wait_send()

    @pl.when(at.dp == first)
    def _():
        for b in range(ndp):
            owner = lax.rem(at.c * ndp + b, n)

            @pl.when(owner != at.c)
            def _():
                out_rows(b, owner).wait_send()


def grads_all(ndp, n, wp, wd, wo, v):
    dma = pltpu.SemaphoreType.DMA
    vmem = pl.BlockSpec(memory_space=pltpu.VMEM)
    return pl.pallas_call(
        partial(grads_kernel, ndp, n),
        out_shape=(
            jax.ShapeDtypeStruct(wp.shape[1:], BF16),
            jax.ShapeDtypeStruct(wd.shape[1:], F32),
            jax.ShapeDtypeStruct(wo.shape[1:], BF16),
            jax.ShapeDtypeStruct((n,) + v.shape, F32),
        ),
        in_specs=[vmem] * 4,
        out_specs=[vmem] * 4,
        scratch_shapes=[
            pltpu.VMEM(wp.shape, BF16),
            pltpu.VMEM(wp.shape[1:], F32),
            pltpu.VMEM(wd.shape, BF16),
            pltpu.VMEM((ndp,) + wo.shape, BF16),
            pltpu.VMEM(wo.shape, BF16),
            pltpu.VMEM((ndp,) + v.shape, F32),
            pltpu.VMEM(v.shape, F32),
            dma((ndp,)), dma((ndp,)), dma((ndp,)), dma((ndp,)), dma((ndp,)), dma((ndp,)), dma((ndp,)), dma((ndp,)),
            dma((n,)), dma((n,)), dma((n,)), dma((n,)), dma((ndp,)), dma,
            dma((1,)),
        ],
        compiler_params=pltpu.CompilerParams(collective_id=3, has_side_effects=True, vmem_limit_bytes=48 * MIB),
    )(wp, wd, wo, v)


def dot(a, b, dims=((1,), (0,))):
    return lax.dot_general(a, b, (dims, ((), ())), preferred_element_type=F32)


NT = ((1,), (1,))
TN = ((0,), (0,))


class SeqGather:
    def __init__(self, at, dst, tok, first, size, sends, recvs):
        self.at, self.dst, self.tok, self.first, self.size, self.sends, self.recvs = at, dst, tok, first, size, sends, recvs

    def rows(self, c):
        return self.dst.at[pl.ds(pl.multiple_of(c * self.tok + self.first, self.size), self.size)]

    def copy(self, block, slot, c):
        return remote(self.rows(block), self.rows(block), self.sends.at[slot], self.recvs.at[block], self.at.dp, c)

    def up_slot(self, k):
        return k

    def down_slot(self, k):
        return self.at.nz - 1 + k

    def side_slot(self, k):
        return 2 * (self.at.nz - 1) + k

    def start(self):
        at = self.at

        @pl.when(at.has_up)
        def _():
            self.copy(at.c, self.up_slot(0), at.c + 2).start()

        @pl.when(at.has_down)
        def _():
            self.copy(at.c, self.down_slot(0), at.c - 2).start()

        self.copy(at.c, self.side_slot(0), at.sib).start()

    def step(self, k):
        at = self.at
        low, high = at.c - 2 * k, at.c + 2 * k

        @pl.when(at.z >= k)
        def _():
            self.copy(low, 0, at.c).wait_recv()

            @pl.when(at.has_up)
            def _():
                self.copy(low, self.up_slot(k), at.c + 2).start()

            self.copy(low, self.side_slot(k), at.sib).start()

        @pl.when(at.z + k < at.nz)
        def _():
            self.copy(high, 0, at.c).wait_recv()

            @pl.when(at.has_down)
            def _():
                self.copy(high, self.down_slot(k), at.c - 2).start()

            self.copy(high, self.side_slot(at.z + k), at.sib).start()

    def land(self):
        for z in range(self.at.nz):
            self.land_chip(z)

    def land_chip(self, z):
        self.copy(2 * z + 1 - self.at.core, 0, self.at.c).wait_recv()


    def drain(self):
        at = self.at
        for k in range(at.nz):
            self.copy(at.c, self.side_slot(k), at.c).wait_send()
            if k == at.nz - 1:
                continue

            @pl.when((at.z >= k) & at.has_up)
            def _():
                self.copy(at.c, self.up_slot(k), at.c).wait_send()

            @pl.when((at.z + k < at.nz) & at.has_down)
            def _():
                self.copy(at.c, self.down_slot(k), at.c).wait_send()


class Pieces:
    def __init__(self, pieces):
        self.pieces = pieces

    def each(self, name, *args):
        for piece in self.pieces:
            getattr(piece, name)(*args)

    def start(self):
        self.each("start")

    def step(self, k):
        self.each("step", k)

    def land(self):
        self.each("land")

    def drain(self):
        self.each("drain")

    def take(self, k, body):
        at = self.pieces[0].at

        def one(t, carry):
            z = at.z - k + 2 * k * t

            @pl.when((z >= 0) & (z < at.nz))
            def _():
                self.each("land_chip", z)
                body(z)

            return carry

        lax.fori_loop(0, 2 if k else 1, one, 0)


class SeqScatter:
    def __init__(self, at, part, sib_buf, in_buf, tok, first, size, sems):
        self.at, self.part, self.tok, self.first, self.size = at, part, tok, first, size
        self.sib_buf, self.in_buf = sib_buf.at[:, pl.ds(first, size)], in_buf.at[:, pl.ds(first, size)]
        self.s_send, self.s_recv, self.up_send, self.up_recv, self.dn_send, self.dn_recv = sems

    def rows(self, c):
        return pl.ds(pl.multiple_of(c * self.tok + self.first, self.size), self.size)

    def cross(self, z):
        at = self.at
        src = self.part.at[self.rows(2 * z + 1 - at.core)]
        return remote(src, self.sib_buf.at[z], self.s_send.at[z], self.s_recv.at[z], at.dp, at.sib)

    def up(self, z):
        at = self.at
        return remote(self.sib_buf.at[z], self.in_buf.at[z], self.up_send.at[z], self.up_recv.at[z], at.dp, at.c + 2)

    def down(self, z, sender=None):
        at = self.at
        slot = jnp.where(z == (at.z - 1 if sender is None else sender - 1), at.nz, z)
        return remote(self.sib_buf.at[z], self.in_buf.at[slot], self.dn_send.at[z], self.dn_recv.at[z], at.dp, at.c - 2)

    def chip_sum(self, z):
        mine = self.part[self.rows(2 * z + self.at.core)].astype(F32)
        return mine + self.sib_buf[z].astype(F32)

    def step(self, t):
        self.step_up(t)
        self.step_down(t)

    def step_up(self, t):
        self.lead_up(t)
        self.follow_up(t)

    def lead_up(self, t):
        at = self.at
        z = at.nz - 1 - t

        @pl.when(at.z == 0)
        def _():
            self.cross(z).wait_recv()
            self.sib_buf[z] = self.chip_sum(z).astype(BF16)
            self.up(z).start()

    def follow_up(self, t):
        at = self.at
        z = at.nz - 1 - t + at.z

        @pl.when((at.z <= t) & at.has_down)
        def _():
            self.cross(z).wait_recv()
            self.up(z).wait_recv()
            self.sib_buf[z] = (self.chip_sum(z) + self.in_buf[z].astype(F32)).astype(BF16)
            self.up(z).start()

    def step_down(self, t):
        self.lead_down(t)
        self.follow_down(t)

    def lead_down(self, t):
        at = self.at

        @pl.when(at.z == at.nz - 1)
        def _():
            self.cross(t).wait_recv()
            self.sib_buf[t] = self.chip_sum(t).astype(BF16)
            self.down(t).start()

    def follow_down(self, t):
        at = self.at
        z = t - (at.nz - 1 - at.z)

        @pl.when((z >= 0) & at.has_up)
        def _():
            self.cross(z).wait_recv()
            self.down(z, at.z + 1).wait_recv()
            self.sib_buf[z] = (self.chip_sum(z) + self.in_buf[z].astype(F32)).astype(BF16)
            self.down(z).start()

    def total(self, acc):
        at = self.at
        acc = acc.at[pl.ds(self.first, self.size)]
        self.cross(at.z).wait_recv()
        acc[...] = self.chip_sum(at.z)

        @pl.when(at.has_down)
        def _():
            self.up(at.z).wait_recv()
            acc[...] += self.in_buf[at.z].astype(F32)

        @pl.when(at.has_up)
        def _():
            self.down(at.z, at.z + 1).wait_recv()
            acc[...] += self.in_buf[at.nz].astype(F32)

    def drain(self):
        at = self.at
        for z in range(at.nz):
            self.cross(z).wait_send()

            @pl.when(z > at.z)
            def _():
                self.up(z).wait_send()

            @pl.when(z < at.z)
            def _():
                self.down(z).wait_send()


class ScatterPieces(Pieces):
    def cross(self, z):
        return Pieces([piece.cross(z) for piece in self.pieces])

    def lead_up(self, t):
        self.each("lead_up", t)

    def lead_down(self, t):
        self.each("lead_down", t)

    def lead(self):
        for t in range(self.pieces[0].at.nz - 1):
            self.lead_up(t)
            self.lead_down(t)

    def follow(self, t):
        for piece in self.pieces:
            piece.follow_up(t)
            piece.follow_down(t)

    def step(self, t):
        for piece in self.pieces:
            piece.step_up(t)
            piece.step_down(t)

    def total(self, acc):
        self.each("total", acc)


class PlaneGather:
    def __init__(self, at, part, sends, recvs):
        self.at, self.part, self.sends, self.recvs = at, part, sends, recvs

    def copy(self, p, h, i, to):
        return remote(self.part(p, h), self.part(p, h), self.sends.at[i], self.recvs.at[i], to, self.at.c)

    def start(self):
        at = self.at
        for h in (0, 1):
            self.copy(at.dp, h, h, at.px).start()
            self.copy(at.dp, 1 - h, 3 - h, at.py).start()

    def forward(self):
        at = self.at
        self.copy(at.px, 0, 0, at.px).wait_recv()
        self.copy(at.px, 0, 4, at.py).start()
        self.copy(at.py, 1, 3, at.py).wait_recv()
        self.copy(at.py, 1, 5, at.px).start()

    def land(self):
        at = self.at
        self.copy(at.px, 1, 1, at.px).wait_recv()
        self.copy(at.py, 0, 2, at.py).wait_recv()
        self.copy(at.diag, 0, 4, at.py).wait_recv()
        self.copy(at.diag, 1, 5, at.px).wait_recv()

    def drain(self):
        at = self.at
        for h in (0, 1):
            self.copy(at.dp, h, h, at.px).wait_send()
            self.copy(at.dp, h, 2 + h, at.py).wait_send()
        self.copy(at.px, 0, 4, at.py).wait_send()
        self.copy(at.py, 1, 5, at.px).wait_send()


class PlaneReduce:
    def __init__(self, at, part, via_x, via_y, from_x, from_y, sends, recvs):
        self.at, self.part, self.sends, self.recvs = at, part, sends, recvs
        self.via_x, self.via_y, self.from_x, self.from_y = via_x, via_y, from_x, from_y

    def copy(self, i):
        at = self.at
        src, dst, to = (
            (lambda: self.part(at.diag, 1), self.via_x, at.px),
            (lambda: self.part(at.diag, 0), self.via_y, at.py),
            (lambda: self.part(at.px, 1), self.from_x(1), at.px),
            (lambda: self.part(at.py, 0), self.from_y(0), at.py),
            (lambda: self.part(at.py, 1), self.from_y(1), at.py),
            (lambda: self.part(at.px, 0), self.from_x(0), at.px),
        )[i]
        return remote(src(), dst, self.sends.at[i], self.recvs.at[i], to, at.c)

    def start(self):
        for i in range(4):
            self.copy(i).start()

    def combine(self):
        at = self.at
        for i, via, p, h in ((0, self.via_x, at.py, 1), (1, self.via_y, at.px, 0)):
            self.copy(i).wait_recv()
            ref = self.part(p, h)
            ref[...] = (ref[...].astype(F32) + via[...].astype(F32)).astype(BF16)
            self.copy(4 + i).start()

    def total(self, h):
        for i in ((5, 3), (2, 4))[h]:
            self.copy(i).wait_recv()
        return self.part(self.at.dp, h)[...].astype(F32) + self.from_x(h)[...].astype(F32) + self.from_y(h)[...].astype(F32)

    def drain(self):
        for i in range(6):
            self.copy(i).wait_send()


def blocks(count, body, hooks=None):
    hooks = hooks or {}

    def one(i, carry):
        body(i)
        for index, events in hooks.items():

            @pl.when(i == index)
            def _():
                for event in events:
                    event()

        return carry

    lax.fori_loop(0, count, one, 0)


def fused_kernel(ndp, n, dims, *refs):
    mb, tok, width, seq, heads, rows_w, rows_d = dims
    nz, block, every = n // 2, 2 * tok, ndp * n
    fu = ndp * rows_d
    (tok_ref, cot_ref, rq_ref, ru_ref, wd_ref, wo_ref, vec_ref, seg_ref, cos_ref, sin_ref) = refs[:10]
    (mixed_out, grad_out, qkv_out, up_out, dwd_out, dwo_out, vec_out) = refs[10:17]
    (xs, gs, ws, wdo, vecs, segs, seg_col, cos_t, sin_t, g1, s1, g2, s2, bo, bq, bu, qkv, hid, gp, stat, ctx, part, ep, dctx, dqkv,
     dk, dv, acc_gain, acc_bu, acc_bq, m_sib, m_in, t_sib, t_in, dwq, dwu, dwdo, q_via, q_from, u_via, u_from, d_via, d_from, vsum, vin, wq_st, wu_st,
     own, dwo_st, vsum_all, v_st, seg_i, wp_st, wq_rx, wu_rx, v_rx, h1_all, h2_all) = refs[17:75]
    probs = refs[75 : 75 + nz]
    (x_s, x_r, c_s, c_r, w1s, w1r, w2s, w2r, v1s, v1r, v2s, v2r, d_s, d_r, o1s, o1r,
     ms_s, ms_r, mu_s, mu_r, md_s, md_r, ts_s, ts_r, tu_s, tu_r, td_s, td_r,
     gq1s, gq1r, gq2s, gq2r, gu1s, gu1r, gu2s, gu2r, gd_s, gd_r, go2s, go2r, gv1s, gv1r, gv2s, gv2r, local) = refs[75 + nz :]
    at = Place(ndp, n)
    at.barrier(True, True, True)
    raw_q, raw_u, raw_t, raw_c = qkv_out, up_out, mixed_out, grad_out
    own_rows = pl.ds(pl.multiple_of(at.c * tok, tok), tok)

    cols = Exchange(at, "ctx", lambda p: wp_st.at[p], lambda s: ws.at[at.dp, s], w1s, w1r)
    vec1 = Exchange(at, "ctx", lambda p: vec_ref, lambda s: vecs.at[at.dp, s], v1s, v1r)
    plane_w = PlaneGather(at, lambda p, h: ws.at[p, pl.ds(h * (n // 2), n // 2)], w2s, w2r)
    plane_v = Exchange(at, "dp", lambda p: vecs.at[at.dp], lambda s: vecs.at[s], v2s, v2r)
    rows_do = rows_d + rows_w
    plane_d = PlaneGather(at, lambda p, h: wdo.at[p, pl.ds(h * (rows_do // 2), rows_do // 2)], d_s, d_r)
    def gather(dst, sends, recvs, counts, s):
        size, first = tok // counts[s], sum(counts[:s])
        return Pieces([SeqGather(at, dst.at[s], tok, h * size, size, sends.at[first + h], recvs.at[first + h]) for h in range(counts[s])])

    x_ag = [gather(xs, x_s, x_r, CUT_TOKENS, s) for s in range(mb)]
    c_ag = [gather(gs, c_s, c_r, CUT_COTANGENT, s) for s in range(mb)]
    copies = [
        pltpu.make_async_copy(rq_ref, raw_q, local.at[0]),
        pltpu.make_async_copy(ru_ref, raw_u, local.at[9]),
        pltpu.make_async_copy(vec_ref, vecs.at[at.dp, at.c], local.at[1]),
        pltpu.make_async_copy(wd_ref, wdo.at[at.dp, pl.ds(0, rows_d)], local.at[2]),
        pltpu.make_async_copy(seg_ref, seg_i, local.at[3]),
        pltpu.make_async_copy(cos_ref, cos_t, local.at[4]),
        pltpu.make_async_copy(sin_ref, sin_t, local.at[5]),
        pltpu.make_async_copy(tok_ref, raw_t, local.at[6]),
        pltpu.make_async_copy(cot_ref, raw_c, local.at[7]),
    ]
    out_rows = remote(wo_ref, wdo.at[at.rows_dp, pl.ds(rows_d, rows_w)], o1s, o1r, at.rows_dp, at.rows_c)
    out_mine = remote(wo_ref, wdo.at[at.dp, pl.ds(rows_d, rows_w)], o1s, o1r, at.rows_dp, at.rows_c)
    own_out = pltpu.make_async_copy(wo_ref, wdo.at[at.dp, pl.ds(rows_d, rows_w)], local.at[8])
    for copy in copies:
        copy.start()
    vec1.start()

    @pl.when(at.moves)
    def _():
        out_rows.start()

    @pl.when(jnp.logical_not(at.moves))
    def _():
        own_out.start()

    copies[0].wait()
    copies[1].wait()
    for p in range(n):
        for part_ in range(3):
            wp_st[p, :, part_ * 128 : (part_ + 1) * 128] = raw_q[:, part_ * width + p * 128 : part_ * width + (p + 1) * 128]
        for d in range(ndp):
            wp_st[p, :, 384 + d * rows_d : 384 + (d + 1) * rows_d] = raw_u[:, (d * n + p) * rows_d : (d * n + p + 1) * rows_d]
    cols.start()
    ws[at.dp, at.c] = wp_st[at.c]
    for copy in copies[2:]:
        copy.wait()
    for s in range(mb):
        xs[s, own_rows] = raw_t[:, s, :]
        gs[s, own_rows] = raw_c[:, s, :]
    segs[...] = jnp.zeros_like(segs)
    segs[0:mb] = seg_i[...]
    cols.wait_recv()
    plane_w.start()
    x_ag[0].start()
    vec1.wait_recv()
    plane_v.start()
    x_ag[0].step(1)
    plane_w.forward()
    x_ag[0].step(2)
    c_ag[0].start()

    @pl.when(at.moves)
    def _():
        out_mine.wait_recv()

    @pl.when(jnp.logical_not(at.moves))
    def _():
        own_out.wait()

    plane_d.start()
    plane_v.wait_recv()

    lane = lax.broadcasted_iota(jnp.int32, (16, 128), 1)
    per = 128 // rows_w
    for q in range(width // 128):
        piece = vecs[(per * q) // n, (per * q) % n]
        for u in range(1, per):
            d = per * q + u
            piece = jnp.where(lane >= u * rows_w, vecs[d // n, d % n], piece)
        span = pl.ds(q * 128, 128)
        bo[:, span] = piece[3:4] + piece[8:9]
        for ref, r in ((g1, 9), (s1, 10), (g2, 11), (s2, 12)):
            ref[:, span] = piece[r : r + 1]
    lane1 = lax.broadcasted_iota(jnp.int32, (1, 128), 1)
    for d in range(ndp):
        rows = vecs[d, at.c]
        piece = rows[4:5]
        for u in range(1, per):
            piece = jnp.where(lane1 >= u * rows_w, rows[4 + u : 5 + u], piece)
        bu[:, pl.ds(d * 128, 128)] = piece
    for p in range(3):
        piece = None
        for u in range(per):
            t = (p * width + at.c * 128) // rows_w + u
            d, r = t // 3, lax.rem(t, 3)
            rows = vecs[d // n, lax.rem(d, n)]
            row = jnp.where(r == 0, rows[0:1], jnp.where(r == 1, rows[1:2], rows[2:3]))
            piece = row if piece is None else jnp.where(lane1 >= u * rows_w, row, piece)
        bq[:, pl.ds(p * 128, 128)] = piece
    seg_t = jnp.transpose(segs[...])
    seg_col[...] = jnp.where(seg_t == 0.0, -1.0, seg_t)

    lanes = lax.broadcasted_iota(jnp.int32, (1, 128), 1)
    in_head = [(lanes >= h * HEAD) & (lanes < (h + 1) * HEAD) for h in range(heads)]
    low_half = (lanes & (HEAD - 1)) < ROT // 2
    w_q = lambda: ws[:, :, :, :384].reshape(width, 384)
    w_u = lambda: ws[:, :, :, 384:].reshape(width, fu)
    w_d = lambda: wdo[:, 0:rows_d].reshape(fu, width)
    w_o = lambda: wdo[:, rows_d:].reshape(128, width)

    def rows_of(i):
        return pl.ds(pl.multiple_of(i * block, block), block)

    def turn(u, rows, sign):
        turned = jnp.where(low_half, pltpu.roll(u, 128 - ROT // 2, 1), pltpu.roll(u, ROT // 2, 1))
        if sign > 0:
            return u * cos_t[rows] + turned * sin_t[rows]
        return u * cos_t[rows] - turned * sin_t[rows]

    def normed_of(s, rows):
        return (xs[s, rows].astype(F32) - stat[s, rows, 0:1]) * stat[s, rows, 1:2]

    def forward_one(s):
        def body(i):
            rows = rows_of(i)
            x = xs[s, rows].astype(F32)
            mean = jnp.mean(x, axis=-1, keepdims=True)
            cen = x - mean
            rstd = lax.rsqrt(jnp.mean(cen * cen, axis=-1, keepdims=True) + 1e-05)
            stat[s, rows, 0:1] = mean
            stat[s, rows, 1:2] = rstd
            nrm = cen * rstd
            h1 = (nrm * g1[...] + s1[...]).astype(BF16)
            h1_all[s, rows] = h1
            joined = dot(h1, w_q()) + bq[...]
            qkv[s, rows, 0:128] = (turn(joined[:, 0:128], rows, 1).astype(BF16).astype(F32) * (HEAD ** (-0.5))).astype(BF16)
            qkv[s, rows, 128:256] = turn(joined[:, 128:256], rows, 1).astype(BF16)
            qkv[s, rows, 256:384] = joined[:, 256:384].astype(BF16)
            h2 = (nrm * g2[...] + s2[...]).astype(BF16)
            h2_all[rows] = h2
            act = dot(h2, w_u()) + bu[...]
            cdf = 0.5 + 0.5 * lax.erf(act * (0.5 ** 0.5))
            hid[s, rows] = (act * cdf).astype(BF16)
            gp[rows] = (cdf + act * (jnp.exp(-0.5 * act * act) * 0.3989422804014327)).astype(BF16)

        return body

    def attend(s, i):
        rows = pl.ds(i * block, block)
        keys = (i + 1) * block
        q_pos = lax.broadcasted_iota(jnp.int32, (block, keys), 0) + i * block
        k_pos = lax.broadcasted_iota(jnp.int32, (block, keys), 1)
        same = segs[s : s + 1, 0:keys] == seg_col[rows, s : s + 1]
        allow = (same & (k_pos <= q_pos)) | (k_pos == q_pos)
        q, k, v = qkv[s, rows, 0:128], qkv[s, 0:keys, 128:256], qkv[s, 0:keys, 256:384]
        out = None
        for h in range(heads):
            scores = dot(jnp.where(in_head[h], q, jnp.zeros_like(q)), k, NT)
            scores = jnp.where(allow, scores, -1e30)
            e = jnp.exp(scores - jnp.max(scores, axis=-1, keepdims=True))
            p = (e * (1.0 / jnp.sum(e, axis=-1, keepdims=True))).astype(BF16)
            probs[i][h] = p
            o = dot(p, v)
            out = o if out is None else jnp.where(in_head[h], o, out)
        ctx[s, rows] = out.astype(BF16)

    def project(s):
        def body(i):
            rows = rows_of(i)
            both = dot(ctx[s, rows], w_o()) + dot(hid[s, rows], w_d())
            part[s, rows] = both.astype(BF16)

        return body

    def fold(ref, row, value):
        count, cols_ = value.shape
        ref[row, :, 0:cols_] += jnp.sum(value.reshape(count // 8, 8, cols_), axis=0)

    def backward_ffn(s):
        def body(i):
            rows = rows_of(i)
            g = gs[s, rows]
            dctx[s, rows] = dot(g, w_o(), NT).astype(BF16)
            d_act = (dot(g, w_d(), NT) * gp[rows].astype(F32)).astype(BF16)
            gp[rows] = d_act
            fold(acc_gain, 4, g.astype(F32))
            fold(acc_bu, 0, d_act.astype(F32))
            d_h = dot(d_act, w_u(), NT)
            fold(acc_gain, 2, d_h * normed_of(s, rows))
            fold(acc_gain, 3, d_h)
            ep[s, rows] = (d_h * g2[...]).astype(BF16)

        return body

    def attend_back(s, i):
        rows = pl.ds(i * block, block)
        keys = (i + 1) * block
        span = pl.ds(0, keys)
        q, k, v = qkv[s, rows, 0:128], qkv[s, span, 128:256], qkv[s, span, 256:384]
        d_c = dctx[s, rows]
        zero = jnp.zeros_like(q)
        d_q = None
        for h in range(heads):
            p = probs[i][h]
            d_h = jnp.where(in_head[h], d_c, zero)
            d_p = dot(d_h, v, NT)
            p_f = p.astype(F32)
            delta = jnp.sum(p_f * d_p, axis=-1, keepdims=True)
            d_s = (p_f * (d_p - delta)).astype(BF16)
            o = dot(d_s, k)
            d_q = o if d_q is None else jnp.where(in_head[h], o, d_q)
            d_k = dot(jnp.where(in_head[h], q, zero), d_s, TN)
            d_v = dot(d_h, p, TN)
            if i == nz - 1 and h == 0:
                dk[...] = d_k
                dv[...] = d_v
            else:
                dk[:, span] += d_k
                dv[:, span] += d_v
        d_q = turn(d_q, rows, -1) * (HEAD ** (-0.5))
        d_k, d_v = jnp.transpose(dk[:, rows]), jnp.transpose(dv[:, rows])
        d_all = jnp.concatenate([d_q, turn(d_k, rows, -1), d_v], axis=1).astype(BF16)
        dqkv[s, rows] = d_all
        fold(acc_bq, 0, d_all.astype(F32))
        d_n = dot(d_all, w_q(), NT)
        fold(acc_gain, 0, d_n * normed_of(s, rows))
        fold(acc_gain, 1, d_n)
        ep[s, rows] = (d_n * g1[...] + ep[s, rows].astype(F32)).astype(BF16)

    def put(ref, rows, s, total):
        if s:
            total = total + ref[rows].astype(F32).reshape(total.shape)
        ref[rows] = total.astype(BF16).reshape(ref[rows].shape)

    def weight_cols(s, out, left, right):
        def body(kt):
            feat = pl.ds(pl.multiple_of(kt * 256, 256), 256)
            put(out, feat, s, dot(left[:, feat], right[...], TN))

        return body

    acc_gain[...] = jnp.zeros_like(acc_gain)
    acc_bu[...] = jnp.zeros_like(acc_bu)
    acc_bq[...] = jnp.zeros_like(acc_bq)

    def scatter(part_, sib_, in_, sems_, counts, s):
        size, first = tok // counts[s], sum(counts[:s])
        return ScatterPieces([SeqScatter(at, part_.at[s], sib_.at[s], in_.at[s], tok, h * size, size, [r.at[first + h] for r in sems_]) for h in range(counts[s])])

    m_rs = [scatter(part, m_sib, m_in, (ms_s, ms_r, mu_s, mu_r, md_s, md_r), CUT_MIXED, s) for s in range(mb)]
    t_rs = [scatter(ep, t_sib, t_in, (ts_s, ts_r, tu_s, tu_r, td_s, td_r), CUT_GRAD, s) for s in range(mb)]
    rows_p = n * rows_w

    def col_halves(ref):
        return lambda p, h: ref.at[pl.ds(pl.multiple_of(p * rows_p + h * (rows_p // 2), rows_p // 2), rows_p // 2)]

    def halves(ref, i, size):
        return lambda h: ref.at[i, pl.ds(h * size, size)]

    half = rows_p // 2
    wq1 = PlaneReduce(at, col_halves(dwq), q_via.at[0], q_via.at[1], halves(q_from, 0, half), halves(q_from, 1, half), gq1s, gq1r)
    wu1 = PlaneReduce(at, col_halves(dwu), u_via.at[0], u_via.at[1], halves(u_from, 0, half), halves(u_from, 1, half), gu1s, gu1r)
    half_do = rows_do // 2
    wd1 = PlaneReduce(at, lambda p, h: dwdo.at[p, pl.ds(h * half_do, half_do)], d_via.at[0], d_via.at[1],
                      halves(d_from, 0, half_do), halves(d_from, 1, half_do), gd_s, gd_r)
    gv1 = Exchange(at, "dp", lambda p: vsum, lambda s: vin.at[s], gv1s, gv1r)
    wq2 = Exchange(at, "ctx", lambda p: wq_st.at[p], lambda s: wq_rx.at[s], gq2s, gq2r)
    wu2 = Exchange(at, "ctx", lambda p: wu_st.at[p], lambda s: wu_rx.at[s], gu2s, gu2r)
    gv2 = Exchange(at, "ctx", lambda p: v_st.at[p], lambda s: v_rx.at[s], gv2s, gv2r)
    out_back = remote(dwo_st, dwo_out, go2s, go2r, at.from_dp, at.from_c)

    def columns_on(first_hop, second_hop, stage, out):
        for h in (0, 1):
            total = first_hop.total(h).astype(BF16)
            stage[pl.ds(h * (n // 2), n // 2)] = total.reshape((n // 2,) + stage.shape[1:])
        second_hop.start()
        out[at.c] = stage[at.c]

    def down_out():
        low, high = wd1.total(0), wd1.total(1)
        dwd_out[pl.ds(0, half_do)] = low
        dwd_out[pl.ds(half_do, rows_d - half_do)] = high[0 : rows_d - half_do]
        rows = high[rows_d - half_do :].astype(BF16)

        @pl.when(at.moves)
        def _():
            dwo_st[...] = rows
            out_back.start()

        @pl.when(jnp.logical_not(at.moves))
        def _():
            dwo_out[...] = rows

    def vectors_out():
        mine = v_rx[at.c]
        index = at.dp * n + at.c
        start = index * (3 * rows_w)
        shift, tile = lax.rem(start, 128), start // 128

        def tile_of(t):
            rows = v_rx[lax.rem(t, n)]
            third = t // n
            return jnp.where(third == 0, rows[8:9], jnp.where(third == 1, rows[9:10], rows[10:11]))

        low, high = tile_of(tile), tile_of(jnp.minimum(tile + 1, 3 * n - 1))
        both = low
        for u in range(1, 128 // rows_w):
            off = u * rows_w
            moved = jnp.where(lane1 < 128 - off, pltpu.roll(low, 128 - off, 1), pltpu.roll(high, 128 - off, 1))
            both = jnp.where(shift == off, moved, both)
        place = lax.rem(index * rows_w, 128)
        base = v_rx[0, 0:8]
        for p in range(1, n):
            base = base + v_rx[p, 0:8]
        row = lax.broadcasted_iota(jnp.int32, (8, 128), 0)
        base = jnp.where(row < 6, base, mine[0:8])
        out = base
        for u in range(1, 128 // rows_w):
            out = jnp.where(place == u * rows_w, pltpu.roll(base, 128 - u * rows_w, 1), out)
        vec_out[...] = out
        vec_out[0:1] = both
        vec_out[1:2] = mine[11:12]
        vec_out[7:8] = out[6:7]

    def starts(rs, zs):
        def event():
            for z in zs:
                rs.cross(z).start()

        return event

    def finish_mixed(s):
        m_rs[s].total(own)
        mixed_out[:, s, :] = (xs[s, own_rows].astype(F32) + own[...] + bo[...]).astype(BF16)

    def finish_grad(s):
        t_rs[s].total(own)
        e = own[...]
        nrm = normed_of(s, own_rows)
        inner = e - jnp.mean(e, axis=-1, keepdims=True) - nrm * jnp.mean(e * nrm, axis=-1, keepdims=True)
        grad_out[:, s, :] = (gs[s, own_rows].astype(F32) + stat[s, own_rows, 1:2] * inner).astype(BF16)

    def down_rows(s):
        def body(kt):
            feat = pl.ds(pl.multiple_of(kt * 256, 256), 256)
            total = dot(hid[s, :, feat], gs[s], TN).reshape(256 // rows_d, rows_d, width)
            mine = dwdo.at[pl.ds(kt * (256 // rows_d), 256 // rows_d), pl.ds(0, rows_d)]
            if s:
                total = total + mine[...].astype(F32)
            mine[...] = total.astype(BF16)

        return body

    def out_grad(s):
        total = dot(ctx[s], gs[s], TN).reshape(ndp, rows_w, width)
        mine = dwdo.at[:, pl.ds(rows_d, rows_w)]
        if s:
            total = total + mine[...].astype(F32)
        mine[...] = total.astype(BF16)

    x_ag[0].step(3)
    plane_w.land()
    x_ag[0].land()
    blocks(nz, forward_one(0), {3: [lambda: c_ag[0].step(1), x_ag[1].start]})
    plane_d.forward()
    for i in range(nz):
        attend(0, i)
    c_ag[0].step(2)
    plane_d.land()
    blocks(nz, project(0))
    starts(m_rs[0], range(nz))()
    m_rs[0].step(0)
    back = backward_ffn(0)
    c_ag[0].take(0, back)
    x_ag[1].step(1)
    c_ag[1].start()
    c_ag[0].take(1, back)
    c_ag[0].take(2, back)
    c_ag[0].step(3)
    c_ag[0].take(3, back)
    m_rs[0].step(1)
    for i in reversed(range(nz)):
        attend_back(0, i)
        t_rs[0].cross(i).start()
        if i == 3:
            x_ag[1].step(2)
    t_rs[0].lead()
    blocks(width // 256, weight_cols(0, dwu, h2_all, gp))
    m_rs[0].step(2)
    ahead = forward_one(1)
    x_ag[1].take(0, ahead)
    c_ag[1].step(1)
    x_ag[1].take(1, ahead)
    x_ag[1].take(2, ahead)
    x_ag[1].step(3)
    x_ag[1].take(3, ahead)
    t_rs[0].follow(1)
    for i in range(nz):
        attend(1, i)
        if i == 2:
            c_ag[1].step(2)
    blocks(nz, project(1))
    starts(m_rs[1], range(nz))()
    m_rs[1].lead()
    t_rs[0].follow(2)
    blocks(width // 256, weight_cols(0, dwq, h1_all.at[0], dqkv.at[0]))
    blocks(fu // 256, down_rows(0))
    out_grad(0)
    back = backward_ffn(1)
    c_ag[1].take(0, back)
    c_ag[1].take(1, back)
    m_rs[1].follow(1)
    c_ag[1].take(2, back)
    c_ag[1].step(3)
    c_ag[1].take(3, back)
    blocks(width // 256, weight_cols(1, dwu, h2_all, gp))
    wu1.start()
    for i in reversed(range(nz)):
        attend_back(1, i)
        t_rs[1].cross(i).start()
        if i < nz - 1:
            t_rs[1].lead_up(nz - 2 - i)
        if i == 1:
            wu1.combine()
    for t in range(nz - 1):
        t_rs[1].lead_down(t)
    m_rs[1].follow(2)
    blocks(width // 256, weight_cols(1, dwq, h1_all.at[1], dqkv.at[1]))
    wq1.start()
    vsum[...] = jnp.zeros_like(vsum)
    vsum[0:1, 0:384] = jnp.sum(acc_bq[0], axis=0, keepdims=True)
    vsum[1:2, 0:fu] = jnp.sum(acc_bu[0], axis=0, keepdims=True)
    for r in range(5):
        vsum[2 + r : 3 + r] = jnp.sum(acc_gain[r], axis=0, keepdims=True)
    gv1.start()
    columns_on(wu1, wu2, wu_st, wu_rx)
    blocks(fu // 256, down_rows(1))
    out_grad(1)
    t_rs[1].follow(1)
    wq1.combine()
    wd1.start()
    finish_mixed(0)
    finish_mixed(1)
    finish_grad(0)
    columns_on(wq1, wq2, wq_st, wq_rx)
    t_rs[1].follow(2)
    gv1.wait_recv()
    total = vsum[...]
    for j in range(1, ndp):
        total = total + vin[lax.rem(at.dp + j, ndp)]
    vsum_all[...] = total
    for p in range(n):
        v_st[p, 0:8] = vsum_all[:, pl.ds(pl.multiple_of((at.dp * n + p) * rows_w // 128 * 128, 128), 128)]
        for r in range(3):
            v_st[p, 8 + r : 9 + r] = total[0:1, r * 128 : (r + 1) * 128]
        v_st[p, 11:12] = vsum_all[1:2, pl.ds(pl.multiple_of(at.dp * rows_d, 128), 128)]
        v_st[p, 12:16] = jnp.zeros((4, 128), F32)
    gv2.start()
    v_rx[at.c] = v_st[at.c]
    wd1.combine()
    finish_grad(1)
    down_out()

    @pl.when(at.moves)
    def _():
        out_rows.wait_send()
        out_back.wait()

    wu2.wait_recv()
    for p in range(n):
        for d in range(ndp):
            up_out[:, (d * n + p) * rows_d : (d * n + p + 1) * rows_d] = wu_rx[p, :, d * rows_d : (d + 1) * rows_d]
    gv2.wait_recv()
    vectors_out()
    wq2.wait_recv()
    for p in range(n):
        for part_ in range(3):
            qkv_out[:, part_ * width + p * 128 : part_ * width + (p + 1) * 128] = wq_rx[p, :, part_ * 128 : (part_ + 1) * 128]
    for part_ in (cols, vec1, plane_v, gv1, wq2, wu2, gv2):
        part_.wait_send()
    for part_ in (plane_w, plane_d, wq1, wu1, wd1):
        part_.drain()
    for s in range(mb):
        x_ag[s].drain()
        c_ag[s].drain()
        m_rs[s].drain()
        t_rs[s].drain()


def fused_layer(ndp, n, dims, tok, cot, rq, ru, wd, wo, vec, seg, cosine, sine):
    mb, tk, width, seq, heads, rows_w, rows_d = dims
    nz, block, fu = n // 2, 2 * tk, ndp * rows_d
    rows_do, rows_p = rows_d + rows_w, n * rows_w
    dma = pltpu.SemaphoreType.DMA
    vm = pltpu.VMEM
    vmem = pl.BlockSpec(memory_space=pltpu.VMEM)
    slots = gather_slots(nz)
    scratch = [
        vm((mb, seq, width), BF16), vm((mb, seq, width), BF16),
        vm((ndp, n, rows_w, 384 + fu), BF16), vm((ndp, rows_d + rows_w, width), BF16),
        vm((ndp, n, 16, 128), F32), vm((8, seq), F32), vm((seq, 8), F32), vm((seq, 128), F32), vm((seq, 128), F32),
        vm((1, width), F32), vm((1, width), F32), vm((1, width), F32), vm((1, width), F32), vm((1, width), F32),
        vm((1, 384), F32), vm((1, fu), F32),
        vm((mb, seq, 384), BF16), vm((mb, seq, fu), BF16), vm((seq, fu), BF16), vm((mb, seq, 2), F32),
        vm((mb, seq, 128), BF16), vm((mb, seq, width), BF16), vm((mb, seq, width), BF16),
        vm((mb, seq, 128), BF16), vm((mb, seq, 384), BF16), vm((128, seq), F32), vm((128, seq), F32),
        vm((5, 8, width), F32), vm((1, 8, fu), F32), vm((1, 8, 384), F32),
        vm((mb, nz, tk, width), BF16), vm((mb, nz + 1, tk, width), BF16), vm((mb, nz, tk, width), BF16), vm((mb, nz + 1, tk, width), BF16),
        vm((width, 384), BF16), vm((width, fu), BF16), vm((ndp, rows_do, width), BF16),
        vm((2, rows_p // 2, 384), BF16), vm((2, rows_p, 384), BF16), vm((2, rows_p // 2, fu), BF16), vm((2, rows_p, fu), BF16),
        vm((2, rows_do // 2, width), BF16), vm((2, rows_do, width), BF16),
        vm((8, width), F32), vm((ndp, 8, width), F32), vm((n, rows_w, 384), BF16), vm((n, rows_w, fu), BF16),
        vm((tk, width), F32), vm((rows_w, width), BF16),
        vm((8, width), F32), vm((n, 16, 128), F32),
        vm((mb, seq), F32), vm((n, rows_w, 384 + fu), BF16),
        vm((n, rows_w, 384), BF16), vm((n, rows_w, fu), BF16), vm((n, 16, 128), F32),
        vm((mb, seq, width), BF16), vm((seq, width), BF16),
    ] + [vm((heads, block, block * (i + 1)), BF16) for i in range(nz)]
    per_seq = [dma((sum(cuts), size)) for cuts in (CUT_TOKENS, CUT_COTANGENT) for size in (3 * nz - 2, n)]
    to_ctx, to_dp, plane = [dma((n,))] * 2, [dma((ndp,))] * 2, [dma((6,))] * 2
    sems = per_seq + to_ctx + plane + to_ctx + to_dp + plane + [dma, dma]
    sems += [dma((sum(CUT_MIXED), nz))] * 6 + [dma((sum(CUT_GRAD), nz))] * 6
    sems += (plane + to_ctx) * 2 + plane + [dma, dma] + to_dp + to_ctx + [dma((10,))]
    return pl.pallas_call(
        partial(fused_kernel, ndp, n, dims),
        out_shape=(
            jax.ShapeDtypeStruct((tk, mb, width), BF16),
            jax.ShapeDtypeStruct((tk, mb, width), BF16),
            jax.ShapeDtypeStruct((rows_w, 3 * width), BF16),
            jax.ShapeDtypeStruct((rows_w, n * fu), BF16),
            jax.ShapeDtypeStruct((rows_d, width), F32),
            jax.ShapeDtypeStruct((rows_w, width), BF16),
            jax.ShapeDtypeStruct((8, 128), F32),
        ),
        in_specs=[ANY] * 10,
        out_specs=[vmem] * 7,
        scratch_shapes=scratch + sems,
        compiler_params=pltpu.CompilerParams(collective_id=5, has_side_effects=True, vmem_limit_bytes=63 * MIB),
    )(tok, cot, rq, ru, wd, wo, vec, seg, cosine, sine)


def rotary_lanes(seq):
    half = ROT // 2
    inverse = (np.float32(10000.0) ** (-(np.float32(2.0) * np.arange(half, dtype=np.float32)) / np.float32(ROT))).astype(np.float32)
    angles = (np.arange(seq, dtype=np.float32)[:, None] * inverse[None, :]).astype(np.float32)
    cosine = np.ones((seq, HEAD), np.float32)
    sine = np.zeros((seq, HEAD), np.float32)
    cosine[:, :half] = cosine[:, half:ROT] = np.cos(angles)
    sine[:, :half] = -np.sin(angles)
    sine[:, half:ROT] = np.sin(angles)
    return np.tile(cosine, (1, 128 // HEAD)), np.tile(sine, (1, 128 // HEAD))


def fused_device(ndp, n, tokens, cotangent, segments, w_qkv, b_qkv, w_out, b_out, w_up, b_up, w_down, b_down, g1, s1, g2, s2):
    tok, mb, width = tokens.shape
    seq = segments.shape[1]
    hc = width // n
    rows_w, rows_d = w_qkv.shape[0], w_down.shape[0]
    seg_f = segments.astype(F32)
    seg_f, small = lax.optimization_barrier((seg_f, (b_qkv, b_out, b_up, b_down, g1, s1, g2, s2)))
    units = jnp.concatenate(small).astype(F32).reshape(-1, rows_w)
    vec = jnp.pad(jnp.tile(units, (1, 128 // rows_w)), ((0, 16 - units.shape[0]), (0, 0)))
    cosine, sine = rotary_lanes(seq)
    dims = (mb, tok, width, seq, hc // HEAD, rows_w, rows_d)
    mixed, t_grad, d_qkv, d_up, dwd, dwo, dv = fused_layer(
        ndp, n, dims, tokens, cotangent, w_qkv, w_up, w_down, w_out, vec, seg_f, jnp.asarray(cosine), jnp.asarray(sine)
    )
    one = lambda r: dv[r, :rows_w]
    return (
        mixed,
        t_grad,
        d_qkv.astype(F32),
        dv[0, : b_qkv.shape[0]],
        dwo.astype(F32),
        one(6),
        d_up.astype(F32),
        dv[1, :rows_d],
        dwd,
        one(7),
        one(2),
        one(3),
        one(4),
        one(5),
    )


def rotary_tables(seq):
    half_rot = ROT // 2
    inverse = 10000.0 ** (-(2.0 * jnp.arange(half_rot, dtype=F32)) / ROT)
    angles = jnp.arange(seq, dtype=jnp.int32).astype(F32)[:, None] * inverse[None, :]
    angles = jnp.concatenate([angles, angles], axis=-1)
    return (jnp.cos(angles)[None, :, None, :], jnp.sin(angles)[None, :, None, :])


def rotate(values, cosine, sine, back=False):
    half_rot = ROT // 2
    lead = values[..., :ROT]
    if back:
        u = lead * sine
        turned = jnp.concatenate([u[..., half_rot:], -u[..., :half_rot]], axis=-1)
        return jnp.concatenate([lead * cosine + turned, values[..., ROT:]], axis=-1)
    turned = jnp.concatenate([-lead[..., half_rot:], lead[..., :half_rot]], axis=-1)
    return jnp.concatenate([lead * cosine + turned * sine, values[..., ROT:]], axis=-1)


def per_device(ndp, n, tokens, cotangent, segments, w_qkv, b_qkv, w_out, b_out, w_up, b_up, w_down, b_down, g1, s1, g2, s2):
    tok, mb, width = tokens.shape
    seq = segments.shape[1]
    heads_all = width // HEAD
    hc = width // n
    heads = hc // HEAD
    rows_w = w_qkv.shape[0]
    rows_d = w_down.shape[0]
    fu = ndp * rows_d
    c = lax.axis_index("ctx")
    dp = lax.axis_index("dp")
    scale = HEAD ** (-0.5)

    cot = jnp.transpose(cotangent, (1, 0, 2))
    toks = jnp.transpose(tokens, (1, 0, 2))
    qkv_cols = w_qkv.reshape(rows_w, 3, n, hc).transpose(2, 0, 1, 3).reshape(n, rows_w, 3 * hc)
    up_cols = w_up.reshape(rows_w, ndp, n, rows_d).transpose(2, 0, 1, 3).reshape(n, rows_w, fu)
    wp = jnp.concatenate([qkv_cols, up_cols], axis=2)
    shard_vecs = (b_qkv, b_out, b_up, b_down, g1, s1, g2, s2)
    sizes = [v.shape[0] for v in shard_vecs]
    vec = jnp.concatenate(shard_vecs)
    lanes = 128
    per_vec = 16 * lanes
    vec = jnp.pad(vec, (0, per_vec - vec.shape[0])).reshape(16, lanes)
    x, g, w, wd, wo, vecs = gather_all(ndp, n, toks, cot, wp, w_down, w_out, vec)
    w = w.reshape(width, 3 * hc + fu)
    wq, wu = w[:, : 3 * hc], w[:, 3 * hc :]
    wd = wd.reshape(fu, width)
    wo = wo.reshape(hc, width)
    flat = vecs.reshape(ndp * n, per_vec).astype(F32)
    starts = [sum(sizes[:i]) for i in range(len(sizes))]
    full = [flat[:, s : s + z].reshape(-1) for s, z in zip(starts, sizes)]
    bq_all, bo, bu_all, bd, gain1, shift1, gain2, shift2 = full
    bq = lax.dynamic_index_in_dim(bq_all.reshape(3, n, hc), c, 1, keepdims=False).reshape(3 * hc)
    bu = lax.dynamic_index_in_dim(bu_all.reshape(ndp, n, rows_d), c, 1, keepdims=False).reshape(fu)

    xf = x.reshape(mb * seq, width).astype(F32)
    gl = g.reshape(mb * seq, width)
    mean = jnp.mean(xf, axis=-1, keepdims=True)
    cen = xf - mean
    rstd = lax.rsqrt(jnp.mean(cen * cen, axis=-1, keepdims=True) + 1e-05)
    normed = cen * rstd
    h1 = (normed * gain1 + shift1).astype(BF16)
    h2 = (normed * gain2 + shift2).astype(BF16)
    joined = (dot(h1, wq) + bq).reshape(mb, seq, 3, heads, HEAD)
    cosine, sine = rotary_tables(seq)
    q = rotate(joined[:, :, 0], cosine, sine).astype(BF16)
    k = rotate(joined[:, :, 1], cosine, sine).astype(BF16)
    v = joined[:, :, 2].astype(BF16)
    pos = jnp.arange(seq, dtype=jnp.int32)
    same = (segments[:, None, :] == segments[:, :, None]) & (segments[:, :, None] > 0)
    allow = (same & (pos[None, None, :] <= pos[None, :, None])) | (pos[None, None, :] == pos[None, :, None])
    scores = jnp.einsum("sqhd,skhd->shqk", q, k, preferred_element_type=F32) * scale
    scores = jnp.where(allow[:, None], scores, -1e30)
    top = jnp.max(scores, axis=-1, keepdims=True)
    e = jnp.exp(scores - top)
    probs = e / jnp.sum(e, axis=-1, keepdims=True)
    pl_low = probs.astype(BF16)
    ctx_f = jnp.einsum("shqk,skhd->sqhd", pl_low, v, preferred_element_type=F32)
    ctx = ctx_f.astype(BF16).reshape(mb * seq, hc)
    act = dot(h2, wu) + bu
    hidden = jax.nn.gelu(act, approximate=False).astype(BF16)
    part = (dot(ctx, wo) + dot(hidden, wd)).astype(BF16).reshape(mb, seq, width)
    mixed_sum = scatter_ctx(ndp, n, part, 1)
    mixed = (toks.astype(F32) + mixed_sum + bo + bd).astype(BF16)

    gf = gl.astype(F32)
    d_wd = dot(hidden, gl, ((0,), (0,)))
    d_wo = dot(ctx, gl, ((0,), (0,)))
    d_hidden = dot(gl, wd, ((1,), (1,)))
    _, pull = jax.vjp(partial(jax.nn.gelu, approximate=False), act)
    d_act = pull(d_hidden)[0].astype(BF16)
    d_wu = dot(h2, d_act, ((0,), (0,)))
    d_bu = jnp.sum(d_act.astype(F32), axis=0)
    d_h2 = dot(d_act, wu, ((1,), (1,)))
    d_ctx = dot(gl, wo, ((1,), (1,))).astype(BF16).reshape(mb, seq, heads, HEAD)
    d_probs = jnp.einsum("sqhd,skhd->shqk", d_ctx, v, preferred_element_type=F32)
    delta = jnp.sum(probs * d_probs, axis=-1, keepdims=True)
    d_scores = jnp.where(allow[:, None], probs * (d_probs - delta), 0.0).astype(BF16)
    d_q = jnp.einsum("shqk,skhd->sqhd", d_scores, k, preferred_element_type=F32) * scale
    d_k = jnp.einsum("shqk,sqhd->skhd", d_scores, q, preferred_element_type=F32) * scale
    d_v = jnp.einsum("shqk,sqhd->skhd", pl_low, d_ctx, preferred_element_type=F32)
    d_q = rotate(d_q, cosine, sine, True)
    d_k = rotate(d_k, cosine, sine, True)
    d_qkv = jnp.stack([d_q, d_k, d_v], axis=2).astype(BF16).reshape(mb * seq, 3 * hc)
    d_wq = dot(h1, d_qkv, ((0,), (0,)))
    d_bq = jnp.sum(d_qkv.astype(F32), axis=0)
    d_h1 = dot(d_qkv, wq, ((1,), (1,)))
    e_sum = (d_h1 * gain1 + d_h2 * gain2).astype(BF16).reshape(mb, seq, width)
    e_own = scatter_ctx(ndp, n, e_sum, 2)
    own_x = toks.astype(F32)
    o_mean = jnp.mean(own_x, axis=-1, keepdims=True)
    o_cen = own_x - o_mean
    o_rstd = lax.rsqrt(jnp.mean(o_cen * o_cen, axis=-1, keepdims=True) + 1e-05)
    o_n = o_cen * o_rstd
    t_grad = o_rstd * (e_own - jnp.mean(e_own, axis=-1, keepdims=True) - o_n * jnp.mean(e_own * o_n, axis=-1, keepdims=True))
    tokens_grad = (cot.astype(F32) + t_grad).astype(BF16)

    rows = [
        jnp.pad(d_bq, (0, width - 3 * hc)),
        jnp.pad(d_bu, (0, width - fu)),
        jnp.sum(d_h1 * normed, axis=0),
        jnp.sum(d_h1, axis=0),
        jnp.sum(d_h2 * normed, axis=0),
        jnp.sum(d_h2, axis=0),
        jnp.sum(gf, axis=0),
        jnp.zeros((width,), F32),
    ]
    dwp = jnp.concatenate([d_wq, d_wu], axis=1).astype(BF16).reshape(ndp, n, rows_w, 3 * hc + fu)
    dw, dwd, dwo, dv = grads_all(
        ndp, n, dwp, d_wd.astype(BF16).reshape(ndp, rows_d, width), d_wo.astype(BF16).reshape(ndp, rows_w, width), jnp.stack(rows)
    )
    index = dp * n + c
    g_qkv = dw[:, :, : 3 * hc].reshape(n, rows_w, 3, hc).transpose(1, 2, 0, 3).reshape(rows_w, 3 * width).astype(F32)
    g_up = dw[:, :, 3 * hc :].reshape(n, rows_w, ndp, rows_d).transpose(1, 2, 0, 3).reshape(rows_w, -1).astype(F32)
    g_bq = lax.dynamic_slice_in_dim(dv[:, 0, : 3 * hc].reshape(n, 3, hc).transpose(1, 0, 2).reshape(-1), index * sizes[0], sizes[0])
    own = lax.dynamic_index_in_dim(dv, c, 0, keepdims=False)
    g_bu = lax.dynamic_slice_in_dim(own[1], dp * rows_d, rows_d)
    four = lax.dynamic_slice_in_dim(jnp.sum(dv[:, 2:6], axis=0), index * rows_w, rows_w, axis=1)
    g_b = lax.dynamic_slice_in_dim(own[6], index * rows_w, rows_w)
    return (
        jnp.transpose(mixed, (1, 0, 2)),
        jnp.transpose(tokens_grad, (1, 0, 2)),
        g_qkv,
        g_bq,
        dwo.astype(F32),
        g_b,
        g_up,
        g_bu,
        dwd,
        g_b,
        four[0],
        four[1],
        four[2],
        four[3],
    )


def program(ndp, n, *args):
    tokens, w_qkv, w_down = args[0], args[3], args[9]
    rows_w = w_qkv.shape[0]
    whole_tiles = ndp == 4 and rows_w % 16 == 0 and tokens.shape[2] // n == 128 and w_down.shape[0] == 128 and tokens.shape[0] % 16 == 0
    return (fused_device if whole_tiles else per_device)(ndp, n, *args)


def solution(mesh):
    every = ("dp", "ctx")
    mat, vec, act = P(every, None), P(every), P("ctx", "dp", None)
    placed = (act, act, P("dp", None), mat, vec, mat, vec, mat, vec, mat, vec, vec, vec, vec, vec)
    return jax.shard_map(
        partial(program, mesh.shape["dp"], mesh.shape["ctx"]),
        mesh=mesh,
        in_specs=placed,
        out_specs=(act, act, mat, vec, mat, vec, mat, vec, mat, vec, vec, vec, vec, vec),
        check_vma=False,
    )
```
